32 devices in a mesh: seq: 8 (over y, x, core), head: 4 (over z).
Axes of the slice: x: 2, y: 2, z: 4, core: 2. Of those that a mesh axis runs over, the one named last changes fastest.
Arguments:
- query_new: bfloat16 [1024, 6144], P('seq', 'head'), may hold values from -18 to 18
- key_new: bfloat16 [1024, 6144], P('seq', 'head'), may hold values from -4 to 4
- value_new: bfloat16 [1024, 6144], P('seq', 'head'), may hold values from -6 to 6
- cache_keys: bfloat16 [512, 6144], P(('seq', 'head')), may hold values from -448 to 448
- cache_values: bfloat16 [512, 6144], P(('seq', 'head')), may hold values from -448 to 448
- key_exponent: int32 [128, 48], P(('seq', 'head')), may hold values from -9 to -6
- value_exponent: int32 [128, 48], P(('seq', 'head')), may hold values from -9 to -6
- block_mask: int32 [16, 16], replicated, may hold values 0 or 1
Outputs:
- attended: bfloat16 [1024, 6144], P('seq', 'head')
The draws below stay inside these ranges and needn't reach their ends.
All inputs are finite; a program needn't handle non-finite values.
Results may differ from the reference program's by a relative error of at most 0.0065.
Values may be sent and summed in bfloat16 or wider, within the bound.
No kernel may reach another device: no remote copies, remote signals or barrier semaphores. Data moves between devices by JAX's collectives and lax.ppermute only.
A program may use at most 64 MiB of HBM per device.

```python
import math
import jax
import jax.numpy as jnp
from jax import lax

H = 48
DH = 128
D = 6144
QBLK = 64
CBLK = 32
SBLK = 4
NEW = 1024
CACHE = 512


def draw_query_new(key, part):
    own_key = jax.random.fold_in(key, 11)
    values = jax.random.truncated_normal(own_key, -6.0, 6.0, (NEW, D), jnp.float32)
    return values.astype(jnp.bfloat16)


def draw_key_new(key, part):
    own_key = jax.random.fold_in(key, 13)
    values = jax.random.truncated_normal(own_key, -4.0, 4.0, (NEW, D), jnp.float32)
    return values.astype(jnp.bfloat16)


def with_ends(drawn, key, low, largest):
    spot = [jax.random.randint(jax.random.fold_in(key, axis), (), 0, length) for axis, length in enumerate(drawn.shape)]
    widest = drawn.shape.index(max(drawn.shape))
    beside = spot[:widest] + [(spot[widest] + 1) % drawn.shape[widest]] + spot[widest + 1:]
    return drawn.at[tuple(spot)].set(low).at[tuple(beside)].set(largest)


def block_levels(key, extent, shards, low, top_value):
    loudness = 1.0
    for axis_at, shards_of in shards:
        steps = jax.random.uniform(jax.random.fold_in(jax.random.fold_in(key, 6), axis_at), (shards_of,), jnp.float32, low / len(shards), top_value / len(shards))
        loudness = loudness * jnp.repeat(jnp.exp(steps), extent[axis_at] // shards_of).reshape((-1,) + (1,) * (len(extent) - 1 - axis_at))
    return loudness


def scatter_about(rng, dims, spread, reach, shards=(), kind=jnp.bfloat16):
    values = jax.random.normal(rng, dims, jnp.float32) * spread
    if len(shards) > 0:
        values = block_levels(rng, dims, shards, -0.22, 0.18) * values
    return jnp.clip(values, min=-reach, max=reach).astype(kind)


def setup_inputs(seed: int = 0) -> dict:
    seeds = jax.random.split(jax.random.key(seed), 9)
    return {
        "query_new": draw_query_new(jax.random.fold_in(seeds[8], 71), 0),
        "key_new": draw_key_new(jax.random.fold_in(seeds[8], 71), 0),
        "value_new": scatter_about(seeds[2], (NEW, D), 1.0, 6.0, ((0, 8), (1, 4))),
        "cache_keys": scatter_about(seeds[3], (CACHE, D), 64.0, 448.0, ((0, 32),)),
        "cache_values": scatter_about(seeds[4], (CACHE, D), 64.0, 448.0, ((0, 32),)),
        "key_exponent": with_ends(jax.random.randint(seeds[5], (CACHE // SBLK, H), -9, -5), jax.random.fold_in(seeds[5], 1), -9, (-5) - 1).astype(jnp.int32),
        "value_exponent": with_ends(jax.random.randint(seeds[6], (CACHE // SBLK, H), -9, -5), jax.random.fold_in(seeds[6], 1), -9, (-5) - 1).astype(jnp.int32),
        "block_mask": with_ends((jax.random.randint(seeds[7], (NEW // QBLK, CACHE // CBLK), 0, 4) < 3).astype(jnp.int32), jax.random.fold_in(seeds[7], 1), 0, 1),
    }


def dequantize(mantissa, exponent):
    block_rows = mantissa.shape[0] // SBLK
    factor = jnp.exp2(exponent.astype(jnp.float32))
    scaled = mantissa.astype(jnp.float32).reshape(block_rows, SBLK, H, DH) * factor[:, None, :, None]
    return scaled.reshape(mantissa.shape).astype(jnp.bfloat16)

def reference(query_new, key_new, value_new, cache_keys, cache_values, key_exponent, value_exponent, block_mask):
    keys = jnp.concatenate([dequantize(cache_keys, key_exponent), key_new], axis=0)
    values = jnp.concatenate([dequantize(cache_values, value_exponent), value_new], axis=0)
    cache_allow = jnp.repeat(block_mask, CBLK, axis=1)
    allow_blocks = jnp.concatenate([cache_allow, jnp.ones((NEW // QBLK, NEW), jnp.int32)], axis=1) == 1
    key_count = keys.shape[0]
    rows_blk = min(512, NEW)
    block_count = NEW // rows_blk
    inv_root = 1.0 / math.sqrt(DH)

    def one_block(position):
        head_index = position // block_count
        block_index = position % block_count
        zero_start = jnp.int32(0)
        query_rows = lax.dynamic_slice(query_new, (block_index * rows_blk, head_index * DH), (rows_blk, DH))
        key_head = lax.dynamic_slice(keys, (zero_start, head_index * DH), (key_count, DH))
        value_head = lax.dynamic_slice(values, (zero_start, head_index * DH), (key_count, DH))
        scores = jnp.dot(query_rows, key_head.T, preferred_element_type=jnp.float32) * inv_root
        allowed = lax.dynamic_slice(allow_blocks, (block_index * (rows_blk // QBLK), zero_start), (rows_blk // QBLK, key_count))
        allowed = jnp.repeat(allowed, QBLK, axis=0)
        peak = lax.optimization_barrier(jnp.max(jnp.where(allowed, scores, -jnp.inf), axis=1, keepdims=True))
        raised = jnp.where(allowed, jnp.exp(scores - peak), 0.0)
        total = lax.optimization_barrier(jnp.sum(raised, axis=1, keepdims=True))
        weights = raised.astype(jnp.bfloat16)
        result = jnp.dot(weights, value_head, preferred_element_type=jnp.float32) / total
        return result.astype(jnp.bfloat16)
    results = lax.map(one_block, jnp.arange(H * block_count, dtype=jnp.int32))
    return results.reshape(H, NEW, DH).transpose(1, 0, 2).reshape(NEW, H * DH)
```

```python
import functools
import math

import jax
import jax.numpy as jnp
from jax import lax
from jax.experimental import pallas as pl
from jax.experimental.pallas import tpu as pltpu
from jax.sharding import PartitionSpec as P

DH = 128
QBLK = 64
CBLK = 32
SBLK = 4
MASKED = -1e30


def partner(index, step, count):
    if count & (count - 1) == 0:
        return index ^ step
    return (index + step) % count


def origin(index, step, count):
    if count & (count - 1) == 0:
        return index ^ step
    return (index + count - step) % count


def columns(chunk, width):
    return pl.ds(pl.multiple_of(chunk * width, DH), width)


def run_copies(copies):
    for copy in copies:
        copy.start()
    for copy in copies:
        copy.wait()


def pack_kernel(groups, gather, width, q_ref, k_ref, v_ref, *rest):
    outs, sems = rest[:-1], rest[-1]
    rows = q_ref.shape[0]
    me = lax.axis_index("seq") // gather
    copies = []
    for t in range(groups):
        cols = columns(partner(me, t, groups), width)
        for src, dst in (
            (k_ref, outs[t].at[pl.ds(0, rows)]),
            (v_ref, outs[t].at[pl.ds(rows, rows)]),
            (q_ref, outs[groups + t]),
        ):
            copies.append(pltpu.make_async_copy(src.at[:, cols], dst, sems.at[len(copies)]))
    run_copies(copies)


def pack(q, k, v, groups, gather):
    rows, width = q.shape[0], q.shape[1] // groups
    outs = pl.pallas_call(
        functools.partial(pack_kernel, groups, gather, width),
        out_shape=[jax.ShapeDtypeStruct((2 * rows, width), q.dtype)] * groups
        + [jax.ShapeDtypeStruct((rows, width), q.dtype)] * groups,
        in_specs=[pl.BlockSpec(memory_space=pl.ANY)] * 3,
        out_specs=[pl.BlockSpec(memory_space=pl.ANY)] * (2 * groups),
        scratch_shapes=[pltpu.SemaphoreType.DMA((3 * groups,))],
        cost_estimate=pl.CostEstimate(flops=0, bytes_accessed=6 * q.size * 2, transcendentals=0),
        name="pack_heads",
    )(q, k, v)
    return outs[:groups], outs[groups:]


def dequantize_kernel(heads, parts, ck_ref, cv_ref, ke_ref, ve_ref, *outs):
    blocks, rows = ke_ref.shape[0], ck_ref.shape[0]
    for which, (m_ref, e_ref) in enumerate(((ck_ref, ke_ref), (cv_ref, ve_ref))):
        power = jnp.left_shift(1, e_ref[...] + 16).astype(jnp.float32) * 2.0**-16
        factor = jnp.concatenate(
            [jnp.broadcast_to(power[i : i + 1], (SBLK, heads)) for i in range(blocks)], axis=0
        )
        for h in range(heads):
            part, at = divmod(h * DH, parts)
            scaled = m_ref[:, h * DH : (h + 1) * DH].astype(jnp.float32) * factor[:, h : h + 1]
            outs[0][part, which, :, at : at + DH] = scaled.astype(jnp.bfloat16)


def dequantize(ck, cv, ke, ve, shards):
    rows, width = ck.shape
    return pl.pallas_call(
        functools.partial(dequantize_kernel, width // DH, width // shards),
        out_shape=jax.ShapeDtypeStruct((shards, 2, rows, width // shards), jnp.bfloat16),
        cost_estimate=pl.CostEstimate(flops=2 * ck.size, bytes_accessed=8 * ck.size, transcendentals=0),
        name="dequantize",
    )(ck, cv, ke, ve)


def attend_kernel(groups, gather, heads, *refs):
    pieces = groups * gather
    q_refs, refs = refs[:groups], refs[groups:]
    kv_refs, refs = refs[:pieces], refs[pieces:]
    c_refs, refs = refs[:pieces], refs[pieces:]
    bias_ref, refs = refs[0], refs[1:]
    o_refs, refs = refs[:groups], refs[groups:]
    q_buf, k_buf, v_buf, sems = refs
    rows, cached = q_refs[0].shape[0], c_refs[0].shape[1]
    new_rows = pieces * rows
    copies = []

    def copy(src, dst):
        copies.append(pltpu.make_async_copy(src, dst, sems.at[len(copies)]))

    for i in range(groups):
        copy(q_refs[i], q_buf.at[pl.ds(i * rows, rows)])
    for i in range(pieces):
        copy(kv_refs[i].at[pl.ds(0, rows)], k_buf.at[pl.ds(i * rows, rows)])
        copy(kv_refs[i].at[pl.ds(rows, rows)], v_buf.at[pl.ds(i * rows, rows)])
        at = pl.ds(new_rows + i * cached, cached)
        copy(c_refs[i].at[0], k_buf.at[at])
        copy(c_refs[i].at[1], v_buf.at[at])
    run_copies(copies)

    scale = math.log2(math.e) / math.sqrt(DH)
    blocks = rows // QBLK
    for i in range(groups):
        bias = jnp.concatenate(
            [
                jnp.broadcast_to(
                    bias_ref[i * blocks + j : i * blocks + j + 1], (QBLK, bias_ref.shape[1])
                )
                for j in range(blocks)
            ],
            axis=0,
        )
        for h in range(heads):
            cols = slice(h * DH, (h + 1) * DH)
            q = q_buf[i * rows : (i + 1) * rows, cols]
            scores = lax.dot_general(
                q, k_buf[:, cols], (((1,), (1,)), ((), ())), preferred_element_type=jnp.float32
            )
            fresh = scores[:, :new_rows] * scale
            old = scores[:, new_rows:] * scale + bias
            peak = jnp.maximum(
                jnp.max(fresh, axis=1, keepdims=True), jnp.max(old, axis=1, keepdims=True)
            )
            fresh = jnp.exp2(fresh - peak)
            old = jnp.exp2(old - peak)
            total = jnp.sum(fresh, axis=1, keepdims=True) + jnp.sum(old, axis=1, keepdims=True)
            weights = jnp.concatenate(
                [fresh.astype(jnp.bfloat16), old.astype(jnp.bfloat16)], axis=1
            )
            product = jnp.dot(weights, v_buf[:, cols], preferred_element_type=jnp.float32)
            o_refs[i][:, cols] = (product / total).astype(jnp.bfloat16)


def attend(q, kv, cache, bias, groups, gather, heads):
    pieces = groups * gather
    rows, width = q[0].shape
    keys = pieces * (rows + cache[0].shape[1])
    any_spec = pl.BlockSpec(memory_space=pl.ANY)
    return pl.pallas_call(
        functools.partial(attend_kernel, groups, gather, heads),
        out_shape=[jax.ShapeDtypeStruct((rows, width), jnp.bfloat16)] * groups,
        in_specs=[any_spec] * (groups + 2 * pieces) + [pl.BlockSpec(memory_space=pltpu.VMEM)],
        out_specs=[pl.BlockSpec(memory_space=pltpu.VMEM)] * groups,
        scratch_shapes=[
            pltpu.VMEM((groups * rows, width), jnp.bfloat16),
            pltpu.VMEM((keys, width), jnp.bfloat16),
            pltpu.VMEM((keys, width), jnp.bfloat16),
            pltpu.SemaphoreType.DMA((groups + 4 * pieces,)),
        ],
        compiler_params=pltpu.CompilerParams(vmem_limit_bytes=48 * 2**20),
        cost_estimate=pl.CostEstimate(
            flops=4 * groups * rows * keys * width,
            bytes_accessed=4 * keys * width,
            transcendentals=groups * rows * keys * heads,
        ),
        name="attend",
    )(*q, *kv, *cache, bias)


def unpack_kernel(groups, gather, width, *refs):
    parts, out_ref, sems = refs[:groups], refs[groups], refs[groups + 1]
    me = lax.axis_index("seq") // gather
    run_copies(
        [
            pltpu.make_async_copy(
                parts[t], out_ref.at[:, columns(partner(me, t, groups), width)], sems.at[t]
            )
            for t in range(groups)
        ]
    )


def unpack(parts, groups, gather):
    rows, width = parts[0].shape
    return pl.pallas_call(
        functools.partial(unpack_kernel, groups, gather, width),
        out_shape=jax.ShapeDtypeStruct((rows, groups * width), jnp.bfloat16),
        in_specs=[pl.BlockSpec(memory_space=pl.ANY)] * groups,
        out_specs=pl.BlockSpec(memory_space=pl.ANY),
        scratch_shapes=[pltpu.SemaphoreType.DMA((groups,))],
        name="unpack_heads",
    )(*parts)


def per_device(
    seq_count,
    head_count,
    query_new,
    key_new,
    value_new,
    cache_keys,
    cache_values,
    key_exponent,
    value_exponent,
    block_mask,
):
    tok_rows, width_dev = query_new.shape
    heads_dev = width_dev // DH
    groups = math.gcd(heads_dev, seq_count)
    gather = seq_count // groups
    heads = heads_dev // groups
    width = width_dev // groups
    cache_rows = cache_keys.shape[0]
    seq_index = lax.axis_index("seq")
    head_index = lax.axis_index("head")
    group, member = seq_index // gather, seq_index % gather

    def to_group(x, t):
        if t == 0:
            return x
        pairs = [
            (s, partner(s // gather, t, groups) * gather + s % gather) for s in range(seq_count)
        ]
        return lax.ppermute(x, "seq", pairs)

    def to_member(x, t):
        if t == 0:
            return x
        pairs = [
            (s, s // gather * gather + partner(s % gather, t, gather)) for s in range(seq_count)
        ]
        return lax.ppermute(x, "seq", pairs)

    def to_head(x, t):
        if t == 0:
            return x
        return lax.ppermute(x, "head", [(h, partner(h, t, head_count)) for h in range(head_count)])

    kv_own, q_own = pack(query_new, key_new, value_new, groups, gather)
    kv = [to_group(kv_own[t], t) for t in range(groups)]
    q = [to_group(q_own[t], t) for t in range(groups)]

    stored = dequantize(cache_keys, cache_values, key_exponent, value_exponent, head_count)
    by_head = [
        to_head(
            lax.dynamic_index_in_dim(stored, partner(head_index, t, head_count), 0, False), t
        )
        for t in range(head_count)
    ]
    by_head = jnp.stack(by_head, axis=1).reshape(2, head_count * cache_rows, width_dev)
    cache = [
        to_group(
            lax.dynamic_slice_in_dim(by_head, partner(group, t, groups) * width, width, 2), t
        )
        for t in range(groups)
    ]

    kv = [to_member(x, s) for s in range(gather) for x in kv]
    cache = [to_member(x, s) for s in range(gather) for x in cache]

    q_source = jnp.stack([origin(group, t, groups) * gather + member for t in range(groups)])
    blocks = tok_rows // QBLK
    q_block = (q_source[:, None] * blocks + jnp.arange(blocks)[None, :]).reshape(-1)
    cache_device = jnp.stack(
        [
            (origin(group, t, groups) * gather + origin(member, s, gather)) * head_count
            + origin(head_index, z, head_count)
            for s in range(gather)
            for t in range(groups)
            for z in range(head_count)
        ]
    )
    cache_block = (
        cache_device[:, None] * cache_rows + jnp.arange(cache_rows)[None, :]
    ).reshape(-1) // CBLK
    q_pick = (q_block[:, None] == jnp.arange(block_mask.shape[0])[None, :]).astype(jnp.float32)
    c_pick = (jnp.arange(block_mask.shape[1])[:, None] == cache_block[None, :]).astype(jnp.float32)
    seen = jnp.dot(jnp.dot(q_pick, block_mask.astype(jnp.float32)), c_pick)
    bias = jnp.where(seen > 0.5, 0.0, MASKED).astype(jnp.float32)

    parts = attend(q, kv, cache, bias, groups, gather, heads)
    back = [to_group_back(parts[t], t, groups, gather, seq_count) for t in range(groups)]
    return unpack(back, groups, gather)


def to_group_back(x, t, groups, gather, seq_count):
    if t == 0:
        return x
    pairs = [(s, origin(s // gather, t, groups) * gather + s % gather) for s in range(seq_count)]
    return lax.ppermute(x, "seq", pairs)


def solution(mesh):
    return jax.shard_map(
        functools.partial(per_device, mesh.shape["seq"], mesh.shape["head"]),
        mesh=mesh,
        in_specs=(
            P("seq", "head"),
            P("seq", "head"),
            P("seq", "head"),
            P(("seq", "head"), None),
            P(("seq", "head"), None),
            P(("seq", "head"), None),
            P(("seq", "head"), None),
            P(),
        ),
        out_specs=P("seq", "head"),
        check_vma=False,
    )
```

```python
import functools
import math

import jax
import jax.numpy as jnp
from jax import lax
from jax.experimental import pallas as pl
from jax.experimental.pallas import tpu as pltpu
from jax.sharding import PartitionSpec as P

DH = 128
QBLK = 64
CBLK = 32
SBLK = 4
MASKED = -1e30


def partner(index, step, count):
    if count & (count - 1) == 0:
        return index ^ step
    return (index + step) % count


def origin(index, step, count):
    if count & (count - 1) == 0:
        return index ^ step
    return (index + count - step) % count


def columns(chunk, width):
    return pl.ds(pl.multiple_of(chunk * width, DH), width)


def run_copies(copies):
    for copy in copies:
        copy.start()
    for copy in copies:
        copy.wait()


def pack_kernel(groups, gather, width, q_ref, k_ref, v_ref, *rest):
    outs, (buf, in_sems, out_sems) = rest[:-3], rest[-3:]
    rows = q_ref.shape[0]
    me = lax.axis_index("seq") // gather
    loads, stores = [], []
    for t in range(groups):
        cols = columns(partner(me, t, groups), width)
        loads.append(
            [
                pltpu.make_async_copy(
                    src.at[:, cols], buf.at[t, pl.ds(i * rows, rows)], in_sems.at[t, i]
                )
                for i, src in enumerate((k_ref, v_ref, q_ref))
            ]
        )
        stores.append(
            [
                pltpu.make_async_copy(
                    buf.at[t, pl.ds(0, 2 * rows)], outs[t], out_sems.at[t, 0]
                ),
                pltpu.make_async_copy(
                    buf.at[t, pl.ds(2 * rows, rows)], outs[groups + t], out_sems.at[t, 1]
                ),
            ]
        )
    for load in loads:
        for copy in load:
            copy.start()
    for load, store in zip(loads, stores):
        for copy in load:
            copy.wait()
        for copy in store:
            copy.start()
    for store in stores:
        for copy in store:
            copy.wait()


def pack(q, k, v, groups, gather):
    rows, width = q.shape[0], q.shape[1] // groups
    outs = pl.pallas_call(
        functools.partial(pack_kernel, groups, gather, width),
        out_shape=[jax.ShapeDtypeStruct((2 * rows, width), q.dtype)] * groups
        + [jax.ShapeDtypeStruct((rows, width), q.dtype)] * groups,
        in_specs=[pl.BlockSpec(memory_space=pl.ANY)] * 3,
        out_specs=[pl.BlockSpec(memory_space=pl.ANY)] * (2 * groups),
        scratch_shapes=[
            pltpu.VMEM((groups, 3 * rows, width), q.dtype),
            pltpu.SemaphoreType.DMA((groups, 3)),
            pltpu.SemaphoreType.DMA((groups, 2)),
        ],
        cost_estimate=pl.CostEstimate(flops=0, bytes_accessed=12 * q.size, transcendentals=0),
        name="pack_heads",
    )(q, k, v)
    return outs[:groups], outs[groups:]


def dequantize_kernel(heads, parts, ck_ref, cv_ref, ke_ref, ve_ref, *outs):
    blocks, rows = ke_ref.shape[0], ck_ref.shape[0]
    for which, (m_ref, e_ref) in enumerate(((ck_ref, ke_ref), (cv_ref, ve_ref))):
        power = jnp.left_shift(1, e_ref[...] + 16).astype(jnp.float32) * 2.0**-16
        factor = jnp.concatenate(
            [jnp.broadcast_to(power[i : i + 1], (SBLK, heads)) for i in range(blocks)], axis=0
        )
        for h in range(heads):
            part, at = divmod(h * DH, parts)
            scaled = m_ref[:, h * DH : (h + 1) * DH].astype(jnp.float32) * factor[:, h : h + 1]
            outs[0][part, which, :, at : at + DH] = scaled.astype(jnp.bfloat16)


def dequantize(ck, cv, ke, ve, shards):
    rows, width = ck.shape
    return pl.pallas_call(
        functools.partial(dequantize_kernel, width // DH, width // shards),
        out_shape=jax.ShapeDtypeStruct((shards, 2, rows, width // shards), jnp.bfloat16),
        cost_estimate=pl.CostEstimate(flops=2 * ck.size, bytes_accessed=8 * ck.size, transcendentals=0),
        name="dequantize",
    )(ck, cv, ke, ve)


def attend_kernel(groups, gather, heads, *refs):
    pieces = groups * gather
    q_refs, refs = refs[:groups], refs[groups:]
    kv_refs, refs = refs[:pieces], refs[pieces:]
    c_refs, refs = refs[:pieces], refs[pieces:]
    bias_ref, refs = refs[0], refs[1:]
    o_refs, refs = refs[:groups], refs[groups:]
    q_buf, k_buf, v_buf, sems = refs
    rows, cached = q_refs[0].shape[0], c_refs[0].shape[1]
    new_rows = pieces * rows
    copies = []

    def copy(src, dst):
        copies.append(pltpu.make_async_copy(src, dst, sems.at[len(copies)]))

    for i in range(groups):
        copy(q_refs[i], q_buf.at[pl.ds(i * rows, rows)])
    for i in range(pieces):
        copy(kv_refs[i].at[pl.ds(0, rows)], k_buf.at[pl.ds(i * rows, rows)])
        copy(kv_refs[i].at[pl.ds(rows, rows)], v_buf.at[pl.ds(i * rows, rows)])
        at = pl.ds(new_rows + i * cached, cached)
        copy(c_refs[i].at[0], k_buf.at[at])
        copy(c_refs[i].at[1], v_buf.at[at])
    run_copies(copies)

    scale = math.log2(math.e) / math.sqrt(DH)
    blocks = rows // QBLK
    for i in range(groups):
        bias = jnp.concatenate(
            [
                jnp.broadcast_to(
                    bias_ref[i * blocks + j : i * blocks + j + 1], (QBLK, bias_ref.shape[1])
                )
                for j in range(blocks)
            ],
            axis=0,
        )
        for h in range(heads):
            cols = slice(h * DH, (h + 1) * DH)
            q = q_buf[i * rows : (i + 1) * rows, cols]
            scores = lax.dot_general(
                q, k_buf[:, cols], (((1,), (1,)), ((), ())), preferred_element_type=jnp.float32
            )
            fresh = scores[:, :new_rows] * scale
            old = scores[:, new_rows:] * scale + bias
            peak = jnp.maximum(
                jnp.max(fresh, axis=1, keepdims=True), jnp.max(old, axis=1, keepdims=True)
            )
            fresh = jnp.exp2(fresh - peak)
            old = jnp.exp2(old - peak)
            total = jnp.sum(fresh, axis=1, keepdims=True) + jnp.sum(old, axis=1, keepdims=True)
            weights = jnp.concatenate(
                [fresh.astype(jnp.bfloat16), old.astype(jnp.bfloat16)], axis=1
            )
            product = jnp.dot(weights, v_buf[:, cols], preferred_element_type=jnp.float32)
            o_refs[i][:, cols] = (product / total).astype(jnp.bfloat16)


def attend(q, kv, cache, bias, groups, gather, heads):
    pieces = groups * gather
    rows, width = q[0].shape
    keys = pieces * (rows + cache[0].shape[1])
    any_spec = pl.BlockSpec(memory_space=pl.ANY)
    return pl.pallas_call(
        functools.partial(attend_kernel, groups, gather, heads),
        out_shape=[jax.ShapeDtypeStruct((rows, width), jnp.bfloat16)] * groups,
        in_specs=[any_spec] * (groups + 2 * pieces) + [pl.BlockSpec(memory_space=pltpu.VMEM)],
        out_specs=[pl.BlockSpec(memory_space=pltpu.VMEM)] * groups,
        scratch_shapes=[
            pltpu.VMEM((groups * rows, width), jnp.bfloat16),
            pltpu.VMEM((keys, width), jnp.bfloat16),
            pltpu.VMEM((keys, width), jnp.bfloat16),
            pltpu.SemaphoreType.DMA((groups + 4 * pieces,)),
        ],
        compiler_params=pltpu.CompilerParams(vmem_limit_bytes=48 * 2**20),
        cost_estimate=pl.CostEstimate(
            flops=4 * groups * rows * keys * width,
            bytes_accessed=4 * keys * width,
            transcendentals=groups * rows * keys * heads,
        ),
        name="attend",
    )(*q, *kv, *cache, bias)


def unpack_kernel(groups, gather, width, *refs):
    parts, out_ref, sems = refs[:groups], refs[groups], refs[groups + 1]
    me = lax.axis_index("seq") // gather
    run_copies(
        [
            pltpu.make_async_copy(
                parts[t], out_ref.at[:, columns(partner(me, t, groups), width)], sems.at[t]
            )
            for t in range(groups)
        ]
    )


def unpack(parts, groups, gather):
    rows, width = parts[0].shape
    return pl.pallas_call(
        functools.partial(unpack_kernel, groups, gather, width),
        out_shape=jax.ShapeDtypeStruct((rows, groups * width), jnp.bfloat16),
        in_specs=[pl.BlockSpec(memory_space=pl.ANY)] * groups,
        out_specs=pl.BlockSpec(memory_space=pltpu.VMEM),
        scratch_shapes=[pltpu.SemaphoreType.DMA((groups,))],
        cost_estimate=pl.CostEstimate(
            flops=0, bytes_accessed=4 * groups * rows * width, transcendentals=0
        ),
        name="unpack_heads",
    )(*parts)


def per_device(
    seq_count,
    head_count,
    query_new,
    key_new,
    value_new,
    cache_keys,
    cache_values,
    key_exponent,
    value_exponent,
    block_mask,
):
    tok_rows, width_dev = query_new.shape
    heads_dev = width_dev // DH
    groups = math.gcd(heads_dev, seq_count)
    gather = seq_count // groups
    heads = heads_dev // groups
    width = width_dev // groups
    cache_rows = cache_keys.shape[0]
    seq_index = lax.axis_index("seq")
    head_index = lax.axis_index("head")
    group, member = seq_index // gather, seq_index % gather

    def to_group(x, t):
        if t == 0:
            return x
        pairs = [
            (s, partner(s // gather, t, groups) * gather + s % gather) for s in range(seq_count)
        ]
        return lax.ppermute(x, "seq", pairs)

    def to_member(x, t):
        if t == 0:
            return x
        pairs = [
            (s, s // gather * gather + partner(s % gather, t, gather)) for s in range(seq_count)
        ]
        return lax.ppermute(x, "seq", pairs)

    def to_head(x, t):
        if t == 0:
            return x
        return lax.ppermute(x, "head", [(h, partner(h, t, head_count)) for h in range(head_count)])

    kv_own, q_own = pack(query_new, key_new, value_new, groups, gather)
    kv = [to_group(kv_own[t], t) for t in range(groups)]
    q = [to_group(q_own[t], t) for t in range(groups)]

    stored = dequantize(cache_keys, cache_values, key_exponent, value_exponent, head_count)
    by_head = [
        to_head(
            lax.dynamic_index_in_dim(stored, partner(head_index, t, head_count), 0, False), t
        )
        for t in range(head_count)
    ]
    by_head = jnp.stack(by_head, axis=1).reshape(2, head_count * cache_rows, width_dev)
    cache = [
        to_group(
            lax.dynamic_slice_in_dim(by_head, partner(group, t, groups) * width, width, 2), t
        )
        for t in range(groups)
    ]

    kv = [to_member(x, s) for s in range(gather) for x in kv]
    cache = [to_member(x, s) for s in range(gather) for x in cache]

    q_source = jnp.stack([origin(group, t, groups) * gather + member for t in range(groups)])
    blocks = tok_rows // QBLK
    q_block = (q_source[:, None] * blocks + jnp.arange(blocks)[None, :]).reshape(-1)
    cache_device = jnp.stack(
        [
            (origin(group, t, groups) * gather + origin(member, s, gather)) * head_count
            + origin(head_index, z, head_count)
            for s in range(gather)
            for t in range(groups)
            for z in range(head_count)
        ]
    )
    cache_block = (
        cache_device[:, None] * cache_rows + jnp.arange(cache_rows)[None, :]
    ).reshape(-1) // CBLK
    q_pick = (q_block[:, None] == jnp.arange(block_mask.shape[0])[None, :]).astype(jnp.float32)
    c_pick = (jnp.arange(block_mask.shape[1])[:, None] == cache_block[None, :]).astype(jnp.float32)
    seen = jnp.dot(jnp.dot(q_pick, block_mask.astype(jnp.float32)), c_pick)
    bias = jnp.where(seen > 0.5, 0.0, MASKED).astype(jnp.float32)

    parts = attend(q, kv, cache, bias, groups, gather, heads)
    back = [to_group_back(parts[t], t, groups, gather, seq_count) for t in range(groups)]
    return unpack(back, groups, gather)


def to_group_back(x, t, groups, gather, seq_count):
    if t == 0:
        return x
    pairs = [(s, origin(s // gather, t, groups) * gather + s % gather) for s in range(seq_count)]
    return lax.ppermute(x, "seq", pairs)


def solution(mesh):
    return jax.shard_map(
        functools.partial(per_device, mesh.shape["seq"], mesh.shape["head"]),
        mesh=mesh,
        in_specs=(
            P("seq", "head"),
            P("seq", "head"),
            P("seq", "head"),
            P(("seq", "head"), None),
            P(("seq", "head"), None),
            P(("seq", "head"), None),
            P(("seq", "head"), None),
            P(),
        ),
        out_specs=P("seq", "head"),
        check_vma=False,
    )
```

```python
import functools
import math

import jax
import jax.numpy as jnp
from jax import lax
from jax.experimental import pallas as pl
from jax.experimental.pallas import tpu as pltpu
from jax.sharding import PartitionSpec as P

DH = 128
QBLK = 64
CBLK = 32
SBLK = 4
MASKED = -1e30
BATCH = 2


def partner(index, step, count):
    if count & (count - 1) == 0:
        return index ^ step
    return (index + step) % count


def origin(index, step, count):
    if count & (count - 1) == 0:
        return index ^ step
    return (index + count - step) % count


def columns(chunk, width):
    return pl.ds(pl.multiple_of(chunk * width, DH), width)


def vmem(count):
    return [pl.BlockSpec(memory_space=pltpu.VMEM)] * count


def pack_kernel(groups, gather, width, q_ref, k_ref, v_ref, *rest):
    outs, sems = rest[:-1], rest[-1]
    rows = q_ref.shape[0]
    me = lax.axis_index("seq") // gather
    copies = []
    for t in reversed(range(groups)):
        cols = columns(partner(me, t, groups), width)
        for i, src in enumerate((k_ref, v_ref, q_ref)):
            dst = outs[t].at[pl.ds(i * rows, rows)]
            copies.append(pltpu.make_async_copy(src.at[:, cols], dst, sems.at[t, i]))
    for copy in copies:
        copy.start()
    for copy in copies:
        copy.wait()


def pack(q, k, v, groups, gather):
    rows, width = q.shape[0], q.shape[1] // groups
    return pl.pallas_call(
        functools.partial(pack_kernel, groups, gather, width),
        out_shape=[jax.ShapeDtypeStruct((3 * rows, width), q.dtype)] * groups,
        in_specs=[pl.BlockSpec(memory_space=pl.ANY)] * 3,
        out_specs=vmem(groups),
        scratch_shapes=[pltpu.SemaphoreType.DMA((groups, 3))],
        cost_estimate=pl.CostEstimate(flops=0, bytes_accessed=6 * q.size, transcendentals=0),
        name="pack_heads",
    )(q, k, v)


def dequantize_kernel(shards, ck_ref, cv_ref, ke_ref, ve_ref, *outs):
    me = lax.axis_index("head")
    blocks, heads = ke_ref.shape
    rows, width = outs[0].shape[1:]
    for which, (m_ref, e_ref) in enumerate(((ck_ref, ke_ref), (cv_ref, ve_ref))):
        power = jnp.left_shift(1, e_ref[...] + 16).astype(jnp.float32) * 2.0**-16
        power = jnp.concatenate(
            [jnp.broadcast_to(power[i : i + 1], (SBLK, heads)) for i in range(blocks)], axis=0
        )
        for t in range(shards):
            part = partner(me, t, shards)
            head = lax.broadcasted_iota(jnp.int32, (heads, width), 0)
            column = lax.broadcasted_iota(jnp.int32, (heads, width), 1)
            spread = (head == part * (width // DH) + column // DH).astype(jnp.float32)
            factor = jnp.dot(power, spread, preferred_element_type=jnp.float32)
            mantissa = m_ref[:, columns(part, width)].astype(jnp.float32)
            outs[t][which] = (mantissa * factor).astype(jnp.bfloat16)


def dequantize(ck, cv, ke, ve, shards):
    rows, width = ck.shape
    return pl.pallas_call(
        functools.partial(dequantize_kernel, shards),
        out_shape=[jax.ShapeDtypeStruct((2, rows, width // shards), jnp.bfloat16)] * shards,
        in_specs=vmem(4),
        out_specs=vmem(shards),
        cost_estimate=pl.CostEstimate(flops=2 * ck.size, bytes_accessed=8 * ck.size, transcendentals=0),
        name="dequantize",
    )(ck, cv, ke, ve)


def stacked(refs, cols, rows):
    return jnp.concatenate([ref[rows, cols] for ref in refs], axis=0)


def attend_keys(queries, kv_refs, c_refs, bias, cols, rows):
    scale = math.log2(math.e) / math.sqrt(DH)
    contract = (((1,), (1,)), ((), ()))
    k_new = stacked(kv_refs, cols, slice(0, rows))
    v_new = stacked(kv_refs, cols, slice(rows, 2 * rows))
    k_old = jnp.concatenate([ref[0, :, cols] for ref in c_refs], axis=0)
    v_old = jnp.concatenate([ref[1, :, cols] for ref in c_refs], axis=0)
    new = lax.dot_general(queries, k_new, contract, preferred_element_type=jnp.float32) * scale
    old = lax.dot_general(queries, k_old, contract, preferred_element_type=jnp.float32) * scale
    old = old + bias
    peak = jnp.maximum(
        jnp.max(new, axis=1, keepdims=True), jnp.max(old, axis=1, keepdims=True)
    )
    new = jnp.exp2(new - peak)
    old = jnp.exp2(old - peak)
    total = jnp.sum(new, axis=1, keepdims=True) + jnp.sum(old, axis=1, keepdims=True)
    product = jnp.dot(
        new.astype(jnp.bfloat16), v_new, preferred_element_type=jnp.float32
    ) + jnp.dot(old.astype(jnp.bfloat16), v_old, preferred_element_type=jnp.float32)
    return peak, total, product


def bias_rows(bias_ref, pieces, blocks):
    width = bias_ref.shape[1]
    return jnp.concatenate(
        [
            jnp.broadcast_to(bias_ref[row : row + 1], (QBLK, width))
            for t in pieces
            for row in range(t * blocks, (t + 1) * blocks)
        ],
        axis=0,
    )


def attend_own_kernel(groups, *refs):
    kv_refs, c_refs, bias_ref = refs[:groups], refs[groups : 2 * groups], refs[2 * groups]
    peak_ref, total_ref, product_ref = refs[2 * groups + 1 :]
    rows, width = kv_refs[0].shape[0] // 3, kv_refs[0].shape[1]
    bias = bias_rows(bias_ref, range(groups), rows // QBLK)
    for at in range(0, width, DH):
        cols = slice(at, at + DH)
        queries = stacked(kv_refs, cols, slice(2 * rows, 3 * rows))
        peak, total, product = attend_keys(queries, kv_refs, c_refs, bias, cols, rows)
        peak_ref[:, cols] = jnp.broadcast_to(peak, product.shape)
        total_ref[:, cols] = jnp.broadcast_to(total, product.shape)
        product_ref[:, cols] = product


def attend_own(kv, cache, bias):
    groups = len(kv)
    rows, width = kv[0].shape[0] // 3, kv[0].shape[1]
    keys = groups * (rows + cache[0].shape[1])
    return pl.pallas_call(
        functools.partial(attend_own_kernel, groups),
        out_shape=[jax.ShapeDtypeStruct((groups * rows, width), jnp.float32)] * 3,
        in_specs=vmem(2 * groups + 1),
        out_specs=vmem(3),
        compiler_params=pltpu.CompilerParams(vmem_limit_bytes=32 * 2**20),
        cost_estimate=pl.CostEstimate(
            flops=4 * groups * rows * keys * width,
            bytes_accessed=4 * keys * width,
            transcendentals=groups * rows * keys * width // DH,
        ),
        name="attend_own",
    )(*kv, *cache, bias)


def attend_other_kernel(pieces, others, *refs):
    count = len(pieces)
    q_refs, refs = refs[:count], refs[count:]
    kv_refs, refs = refs[:others], refs[others:]
    c_refs, refs = refs[:others], refs[others:]
    bias_ref, peak_ref, total_ref, product_ref = refs[:4]
    o_refs = refs[4:]
    rows, width = o_refs[0].shape
    if others:
        bias = bias_rows(bias_ref, pieces, rows // QBLK)
    for at in range(0, width, DH):
        cols = slice(at, at + DH)
        mine = [slice(t * rows, (t + 1) * rows) for t in pieces]
        total = jnp.concatenate([total_ref[m, cols] for m in mine], axis=0)
        product = jnp.concatenate([product_ref[m, cols] for m in mine], axis=0)
        if others:
            queries = stacked(q_refs, cols, slice(2 * rows, 3 * rows))
            peak = jnp.concatenate([peak_ref[m, cols] for m in mine], axis=0)
            peak_2, total_2, product_2 = attend_keys(
                queries, kv_refs, c_refs, bias, cols, rows
            )
            top = jnp.maximum(peak, peak_2)
            share, share_2 = jnp.exp2(peak - top), jnp.exp2(peak_2 - top)
            total = total * share + total_2 * share_2
            product = product * share + product_2 * share_2
        result = (product / total).astype(jnp.bfloat16)
        for i in range(count):
            o_refs[i][:, cols] = result[i * rows : (i + 1) * rows]


def attend_other(pieces, kv, kv_other, cache_other, bias, own):
    rows, width = kv[0].shape[0] // 3, kv[0].shape[1]
    count, others = len(pieces), len(kv_other)
    keys = others * (rows + (cache_other[0].shape[1] if others else 0))
    return pl.pallas_call(
        functools.partial(attend_other_kernel, pieces, others),
        out_shape=[jax.ShapeDtypeStruct((rows, width), jnp.bfloat16)] * count,
        in_specs=vmem(count + 2 * others + 4),
        out_specs=vmem(count),
        compiler_params=pltpu.CompilerParams(vmem_limit_bytes=32 * 2**20),
        cost_estimate=pl.CostEstimate(
            flops=4 * count * rows * keys * width,
            bytes_accessed=4 * keys * width,
            transcendentals=count * rows * keys * width // DH,
        ),
        name="attend_other",
    )(*[kv[t] for t in pieces], *kv_other, *cache_other, bias, *own)


def unpack_kernel(groups, gather, width, *refs):
    parts, out_ref, sems = refs[:groups], refs[groups], refs[groups + 1]
    me = lax.axis_index("seq") // gather
    copies = [
        pltpu.make_async_copy(
            parts[t], out_ref.at[:, columns(partner(me, t, groups), width)], sems.at[t]
        )
        for t in range(groups)
    ]
    for copy in copies:
        copy.start()
    for copy in copies:
        copy.wait()


def unpack(parts, groups, gather):
    rows, width = parts[0].shape
    return pl.pallas_call(
        functools.partial(unpack_kernel, groups, gather, width),
        out_shape=jax.ShapeDtypeStruct((rows, groups * width), jnp.bfloat16),
        in_specs=vmem(groups),
        out_specs=pl.BlockSpec(memory_space=pl.ANY),
        scratch_shapes=[pltpu.SemaphoreType.DMA((groups,))],
        cost_estimate=pl.CostEstimate(
            flops=0, bytes_accessed=4 * groups * rows * width, transcendentals=0
        ),
        name="unpack_heads",
    )(*parts)


def per_device(
    seq_count,
    head_count,
    query_new,
    key_new,
    value_new,
    cache_keys,
    cache_values,
    key_exponent,
    value_exponent,
    block_mask,
):
    tok_rows, width_dev = query_new.shape
    groups = math.gcd(width_dev // DH, seq_count)
    gather = seq_count // groups
    width = width_dev // groups
    cache_rows = cache_keys.shape[0]
    seq_index = lax.axis_index("seq")
    head_index = lax.axis_index("head")
    group, member = seq_index // gather, seq_index % gather

    def to_group(x, t):
        if t == 0:
            return x
        pairs = [
            (s, partner(s // gather, t, groups) * gather + s % gather) for s in range(seq_count)
        ]
        return lax.ppermute(x, "seq", pairs)

    def from_group(x, t):
        if t == 0:
            return x
        pairs = [
            (s, origin(s // gather, t, groups) * gather + s % gather) for s in range(seq_count)
        ]
        return lax.ppermute(x, "seq", pairs)

    def to_member(x, t):
        pairs = [
            (s, s // gather * gather + partner(s % gather, t, gather)) for s in range(seq_count)
        ]
        return lax.ppermute(x, "seq", pairs)

    def to_head(x, t):
        if t == 0:
            return x
        return lax.ppermute(x, "head", [(h, partner(h, t, head_count)) for h in range(head_count)])

    kv_own = pack(query_new, key_new, value_new, groups, gather)
    *kv_own, cache_keys, cache_values = lax.optimization_barrier(
        (*kv_own, cache_keys, cache_values)
    )
    kv = [to_group(kv_own[t], t) for t in range(groups)]

    stored = dequantize(cache_keys, cache_values, key_exponent, value_exponent, head_count)
    by_head = [to_head(stored[t], t) for t in range(head_count)]
    by_head = jnp.stack(by_head, axis=1).reshape(2, head_count * cache_rows, width_dev)
    cache = [
        to_group(
            lax.dynamic_slice_in_dim(by_head, partner(group, t, groups) * width, width, 2), t
        )
        for t in range(groups)
    ]

    kv_other = [to_member(x[: 2 * tok_rows], s) for s in range(1, gather) for x in kv]
    cache_other = [to_member(x, s) for s in range(1, gather) for x in cache]

    q_source = jnp.stack([origin(group, t, groups) * gather + member for t in range(groups)])
    blocks = tok_rows // QBLK
    q_block = (q_source[:, None] * blocks + jnp.arange(blocks)[None, :]).reshape(-1)
    q_pick = (q_block[:, None] == jnp.arange(block_mask.shape[0])[None, :]).astype(jnp.float32)
    row_mask = jnp.dot(q_pick, block_mask.astype(jnp.float32))

    def bias_of(steps):
        device = jnp.stack(
            [
                (origin(group, t, groups) * gather + origin(member, s, gather)) * head_count
                + origin(head_index, z, head_count)
                for s in steps
                for t in range(groups)
                for z in range(head_count)
            ]
        )
        block = (device[:, None] * cache_rows + jnp.arange(cache_rows)[None, :]).reshape(-1)
        pick = jnp.arange(block_mask.shape[1])[:, None] == (block // CBLK)[None, :]
        seen = jnp.dot(row_mask, pick.astype(jnp.float32))
        return jnp.where(seen > 0.5, 0.0, MASKED).astype(jnp.float32)

    own_bias = bias_of([0])
    other_bias = bias_of(range(1, gather)) if gather > 1 else own_bias
    own = attend_own(kv, cache, own_bias)
    order = list(reversed(range(groups)))
    parts = [None] * groups
    for first in range(0, groups, BATCH):
        batch = tuple(order[first : first + BATCH])
        done = attend_other(batch, kv, kv_other, cache_other, other_bias, own)
        for t, part in zip(batch, done):
            parts[t] = from_group(part, t)
    return unpack(parts, groups, gather)


def solution(mesh):
    return jax.shard_map(
        functools.partial(per_device, mesh.shape["seq"], mesh.shape["head"]),
        mesh=mesh,
        in_specs=(
            P("seq", "head"),
            P("seq", "head"),
            P("seq", "head"),
            P(("seq", "head"), None),
            P(("seq", "head"), None),
            P(("seq", "head"), None),
            P(("seq", "head"), None),
            P(),
        ),
        out_specs=P("seq", "head"),
        check_vma=False,
    )
```

```python
import functools
import math

import jax
import jax.numpy as jnp
from jax import lax
from jax.experimental import pallas as pl
from jax.experimental.pallas import tpu as pltpu
from jax.sharding import PartitionSpec as P

DH = 128
QBLK = 64
CBLK = 32
SBLK = 4
MASKED = -1e30
SMALL = 16 * 2**20
LARGE = 32 * 2**20


def partner(index, step, count):
    if count & (count - 1) == 0:
        return index ^ step
    return (index + step) % count


def origin(index, step, count):
    if count & (count - 1) == 0:
        return index ^ step
    return (index + count - step) % count


def columns(chunk, width):
    return pl.ds(pl.multiple_of(chunk * width, DH), width)


def vmem(count):
    return [pl.BlockSpec(memory_space=pltpu.VMEM)] * count


def pack_kernel(groups, gather, width, q_ref, k_ref, v_ref, *rest):
    outs, sems = rest[:-1], rest[-1]
    rows = q_ref.shape[0]
    me = lax.axis_index("seq") // gather
    copies = []
    for t in reversed(range(groups)):
        cols = columns(partner(me, t, groups), width)
        for i, src in enumerate((k_ref, v_ref, q_ref)):
            dst = outs[t].at[pl.ds(i * rows, rows)]
            copies.append(pltpu.make_async_copy(src.at[:, cols], dst, sems.at[t, i]))
    for copy in copies:
        copy.start()
    for copy in copies:
        copy.wait()


def pack(q, k, v, groups, gather):
    rows, width = q.shape[0], q.shape[1] // groups
    return pl.pallas_call(
        functools.partial(pack_kernel, groups, gather, width),
        out_shape=[jax.ShapeDtypeStruct((3 * rows, width), q.dtype)] * groups,
        in_specs=[pl.BlockSpec(memory_space=pl.ANY)] * 3,
        out_specs=vmem(groups),
        scratch_shapes=[pltpu.SemaphoreType.DMA((groups, 3))],
        compiler_params=pltpu.CompilerParams(vmem_limit_bytes=SMALL),
        cost_estimate=pl.CostEstimate(flops=0, bytes_accessed=6 * q.size, transcendentals=0),
        name="pack_heads",
    )(q, k, v)


def dequantize_kernel(shards, ck_ref, cv_ref, ke_ref, ve_ref, *outs):
    me = lax.axis_index("head")
    blocks, heads = ke_ref.shape
    rows, width = outs[0].shape[1:]
    exponent = jnp.concatenate(
        [
            jnp.broadcast_to(ref[i : i + 1], (SBLK, heads))
            for ref in (ke_ref, ve_ref)
            for i in range(blocks)
        ],
        axis=0,
    )
    power = jnp.left_shift(1, exponent + 16).astype(jnp.float32) * 2.0**-16
    power = power.astype(jnp.bfloat16)
    head = lax.broadcasted_iota(jnp.int32, (heads, width), 0)
    head -= lax.broadcasted_iota(jnp.int32, (heads, width), 1) // DH
    for t in range(shards):
        part = partner(me, t, shards)
        spread = (head == part * (width // DH)).astype(jnp.float32).astype(jnp.bfloat16)
        factor = jnp.dot(power, spread, preferred_element_type=jnp.float32)
        for which, m_ref in enumerate((ck_ref, cv_ref)):
            mantissa = m_ref[:, columns(part, width)].astype(jnp.float32)
            scaled = mantissa * factor[which * rows : (which + 1) * rows]
            outs[t][which] = scaled.astype(jnp.bfloat16)


def dequantize(ck, cv, ke, ve, shards):
    rows, width = ck.shape
    return pl.pallas_call(
        functools.partial(dequantize_kernel, shards),
        out_shape=[jax.ShapeDtypeStruct((2, rows, width // shards), jnp.bfloat16)] * shards,
        in_specs=vmem(4),
        out_specs=vmem(shards),
        compiler_params=pltpu.CompilerParams(vmem_limit_bytes=SMALL),
        cost_estimate=pl.CostEstimate(flops=2 * ck.size, bytes_accessed=8 * ck.size, transcendentals=0),
        name="dequantize",
    )(ck, cv, ke, ve)


def stacked(refs, cols, rows):
    if isinstance(rows, slice):
        rows = [rows] * len(refs)
    return jnp.concatenate([ref[r, cols] for ref, r in zip(refs, rows)], axis=0)


def attend_keys(queries, kv, cache, bias):
    scale = math.log2(math.e) / math.sqrt(DH)
    contract = (((1,), (1,)), ((), ()))
    (k_new, v_new), (k_old, v_old) = kv, cache
    new = lax.dot_general(queries, k_new, contract, preferred_element_type=jnp.float32) * scale
    old = lax.dot_general(queries, k_old, contract, preferred_element_type=jnp.float32) * scale
    old = old + bias
    peak = jnp.maximum(
        jnp.max(new, axis=1, keepdims=True), jnp.max(old, axis=1, keepdims=True)
    )
    new = jnp.exp2(new - peak)
    old = jnp.exp2(old - peak)
    total = jnp.sum(new, axis=1, keepdims=True) + jnp.sum(old, axis=1, keepdims=True)
    product = jnp.dot(
        new.astype(jnp.bfloat16), v_new, preferred_element_type=jnp.float32
    ) + jnp.dot(old.astype(jnp.bfloat16), v_old, preferred_element_type=jnp.float32)
    return peak, total, product


def bias_rows(bias_ref, pieces, blocks):
    width = bias_ref.shape[1]
    return jnp.concatenate(
        [
            jnp.broadcast_to(bias_ref[row : row + 1], (QBLK, width))
            for t in pieces
            for row in range(t * blocks, (t + 1) * blocks)
        ],
        axis=0,
    )


def attend_own_kernel(groups, *refs):
    kv_refs, c_refs, bias_ref = refs[:groups], refs[groups : 2 * groups], refs[2 * groups]
    peak_ref, total_ref, product_ref = refs[2 * groups + 1 :]
    rows, width = kv_refs[0].shape[0] // 3, kv_refs[0].shape[1]
    bias = bias_rows(bias_ref, range(groups), rows // QBLK)
    for at in range(0, width, DH):
        cols = slice(at, at + DH)
        queries = stacked(kv_refs, cols, slice(2 * rows, 3 * rows))
        kv = [stacked(kv_refs, cols, slice(i * rows, (i + 1) * rows)) for i in range(2)]
        cache = [jnp.concatenate([ref[i, :, cols] for ref in c_refs], axis=0) for i in range(2)]
        peak, total, product = attend_keys(queries, kv, cache, bias)
        peak_ref[:, cols] = jnp.broadcast_to(peak, product.shape)
        total_ref[:, cols] = jnp.broadcast_to(total, product.shape)
        product_ref[:, cols] = product


def attend_own(kv, cache, bias):
    groups = len(kv)
    rows, width = kv[0].shape[0] // 3, kv[0].shape[1]
    keys = groups * (rows + cache[0].shape[1])
    return pl.pallas_call(
        functools.partial(attend_own_kernel, groups),
        out_shape=[jax.ShapeDtypeStruct((groups * rows, width), jnp.float32)] * 3,
        in_specs=vmem(2 * groups + 1),
        out_specs=vmem(3),
        compiler_params=pltpu.CompilerParams(vmem_limit_bytes=LARGE),
        cost_estimate=pl.CostEstimate(
            flops=4 * groups * rows * keys * width,
            bytes_accessed=4 * keys * width,
            transcendentals=groups * rows * keys * width // DH,
        ),
        name="attend_own",
    )(*kv, *cache, bias)


def attend_other_kernel(pieces, *refs):
    count = len(pieces)
    q_refs, refs = refs[:count], refs[count:]
    peak_ref, total_ref, product_ref = refs[:3]
    o_refs, refs = refs[-count:], refs[3:-count]
    rows, width = o_refs[0].shape
    mine = [slice(t * rows, (t + 1) * rows) for t in pieces]
    if refs:
        kv_ref, c_ref, bias_ref = refs
        bias = bias_rows(bias_ref, pieces, rows // QBLK)
    for at in range(0, width, DH):
        cols = slice(at, at + DH)
        total = stacked([total_ref] * count, cols, mine)
        product = stacked([product_ref] * count, cols, mine)
        if refs:
            queries = stacked(q_refs, cols, slice(2 * rows, 3 * rows))
            new, old = kv_ref.shape[1] // 2, c_ref.shape[2]
            kv = [
                kv_ref[:, i * new : (i + 1) * new, cols].reshape(-1, DH) for i in range(2)
            ]
            cache = [c_ref[:, i, :, cols].reshape(-1, DH) for i in range(2)]
            peak = stacked([peak_ref] * count, cols, mine)
            peak_2, total_2, product_2 = attend_keys(queries, kv, cache, bias)
            top = jnp.maximum(peak, peak_2)
            share, share_2 = jnp.exp2(peak - top), jnp.exp2(peak_2 - top)
            total = total * share + total_2 * share_2
            product = product * share + product_2 * share_2
        result = (product / total).astype(jnp.bfloat16)
        for i in range(count):
            o_refs[i][:, cols] = result[i * rows : (i + 1) * rows]


def attend_other(pieces, kv, own, other):
    rows, width = kv[0].shape[0] // 3, kv[0].shape[1]
    count = len(pieces)
    keys = (other[0].size // 2 + other[1].size // 2) // width if other else 0
    return pl.pallas_call(
        functools.partial(attend_other_kernel, pieces),
        out_shape=[jax.ShapeDtypeStruct((rows, width), jnp.bfloat16)] * count,
        in_specs=vmem(count + 3 + len(other)),
        out_specs=vmem(count),
        compiler_params=pltpu.CompilerParams(vmem_limit_bytes=LARGE),
        cost_estimate=pl.CostEstimate(
            flops=4 * count * rows * keys * width,
            bytes_accessed=4 * keys * width,
            transcendentals=count * rows * keys * width // DH,
        ),
        name="attend_other",
    )(*[kv[t] for t in pieces], *own, *other)


def unpack_kernel(groups, gather, width, *refs):
    parts, out_ref, sems = refs[:groups], refs[groups], refs[groups + 1]
    me = lax.axis_index("seq") // gather
    copies = [
        pltpu.make_async_copy(
            parts[t], out_ref.at[:, columns(partner(me, t, groups), width)], sems.at[t]
        )
        for t in range(groups)
    ]
    for copy in copies:
        copy.start()
    for copy in copies:
        copy.wait()


def unpack(parts, groups, gather):
    rows, width = parts[0].shape
    return pl.pallas_call(
        functools.partial(unpack_kernel, groups, gather, width),
        out_shape=jax.ShapeDtypeStruct((rows, groups * width), jnp.bfloat16),
        in_specs=vmem(groups),
        out_specs=pl.BlockSpec(memory_space=pl.ANY),
        scratch_shapes=[pltpu.SemaphoreType.DMA((groups,))],
        compiler_params=pltpu.CompilerParams(vmem_limit_bytes=SMALL),
        cost_estimate=pl.CostEstimate(
            flops=0, bytes_accessed=4 * groups * rows * width, transcendentals=0
        ),
        name="unpack_heads",
    )(*parts)


def per_device(
    seq_count,
    head_count,
    query_new,
    key_new,
    value_new,
    cache_keys,
    cache_values,
    key_exponent,
    value_exponent,
    block_mask,
):
    tok_rows, width_dev = query_new.shape
    groups = math.gcd(width_dev // DH, seq_count)
    gather = seq_count // groups
    width = width_dev // groups
    cache_rows = cache_keys.shape[0]
    seq_index = lax.axis_index("seq")
    head_index = lax.axis_index("head")
    group, member = seq_index // gather, seq_index % gather

    def to_group(x, t):
        if t == 0:
            return x
        pairs = [
            (s, partner(s // gather, t, groups) * gather + s % gather) for s in range(seq_count)
        ]
        return lax.ppermute(x, "seq", pairs)

    def from_group(x, t):
        if t == 0:
            return x
        pairs = [
            (s, origin(s // gather, t, groups) * gather + s % gather) for s in range(seq_count)
        ]
        return lax.ppermute(x, "seq", pairs)

    def to_member(x, t):
        pairs = [
            (s, s // gather * gather + partner(s % gather, t, gather)) for s in range(seq_count)
        ]
        return lax.ppermute(x, "seq", pairs)

    def to_head(x, t):
        if t == 0:
            return x
        return lax.ppermute(x, "head", [(h, partner(h, t, head_count)) for h in range(head_count)])

    kv_own = pack(query_new, key_new, value_new, groups, gather)
    *kv_own, cache_keys, cache_values = lax.optimization_barrier(
        (*kv_own, cache_keys, cache_values)
    )
    kv = [to_group(kv_own[t], t) for t in range(groups)]

    stored = dequantize(cache_keys, cache_values, key_exponent, value_exponent, head_count)
    by_head = []
    for t in range(head_count):
        x = stored[t]
        if t > 2:
            x, _ = lax.optimization_barrier((x, by_head[t - 2]))
        by_head.append(to_head(x, t))
    by_head = jnp.stack(by_head, axis=1).reshape(2, head_count * cache_rows, width_dev)
    if groups > 1:
        by_head, kv[1] = lax.optimization_barrier((by_head, kv[1]))
    cache = []
    for t in range(groups):
        x = lax.dynamic_slice_in_dim(by_head, partner(group, t, groups) * width, width, 2)
        cache.append(to_group(x, t))

    kv_swap = jnp.stack([x[: 2 * tok_rows] for x in kv])
    cache_swap = jnp.stack(cache)
    members = range(1, gather)

    q_source = jnp.stack([origin(group, t, groups) * gather + member for t in range(groups)])
    blocks = tok_rows // QBLK
    q_block = (q_source[:, None] * blocks + jnp.arange(blocks)[None, :]).reshape(-1)
    q_pick = (q_block[:, None] == jnp.arange(block_mask.shape[0])[None, :]).astype(jnp.float32)
    row_mask = jnp.dot(q_pick, block_mask.astype(jnp.float32))

    def bias_of(steps):
        device = jnp.stack(
            [
                (origin(group, t, groups) * gather + origin(member, s, gather)) * head_count
                + origin(head_index, z, head_count)
                for s in steps
                for t in range(groups)
                for z in range(head_count)
            ]
        )
        block = (device[:, None] * cache_rows + jnp.arange(cache_rows)[None, :]).reshape(-1)
        pick = jnp.arange(block_mask.shape[1])[:, None] == (block // CBLK)[None, :]
        seen = jnp.dot(row_mask, pick.astype(jnp.float32))
        return jnp.where(seen > 0.5, 0.0, MASKED).astype(jnp.float32)

    other = []
    if gather > 1:
        other = [
            jnp.concatenate([to_member(kv_swap, s) for s in members]),
            jnp.concatenate([to_member(cache_swap, s) for s in members]),
            bias_of(members),
        ]
    own = attend_own(kv, cache, bias_of([0]))
    batches = [(groups - 1,), tuple(range(1, groups - 1)), (0,)] if groups > 2 else [tuple(range(groups))]
    parts = [None] * groups
    for batch in batches:
        done = attend_other(batch, kv, own, other)
        for t, part in zip(batch, done):
            parts[t] = from_group(part, t)
    return unpack(parts, groups, gather)


def solution(mesh):
    return jax.shard_map(
        functools.partial(per_device, mesh.shape["seq"], mesh.shape["head"]),
        mesh=mesh,
        in_specs=(
            P("seq", "head"),
            P("seq", "head"),
            P("seq", "head"),
            P(("seq", "head"), None),
            P(("seq", "head"), None),
            P(("seq", "head"), None),
            P(("seq", "head"), None),
            P(),
        ),
        out_specs=P("seq", "head"),
        check_vma=False,
    )
```

```python
import functools
import math

import jax
import jax.numpy as jnp
from jax import lax
from jax.experimental import pallas as pl
from jax.experimental.pallas import tpu as pltpu
from jax.sharding import PartitionSpec as P

DH = 128
QBLK = 64
CBLK = 32
SBLK = 4
MASKED = -1e30
SMALL = 16 * 2**20
LARGE = 32 * 2**20


def partner(index, step, count):
    if count & (count - 1) == 0:
        return index ^ step
    return (index + step) % count


def origin(index, step, count):
    if count & (count - 1) == 0:
        return index ^ step
    return (index + count - step) % count


def columns(chunk, width):
    return pl.ds(pl.multiple_of(chunk * width, DH), width)


def vmem(count):
    return [pl.BlockSpec(memory_space=pltpu.VMEM)] * count


def pack_kernel(groups, gather, width, q_ref, k_ref, v_ref, *rest):
    outs, sems = rest[:-1], rest[-1]
    rows = q_ref.shape[0]
    me = lax.axis_index("seq") // gather
    copies = []
    for t in reversed(range(groups)):
        cols = columns(partner(me, t, groups), width)
        for i, src in enumerate((k_ref, v_ref, q_ref)):
            dst = outs[t].at[pl.ds(i * rows, rows)]
            copies.append(pltpu.make_async_copy(src.at[:, cols], dst, sems.at[t, i]))
    for copy in copies:
        copy.start()
    for copy in copies:
        copy.wait()


def pack(q, k, v, groups, gather):
    rows, width = q.shape[0], q.shape[1] // groups
    return pl.pallas_call(
        functools.partial(pack_kernel, groups, gather, width),
        out_shape=[jax.ShapeDtypeStruct((3 * rows, width), q.dtype)] * groups,
        in_specs=[pl.BlockSpec(memory_space=pltpu.HBM)] * 3,
        out_specs=vmem(groups),
        scratch_shapes=[pltpu.SemaphoreType.DMA((groups, 3))],
        compiler_params=pltpu.CompilerParams(vmem_limit_bytes=SMALL),
        cost_estimate=pl.CostEstimate(flops=0, bytes_accessed=6 * q.size, transcendentals=0),
        name="pack_heads",
    )(*[pltpu.with_memory_space_constraint(x, pltpu.HBM) for x in (q, k, v)])


def dequantize_kernel(shards, ck_ref, cv_ref, ke_ref, ve_ref, *outs):
    me = lax.axis_index("head")
    blocks, heads = ke_ref.shape
    rows, width = outs[0].shape[1:]
    exponent = jnp.concatenate(
        [
            jnp.broadcast_to(ref[i : i + 1], (SBLK, heads))
            for ref in (ke_ref, ve_ref)
            for i in range(blocks)
        ],
        axis=0,
    )
    power = jnp.left_shift(1, exponent + 16).astype(jnp.float32) * 2.0**-16
    power = power.astype(jnp.bfloat16)
    head = lax.broadcasted_iota(jnp.int32, (heads, width), 0)
    head -= lax.broadcasted_iota(jnp.int32, (heads, width), 1) // DH
    for t in range(shards):
        part = partner(me, t, shards)
        spread = (head == part * (width // DH)).astype(jnp.float32).astype(jnp.bfloat16)
        factor = jnp.dot(power, spread, preferred_element_type=jnp.float32)
        for which, m_ref in enumerate((ck_ref, cv_ref)):
            mantissa = m_ref[:, columns(part, width)].astype(jnp.float32)
            scaled = mantissa * factor[which * rows : (which + 1) * rows]
            outs[t][which] = scaled.astype(jnp.bfloat16)


def dequantize(ck, cv, ke, ve, shards):
    rows, width = ck.shape
    return pl.pallas_call(
        functools.partial(dequantize_kernel, shards),
        out_shape=[jax.ShapeDtypeStruct((2, rows, width // shards), jnp.bfloat16)] * shards,
        in_specs=vmem(4),
        out_specs=vmem(shards),
        compiler_params=pltpu.CompilerParams(vmem_limit_bytes=SMALL),
        cost_estimate=pl.CostEstimate(flops=2 * ck.size, bytes_accessed=8 * ck.size, transcendentals=0),
        name="dequantize",
    )(ck, cv, ke, ve)


def rows_of(refs, start, count, cols):
    parts = []
    for ref in refs:
        if len(ref.shape) == 2:
            parts.append(ref[start : start + count, cols])
        else:
            parts.append(ref[:, start : start + count, cols].reshape(-1, cols.stop - cols.start))
    return parts[0] if len(parts) == 1 else jnp.concatenate(parts, axis=0)


def attend_keys(queries, keys, values, bias):
    scale = math.log2(math.e) / math.sqrt(DH)
    scores = lax.dot_general(
        queries, keys, (((1,), (1,)), ((), ())), preferred_element_type=jnp.float32
    )
    scores = scores * scale
    if bias is not None:
        scores = scores + bias
    peak = jnp.max(scores, axis=1, keepdims=True)
    raised = jnp.exp2(scores - peak)
    total = jnp.sum(raised, axis=1, keepdims=True)
    product = jnp.dot(raised.astype(jnp.bfloat16), values, preferred_element_type=jnp.float32)
    return peak, total, product


def bias_rows(bias_ref):
    count, width = bias_ref.shape
    return jnp.concatenate(
        [jnp.broadcast_to(bias_ref[row : row + 1], (QBLK, width)) for row in range(count)], axis=0
    )


def attend_kernel(q_count, k_count, q_start, rows, masked, merge, final, *refs):
    q_refs, refs = refs[:q_count], refs[q_count:]
    k_refs, refs = refs[:k_count], refs[k_count:]
    bias = None
    if masked:
        bias, refs = bias_rows(refs[0]), refs[1:]
    if merge:
        state, refs = refs[:3], refs[3:]
    width = q_refs[0].shape[1]
    half = k_refs[-1].shape[-2] // 2 if masked else rows
    for at in range(0, width, DH):
        cols = slice(at, at + DH)
        queries = rows_of(q_refs, q_start, rows, cols)
        keys = rows_of(k_refs, 0, half, cols)
        values = rows_of(k_refs, half, half, cols)
        peak, total, product = attend_keys(queries, keys, values, bias)
        if merge:
            peak_1, total_1, product_1 = [ref[:, cols] for ref in state]
            top = jnp.maximum(peak, peak_1)
            share, share_1 = jnp.exp2(peak - top), jnp.exp2(peak_1 - top)
            peak = top
            total = total * share + total_1 * share_1
            product = product * share + product_1 * share_1
        if final:
            result = (product / total).astype(jnp.bfloat16)
            for i in range(q_count):
                refs[i][:, cols] = result[i * rows : (i + 1) * rows]
        else:
            for ref, x in zip(refs, (peak, total, product)):
                ref[:, cols] = jnp.broadcast_to(x, product.shape)


def attend(q, keys, name, bias=None, state=(), final=False):
    groups = len(q)
    rows, width = q[0].shape[0] // 3, q[0].shape[1]
    half = keys[-1].shape[-2] // 2 if bias is not None else rows
    count = sum(x.shape[0] if x.ndim == 3 else 1 for x in keys) * half
    if final:
        out_shape = [jax.ShapeDtypeStruct((rows, width), jnp.bfloat16)] * groups
    else:
        out_shape = [jax.ShapeDtypeStruct((groups * rows, width), jnp.float32)] * 3
    operands = (*q, *keys, *([] if bias is None else [bias]), *state)
    return pl.pallas_call(
        functools.partial(
            attend_kernel,
            groups,
            len(keys),
            2 * rows,
            rows,
            bias is not None,
            bool(state),
            final,
        ),
        out_shape=out_shape,
        in_specs=vmem(len(operands)),
        out_specs=vmem(len(out_shape)),
        compiler_params=pltpu.CompilerParams(vmem_limit_bytes=LARGE),
        cost_estimate=pl.CostEstimate(
            flops=4 * groups * rows * count * width,
            bytes_accessed=4 * count * width,
            transcendentals=groups * rows * count * width // DH,
        ),
        name=name,
    )(*operands)


def unpack_kernel(groups, gather, width, *refs):
    parts, out_ref, sems = refs[:groups], refs[groups], refs[groups + 1]
    me = lax.axis_index("seq") // gather
    copies = [
        pltpu.make_async_copy(
            parts[t], out_ref.at[:, columns(partner(me, t, groups), width)], sems.at[t]
        )
        for t in range(groups)
    ]
    for copy in copies:
        copy.start()
    for copy in copies:
        copy.wait()


def unpack(parts, groups, gather):
    rows, width = parts[0].shape
    return pl.pallas_call(
        functools.partial(unpack_kernel, groups, gather, width),
        out_shape=jax.ShapeDtypeStruct((rows, groups * width), jnp.bfloat16),
        in_specs=vmem(groups),
        out_specs=pl.BlockSpec(memory_space=pl.ANY),
        scratch_shapes=[pltpu.SemaphoreType.DMA((groups,))],
        compiler_params=pltpu.CompilerParams(vmem_limit_bytes=SMALL),
        cost_estimate=pl.CostEstimate(
            flops=0, bytes_accessed=4 * groups * rows * width, transcendentals=0
        ),
        name="unpack_heads",
    )(*parts)


def per_device(
    seq_count,
    head_count,
    query_new,
    key_new,
    value_new,
    cache_keys,
    cache_values,
    key_exponent,
    value_exponent,
    block_mask,
):
    tok_rows, width_dev = query_new.shape
    groups = math.gcd(width_dev // DH, seq_count)
    gather = seq_count // groups
    width = width_dev // groups
    cache_rows = cache_keys.shape[0]
    seq_index = lax.axis_index("seq")
    head_index = lax.axis_index("head")
    group, member = seq_index // gather, seq_index % gather

    def to_group(x, t):
        if t == 0:
            return x
        pairs = [
            (s, partner(s // gather, t, groups) * gather + s % gather) for s in range(seq_count)
        ]
        return lax.ppermute(x, "seq", pairs)

    def from_group(x, t):
        if t == 0:
            return x
        pairs = [
            (s, origin(s // gather, t, groups) * gather + s % gather) for s in range(seq_count)
        ]
        return lax.ppermute(x, "seq", pairs)

    def to_member(x, t):
        pairs = [
            (s, s // gather * gather + partner(s % gather, t, gather)) for s in range(seq_count)
        ]
        return lax.ppermute(x, "seq", pairs)

    def to_head(x, t):
        if t == 0:
            return x
        return lax.ppermute(x, "head", [(h, partner(h, t, head_count)) for h in range(head_count)])

    members = range(1, gather)
    kv_own = pack(query_new, key_new, value_new, groups, gather)
    kv = [to_group(kv_own[t], t) for t in range(groups)]
    kv_other = [to_member(kv_own[0][: 2 * tok_rows], s) for s in members]
    if gather > 1:
        cache_keys, cache_values, kv_other[0] = lax.optimization_barrier(
            (cache_keys, cache_values, kv_other[0])
        )

    stored = dequantize(cache_keys, cache_values, key_exponent, value_exponent, head_count)
    by_head = []
    for t in range(head_count):
        x = stored[t]
        if t > 2:
            x, _ = lax.optimization_barrier((x, by_head[t - 2]))
        by_head.append(to_head(x, t))
    by_head = jnp.stack(by_head, axis=1).reshape(2 * head_count * cache_rows, width_dev)
    if groups > 1:
        by_head, kv[1] = lax.optimization_barrier((by_head, kv[1]))
    cache = [
        to_group(
            lax.dynamic_slice_in_dim(by_head, partner(group, t, groups) * width, width, 1), t
        )
        for t in range(groups)
    ]

    if groups > 1:
        swap = jnp.stack([x[: 2 * tok_rows] for x in kv[1:]])
        kv_other += [to_member(swap, s) for s in members]
    swap = jnp.stack(cache)
    cache_other = [to_member(swap, s) for s in members]

    q_source = jnp.stack([origin(group, t, groups) * gather + member for t in range(groups)])
    blocks = tok_rows // QBLK
    q_block = (q_source[:, None] * blocks + jnp.arange(blocks)[None, :]).reshape(-1)
    q_pick = (q_block[:, None] == jnp.arange(block_mask.shape[0])[None, :]).astype(jnp.float32)
    row_mask = jnp.dot(q_pick, block_mask.astype(jnp.float32))

    def bias_of(steps):
        device = jnp.stack(
            [
                (origin(group, t, groups) * gather + origin(member, s, gather)) * head_count
                + origin(head_index, z, head_count)
                for s in steps
                for t in range(groups)
                for z in range(head_count)
            ]
        )
        block = (device[:, None] * cache_rows + jnp.arange(cache_rows)[None, :]).reshape(-1)
        pick = jnp.arange(block_mask.shape[1])[:, None] == (block // CBLK)[None, :]
        seen = jnp.dot(row_mask, pick.astype(jnp.float32))
        return jnp.where(seen > 0.5, 0.0, MASKED).astype(jnp.float32)

    state = attend(kv, kv + kv_other, "attend_new")
    own = attend(kv, cache, "attend_cache_own", bias_of([0]), state, final=gather == 1)
    parts = own
    if gather > 1:
        parts = attend(kv, cache_other, "attend_cache_other", bias_of(members), own, final=True)
    back = [from_group(parts[t], t) for t in range(groups)]
    return unpack(back, groups, gather)


def solution(mesh):
    return jax.shard_map(
        functools.partial(per_device, mesh.shape["seq"], mesh.shape["head"]),
        mesh=mesh,
        in_specs=(
            P("seq", "head"),
            P("seq", "head"),
            P("seq", "head"),
            P(("seq", "head"), None),
            P(("seq", "head"), None),
            P(("seq", "head"), None),
            P(("seq", "head"), None),
            P(),
        ),
        out_specs=P("seq", "head"),
        check_vma=False,
    )
```

```python
import functools
import math

import jax
import jax.numpy as jnp
from jax import lax
from jax.experimental import pallas as pl
from jax.experimental.pallas import tpu as pltpu
from jax.sharding import PartitionSpec as P

DH = 128
QBLK = 64
CBLK = 32
SBLK = 4
MASKED = -1e30
SMALL = 16 * 2**20
LARGE = 32 * 2**20


def partner(index, step, count):
    if count & (count - 1) == 0:
        return index ^ step
    return (index + step) % count


def origin(index, step, count):
    if count & (count - 1) == 0:
        return index ^ step
    return (index + count - step) % count


def columns(chunk, width):
    return pl.ds(pl.multiple_of(chunk * width, DH), width)


def vmem(count):
    return [pl.BlockSpec(memory_space=pltpu.VMEM)] * count


def pack_kernel(groups, gather, width, q_ref, k_ref, v_ref, *rest):
    outs, sems = rest[:-1], rest[-1]
    rows = q_ref.shape[0]
    me = lax.axis_index("seq") // gather
    copies = []
    for t in reversed(range(groups)):
        cols = columns(partner(me, t, groups), width)
        for i, src in enumerate((k_ref, v_ref, q_ref)):
            dst = outs[t].at[pl.ds(i * rows, rows)]
            copies.append(pltpu.make_async_copy(src.at[:, cols], dst, sems.at[t, i]))
    for copy in copies:
        copy.start()
    for copy in copies:
        copy.wait()


def pack(q, k, v, groups, gather):
    rows, width = q.shape[0], q.shape[1] // groups
    return pl.pallas_call(
        functools.partial(pack_kernel, groups, gather, width),
        out_shape=[jax.ShapeDtypeStruct((3 * rows, width), q.dtype)] * groups,
        in_specs=[pl.BlockSpec(memory_space=pltpu.HBM)] * 3,
        out_specs=vmem(groups),
        scratch_shapes=[pltpu.SemaphoreType.DMA((groups, 3))],
        compiler_params=pltpu.CompilerParams(vmem_limit_bytes=SMALL),
        cost_estimate=pl.CostEstimate(flops=0, bytes_accessed=6 * q.size, transcendentals=0),
        name="pack_heads",
    )(*[pltpu.with_memory_space_constraint(x, pltpu.HBM) for x in (q, k, v)])


def dequantize_kernel(shards, ck_ref, cv_ref, ke_ref, ve_ref, *outs):
    me = lax.axis_index("head")
    blocks, heads = ke_ref.shape
    rows, width = outs[0].shape[1:]
    exponent = jnp.concatenate(
        [
            jnp.broadcast_to(ref[i : i + 1], (SBLK, heads))
            for ref in (ke_ref, ve_ref)
            for i in range(blocks)
        ],
        axis=0,
    )
    power = jnp.left_shift(1, exponent + 16).astype(jnp.float32) * 2.0**-16
    power = power.astype(jnp.bfloat16)
    head = lax.broadcasted_iota(jnp.int32, (heads, width), 0)
    head -= lax.broadcasted_iota(jnp.int32, (heads, width), 1) // DH
    for t in range(shards):
        part = partner(me, t, shards)
        spread = (head == part * (width // DH)).astype(jnp.float32).astype(jnp.bfloat16)
        factor = jnp.dot(power, spread, preferred_element_type=jnp.float32)
        for which, m_ref in enumerate((ck_ref, cv_ref)):
            mantissa = m_ref[:, columns(part, width)].astype(jnp.float32)
            scaled = mantissa * factor[which * rows : (which + 1) * rows]
            outs[t][which] = scaled.astype(jnp.bfloat16)


def dequantize(ck, cv, ke, ve, shards):
    rows, width = ck.shape
    return pl.pallas_call(
        functools.partial(dequantize_kernel, shards),
        out_shape=[jax.ShapeDtypeStruct((2, rows, width // shards), jnp.bfloat16)] * shards,
        in_specs=vmem(4),
        out_specs=vmem(shards),
        compiler_params=pltpu.CompilerParams(vmem_limit_bytes=SMALL),
        cost_estimate=pl.CostEstimate(flops=2 * ck.size, bytes_accessed=8 * ck.size, transcendentals=0),
        name="dequantize",
    )(ck, cv, ke, ve)


def rows_of(refs, start, count, cols):
    parts = []
    for ref in refs:
        if len(ref.shape) == 2:
            parts.append(ref[start : start + count, cols])
        else:
            parts.append(ref[:, start : start + count, cols].reshape(-1, cols.stop - cols.start))
    return parts[0] if len(parts) == 1 else jnp.concatenate(parts, axis=0)


def attend_keys(queries, keys, values, bias):
    scale = math.log2(math.e) / math.sqrt(DH)
    scores = lax.dot_general(
        queries, keys, (((1,), (1,)), ((), ())), preferred_element_type=jnp.float32
    )
    scores = scores * scale
    if bias is not None:
        scores = scores + bias
    peak = jnp.max(scores, axis=1, keepdims=True)
    raised = jnp.exp2(scores - peak)
    total = jnp.sum(raised, axis=1, keepdims=True)
    product = jnp.dot(raised.astype(jnp.bfloat16), values, preferred_element_type=jnp.float32)
    return peak, total, product


def bias_rows(bias_ref, pieces, blocks):
    width = bias_ref.shape[1]
    return jnp.concatenate(
        [
            jnp.broadcast_to(bias_ref[row : row + 1], (QBLK, width))
            for t in pieces
            for row in range(t * blocks, (t + 1) * blocks)
        ],
        axis=0,
    )


def attend_kernel(pieces, k_count, q_start, rows, masked, merge, final, *refs):
    q_count = len(pieces)
    q_refs, refs = refs[:q_count], refs[q_count:]
    k_refs, refs = refs[:k_count], refs[k_count:]
    bias = None
    if masked:
        bias, refs = bias_rows(refs[0], pieces, rows // QBLK), refs[1:]
    states, refs = [refs[3 * i : 3 * i + 3] for i in range(merge)], refs[3 * merge :]
    width = q_refs[0].shape[1]
    half = k_refs[-1].shape[-2] // 2 if masked else rows
    for at in range(0, width, DH):
        cols = slice(at, at + DH)
        queries = rows_of(q_refs, q_start, rows, cols)
        keys = rows_of(k_refs, 0, half, cols)
        values = rows_of(k_refs, half, half, cols)
        peak, total, product = attend_keys(queries, keys, values, bias)
        for state in states:
            peak_1, total_1, product_1 = [
                jnp.concatenate([ref[t * rows : (t + 1) * rows, cols] for t in pieces], axis=0)
                for ref in state
            ]
            top = jnp.maximum(peak, peak_1)
            share, share_1 = jnp.exp2(peak - top), jnp.exp2(peak_1 - top)
            peak = top
            total = total * share + total_1 * share_1
            product = product * share + product_1 * share_1
        if final:
            result = (product / total).astype(jnp.bfloat16)
            for i in range(q_count):
                refs[i][:, cols] = result[i * rows : (i + 1) * rows]
        else:
            for ref, x in zip(refs, (peak, total, product)):
                ref[:, cols] = jnp.broadcast_to(x, product.shape)


def attend(q, keys, name, bias=None, states=(), final=False, pieces=None):
    pieces = tuple(range(len(q))) if pieces is None else pieces
    q = [q[t] for t in pieces]
    groups = len(q)
    rows, width = q[0].shape[0] // 3, q[0].shape[1]
    half = keys[-1].shape[-2] // 2 if bias is not None else rows
    count = sum(x.shape[0] if x.ndim == 3 else 1 for x in keys) * half
    if final:
        out_shape = [jax.ShapeDtypeStruct((rows, width), jnp.bfloat16)] * groups
    else:
        out_shape = [jax.ShapeDtypeStruct((groups * rows, width), jnp.float32)] * 3
    operands = (*q, *keys, *([] if bias is None else [bias]), *(x for state in states for x in state))
    return pl.pallas_call(
        functools.partial(
            attend_kernel,
            pieces,
            len(keys),
            2 * rows,
            rows,
            bias is not None,
            len(states),
            final,
        ),
        out_shape=out_shape,
        in_specs=vmem(len(operands)),
        out_specs=vmem(len(out_shape)),
        compiler_params=pltpu.CompilerParams(vmem_limit_bytes=LARGE),
        cost_estimate=pl.CostEstimate(
            flops=4 * groups * rows * count * width,
            bytes_accessed=4 * count * width,
            transcendentals=groups * rows * count * width // DH,
        ),
        name=name,
    )(*operands)


def unpack_kernel(groups, gather, width, *refs):
    parts, out_ref, sems = refs[:groups], refs[groups], refs[groups + 1]
    me = lax.axis_index("seq") // gather
    copies = [
        pltpu.make_async_copy(
            parts[t], out_ref.at[:, columns(partner(me, t, groups), width)], sems.at[t]
        )
        for t in range(groups)
    ]
    for copy in copies:
        copy.start()
    for copy in copies:
        copy.wait()


def unpack(parts, groups, gather):
    rows, width = parts[0].shape
    return pl.pallas_call(
        functools.partial(unpack_kernel, groups, gather, width),
        out_shape=jax.ShapeDtypeStruct((rows, groups * width), jnp.bfloat16),
        in_specs=vmem(groups),
        out_specs=pl.BlockSpec(memory_space=pl.ANY),
        scratch_shapes=[pltpu.SemaphoreType.DMA((groups,))],
        compiler_params=pltpu.CompilerParams(vmem_limit_bytes=SMALL),
        cost_estimate=pl.CostEstimate(
            flops=0, bytes_accessed=4 * groups * rows * width, transcendentals=0
        ),
        name="unpack_heads",
    )(*parts)


def per_device(
    seq_count,
    head_count,
    query_new,
    key_new,
    value_new,
    cache_keys,
    cache_values,
    key_exponent,
    value_exponent,
    block_mask,
):
    tok_rows, width_dev = query_new.shape
    groups = math.gcd(width_dev // DH, seq_count)
    gather = seq_count // groups
    width = width_dev // groups
    cache_rows = cache_keys.shape[0]
    seq_index = lax.axis_index("seq")
    head_index = lax.axis_index("head")
    group, member = seq_index // gather, seq_index % gather

    def to_group(x, t):
        if t == 0:
            return x
        pairs = [
            (s, partner(s // gather, t, groups) * gather + s % gather) for s in range(seq_count)
        ]
        return lax.ppermute(x, "seq", pairs)

    def from_group(x, t):
        if t == 0:
            return x
        pairs = [
            (s, origin(s // gather, t, groups) * gather + s % gather) for s in range(seq_count)
        ]
        return lax.ppermute(x, "seq", pairs)

    def to_member(x, t):
        pairs = [
            (s, s // gather * gather + partner(s % gather, t, gather)) for s in range(seq_count)
        ]
        return lax.ppermute(x, "seq", pairs)

    def to_head(x, t):
        if t == 0:
            return x
        return lax.ppermute(x, "head", [(h, partner(h, t, head_count)) for h in range(head_count)])

    members = range(1, gather)
    kv_own = pack(query_new, key_new, value_new, groups, gather)
    kv = [to_group(kv_own[t], t) for t in range(groups)]
    kv_other = [to_member(kv_own[0][: 2 * tok_rows], s) for s in members]
    if gather > 1:
        cache_keys, cache_values, kv_other[0] = lax.optimization_barrier(
            (cache_keys, cache_values, kv_other[0])
        )

    stored = dequantize(cache_keys, cache_values, key_exponent, value_exponent, head_count)
    by_head = []
    for t in range(head_count):
        x = stored[t]
        if t > 2:
            x, _ = lax.optimization_barrier((x, by_head[t - 2]))
        by_head.append(to_head(x, t))
    by_head = jnp.stack(by_head, axis=1).reshape(2 * head_count * cache_rows, width_dev)
    kv[1:] = [lax.optimization_barrier((x, by_head))[0] for x in kv[1:]]
    cache = [
        to_group(
            lax.dynamic_slice_in_dim(by_head, partner(group, t, groups) * width, width, 1), t
        )
        for t in range(groups)
    ]

    if groups > 1:
        swap = jnp.stack([x[: 2 * tok_rows] for x in kv[1:]])
        kv_other += [to_member(swap, s) for s in members]
    swap = jnp.stack(cache)
    cache_other = [to_member(swap, s) for s in members]

    q_source = jnp.stack([origin(group, t, groups) * gather + member for t in range(groups)])
    blocks = tok_rows // QBLK
    q_block = (q_source[:, None] * blocks + jnp.arange(blocks)[None, :]).reshape(-1)
    q_pick = (q_block[:, None] == jnp.arange(block_mask.shape[0])[None, :]).astype(jnp.float32)
    row_mask = jnp.dot(q_pick, block_mask.astype(jnp.float32))

    def bias_of(steps):
        device = jnp.stack(
            [
                (origin(group, t, groups) * gather + origin(member, s, gather)) * head_count
                + origin(head_index, z, head_count)
                for s in steps
                for t in range(groups)
                for z in range(head_count)
            ]
        )
        block = (device[:, None] * cache_rows + jnp.arange(cache_rows)[None, :]).reshape(-1)
        pick = jnp.arange(block_mask.shape[1])[:, None] == (block // CBLK)[None, :]
        seen = jnp.dot(row_mask, pick.astype(jnp.float32))
        return jnp.where(seen > 0.5, 0.0, MASKED).astype(jnp.float32)

    new = attend(kv, kv + kv_other, "attend_new")
    if gather == 1:
        parts = attend(kv, cache, "attend_cache_own", bias_of([0]), [new], final=True)
    else:
        own = attend(kv, cache, "attend_cache_own", bias_of([0]))
        parts = [None] * groups
        bias = bias_of(members)
        steps = tuple(range(1, groups))
        for pieces in filter(None, (steps[-1:], steps[:-1], (0,))):
            done = attend(kv, cache_other, "attend_cache_other", bias, [new, own], True, pieces)
            for t, part in zip(pieces, done):
                parts[t] = part
    back = [from_group(parts[t], t) for t in range(groups)]
    return unpack(back, groups, gather)


def solution(mesh):
    return jax.shard_map(
        functools.partial(per_device, mesh.shape["seq"], mesh.shape["head"]),
        mesh=mesh,
        in_specs=(
            P("seq", "head"),
            P("seq", "head"),
            P("seq", "head"),
            P(("seq", "head"), None),
            P(("seq", "head"), None),
            P(("seq", "head"), None),
            P(("seq", "head"), None),
            P(),
        ),
        out_specs=P("seq", "head"),
        check_vma=False,
    )
```

```python
import functools
import math

import jax
import jax.numpy as jnp
from jax import lax
from jax.experimental import pallas as pl
from jax.experimental.pallas import tpu as pltpu
from jax.sharding import PartitionSpec as P

DH = 128
QBLK = 64
CBLK = 32
SBLK = 4
MASKED = -1e30
SMALL = 16 * 2**20
LARGE = 32 * 2**20


def partner(index, step, count):
    if count & (count - 1) == 0:
        return index ^ step
    return (index + step) % count


def origin(index, step, count):
    if count & (count - 1) == 0:
        return index ^ step
    return (index + count - step) % count


def columns(chunk, width):
    return pl.ds(pl.multiple_of(chunk * width, DH), width)


def vmem(count):
    return [pl.BlockSpec(memory_space=pltpu.VMEM)] * count


def pack_kernel(groups, gather, width, q_ref, k_ref, v_ref, *rest):
    outs, sems = rest[:-1], rest[-1]
    rows = q_ref.shape[0]
    me = lax.axis_index("seq") // gather
    copies = []
    for t in reversed(range(groups)):
        cols = columns(partner(me, t, groups), width)
        for i, src in enumerate((k_ref, v_ref, q_ref)):
            dst = outs[t].at[pl.ds(i * rows, rows)]
            copies.append(pltpu.make_async_copy(src.at[:, cols], dst, sems.at[t, i]))
    for copy in copies:
        copy.start()
    for copy in copies:
        copy.wait()


def pack(q, k, v, groups, gather):
    rows, width = q.shape[0], q.shape[1] // groups
    return pl.pallas_call(
        functools.partial(pack_kernel, groups, gather, width),
        out_shape=[jax.ShapeDtypeStruct((3 * rows, width), q.dtype)] * groups,
        in_specs=[pl.BlockSpec(memory_space=pltpu.HBM)] * 3,
        out_specs=vmem(groups),
        scratch_shapes=[pltpu.SemaphoreType.DMA((groups, 3))],
        compiler_params=pltpu.CompilerParams(vmem_limit_bytes=SMALL),
        cost_estimate=pl.CostEstimate(flops=0, bytes_accessed=6 * q.size, transcendentals=0),
        name="pack_heads",
    )(*[pltpu.with_memory_space_constraint(x, pltpu.HBM) for x in (q, k, v)])


def dequantize_kernel(groups, gather, shards, ck_ref, cv_ref, ke_ref, ve_ref, *outs):
    group, shard = lax.axis_index("seq") // gather, lax.axis_index("head")
    blocks, heads = ke_ref.shape
    rows, width = outs[0].shape[2:]
    exponent = jnp.concatenate(
        [
            jnp.broadcast_to(ref[i : i + 1], (SBLK, heads))
            for ref in (ke_ref, ve_ref)
            for i in range(blocks)
        ],
        axis=0,
    )
    power = jnp.left_shift(1, exponent + 16).astype(jnp.float32) * 2.0**-16
    power = power.astype(jnp.bfloat16)
    head = lax.broadcasted_iota(jnp.int32, (heads, width), 0)
    head -= lax.broadcasted_iota(jnp.int32, (heads, width), 1) // DH
    for t in range(groups):
        for s in range(shards):
            part = partner(shard, s, shards) * groups + partner(group, t, groups)
            spread = (head == part * (width // DH)).astype(jnp.float32).astype(jnp.bfloat16)
            factor = jnp.dot(power, spread, preferred_element_type=jnp.float32)
            for which, m_ref in enumerate((ck_ref, cv_ref)):
                mantissa = m_ref[:, columns(part, width)].astype(jnp.float32)
                scaled = mantissa * factor[which * rows : (which + 1) * rows]
                outs[t][s, which] = scaled.astype(jnp.bfloat16)


def dequantize(ck, cv, ke, ve, groups, gather, shards):
    rows, width = ck.shape[0], ck.shape[1] // (shards * groups)
    return pl.pallas_call(
        functools.partial(dequantize_kernel, groups, gather, shards),
        out_shape=[jax.ShapeDtypeStruct((shards, 2, rows, width), jnp.bfloat16)] * groups,
        in_specs=vmem(4),
        out_specs=vmem(groups),
        compiler_params=pltpu.CompilerParams(vmem_limit_bytes=SMALL),
        cost_estimate=pl.CostEstimate(flops=2 * ck.size, bytes_accessed=8 * ck.size, transcendentals=0),
        name="dequantize",
    )(ck, cv, ke, ve)


def rows_of(refs, start, count, cols):
    parts = []
    for ref in refs:
        if len(ref.shape) == 2:
            parts.append(ref[start : start + count, cols])
        else:
            parts.append(ref[:, start : start + count, cols].reshape(-1, cols.stop - cols.start))
    return parts[0] if len(parts) == 1 else jnp.concatenate(parts, axis=0)


def attend_sets(queries, sets):
    scale = math.log2(math.e) / math.sqrt(DH)
    scores = []
    for keys, _, bias in sets:
        x = lax.dot_general(
            queries, keys, (((1,), (1,)), ((), ())), preferred_element_type=jnp.float32
        )
        scores.append(x * scale if bias is None else x * scale + bias)
    peak = functools.reduce(
        jnp.maximum, [jnp.max(x, axis=1, keepdims=True) for x in scores]
    )
    total, product = 0.0, 0.0
    for x, (_, values, _) in zip(scores, sets):
        raised = jnp.exp2(x - peak)
        total += jnp.sum(raised, axis=1, keepdims=True)
        product += jnp.dot(
            raised.astype(jnp.bfloat16), values, preferred_element_type=jnp.float32
        )
    return peak, total, product


def bias_rows(bias_ref, pieces, blocks):
    width = bias_ref.shape[1]
    return jnp.concatenate(
        [
            jnp.broadcast_to(bias_ref[row : row + 1], (QBLK, width))
            for t in pieces
            for row in range(t * blocks, (t + 1) * blocks)
        ],
        axis=0,
    )


def attend_kernel(groups, counts, q_start, rows, merge, final, *refs):
    q_refs, refs = refs[:groups], refs[groups:]
    sets = []
    for count, masked in counts:
        bias = bias_rows(refs[count], range(groups), rows // QBLK) if masked else None
        sets.append((refs[:count], refs[0].shape[-2] // 2 if masked else rows, bias))
        refs = refs[count + masked :]
    state, refs = (refs[:3], refs[3:]) if merge else (None, refs)
    width = q_refs[0].shape[1]
    for at in range(0, width, DH):
        cols = slice(at, at + DH)
        queries = rows_of(q_refs, q_start, rows, cols)
        peak, total, product = attend_sets(
            queries,
            [
                (rows_of(k_refs, 0, half, cols), rows_of(k_refs, half, half, cols), bias)
                for k_refs, half, bias in sets
            ],
        )
        if merge:
            peak_1, total_1, product_1 = [ref[:, cols] for ref in state]
            top = jnp.maximum(peak, peak_1)
            share, share_1 = jnp.exp2(peak - top), jnp.exp2(peak_1 - top)
            total = total * share + total_1 * share_1
            product = product * share + product_1 * share_1
        if final:
            result = (product / total).astype(jnp.bfloat16)
            for i in range(groups):
                refs[i][:, cols] = result[i * rows : (i + 1) * rows]
        else:
            for ref, x in zip(refs, (peak, total, product)):
                ref[:, cols] = jnp.broadcast_to(x, product.shape)


def attend(q, new, cache, bias, name, state=(), final=False):
    groups = len(q)
    rows, width = q[0].shape[0] // 3, q[0].shape[1]
    count = sum(x.shape[0] if x.ndim == 3 else 1 for x in new) * rows
    count += sum(x.size for x in cache) // (2 * width)
    if final:
        out_shape = [jax.ShapeDtypeStruct((rows, width), jnp.bfloat16)] * groups
    else:
        out_shape = [jax.ShapeDtypeStruct((groups * rows, width), jnp.float32)] * 3
    operands = (*q, *new, *cache, bias, *state)
    return pl.pallas_call(
        functools.partial(
            attend_kernel,
            groups,
            ((len(new), False), (len(cache), True)),
            2 * rows,
            rows,
            bool(state),
            final,
        ),
        out_shape=out_shape,
        in_specs=vmem(len(operands)),
        out_specs=vmem(len(out_shape)),
        compiler_params=pltpu.CompilerParams(vmem_limit_bytes=LARGE),
        cost_estimate=pl.CostEstimate(
            flops=4 * groups * rows * count * width,
            bytes_accessed=4 * count * width,
            transcendentals=groups * rows * count * width // DH,
        ),
        name=name,
    )(*operands)


def unpack_kernel(steps, gather, width, *refs):
    groups = len(steps)
    parts, out_ref, sems = refs[:groups], refs[groups], refs[groups + 1]
    me = lax.axis_index("seq") // gather
    copies = [
        pltpu.make_async_copy(
            parts[i], out_ref.at[:, columns(partner(me, t, groups), width)], sems.at[i]
        )
        for i, t in enumerate(steps)
    ]
    for copy in copies:
        copy.start()
    for copy in copies:
        copy.wait()


def unpack(parts, steps, gather):
    rows, width = parts[0].shape
    groups = len(steps)
    return pl.pallas_call(
        functools.partial(unpack_kernel, tuple(steps), gather, width),
        out_shape=jax.ShapeDtypeStruct((rows, groups * width), jnp.bfloat16),
        in_specs=vmem(groups),
        out_specs=pl.BlockSpec(memory_space=pl.ANY),
        scratch_shapes=[pltpu.SemaphoreType.DMA((groups,))],
        compiler_params=pltpu.CompilerParams(vmem_limit_bytes=SMALL),
        cost_estimate=pl.CostEstimate(
            flops=0, bytes_accessed=4 * groups * rows * width, transcendentals=0
        ),
        name="unpack_heads",
    )(*parts)


def per_device(
    seq_count,
    head_count,
    query_new,
    key_new,
    value_new,
    cache_keys,
    cache_values,
    key_exponent,
    value_exponent,
    block_mask,
):
    tok_rows, width_dev = query_new.shape
    groups = math.gcd(width_dev // DH, seq_count)
    gather = seq_count // groups
    width = width_dev // groups
    cache_rows = cache_keys.shape[0]
    seq_index = lax.axis_index("seq")
    head_index = lax.axis_index("head")
    group, member = seq_index // gather, seq_index % gather

    def to_group(x, t):
        if t == 0:
            return x
        pairs = [
            (s, partner(s // gather, t, groups) * gather + s % gather) for s in range(seq_count)
        ]
        return lax.ppermute(x, "seq", pairs)

    def from_group(x, t):
        if t == 0:
            return x
        pairs = [
            (s, origin(s // gather, t, groups) * gather + s % gather) for s in range(seq_count)
        ]
        return lax.ppermute(x, "seq", pairs)

    def to_member(x, t):
        pairs = [
            (s, s // gather * gather + partner(s % gather, t, gather)) for s in range(seq_count)
        ]
        return lax.ppermute(x, "seq", pairs)

    def to_head(x, t):
        if t == 0:
            return x
        return lax.ppermute(x, "head", [(h, partner(h, t, head_count)) for h in range(head_count)])

    members = range(1, gather)
    kv_own = pack(query_new, key_new, value_new, groups, gather)
    stored = dequantize(
        cache_keys, cache_values, key_exponent, value_exponent, groups, gather, head_count
    )
    stored = [to_group(stored[t], t) for t in range(groups)]
    kv = [to_group(kv_own[t], t) for t in range(groups)]

    cache = []
    for s in range(head_count):
        x = jnp.stack([stored[t][s] for t in range(groups)])
        if s > 2:
            x, cache[s - 2] = lax.optimization_barrier((x, cache[s - 2]))
        cache.append(to_head(x, s))
    cache = jnp.stack(cache).transpose(2, 0, 1, 3, 4).reshape(-1, width)

    kv_swap = jnp.stack([x[: 2 * tok_rows] for x in kv])
    kv_other = [to_member(kv_swap, s) for s in members]
    cache_other = [to_member(cache, s) for s in members]

    q_source = jnp.stack([origin(group, t, groups) * gather + member for t in range(groups)])
    blocks = tok_rows // QBLK
    q_block = (q_source[:, None] * blocks + jnp.arange(blocks)[None, :]).reshape(-1)
    q_pick = (q_block[:, None] == jnp.arange(block_mask.shape[0])[None, :]).astype(jnp.float32)
    row_mask = jnp.dot(q_pick, block_mask.astype(jnp.float32))

    def bias_of(steps):
        device = jnp.stack(
            [
                (origin(group, t, groups) * gather + origin(member, s, gather)) * head_count
                + origin(head_index, z, head_count)
                for s in steps
                for z in range(head_count)
                for t in range(groups)
            ]
        )
        block = (device[:, None] * cache_rows + jnp.arange(cache_rows)[None, :]).reshape(-1)
        pick = jnp.arange(block_mask.shape[1])[:, None] == (block // CBLK)[None, :]
        seen = jnp.dot(row_mask, pick.astype(jnp.float32))
        return jnp.where(seen > 0.5, 0.0, MASKED).astype(jnp.float32)

    parts = attend(kv, kv, [cache], bias_of([0]), "attend_own", final=gather == 1)
    if gather > 1:
        bias = bias_of(members)
        parts = attend(kv, kv_other, cache_other, bias, "attend_other", parts, final=True)
    steps = [t for t in reversed(range(groups))]
    return unpack([from_group(parts[t], t) for t in steps], steps, gather)


def solution(mesh):
    return jax.shard_map(
        functools.partial(per_device, mesh.shape["seq"], mesh.shape["head"]),
        mesh=mesh,
        in_specs=(
            P("seq", "head"),
            P("seq", "head"),
            P("seq", "head"),
            P(("seq", "head"), None),
            P(("seq", "head"), None),
            P(("seq", "head"), None),
            P(("seq", "head"), None),
            P(),
        ),
        out_specs=P("seq", "head"),
        check_vma=False,
    )
```

```python
import functools
import math

import jax
import jax.numpy as jnp
from jax import lax
from jax.experimental import pallas as pl
from jax.experimental.pallas import tpu as pltpu
from jax.sharding import PartitionSpec as P

DH = 128
QBLK = 64
CBLK = 32
SBLK = 4
MASKED = -1e30
SMALL = 16 * 2**20
LARGE = 32 * 2**20


def partner(index, step, count):
    if count & (count - 1) == 0:
        return index ^ step
    return (index + step) % count


def origin(index, step, count):
    if count & (count - 1) == 0:
        return index ^ step
    return (index + count - step) % count


def columns(chunk, width):
    return pl.ds(pl.multiple_of(chunk * width, DH), width)


def vmem(count):
    return [pl.BlockSpec(memory_space=pltpu.VMEM)] * count


def prepare_kernel(groups, gather, shards, *refs):
    new_refs, cache_refs, outs, scratch = refs[:3], refs[3:7], refs[7:-6], refs[-6:]
    pieces, cached = outs[:groups], outs[groups:]
    ck_buf, cv_buf, ke_buf, ve_buf, cache_sems, new_sems = scratch
    group, shard = lax.axis_index("seq") // gather, lax.axis_index("head")

    loads = [
        pltpu.make_async_copy(src, dst, cache_sems.at[i])
        for i, (src, dst) in enumerate(zip(cache_refs, (ck_buf, cv_buf, ke_buf, ve_buf)))
    ]
    rows, width = pieces[0].shape[0] // 3, pieces[0].shape[1]
    copies = []
    for t in range(groups):
        cols = columns(partner(group, t, groups), width)
        for i, src in enumerate(new_refs):
            dst = pieces[t].at[pl.ds(i * rows, rows)]
            copies.append(pltpu.make_async_copy(src.at[:, cols], dst, new_sems.at[t, i]))
    for copy in loads + copies:
        copy.start()
    for copy in loads:
        copy.wait()

    blocks, heads = ke_buf.shape
    cache_rows = ck_buf.shape[0]
    exponent = jnp.concatenate(
        [
            jnp.broadcast_to(ref[i : i + 1], (SBLK, heads))
            for ref in (ke_buf, ve_buf)
            for i in range(blocks)
        ],
        axis=0,
    )
    power = jnp.left_shift(1, exponent + 16).astype(jnp.float32) * 2.0**-16
    power = power.astype(jnp.bfloat16)
    head = lax.broadcasted_iota(jnp.int32, (heads, width), 0)
    head -= lax.broadcasted_iota(jnp.int32, (heads, width), 1) // DH
    for t in range(groups):
        for s in range(shards):
            part = partner(shard, s, shards) * groups + partner(group, t, groups)
            spread = (head == part * (width // DH)).astype(jnp.float32).astype(jnp.bfloat16)
            factor = jnp.dot(power, spread, preferred_element_type=jnp.float32)
            for which, buf in enumerate((ck_buf, cv_buf)):
                mantissa = buf[:, columns(part, width)].astype(jnp.float32)
                scaled = mantissa * factor[which * cache_rows : (which + 1) * cache_rows]
                cached[t][s, which] = scaled.astype(jnp.bfloat16)
    for copy in copies:
        copy.wait()


def prepare(q, k, v, ck, cv, ke, ve, groups, gather, shards):
    rows, width = q.shape[0], q.shape[1] // groups
    operands = (k, v, q, ck, cv, ke, ve)
    outs = pl.pallas_call(
        functools.partial(prepare_kernel, groups, gather, shards),
        out_shape=[jax.ShapeDtypeStruct((3 * rows, width), jnp.bfloat16)] * groups
        + [jax.ShapeDtypeStruct((shards, 2, ck.shape[0], width), jnp.bfloat16)] * groups,
        in_specs=[pl.BlockSpec(memory_space=pltpu.HBM)] * len(operands),
        out_specs=vmem(2 * groups),
        scratch_shapes=[pltpu.VMEM(x.shape, x.dtype) for x in (ck, cv, ke, ve)]
        + [pltpu.SemaphoreType.DMA((4,)), pltpu.SemaphoreType.DMA((groups, 3))],
        compiler_params=pltpu.CompilerParams(vmem_limit_bytes=SMALL),
        cost_estimate=pl.CostEstimate(
            flops=4 * ck.size, bytes_accessed=12 * q.size + 8 * ck.size, transcendentals=0
        ),
        name="prepare",
    )(*[pltpu.with_memory_space_constraint(x, pltpu.HBM) for x in operands])
    return outs[:groups], outs[groups:]


def rows_of(refs, start, count, cols):
    parts = []
    for ref in refs:
        if len(ref.shape) == 2:
            parts.append(ref[start : start + count, cols])
        else:
            parts.append(ref[:, start : start + count, cols].reshape(-1, cols.stop - cols.start))
    return parts[0] if len(parts) == 1 else jnp.concatenate(parts, axis=0)


def attend_sets(queries, sets):
    scale = math.log2(math.e) / math.sqrt(DH)
    scores = []
    for keys, _, bias in sets:
        x = lax.dot_general(
            queries, keys, (((1,), (1,)), ((), ())), preferred_element_type=jnp.float32
        )
        scores.append(x * scale if bias is None else x * scale + bias)
    peak = functools.reduce(
        jnp.maximum, [jnp.max(x, axis=1, keepdims=True) for x in scores]
    )
    total, product = 0.0, 0.0
    for x, (_, values, _) in zip(scores, sets):
        raised = jnp.exp2(x - peak)
        total += jnp.sum(raised, axis=1, keepdims=True)
        product += jnp.dot(
            raised.astype(jnp.bfloat16), values, preferred_element_type=jnp.float32
        )
    return peak, total, product


def bias_rows(bias_ref, pieces, blocks):
    width = bias_ref.shape[1]
    return jnp.concatenate(
        [
            jnp.broadcast_to(bias_ref[row : row + 1], (QBLK, width))
            for t in pieces
            for row in range(t * blocks, (t + 1) * blocks)
        ],
        axis=0,
    )


def attend_kernel(pieces, counts, q_start, rows, merge, final, *refs):
    q_refs, refs = refs[: len(pieces)], refs[len(pieces) :]
    sets = []
    for count, masked in counts:
        bias = bias_rows(refs[count], pieces, rows // QBLK) if masked else None
        sets.append((refs[:count], refs[0].shape[-2] // 2 if masked else rows, bias))
        refs = refs[count + masked :]
    state, refs = (refs[:3], refs[3:]) if merge else (None, refs)
    width = q_refs[0].shape[1]
    for at in range(0, width, DH):
        cols = slice(at, at + DH)
        queries = rows_of(q_refs, q_start, rows, cols)
        peak, total, product = attend_sets(
            queries,
            [
                (rows_of(k_refs, 0, half, cols), rows_of(k_refs, half, half, cols), bias)
                for k_refs, half, bias in sets
            ],
        )
        if merge:
            peak_1, total_1, product_1 = [
                jnp.concatenate([ref[t * rows : (t + 1) * rows, cols] for t in pieces], axis=0)
                for ref in state
            ]
            top = jnp.maximum(peak, peak_1)
            share, share_1 = jnp.exp2(peak - top), jnp.exp2(peak_1 - top)
            total = total * share + total_1 * share_1
            product = product * share + product_1 * share_1
        if final:
            result = (product / total).astype(jnp.bfloat16)
            for i in range(len(pieces)):
                refs[i][:, cols] = result[i * rows : (i + 1) * rows]
        else:
            for ref, x in zip(refs, (peak, total, product)):
                ref[:, cols] = jnp.broadcast_to(x, product.shape)


def attend(q, pieces, new, cache, bias, name, state=(), final=False):
    groups = len(pieces)
    rows, width = q[0].shape[0] // 3, q[0].shape[1]
    count = sum(x.shape[0] if x.ndim == 3 else 1 for x in new) * rows
    count += sum(x.size for x in cache) // (2 * width)
    if final:
        out_shape = [jax.ShapeDtypeStruct((rows, width), jnp.bfloat16)] * groups
    else:
        out_shape = [jax.ShapeDtypeStruct((groups * rows, width), jnp.float32)] * 3
    operands = (*[q[t] for t in pieces], *new, *cache, bias, *state)
    return pl.pallas_call(
        functools.partial(
            attend_kernel,
            tuple(pieces),
            ((len(new), False), (len(cache), True)),
            2 * rows,
            rows,
            bool(state),
            final,
        ),
        out_shape=out_shape,
        in_specs=vmem(len(operands)),
        out_specs=vmem(len(out_shape)),
        compiler_params=pltpu.CompilerParams(vmem_limit_bytes=LARGE),
        cost_estimate=pl.CostEstimate(
            flops=4 * groups * rows * count * width,
            bytes_accessed=4 * count * width,
            transcendentals=groups * rows * count * width // DH,
        ),
        name=name,
    )(*operands)


def unpack_kernel(steps, gather, width, *refs):
    groups = len(steps)
    parts, out_ref, sems = refs[:groups], refs[groups], refs[groups + 1]
    me = lax.axis_index("seq") // gather
    copies = [
        pltpu.make_async_copy(
            parts[i], out_ref.at[:, columns(partner(me, t, groups), width)], sems.at[i]
        )
        for i, t in enumerate(steps)
    ]
    for copy in copies:
        copy.start()
    for copy in copies:
        copy.wait()


def unpack(parts, steps, gather):
    rows, width = parts[0].shape
    groups = len(steps)
    return pl.pallas_call(
        functools.partial(unpack_kernel, tuple(steps), gather, width),
        out_shape=jax.ShapeDtypeStruct((rows, groups * width), jnp.bfloat16),
        in_specs=vmem(groups),
        out_specs=pl.BlockSpec(memory_space=pl.ANY),
        scratch_shapes=[pltpu.SemaphoreType.DMA((groups,))],
        compiler_params=pltpu.CompilerParams(vmem_limit_bytes=SMALL),
        cost_estimate=pl.CostEstimate(
            flops=0, bytes_accessed=4 * groups * rows * width, transcendentals=0
        ),
        name="unpack_heads",
    )(*parts)


def per_device(
    seq_count,
    head_count,
    query_new,
    key_new,
    value_new,
    cache_keys,
    cache_values,
    key_exponent,
    value_exponent,
    block_mask,
):
    tok_rows, width_dev = query_new.shape
    groups = math.gcd(width_dev // DH, seq_count)
    gather = seq_count // groups
    width = width_dev // groups
    cache_rows = cache_keys.shape[0]
    seq_index = lax.axis_index("seq")
    head_index = lax.axis_index("head")
    group, member = seq_index // gather, seq_index % gather

    def to_group(x, t):
        if t == 0:
            return x
        pairs = [
            (s, partner(s // gather, t, groups) * gather + s % gather) for s in range(seq_count)
        ]
        return lax.ppermute(x, "seq", pairs)

    def from_group(x, t):
        if t == 0:
            return x
        pairs = [
            (s, origin(s // gather, t, groups) * gather + s % gather) for s in range(seq_count)
        ]
        return lax.ppermute(x, "seq", pairs)

    def to_member(x, t):
        pairs = [
            (s, s // gather * gather + partner(s % gather, t, gather)) for s in range(seq_count)
        ]
        return lax.ppermute(x, "seq", pairs)

    def to_head(x, t):
        if t == 0:
            return x
        return lax.ppermute(x, "head", [(h, partner(h, t, head_count)) for h in range(head_count)])

    members = range(1, gather)
    kv_own, stored = prepare(
        query_new,
        key_new,
        value_new,
        cache_keys,
        cache_values,
        key_exponent,
        value_exponent,
        groups,
        gather,
        head_count,
    )
    stored = [to_group(stored[t], t) for t in range(groups)]
    kv = [to_group(kv_own[t], t) for t in range(groups)]

    cache = []
    for s in range(head_count):
        x = jnp.stack([stored[t][s] for t in range(groups)])
        if s > 2:
            x, cache[s - 2] = lax.optimization_barrier((x, cache[s - 2]))
        cache.append(to_head(x, s))
    cache = jnp.stack(cache).transpose(2, 0, 1, 3, 4).reshape(-1, width)

    kv[1:] = [lax.optimization_barrier((x, cache))[0] for x in kv[1:]]
    kv_swap = jnp.stack([x[: 2 * tok_rows] for x in kv])
    kv_other = [to_member(kv_swap, s) for s in members]
    cache_other = [to_member(cache, s) for s in members]

    q_source = jnp.stack([origin(group, t, groups) * gather + member for t in range(groups)])
    blocks = tok_rows // QBLK
    q_block = (q_source[:, None] * blocks + jnp.arange(blocks)[None, :]).reshape(-1)
    q_pick = (q_block[:, None] == jnp.arange(block_mask.shape[0])[None, :]).astype(jnp.float32)
    row_mask = jnp.dot(q_pick, block_mask.astype(jnp.float32))

    def bias_of(steps):
        device = jnp.stack(
            [
                (origin(group, t, groups) * gather + origin(member, s, gather)) * head_count
                + origin(head_index, z, head_count)
                for s in steps
                for z in range(head_count)
                for t in range(groups)
            ]
        )
        block = (device[:, None] * cache_rows + jnp.arange(cache_rows)[None, :]).reshape(-1)
        pick = jnp.arange(block_mask.shape[1])[:, None] == (block // CBLK)[None, :]
        seen = jnp.dot(row_mask, pick.astype(jnp.float32))
        return jnp.where(seen > 0.5, 0.0, MASKED).astype(jnp.float32)

    every = range(groups)
    parts = attend(kv, every, kv, [cache], bias_of([0]), "attend_own", final=gather == 1)
    steps = [*every[-1:], *every[1:-1], *every[:1]] if groups > 1 else [0]
    if gather > 1:
        bias, state, parts = bias_of(members), parts, {}
        for pieces in filter(None, (steps[:-1], steps[-1:])):
            done = attend(kv, pieces, kv_other, cache_other, bias, "attend_other", state, True)
            parts.update(zip(pieces, done))
    return unpack([from_group(parts[t], t) for t in steps], steps, gather)


def solution(mesh):
    return jax.shard_map(
        functools.partial(per_device, mesh.shape["seq"], mesh.shape["head"]),
        mesh=mesh,
        in_specs=(
            P("seq", "head"),
            P("seq", "head"),
            P("seq", "head"),
            P(("seq", "head"), None),
            P(("seq", "head"), None),
            P(("seq", "head"), None),
            P(("seq", "head"), None),
            P(),
        ),
        out_specs=P("seq", "head"),
        check_vma=False,
    )
```

```python
import functools
import math

import jax
import jax.numpy as jnp
from jax import lax
from jax.experimental import pallas as pl
from jax.experimental.pallas import tpu as pltpu
from jax.sharding import PartitionSpec as P

DH = 128
QBLK = 64
CBLK = 32
SBLK = 4
MASKED = -1e30
SMALL = 16 * 2**20
LARGE = 32 * 2**20


def partner(index, step, count):
    if count & (count - 1) == 0:
        return index ^ step
    return (index + step) % count


def origin(index, step, count):
    if count & (count - 1) == 0:
        return index ^ step
    return (index + count - step) % count


def columns(chunk, width):
    return pl.ds(pl.multiple_of(chunk * width, DH), width)


def vmem(count):
    return [pl.BlockSpec(memory_space=pltpu.VMEM)] * count


def prepare_kernel(groups, gather, shards, *refs):
    new_refs, cache_refs, outs, scratch = refs[:3], refs[3:7], refs[7:-6], refs[-6:]
    pieces, cached = outs[:groups], outs[groups:]
    ck_buf, cv_buf, ke_buf, ve_buf, cache_sems, new_sems = scratch
    group, shard = lax.axis_index("seq") // gather, lax.axis_index("head")

    loads = [
        pltpu.make_async_copy(src, dst, cache_sems.at[i])
        for i, (src, dst) in enumerate(zip(cache_refs, (ck_buf, cv_buf, ke_buf, ve_buf)))
    ]
    rows, width = pieces[0].shape[0] // 3, pieces[0].shape[1]
    copies = []
    for t in range(groups):
        cols = columns(partner(group, t, groups), width)
        for i, src in enumerate(new_refs):
            dst = pieces[t].at[pl.ds(i * rows, rows)]
            copies.append(pltpu.make_async_copy(src.at[:, cols], dst, new_sems.at[t, i]))
    for copy in loads + copies:
        copy.start()
    for copy in loads:
        copy.wait()

    blocks, heads = ke_buf.shape
    cache_rows = ck_buf.shape[0]
    exponent = jnp.concatenate(
        [
            jnp.broadcast_to(ref[i : i + 1], (SBLK, heads))
            for ref in (ke_buf, ve_buf)
            for i in range(blocks)
        ],
        axis=0,
    )
    power = jnp.left_shift(1, exponent + 16).astype(jnp.float32) * 2.0**-16
    power = power.astype(jnp.bfloat16)
    head = lax.broadcasted_iota(jnp.int32, (heads, width), 0)
    head -= lax.broadcasted_iota(jnp.int32, (heads, width), 1) // DH
    for t in range(groups):
        for s in range(shards):
            part = partner(shard, s, shards) * groups + partner(group, t, groups)
            spread = (head == part * (width // DH)).astype(jnp.float32).astype(jnp.bfloat16)
            factor = jnp.dot(power, spread, preferred_element_type=jnp.float32)
            for which, buf in enumerate((ck_buf, cv_buf)):
                mantissa = buf[:, columns(part, width)].astype(jnp.float32)
                scaled = mantissa * factor[which * cache_rows : (which + 1) * cache_rows]
                cached[s][t, which] = scaled.astype(jnp.bfloat16)
    for copy in copies:
        copy.wait()


def prepare(q, k, v, ck, cv, ke, ve, groups, gather, shards):
    rows, width = q.shape[0], q.shape[1] // groups
    operands = (k, v, q, ck, cv, ke, ve)
    outs = pl.pallas_call(
        functools.partial(prepare_kernel, groups, gather, shards),
        out_shape=[jax.ShapeDtypeStruct((3 * rows, width), jnp.bfloat16)] * groups
        + [jax.ShapeDtypeStruct((groups, 2, ck.shape[0], width), jnp.bfloat16)] * shards,
        in_specs=[pl.BlockSpec(memory_space=pltpu.HBM)] * len(operands),
        out_specs=vmem(groups + shards),
        scratch_shapes=[pltpu.VMEM(x.shape, x.dtype) for x in (ck, cv, ke, ve)]
        + [pltpu.SemaphoreType.DMA((4,)), pltpu.SemaphoreType.DMA((groups, 3))],
        compiler_params=pltpu.CompilerParams(vmem_limit_bytes=SMALL),
        cost_estimate=pl.CostEstimate(
            flops=4 * ck.size, bytes_accessed=12 * q.size + 8 * ck.size, transcendentals=0
        ),
        name="prepare",
    )(*[pltpu.with_memory_space_constraint(x, pltpu.HBM) for x in operands])
    return outs[:groups], outs[groups:]


def rows_of(refs, start, count, cols):
    parts = []
    for ref in refs:
        if len(ref.shape) == 2:
            parts.append(ref[start : start + count, cols])
        else:
            parts.append(ref[:, start : start + count, cols].reshape(-1, cols.stop - cols.start))
    return parts[0] if len(parts) == 1 else jnp.concatenate(parts, axis=0)


def attend_sets(queries, sets):
    scale = math.log2(math.e) / math.sqrt(DH)
    scores = []
    for keys, _, bias in sets:
        x = lax.dot_general(
            queries, keys, (((1,), (1,)), ((), ())), preferred_element_type=jnp.float32
        )
        scores.append(x * scale if bias is None else x * scale + bias)
    peak = functools.reduce(
        jnp.maximum, [jnp.max(x, axis=1, keepdims=True) for x in scores]
    )
    total, product = 0.0, 0.0
    for x, (_, values, _) in zip(scores, sets):
        raised = jnp.exp2(x - peak)
        total += jnp.sum(raised, axis=1, keepdims=True)
        product += jnp.dot(
            raised.astype(jnp.bfloat16), values, preferred_element_type=jnp.float32
        )
    return peak, total, product


def bias_rows(bias_ref, pieces, blocks):
    width = bias_ref.shape[1]
    return jnp.concatenate(
        [
            jnp.broadcast_to(bias_ref[row : row + 1], (QBLK, width))
            for t in pieces
            for row in range(t * blocks, (t + 1) * blocks)
        ],
        axis=0,
    )


def attend_kernel(pieces, counts, q_start, rows, merge, final, *refs):
    q_refs, refs = refs[: len(pieces)], refs[len(pieces) :]
    sets = []
    for count, masked in counts:
        bias = bias_rows(refs[count], pieces, rows // QBLK) if masked else None
        sets.append((refs[:count], refs[0].shape[-2] // 2 if masked else rows, bias))
        refs = refs[count + masked :]
    state, refs = (refs[:3], refs[3:]) if merge else (None, refs)
    width = q_refs[0].shape[1]
    for at in range(0, width, DH):
        cols = slice(at, at + DH)
        queries = rows_of(q_refs, q_start, rows, cols)
        peak, total, product = attend_sets(
            queries,
            [
                (rows_of(k_refs, 0, half, cols), rows_of(k_refs, half, half, cols), bias)
                for k_refs, half, bias in sets
            ],
        )
        if merge:
            peak_1, total_1, product_1 = [
                jnp.concatenate([ref[t * rows : (t + 1) * rows, cols] for t in pieces], axis=0)
                for ref in state
            ]
            top = jnp.maximum(peak, peak_1)
            share, share_1 = jnp.exp2(peak - top), jnp.exp2(peak_1 - top)
            total = total * share + total_1 * share_1
            product = product * share + product_1 * share_1
        if final:
            result = (product / total).astype(jnp.bfloat16)
            for i in range(len(pieces)):
                refs[i][:, cols] = result[i * rows : (i + 1) * rows]
        else:
            for ref, x in zip(refs, (peak, total, product)):
                ref[:, cols] = jnp.broadcast_to(x, product.shape)


def attend(q, pieces, new, cache, bias, name, state=(), final=False):
    groups = len(pieces)
    rows, width = q[0].shape[0] // 3, q[0].shape[1]
    count = sum(x.shape[0] if x.ndim == 3 else 1 for x in new) * rows
    count += sum(x.size for x in cache) // (2 * width)
    if final:
        out_shape = [jax.ShapeDtypeStruct((rows, width), jnp.bfloat16)] * groups
    else:
        out_shape = [jax.ShapeDtypeStruct((groups * rows, width), jnp.float32)] * 3
    operands = (*[q[t] for t in pieces], *new, *cache, bias, *state)
    return pl.pallas_call(
        functools.partial(
            attend_kernel,
            tuple(pieces),
            ((len(new), False), (len(cache), True)),
            2 * rows,
            rows,
            bool(state),
            final,
        ),
        out_shape=out_shape,
        in_specs=vmem(len(operands)),
        out_specs=vmem(len(out_shape)),
        compiler_params=pltpu.CompilerParams(vmem_limit_bytes=LARGE),
        cost_estimate=pl.CostEstimate(
            flops=4 * groups * rows * count * width,
            bytes_accessed=4 * count * width,
            transcendentals=groups * rows * count * width // DH,
        ),
        name=name,
    )(*operands)


def unpack_kernel(steps, gather, width, *refs):
    groups = len(steps)
    parts, out_ref, sems = refs[:groups], refs[groups], refs[groups + 1]
    me = lax.axis_index("seq") // gather
    copies = [
        pltpu.make_async_copy(
            parts[i], out_ref.at[:, columns(partner(me, t, groups), width)], sems.at[i]
        )
        for i, t in enumerate(steps)
    ]
    for copy in copies:
        copy.start()
    for copy in copies:
        copy.wait()


def unpack(parts, steps, gather):
    rows, width = parts[0].shape
    groups = len(steps)
    return pl.pallas_call(
        functools.partial(unpack_kernel, tuple(steps), gather, width),
        out_shape=jax.ShapeDtypeStruct((rows, groups * width), jnp.bfloat16),
        in_specs=vmem(groups),
        out_specs=pl.BlockSpec(memory_space=pl.ANY),
        scratch_shapes=[pltpu.SemaphoreType.DMA((groups,))],
        compiler_params=pltpu.CompilerParams(vmem_limit_bytes=SMALL),
        cost_estimate=pl.CostEstimate(
            flops=0, bytes_accessed=4 * groups * rows * width, transcendentals=0
        ),
        name="unpack_heads",
    )(*parts)


def per_device(
    seq_count,
    head_count,
    query_new,
    key_new,
    value_new,
    cache_keys,
    cache_values,
    key_exponent,
    value_exponent,
    block_mask,
):
    tok_rows, width_dev = query_new.shape
    groups = math.gcd(width_dev // DH, seq_count)
    gather = seq_count // groups
    width = width_dev // groups
    cache_rows = cache_keys.shape[0]
    seq_index = lax.axis_index("seq")
    head_index = lax.axis_index("head")
    group, member = seq_index // gather, seq_index % gather

    def to_group(x, t):
        if t == 0:
            return x
        pairs = [
            (s, partner(s // gather, t, groups) * gather + s % gather) for s in range(seq_count)
        ]
        return lax.ppermute(x, "seq", pairs)

    def from_group(x, t):
        if t == 0:
            return x
        pairs = [
            (s, origin(s // gather, t, groups) * gather + s % gather) for s in range(seq_count)
        ]
        return lax.ppermute(x, "seq", pairs)

    def to_member(x, t):
        pairs = [
            (s, s // gather * gather + partner(s % gather, t, gather)) for s in range(seq_count)
        ]
        return lax.ppermute(x, "seq", pairs)

    def to_head(x, t):
        if t == 0:
            return x
        return lax.ppermute(x, "head", [(h, partner(h, t, head_count)) for h in range(head_count)])

    members = range(1, gather)
    kv_own, stored = prepare(
        query_new,
        key_new,
        value_new,
        cache_keys,
        cache_values,
        key_exponent,
        value_exponent,
        groups,
        gather,
        head_count,
    )
    kv = [to_group(kv_own[t], t) for t in range(groups)]
    kv_other = [to_member(kv_own[0][: 2 * tok_rows], s) for s in members]
    if gather > 1:
        *stored, kv_other[0] = lax.optimization_barrier((*stored, kv_other[0]))

    by_head = []
    for s in range(head_count):
        x = stored[s]
        if s > 2:
            x, by_head[s - 2] = lax.optimization_barrier((x, by_head[s - 2]))
        by_head.append(to_head(x, s))
    kv[1:] = [lax.optimization_barrier((x, by_head))[0] for x in kv[1:]]
    block_mask, _ = lax.optimization_barrier((block_mask, by_head))
    cache = [to_group(jnp.stack([x[t] for x in by_head]), t) for t in range(groups)]
    cache = jnp.stack(cache).transpose(2, 0, 1, 3, 4).reshape(-1, width)

    if groups > 1:
        swap = jnp.stack([x[: 2 * tok_rows] for x in kv[1:]])
        kv_other += [to_member(swap, s) for s in members]
    cache_other = [to_member(cache, s) for s in members]

    q_source = jnp.stack([origin(group, t, groups) * gather + member for t in range(groups)])
    blocks = tok_rows // QBLK
    q_block = (q_source[:, None] * blocks + jnp.arange(blocks)[None, :]).reshape(-1)
    q_pick = (q_block[:, None] == jnp.arange(block_mask.shape[0])[None, :]).astype(jnp.float32)
    row_mask = jnp.dot(q_pick, block_mask.astype(jnp.float32))

    def bias_of(steps):
        device = jnp.stack(
            [
                (origin(group, t, groups) * gather + origin(member, s, gather)) * head_count
                + origin(head_index, z, head_count)
                for s in steps
                for t in range(groups)
                for z in range(head_count)
            ]
        )
        block = (device[:, None] * cache_rows + jnp.arange(cache_rows)[None, :]).reshape(-1)
        pick = jnp.arange(block_mask.shape[1])[:, None] == (block // CBLK)[None, :]
        seen = jnp.dot(row_mask, pick.astype(jnp.float32))
        return jnp.where(seen > 0.5, 0.0, MASKED).astype(jnp.float32)

    every = range(groups)
    parts = attend(kv, every, kv, [cache], bias_of([0]), "attend_own", final=gather == 1)
    steps = [*every[-1:], *every[1:-1], *every[:1]] if groups > 1 else [0]
    if gather > 1:
        bias, state, parts = bias_of(members), parts, {}
        for pieces in filter(None, (steps[:-1], steps[-1:])):
            done = attend(kv, pieces, kv_other, cache_other, bias, "attend_other", state, True)
            parts.update(zip(pieces, done))
    return unpack([from_group(parts[t], t) for t in steps], steps, gather)


def solution(mesh):
    return jax.shard_map(
        functools.partial(per_device, mesh.shape["seq"], mesh.shape["head"]),
        mesh=mesh,
        in_specs=(
            P("seq", "head"),
            P("seq", "head"),
            P("seq", "head"),
            P(("seq", "head"), None),
            P(("seq", "head"), None),
            P(("seq", "head"), None),
            P(("seq", "head"), None),
            P(),
        ),
        out_specs=P("seq", "head"),
        check_vma=False,
    )
```

```python
import functools
import math

import jax
import jax.numpy as jnp
from jax import lax
from jax.experimental import pallas as pl
from jax.experimental.pallas import tpu as pltpu
from jax.sharding import PartitionSpec as P

DH = 128
QBLK = 64
CBLK = 32
SBLK = 4
MASKED = -1e30
SMALL = 16 * 2**20
LARGE = 32 * 2**20


def partner(index, step, count):
    if count & (count - 1) == 0:
        return index ^ step
    return (index + step) % count


def origin(index, step, count):
    if count & (count - 1) == 0:
        return index ^ step
    return (index + count - step) % count


def columns(chunk, width):
    return pl.ds(pl.multiple_of(chunk * width, DH), width)


def vmem(count):
    return [pl.BlockSpec(memory_space=pltpu.VMEM)] * count


def prepare_kernel(groups, gather, shards, *refs):
    new_refs, cache_refs, outs, scratch = refs[:3], refs[3:7], refs[7:-6], refs[-6:]
    pieces, cached = outs[:groups], outs[groups:]
    ck_buf, cv_buf, ke_buf, ve_buf, cache_sems, new_sems = scratch
    group, shard = lax.axis_index("seq") // gather, lax.axis_index("head")

    loads = [
        pltpu.make_async_copy(src, dst, cache_sems.at[i])
        for i, (src, dst) in enumerate(zip(cache_refs, (ck_buf, cv_buf, ke_buf, ve_buf)))
    ]
    rows, width = pieces[0].shape[0] // 3, pieces[0].shape[1]
    copies = []
    for t in range(groups):
        cols = columns(partner(group, t, groups), width)
        for i, src in enumerate(new_refs):
            dst = pieces[t].at[pl.ds(i * rows, rows)]
            copies.append(pltpu.make_async_copy(src.at[:, cols], dst, new_sems.at[t, i]))
    for copy in loads + copies:
        copy.start()
    for copy in loads:
        copy.wait()

    blocks, heads = ke_buf.shape
    cache_rows = ck_buf.shape[0]
    exponent = jnp.concatenate(
        [
            jnp.broadcast_to(ref[i : i + 1], (SBLK, heads))
            for ref in (ke_buf, ve_buf)
            for i in range(blocks)
        ],
        axis=0,
    )
    power = jnp.left_shift(1, exponent + 16).astype(jnp.float32) * 2.0**-16
    power = power.astype(jnp.bfloat16)
    head = lax.broadcasted_iota(jnp.int32, (heads, width), 0)
    head -= lax.broadcasted_iota(jnp.int32, (heads, width), 1) // DH
    for t in range(groups):
        for s in range(shards):
            part = partner(shard, s, shards) * groups + partner(group, t, groups)
            spread = (head == part * (width // DH)).astype(jnp.float32).astype(jnp.bfloat16)
            factor = jnp.dot(power, spread, preferred_element_type=jnp.float32)
            for which, buf in enumerate((ck_buf, cv_buf)):
                mantissa = buf[:, columns(part, width)].astype(jnp.float32)
                scaled = mantissa * factor[which * cache_rows : (which + 1) * cache_rows]
                cached[s][t, which] = scaled.astype(jnp.bfloat16)
    for copy in copies:
        copy.wait()


def prepare(q, k, v, ck, cv, ke, ve, groups, gather, shards):
    rows, width = q.shape[0], q.shape[1] // groups
    operands = (k, v, q, ck, cv, ke, ve)
    outs = pl.pallas_call(
        functools.partial(prepare_kernel, groups, gather, shards),
        out_shape=[jax.ShapeDtypeStruct((3 * rows, width), jnp.bfloat16)] * groups
        + [jax.ShapeDtypeStruct((groups, 2, ck.shape[0], width), jnp.bfloat16)] * shards,
        in_specs=[pl.BlockSpec(memory_space=pltpu.HBM)] * len(operands),
        out_specs=vmem(groups + shards),
        scratch_shapes=[pltpu.VMEM(x.shape, x.dtype) for x in (ck, cv, ke, ve)]
        + [pltpu.SemaphoreType.DMA((4,)), pltpu.SemaphoreType.DMA((groups, 3))],
        compiler_params=pltpu.CompilerParams(vmem_limit_bytes=SMALL),
        cost_estimate=pl.CostEstimate(
            flops=4 * ck.size, bytes_accessed=12 * q.size + 8 * ck.size, transcendentals=0
        ),
        name="prepare",
    )(*[pltpu.with_memory_space_constraint(x, pltpu.HBM) for x in operands])
    return list(outs[:groups]), list(outs[groups:])


def rows_of(refs, start, count, cols):
    parts = []
    for ref in refs:
        if len(ref.shape) == 2:
            parts.append(ref[start : start + count, cols])
        else:
            parts.append(ref[:, start : start + count, cols].reshape(-1, cols.stop - cols.start))
    return parts[0] if len(parts) == 1 else jnp.concatenate(parts, axis=0)


def attend_sets(queries, sets):
    scale = math.log2(math.e) / math.sqrt(DH)
    scores = []
    for keys, _, bias in sets:
        x = lax.dot_general(
            queries, keys, (((1,), (1,)), ((), ())), preferred_element_type=jnp.float32
        )
        scores.append(x * scale if bias is None else x * scale + bias)
    peak = functools.reduce(
        jnp.maximum, [jnp.max(x, axis=1, keepdims=True) for x in scores]
    )
    total, product = 0.0, 0.0
    for x, (_, values, _) in zip(scores, sets):
        raised = jnp.exp2(x - peak)
        total += jnp.sum(raised, axis=1, keepdims=True)
        product += jnp.dot(
            raised.astype(jnp.bfloat16), values, preferred_element_type=jnp.float32
        )
    return peak, total, product


def bias_rows(bias_ref, pieces, blocks):
    width = bias_ref.shape[1]
    return jnp.concatenate(
        [
            jnp.broadcast_to(bias_ref[row : row + 1], (QBLK, width))
            for t in pieces
            for row in range(t * blocks, (t + 1) * blocks)
        ],
        axis=0,
    )


def attend_kernel(pieces, counts, q_start, rows, merge, final, *refs):
    q_refs, refs = refs[: len(pieces)], refs[len(pieces) :]
    sets = []
    for count, masked in counts:
        bias = bias_rows(refs[count], pieces, rows // QBLK) if masked else None
        sets.append((refs[:count], refs[0].shape[-2] // 2 if masked else rows, bias))
        refs = refs[count + masked :]
    state, refs = (refs[:3], refs[3:]) if merge else (None, refs)
    width = q_refs[0].shape[1]
    for at in range(0, width, DH):
        cols = slice(at, at + DH)
        queries = rows_of(q_refs, q_start, rows, cols)
        peak, total, product = attend_sets(
            queries,
            [
                (rows_of(k_refs, 0, half, cols), rows_of(k_refs, half, half, cols), bias)
                for k_refs, half, bias in sets
            ],
        )
        if merge:
            peak_1, total_1, product_1 = [
                jnp.concatenate([ref[t * rows : (t + 1) * rows, cols] for t in pieces], axis=0)
                for ref in state
            ]
            top = jnp.maximum(peak, peak_1)
            share, share_1 = jnp.exp2(peak - top), jnp.exp2(peak_1 - top)
            total = total * share + total_1 * share_1
            product = product * share + product_1 * share_1
        if final:
            result = (product / total).astype(jnp.bfloat16)
            for i in range(len(pieces)):
                refs[i][:, cols] = result[i * rows : (i + 1) * rows]
        else:
            for ref, x in zip(refs, (peak, total, product)):
                ref[:, cols] = jnp.broadcast_to(x, product.shape)


def attend(q, pieces, new, cache, bias, name, state=(), final=False):
    groups = len(pieces)
    rows, width = q[0].shape[0] // 3, q[0].shape[1]
    count = sum(x.shape[0] if x.ndim == 3 else 1 for x in new) * rows
    count += sum(x.size for x in cache) // (2 * width)
    if final:
        out_shape = [jax.ShapeDtypeStruct((rows, width), jnp.bfloat16)] * groups
    else:
        out_shape = [jax.ShapeDtypeStruct((groups * rows, width), jnp.float32)] * 3
    operands = (*[q[t] for t in pieces], *new, *cache, bias, *state)
    return pl.pallas_call(
        functools.partial(
            attend_kernel,
            tuple(pieces),
            ((len(new), False), (len(cache), True)),
            2 * rows,
            rows,
            bool(state),
            final,
        ),
        out_shape=out_shape,
        in_specs=vmem(len(operands)),
        out_specs=vmem(len(out_shape)),
        compiler_params=pltpu.CompilerParams(vmem_limit_bytes=LARGE),
        cost_estimate=pl.CostEstimate(
            flops=4 * groups * rows * count * width,
            bytes_accessed=4 * count * width,
            transcendentals=groups * rows * count * width // DH,
        ),
        name=name,
    )(*operands)


def unpack_kernel(steps, gather, width, *refs):
    groups = len(steps)
    parts, out_ref, sems = refs[:groups], refs[groups], refs[groups + 1]
    me = lax.axis_index("seq") // gather
    copies = [
        pltpu.make_async_copy(
            parts[i], out_ref.at[:, columns(partner(me, t, groups), width)], sems.at[i]
        )
        for i, t in enumerate(steps)
    ]
    for copy in copies:
        copy.start()
    for copy in copies:
        copy.wait()


def unpack(parts, steps, gather):
    rows, width = parts[0].shape
    groups = len(steps)
    return pl.pallas_call(
        functools.partial(unpack_kernel, tuple(steps), gather, width),
        out_shape=jax.ShapeDtypeStruct((rows, groups * width), jnp.bfloat16),
        in_specs=vmem(groups),
        out_specs=pl.BlockSpec(memory_space=pl.ANY),
        scratch_shapes=[pltpu.SemaphoreType.DMA((groups,))],
        compiler_params=pltpu.CompilerParams(vmem_limit_bytes=SMALL),
        cost_estimate=pl.CostEstimate(
            flops=0, bytes_accessed=4 * groups * rows * width, transcendentals=0
        ),
        name="unpack_heads",
    )(*parts)


def per_device(
    seq_count,
    head_count,
    query_new,
    key_new,
    value_new,
    cache_keys,
    cache_values,
    key_exponent,
    value_exponent,
    block_mask,
):
    tok_rows, width_dev = query_new.shape
    groups = math.gcd(width_dev // DH, seq_count)
    gather = seq_count // groups
    width = width_dev // groups
    cache_rows = cache_keys.shape[0]
    seq_index = lax.axis_index("seq")
    head_index = lax.axis_index("head")
    group, member = seq_index // gather, seq_index % gather

    def to_group(x, t):
        if t == 0:
            return x
        pairs = [
            (s, partner(s // gather, t, groups) * gather + s % gather) for s in range(seq_count)
        ]
        return lax.ppermute(x, "seq", pairs)

    def from_group(x, t):
        if t == 0:
            return x
        pairs = [
            (s, origin(s // gather, t, groups) * gather + s % gather) for s in range(seq_count)
        ]
        return lax.ppermute(x, "seq", pairs)

    def to_member(x, t):
        pairs = [
            (s, s // gather * gather + partner(s % gather, t, gather)) for s in range(seq_count)
        ]
        return lax.ppermute(x, "seq", pairs)

    def to_head(x, t):
        if t == 0:
            return x
        return lax.ppermute(x, "head", [(h, partner(h, t, head_count)) for h in range(head_count)])

    members = range(1, gather)
    kv_own, stored = prepare(
        query_new,
        key_new,
        value_new,
        cache_keys,
        cache_values,
        key_exponent,
        value_exponent,
        groups,
        gather,
        head_count,
    )
    kv_other = [to_member(kv_own[0][: 2 * tok_rows], s) for s in members]
    if gather > 1:
        *stored, kv_other[0] = lax.optimization_barrier((*stored, kv_other[0]))

    by_head = [to_head(stored[s], s) for s in range(head_count)]
    if groups > 2 and head_count > 1:
        kv_own[-1], by_head[1] = lax.optimization_barrier((kv_own[-1], by_head[1]))
    kv = [to_group(kv_own[t], t) for t in range(groups)]
    kv[1:-1], by_head = lax.optimization_barrier((kv[1:-1], by_head))
    kv[1:] = [lax.optimization_barrier((x, by_head))[0] for x in kv[1:]]
    block_mask, _ = lax.optimization_barrier((block_mask, by_head))
    cache = [to_group(jnp.stack([x[t] for x in by_head]), t) for t in range(groups)]
    cache = jnp.stack(cache).transpose(2, 0, 1, 3, 4).reshape(-1, width)

    if groups > 1:
        swap = jnp.stack([x[: 2 * tok_rows] for x in kv[1:]])
        kv_other += [to_member(swap, s) for s in members]
    cache_other = [to_member(cache, s) for s in members]

    q_source = jnp.stack([origin(group, t, groups) * gather + member for t in range(groups)])
    blocks = tok_rows // QBLK
    q_block = (q_source[:, None] * blocks + jnp.arange(blocks)[None, :]).reshape(-1)
    q_pick = (q_block[:, None] == jnp.arange(block_mask.shape[0])[None, :]).astype(jnp.float32)
    row_mask = jnp.dot(q_pick, block_mask.astype(jnp.float32))

    def bias_of(steps):
        device = jnp.stack(
            [
                (origin(group, t, groups) * gather + origin(member, s, gather)) * head_count
                + origin(head_index, z, head_count)
                for s in steps
                for t in range(groups)
                for z in range(head_count)
            ]
        )
        block = (device[:, None] * cache_rows + jnp.arange(cache_rows)[None, :]).reshape(-1)
        pick = jnp.arange(block_mask.shape[1])[:, None] == (block // CBLK)[None, :]
        seen = jnp.dot(row_mask, pick.astype(jnp.float32))
        return jnp.where(seen > 0.5, 0.0, MASKED).astype(jnp.float32)

    every = range(groups)
    parts = attend(kv, every, kv, [cache], bias_of([0]), "attend_own", final=gather == 1)
    steps = [*every[-1:], *every[1:-1], *every[:1]] if groups > 1 else [0]
    if gather > 1:
        bias, state, parts = bias_of(members), parts, {}
        for pieces in filter(None, (steps[:-1], steps[-1:])):
            done = attend(kv, pieces, kv_other, cache_other, bias, "attend_other", state, True)
            parts.update(zip(pieces, done))
    return unpack([from_group(parts[t], t) for t in steps], steps, gather)


def solution(mesh):
    return jax.shard_map(
        functools.partial(per_device, mesh.shape["seq"], mesh.shape["head"]),
        mesh=mesh,
        in_specs=(
            P("seq", "head"),
            P("seq", "head"),
            P("seq", "head"),
            P(("seq", "head"), None),
            P(("seq", "head"), None),
            P(("seq", "head"), None),
            P(("seq", "head"), None),
            P(),
        ),
        out_specs=P("seq", "head"),
        check_vma=False,
    )
```

```python
import functools
import math

import jax
import jax.numpy as jnp
from jax import lax
from jax.experimental import pallas as pl
from jax.experimental.pallas import tpu as pltpu
from jax.sharding import PartitionSpec as P

DH = 128
QBLK = 64
CBLK = 32
SBLK = 4
MASKED = -1e30
SMALL = 16 * 2**20
LARGE = 32 * 2**20


def partner(index, step, count):
    if count & (count - 1) == 0:
        return index ^ step
    return (index + step) % count


def origin(index, step, count):
    if count & (count - 1) == 0:
        return index ^ step
    return (index + count - step) % count


def columns(chunk, width):
    return pl.ds(pl.multiple_of(chunk * width, DH), width)


def vmem(count):
    return [pl.BlockSpec(memory_space=pltpu.VMEM)] * count


def prepare_kernel(groups, gather, shards, *refs):
    new_refs, cache_refs, outs, scratch = refs[:3], refs[3:7], refs[7:-6], refs[-6:]
    pieces, cached = outs[:groups], outs[groups:]
    ck_buf, cv_buf, ke_buf, ve_buf, cache_sems, new_sems = scratch
    group, shard = lax.axis_index("seq") // gather, lax.axis_index("head")

    loads = [
        pltpu.make_async_copy(src, dst, cache_sems.at[i])
        for i, (src, dst) in enumerate(zip(cache_refs, (ck_buf, cv_buf, ke_buf, ve_buf)))
    ]
    rows, width = pieces[0].shape[0] // 3, pieces[0].shape[1]
    copies = []
    for t in range(groups):
        cols = columns(partner(group, t, groups), width)
        for i, src in enumerate(new_refs):
            dst = pieces[t].at[pl.ds(i * rows, rows)]
            copies.append(pltpu.make_async_copy(src.at[:, cols], dst, new_sems.at[t, i]))
    for copy in loads + copies:
        copy.start()
    for copy in loads:
        copy.wait()

    blocks, heads = ke_buf.shape
    cache_rows = ck_buf.shape[0]
    exponent = jnp.concatenate(
        [
            jnp.broadcast_to(ref[i : i + 1], (SBLK, heads))
            for ref in (ke_buf, ve_buf)
            for i in range(blocks)
        ],
        axis=0,
    )
    power = jnp.left_shift(1, exponent + 16).astype(jnp.float32) * 2.0**-16
    power = power.astype(jnp.bfloat16)
    head = lax.broadcasted_iota(jnp.int32, (heads, width), 0)
    head -= lax.broadcasted_iota(jnp.int32, (heads, width), 1) // DH
    for t in range(groups):
        for s in range(shards):
            part = partner(shard, s, shards) * groups + partner(group, t, groups)
            spread = (head == part * (width // DH)).astype(jnp.float32).astype(jnp.bfloat16)
            factor = jnp.dot(power, spread, preferred_element_type=jnp.float32)
            for which, buf in enumerate((ck_buf, cv_buf)):
                mantissa = buf[:, columns(part, width)].astype(jnp.float32)
                scaled = mantissa * factor[which * cache_rows : (which + 1) * cache_rows]
                cached[s][t, which] = scaled.astype(jnp.bfloat16)
    for copy in copies:
        copy.wait()


def prepare(q, k, v, ck, cv, ke, ve, groups, gather, shards):
    rows, width = q.shape[0], q.shape[1] // groups
    operands = (k, v, q, ck, cv, ke, ve)
    outs = pl.pallas_call(
        functools.partial(prepare_kernel, groups, gather, shards),
        out_shape=[jax.ShapeDtypeStruct((3 * rows, width), jnp.bfloat16)] * groups
        + [jax.ShapeDtypeStruct((groups, 2, ck.shape[0], width), jnp.bfloat16)] * shards,
        in_specs=[pl.BlockSpec(memory_space=pltpu.HBM)] * len(operands),
        out_specs=vmem(groups + shards),
        scratch_shapes=[pltpu.VMEM(x.shape, x.dtype) for x in (ck, cv, ke, ve)]
        + [pltpu.SemaphoreType.DMA((4,)), pltpu.SemaphoreType.DMA((groups, 3))],
        compiler_params=pltpu.CompilerParams(vmem_limit_bytes=SMALL),
        cost_estimate=pl.CostEstimate(
            flops=4 * ck.size, bytes_accessed=12 * q.size + 8 * ck.size, transcendentals=0
        ),
        name="prepare",
    )(*[pltpu.with_memory_space_constraint(x, pltpu.HBM) for x in operands])
    return list(outs[:groups]), list(outs[groups:])


def rows_of(refs, start, count, cols):
    parts = []
    for ref in refs:
        if len(ref.shape) == 2:
            parts.append(ref[start : start + count, cols])
        else:
            parts.append(ref[:, start : start + count, cols].reshape(-1, cols.stop - cols.start))
    return parts[0] if len(parts) == 1 else jnp.concatenate(parts, axis=0)


def attend_sets(queries, sets):
    scale = math.log2(math.e) / math.sqrt(DH)
    scores = []
    for keys, _, bias in sets:
        x = lax.dot_general(
            queries, keys, (((1,), (1,)), ((), ())), preferred_element_type=jnp.float32
        )
        scores.append(x * scale if bias is None else x * scale + bias)
    peak = functools.reduce(
        jnp.maximum, [jnp.max(x, axis=1, keepdims=True) for x in scores]
    )
    total, product = 0.0, 0.0
    for x, (_, values, _) in zip(scores, sets):
        raised = jnp.exp2(x - peak)
        total += jnp.sum(raised, axis=1, keepdims=True)
        product += jnp.dot(
            raised.astype(jnp.bfloat16), values, preferred_element_type=jnp.float32
        )
    return peak, total, product


def bias_rows(bias_ref, pieces, blocks):
    width = bias_ref.shape[1]
    return jnp.concatenate(
        [
            jnp.broadcast_to(bias_ref[row : row + 1], (QBLK, width))
            for t in pieces
            for row in range(t * blocks, (t + 1) * blocks)
        ],
        axis=0,
    )


def attend_kernel(pieces, counts, q_start, rows, merge, final, *refs):
    q_refs, refs = refs[: len(pieces)], refs[len(pieces) :]
    sets = []
    for count, masked in counts:
        bias = bias_rows(refs[count], pieces, rows // QBLK) if masked else None
        sets.append((refs[:count], refs[0].shape[0] // 2 if masked else rows, bias))
        refs = refs[count + masked :]
    state, refs = (refs[:3], refs[3:]) if merge else (None, refs)
    width = q_refs[0].shape[1]
    for at in range(0, width, DH):
        cols = slice(at, at + DH)
        queries = rows_of(q_refs, q_start, rows, cols)
        peak, total, product = attend_sets(
            queries,
            [
                (rows_of(k_refs, 0, half, cols), rows_of(k_refs, half, half, cols), bias)
                for k_refs, half, bias in sets
            ],
        )
        if merge:
            peak_1, total_1, product_1 = [ref[:, cols] for ref in state]
            top = jnp.maximum(peak, peak_1)
            share, share_1 = jnp.exp2(peak - top), jnp.exp2(peak_1 - top)
            total = total * share + total_1 * share_1
            product = product * share + product_1 * share_1
            peak = top
        if final:
            result = (product / total).astype(jnp.bfloat16)
            for i in range(len(pieces)):
                refs[i][:, cols] = result[i * rows : (i + 1) * rows]
        else:
            for ref, x in zip(refs, (peak, total, product)):
                ref[:, cols] = jnp.broadcast_to(x, product.shape)


def attend(q, pieces, sets, state=(), final=False):
    groups = len(pieces)
    rows, width = q[0].shape[0] // 3, q[0].shape[1]
    count = 0
    for arrays, bias in sets:
        for x in arrays:
            count += rows * (x.shape[0] if x.ndim == 3 else 1) if bias is None else x.shape[0] // 2
    if final:
        out_shape = [jax.ShapeDtypeStruct((rows, width), jnp.bfloat16)] * groups
    else:
        out_shape = [jax.ShapeDtypeStruct((groups * rows, width), jnp.float32)] * 3
    operands = [q[t] for t in pieces]
    for arrays, bias in sets:
        operands += [*arrays] if bias is None else [*arrays, bias]
    operands += state
    return pl.pallas_call(
        functools.partial(
            attend_kernel,
            tuple(pieces),
            tuple((len(arrays), bias is not None) for arrays, bias in sets),
            2 * rows,
            rows,
            bool(state),
            final,
        ),
        out_shape=out_shape,
        in_specs=vmem(len(operands)),
        out_specs=vmem(len(out_shape)),
        compiler_params=pltpu.CompilerParams(vmem_limit_bytes=LARGE),
        cost_estimate=pl.CostEstimate(
            flops=4 * groups * rows * count * width,
            bytes_accessed=4 * count * width,
            transcendentals=groups * rows * count * width // DH,
        ),
        name="attend",
    )(*operands)


def unpack_kernel(steps, gather, width, *refs):
    groups = len(steps)
    parts, out_ref, sems = refs[:groups], refs[groups], refs[groups + 1]
    me = lax.axis_index("seq") // gather
    copies = [
        pltpu.make_async_copy(
            parts[i], out_ref.at[:, columns(partner(me, t, groups), width)], sems.at[i]
        )
        for i, t in enumerate(steps)
    ]
    for copy in copies:
        copy.start()
    for copy in copies:
        copy.wait()


def unpack(parts, steps, gather):
    rows, width = parts[0].shape
    groups = len(steps)
    return pl.pallas_call(
        functools.partial(unpack_kernel, tuple(steps), gather, width),
        out_shape=jax.ShapeDtypeStruct((rows, groups * width), jnp.bfloat16),
        in_specs=vmem(groups),
        out_specs=pl.BlockSpec(memory_space=pl.ANY),
        scratch_shapes=[pltpu.SemaphoreType.DMA((groups,))],
        compiler_params=pltpu.CompilerParams(vmem_limit_bytes=SMALL),
        cost_estimate=pl.CostEstimate(
            flops=0, bytes_accessed=4 * groups * rows * width, transcendentals=0
        ),
        name="unpack_heads",
    )(*parts)


def per_device(
    seq_count,
    head_count,
    query_new,
    key_new,
    value_new,
    cache_keys,
    cache_values,
    key_exponent,
    value_exponent,
    block_mask,
):
    tok_rows, width_dev = query_new.shape
    groups = math.gcd(width_dev // DH, seq_count)
    gather = seq_count // groups
    width = width_dev // groups
    cache_rows = cache_keys.shape[0]
    seq_index = lax.axis_index("seq")
    head_index = lax.axis_index("head")
    group, member = seq_index // gather, seq_index % gather

    def to_group(x, t):
        if t == 0:
            return x
        pairs = [
            (s, partner(s // gather, t, groups) * gather + s % gather) for s in range(seq_count)
        ]
        return lax.ppermute(x, "seq", pairs)

    def from_group(x, t):
        if t == 0:
            return x
        pairs = [
            (s, origin(s // gather, t, groups) * gather + s % gather) for s in range(seq_count)
        ]
        return lax.ppermute(x, "seq", pairs)

    def to_member(x, t):
        pairs = [
            (s, s // gather * gather + partner(s % gather, t, gather)) for s in range(seq_count)
        ]
        return lax.ppermute(x, "seq", pairs)

    def to_head(x, t):
        if t == 0:
            return x
        return lax.ppermute(x, "head", [(h, partner(h, t, head_count)) for h in range(head_count)])

    members = range(1, gather)
    kv_own, stored = prepare(
        query_new,
        key_new,
        value_new,
        cache_keys,
        cache_values,
        key_exponent,
        value_exponent,
        groups,
        gather,
        head_count,
    )
    kv_other = [to_member(kv_own[0][: 2 * tok_rows], s) for s in members]
    kv = [to_group(kv_own[t], t) for t in range(groups)]
    if gather > 1:
        *stored, kv_other[0] = lax.optimization_barrier((*stored, kv_other[0]))
    by_head = []
    for s in range(head_count):
        x = stored[s]
        if s > 2:
            x, by_head[s - 2] = lax.optimization_barrier((x, by_head[s - 2]))
        by_head.append(to_head(x, s))
    kv[1:] = [lax.optimization_barrier((x, by_head))[0] for x in kv[1:]]
    block_mask, group, member, head_index, _ = lax.optimization_barrier(
        (block_mask, group, member, head_index, by_head)
    )
    cache = [to_group(jnp.stack([x[t] for x in by_head]), t) for t in range(groups)]
    if groups > 1:
        swap = jnp.stack([x[: 2 * tok_rows] for x in kv[1:]])
        kv_other += [to_member(swap, s) for s in members]

    q_source = jnp.stack([origin(group, t, groups) * gather + member for t in range(groups)])
    blocks = tok_rows // QBLK
    q_block = (q_source[:, None] * blocks + jnp.arange(blocks)[None, :]).reshape(-1)
    q_pick = (q_block[:, None] == jnp.arange(block_mask.shape[0])[None, :]).astype(jnp.float32)
    row_mask = jnp.dot(q_pick, block_mask.astype(jnp.float32))

    def bias_of(steps):
        device = jnp.stack(
            [
                (origin(group, t, groups) * gather + origin(member, s, gather)) * head_count
                + origin(head_index, z, head_count)
                for s in steps
                for t in range(groups)
                for z in range(head_count)
            ]
        )
        block = (device[:, None] * cache_rows + jnp.arange(cache_rows)[None, :]).reshape(-1)
        pick = jnp.arange(block_mask.shape[1])[:, None] == (block // CBLK)[None, :]
        seen = jnp.dot(row_mask, pick.astype(jnp.float32))
        return jnp.where(seen > 0.5, 0.0, MASKED).astype(jnp.float32)

    every = range(groups)
    steps = [*every[-1:], *every[1:-1], *every[:1]] if groups > 1 else [0]
    bias = [bias_of([0])] + ([bias_of(members)] if gather > 1 else [])
    away, new = steps[:-1], [*kv, *kv_other]
    if groups > 1:
        state = attend(kv, away, [(new, None)])
        cache, state = lax.optimization_barrier((cache, state))
    cache = jnp.stack(cache).transpose(2, 0, 1, 3, 4).reshape(-1, width)
    old = [([cache], bias[0])]
    if gather > 1:
        old.append(([to_member(cache, s) for s in members], bias[1]))
    parts = {}
    if groups > 1:
        for one in old:
            state = attend(kv, away, [one], state, one is old[-1])
        parts.update(zip(away, state))
    parts[0] = attend(kv, [0], [(new, None), *old], (), True)[0]
    return unpack([from_group(parts[t], t) for t in steps], steps, gather)


def solution(mesh):
    return jax.shard_map(
        functools.partial(per_device, mesh.shape["seq"], mesh.shape["head"]),
        mesh=mesh,
        in_specs=(
            P("seq", "head"),
            P("seq", "head"),
            P("seq", "head"),
            P(("seq", "head"), None),
            P(("seq", "head"), None),
            P(("seq", "head"), None),
            P(("seq", "head"), None),
            P(),
        ),
        out_specs=P("seq", "head"),
        check_vma=False,
    )
```

```python
import functools
import math

import jax
import jax.numpy as jnp
from jax import lax
from jax.experimental import pallas as pl
from jax.experimental.pallas import tpu as pltpu
from jax.sharding import PartitionSpec as P

DH = 128
QBLK = 64
CBLK = 32
SBLK = 4
MASKED = -1e30
SMALL = 16 * 2**20
LARGE = 32 * 2**20


def partner(index, step, count):
    if count & (count - 1) == 0:
        return index ^ step
    return (index + step) % count


def origin(index, step, count):
    if count & (count - 1) == 0:
        return index ^ step
    return (index + count - step) % count


def columns(chunk, width):
    return pl.ds(pl.multiple_of(chunk * width, DH), width)


def vmem(count):
    return [pl.BlockSpec(memory_space=pltpu.VMEM)] * count


def prepare_kernel(groups, gather, shards, *refs):
    new_refs, cache_refs, outs, scratch = refs[:3], refs[3:7], refs[7:-6], refs[-6:]
    pieces, cached = outs[:groups], outs[groups:]
    ck_buf, cv_buf, ke_buf, ve_buf, cache_sems, new_sems = scratch
    group, shard = lax.axis_index("seq") // gather, lax.axis_index("head")

    loads = [
        pltpu.make_async_copy(src, dst, cache_sems.at[i])
        for i, (src, dst) in enumerate(zip(cache_refs, (ck_buf, cv_buf, ke_buf, ve_buf)))
    ]
    rows, width = pieces[0].shape[0] // 3, pieces[0].shape[1]
    copies = []
    for t in range(groups):
        cols = columns(partner(group, t, groups), width)
        for i, src in enumerate(new_refs):
            dst = pieces[t].at[pl.ds(i * rows, rows)]
            copies.append(pltpu.make_async_copy(src.at[:, cols], dst, new_sems.at[t, i]))
    for copy in loads + copies:
        copy.start()
    for copy in loads:
        copy.wait()

    blocks, heads = ke_buf.shape
    cache_rows = ck_buf.shape[0]
    exponent = jnp.concatenate(
        [
            jnp.broadcast_to(ref[i : i + 1], (SBLK, heads))
            for ref in (ke_buf, ve_buf)
            for i in range(blocks)
        ],
        axis=0,
    )
    power = jnp.left_shift(1, exponent + 16).astype(jnp.float32) * 2.0**-16
    power = power.astype(jnp.bfloat16)
    head = lax.broadcasted_iota(jnp.int32, (heads, width), 0)
    head -= lax.broadcasted_iota(jnp.int32, (heads, width), 1) // DH
    for t in range(groups):
        for s in range(shards):
            part = partner(shard, s, shards) * groups + partner(group, t, groups)
            spread = (head == part * (width // DH)).astype(jnp.float32).astype(jnp.bfloat16)
            factor = jnp.dot(power, spread, preferred_element_type=jnp.float32)
            for which, buf in enumerate((ck_buf, cv_buf)):
                mantissa = buf[:, columns(part, width)].astype(jnp.float32)
                scaled = mantissa * factor[which * cache_rows : (which + 1) * cache_rows]
                cached[s][t, which] = scaled.astype(jnp.bfloat16)
    for copy in copies:
        copy.wait()


def prepare(q, k, v, ck, cv, ke, ve, groups, gather, shards):
    rows, width = q.shape[0], q.shape[1] // groups
    operands = (k, v, q, ck, cv, ke, ve)
    outs = pl.pallas_call(
        functools.partial(prepare_kernel, groups, gather, shards),
        out_shape=[jax.ShapeDtypeStruct((3 * rows, width), jnp.bfloat16)] * groups
        + [jax.ShapeDtypeStruct((groups, 2, ck.shape[0], width), jnp.bfloat16)] * shards,
        in_specs=[pl.BlockSpec(memory_space=pltpu.HBM)] * len(operands),
        out_specs=vmem(groups + shards),
        scratch_shapes=[pltpu.VMEM(x.shape, x.dtype) for x in (ck, cv, ke, ve)]
        + [pltpu.SemaphoreType.DMA((4,)), pltpu.SemaphoreType.DMA((groups, 3))],
        compiler_params=pltpu.CompilerParams(vmem_limit_bytes=SMALL),
        cost_estimate=pl.CostEstimate(
            flops=4 * ck.size, bytes_accessed=12 * q.size + 8 * ck.size, transcendentals=0
        ),
        name="prepare",
    )(*[pltpu.with_memory_space_constraint(x, pltpu.HBM) for x in operands])
    return list(outs[:groups]), list(outs[groups:])


def rows_of(refs, start, count, cols):
    parts = []
    for ref in refs:
        if len(ref.shape) == 2:
            parts.append(ref[start : start + count, cols])
        else:
            parts.append(ref[:, start : start + count, cols].reshape(-1, cols.stop - cols.start))
    return parts[0] if len(parts) == 1 else jnp.concatenate(parts, axis=0)


def attend_sets(queries, sets):
    scale = math.log2(math.e) / math.sqrt(DH)
    scores = []
    for keys, _, bias in sets:
        x = lax.dot_general(
            queries, keys, (((1,), (1,)), ((), ())), preferred_element_type=jnp.float32
        )
        scores.append(x * scale if bias is None else x * scale + bias)
    peak = functools.reduce(
        jnp.maximum, [jnp.max(x, axis=1, keepdims=True) for x in scores]
    )
    total, product = 0.0, 0.0
    for x, (_, values, _) in zip(scores, sets):
        raised = jnp.exp2(x - peak)
        total += jnp.sum(raised, axis=1, keepdims=True)
        product += jnp.dot(
            raised.astype(jnp.bfloat16), values, preferred_element_type=jnp.float32
        )
    return peak, total, product


def bias_rows(bias_ref, pieces, blocks):
    width = bias_ref.shape[1]
    return jnp.concatenate(
        [
            jnp.broadcast_to(bias_ref[row : row + 1], (QBLK, width))
            for t in pieces
            for row in range(t * blocks, (t + 1) * blocks)
        ],
        axis=0,
    )


def attend_kernel(pieces, counts, q_start, rows, merge, final, *refs):
    q_refs, refs = refs[: len(pieces)], refs[len(pieces) :]
    sets = []
    for count, masked in counts:
        bias = bias_rows(refs[count], pieces, rows // QBLK) if masked else None
        sets.append((refs[:count], refs[0].shape[0] // 2 if masked else rows, bias))
        refs = refs[count + masked :]
    state, refs = (refs[:3], refs[3:]) if merge else (None, refs)
    width = q_refs[0].shape[1]
    for at in range(0, width, DH):
        cols = slice(at, at + DH)
        queries = rows_of(q_refs, q_start, rows, cols)
        peak, total, product = attend_sets(
            queries,
            [
                (rows_of(k_refs, 0, half, cols), rows_of(k_refs, half, half, cols), bias)
                for k_refs, half, bias in sets
            ],
        )
        if merge:
            peak_1, total_1, product_1 = [ref[:, cols] for ref in state]
            top = jnp.maximum(peak, peak_1)
            share, share_1 = jnp.exp2(peak - top), jnp.exp2(peak_1 - top)
            total = total * share + total_1 * share_1
            product = product * share + product_1 * share_1
            peak = top
        if final:
            result = (product / total).astype(jnp.bfloat16)
            for i in range(len(pieces)):
                refs[i][:, cols] = result[i * rows : (i + 1) * rows]
        else:
            for ref, x in zip(refs, (peak, total, product)):
                ref[:, cols] = jnp.broadcast_to(x, product.shape)


def attend(q, pieces, sets, state=(), final=False, hidden=False):
    groups = len(pieces)
    rows, width = q[0].shape[0] // 3, q[0].shape[1]
    count = 0
    for arrays, bias in sets:
        for x in arrays:
            count += rows * (x.shape[0] if x.ndim == 3 else 1) if bias is None else x.shape[0] // 2
    if final:
        out_shape = [jax.ShapeDtypeStruct((rows, width), jnp.bfloat16)] * groups
    else:
        out_shape = [jax.ShapeDtypeStruct((groups * rows, width), jnp.float32)] * 3
    operands = [q[t] for t in pieces]
    for arrays, bias in sets:
        operands += [*arrays] if bias is None else [*arrays, bias]
    operands += state
    return pl.pallas_call(
        functools.partial(
            attend_kernel,
            tuple(pieces),
            tuple((len(arrays), bias is not None) for arrays, bias in sets),
            2 * rows,
            rows,
            bool(state),
            final,
        ),
        out_shape=out_shape,
        in_specs=vmem(len(operands)),
        out_specs=vmem(len(out_shape)),
        compiler_params=pltpu.CompilerParams(vmem_limit_bytes=LARGE),
        cost_estimate=pl.CostEstimate(
            flops=0 if hidden else 4 * groups * rows * count * width,
            bytes_accessed=0 if hidden else 4 * count * width,
            transcendentals=0 if hidden else groups * rows * count * width // DH,
        ),
        name="attend",
    )(*operands)


def unpack_kernel(steps, gather, width, *refs):
    groups = len(steps)
    parts, out_ref, sems = refs[:groups], refs[groups], refs[groups + 1]
    me = lax.axis_index("seq") // gather
    copies = [
        pltpu.make_async_copy(
            parts[i], out_ref.at[:, columns(partner(me, t, groups), width)], sems.at[i]
        )
        for i, t in enumerate(steps)
    ]
    for copy in copies:
        copy.start()
    for copy in copies:
        copy.wait()


def unpack(parts, steps, gather):
    rows, width = parts[0].shape
    groups = len(steps)
    return pl.pallas_call(
        functools.partial(unpack_kernel, tuple(steps), gather, width),
        out_shape=jax.ShapeDtypeStruct((rows, groups * width), jnp.bfloat16),
        in_specs=vmem(groups),
        out_specs=pl.BlockSpec(memory_space=pl.ANY),
        scratch_shapes=[pltpu.SemaphoreType.DMA((groups,))],
        compiler_params=pltpu.CompilerParams(vmem_limit_bytes=SMALL),
        cost_estimate=pl.CostEstimate(
            flops=0, bytes_accessed=4 * groups * rows * width, transcendentals=0
        ),
        name="unpack_heads",
    )(*parts)


def per_device(
    seq_count,
    head_count,
    query_new,
    key_new,
    value_new,
    cache_keys,
    cache_values,
    key_exponent,
    value_exponent,
    block_mask,
):
    tok_rows, width_dev = query_new.shape
    groups = math.gcd(width_dev // DH, seq_count)
    gather = seq_count // groups
    width = width_dev // groups
    cache_rows = cache_keys.shape[0]
    seq_index = lax.axis_index("seq")
    head_index = lax.axis_index("head")
    group, member = seq_index // gather, seq_index % gather

    def to_group(x, t):
        if t == 0:
            return x
        pairs = [
            (s, partner(s // gather, t, groups) * gather + s % gather) for s in range(seq_count)
        ]
        return lax.ppermute(x, "seq", pairs)

    def from_group(x, t):
        if t == 0:
            return x
        pairs = [
            (s, origin(s // gather, t, groups) * gather + s % gather) for s in range(seq_count)
        ]
        return lax.ppermute(x, "seq", pairs)

    def to_member(x, t):
        pairs = [
            (s, s // gather * gather + partner(s % gather, t, gather)) for s in range(seq_count)
        ]
        return lax.ppermute(x, "seq", pairs)

    def to_head(x, t):
        if t == 0:
            return x
        return lax.ppermute(x, "head", [(h, partner(h, t, head_count)) for h in range(head_count)])

    members = range(1, gather)
    kv_own, stored = prepare(
        query_new,
        key_new,
        value_new,
        cache_keys,
        cache_values,
        key_exponent,
        value_exponent,
        groups,
        gather,
        head_count,
    )
    kv_other = [to_member(kv_own[0][: 2 * tok_rows], s) for s in members]
    kv = [to_group(kv_own[t], t) for t in range(groups)]
    if gather > 1:
        *stored, kv_other[0] = lax.optimization_barrier((*stored, kv_other[0]))
    by_head = []
    for s in range(head_count):
        x = stored[s]
        if s > 2:
            x, by_head[s - 2] = lax.optimization_barrier((x, by_head[s - 2]))
        by_head.append(to_head(x, s))
    kv[1:] = [lax.optimization_barrier((x, by_head))[0] for x in kv[1:]]
    block_mask, group, member, head_index, _ = lax.optimization_barrier(
        (block_mask, group, member, head_index, by_head)
    )
    cache = [to_group(jnp.stack([x[t] for x in by_head]), t) for t in range(groups)]
    if groups > 1:
        swap = jnp.stack([x[: 2 * tok_rows] for x in kv[1:]])
        kv_other += [to_member(swap, s) for s in members]

    q_source = jnp.stack([origin(group, t, groups) * gather + member for t in range(groups)])
    blocks = tok_rows // QBLK
    q_block = (q_source[:, None] * blocks + jnp.arange(blocks)[None, :]).reshape(-1)
    q_pick = (q_block[:, None] == jnp.arange(block_mask.shape[0])[None, :]).astype(jnp.float32)
    row_mask = jnp.dot(q_pick, block_mask.astype(jnp.float32))

    def bias_of(steps):
        device = jnp.stack(
            [
                (origin(group, t, groups) * gather + origin(member, s, gather)) * head_count
                + origin(head_index, z, head_count)
                for s in steps
                for t in range(groups)
                for z in range(head_count)
            ]
        )
        block = (device[:, None] * cache_rows + jnp.arange(cache_rows)[None, :]).reshape(-1)
        pick = jnp.arange(block_mask.shape[1])[:, None] == (block // CBLK)[None, :]
        seen = jnp.dot(row_mask, pick.astype(jnp.float32))
        return jnp.where(seen > 0.5, 0.0, MASKED).astype(jnp.float32)

    every = range(groups)
    steps = [*every[-1:], *every[1:-1], *every[:1]] if groups > 1 else [0]
    bias = [bias_of([0])] + ([bias_of(members)] if gather > 1 else [])
    away = steps[:-1]
    if groups > 1:
        state = attend(kv, away, [(kv, None)], hidden=True)
        cache, state = lax.optimization_barrier((cache, state))
    cache = jnp.stack(cache).transpose(2, 0, 1, 3, 4).reshape(-1, width)
    own, other = [([cache], bias[0])], []
    if gather > 1:
        other = [(kv_other, None), ([to_member(cache, s) for s in members], bias[1])]
    parts = {}
    if groups > 1:
        state = attend(kv, away, own, state, not other)
        if other:
            state = attend(kv, away, other, state, True)
        parts.update(zip(away, state))
    parts[0] = attend(kv, [0], [(kv, None), *own, *other], (), True)[0]
    return unpack([from_group(parts[t], t) for t in steps], steps, gather)


def solution(mesh):
    return jax.shard_map(
        functools.partial(per_device, mesh.shape["seq"], mesh.shape["head"]),
        mesh=mesh,
        in_specs=(
            P("seq", "head"),
            P("seq", "head"),
            P("seq", "head"),
            P(("seq", "head"), None),
            P(("seq", "head"), None),
            P(("seq", "head"), None),
            P(("seq", "head"), None),
            P(),
        ),
        out_specs=P("seq", "head"),
        check_vma=False,
    )
```

```python
import functools
import math

import jax
import jax.numpy as jnp
from jax import lax
from jax.experimental import pallas as pl
from jax.experimental.pallas import tpu as pltpu
from jax.sharding import PartitionSpec as P

DH = 128
QBLK = 64
CBLK = 32
SBLK = 4
MASKED = -1e30
SMALL = 16 * 2**20
LARGE = 16 * 2**20


def partner(index, step, count):
    if count & (count - 1) == 0:
        return index ^ step
    return (index + step) % count


def origin(index, step, count):
    if count & (count - 1) == 0:
        return index ^ step
    return (index + count - step) % count


def columns(chunk, width):
    return pl.ds(pl.multiple_of(chunk * width, DH), width)


def vmem(count):
    return [pl.BlockSpec(memory_space=pltpu.VMEM)] * count


def prepare_kernel(groups, gather, shards, *refs):
    new_refs, cache_refs, outs, scratch = refs[:3], refs[3:7], refs[7:-6], refs[-6:]
    pieces, cached = outs[:groups], outs[groups:]
    ck_buf, cv_buf, ke_buf, ve_buf, cache_sems, new_sems = scratch
    group, shard = lax.axis_index("seq") // gather, lax.axis_index("head")

    loads = [
        pltpu.make_async_copy(src, dst, cache_sems.at[i])
        for i, (src, dst) in enumerate(zip(cache_refs, (ck_buf, cv_buf, ke_buf, ve_buf)))
    ]
    rows, width = pieces[0].shape[0] // 3, pieces[0].shape[1]
    copies = []
    for t in range(groups):
        cols = columns(partner(group, t, groups), width)
        for i, src in enumerate(new_refs):
            dst = pieces[t].at[pl.ds(i * rows, rows)]
            copies.append(pltpu.make_async_copy(src.at[:, cols], dst, new_sems.at[t, i]))
    for copy in loads + copies:
        copy.start()
    for copy in loads:
        copy.wait()

    blocks, heads = ke_buf.shape
    cache_rows = ck_buf.shape[0]
    exponent = jnp.concatenate(
        [
            jnp.broadcast_to(ref[i : i + 1], (SBLK, heads))
            for ref in (ke_buf, ve_buf)
            for i in range(blocks)
        ],
        axis=0,
    )
    power = jnp.left_shift(1, exponent + 16).astype(jnp.float32) * 2.0**-16
    power = power.astype(jnp.bfloat16)
    head = lax.broadcasted_iota(jnp.int32, (heads, width), 0)
    head -= lax.broadcasted_iota(jnp.int32, (heads, width), 1) // DH
    for t in range(groups):
        for s in range(shards):
            part = partner(shard, s, shards) * groups + partner(group, t, groups)
            spread = (head == part * (width // DH)).astype(jnp.float32).astype(jnp.bfloat16)
            factor = jnp.dot(power, spread, preferred_element_type=jnp.float32)
            for which, buf in enumerate((ck_buf, cv_buf)):
                mantissa = buf[:, columns(part, width)].astype(jnp.float32)
                scaled = mantissa * factor[which * cache_rows : (which + 1) * cache_rows]
                cached[s][t, which] = scaled.astype(jnp.bfloat16)
    for copy in copies:
        copy.wait()


def prepare(q, k, v, ck, cv, ke, ve, groups, gather, shards):
    rows, width = q.shape[0], q.shape[1] // groups
    operands = (k, v, q, ck, cv, ke, ve)
    outs = pl.pallas_call(
        functools.partial(prepare_kernel, groups, gather, shards),
        out_shape=[jax.ShapeDtypeStruct((3 * rows, width), jnp.bfloat16)] * groups
        + [jax.ShapeDtypeStruct((groups, 2, ck.shape[0], width), jnp.bfloat16)] * shards,
        in_specs=[pl.BlockSpec(memory_space=pltpu.HBM)] * len(operands),
        out_specs=vmem(groups + shards),
        scratch_shapes=[pltpu.VMEM(x.shape, x.dtype) for x in (ck, cv, ke, ve)]
        + [pltpu.SemaphoreType.DMA((4,)), pltpu.SemaphoreType.DMA((groups, 3))],
        compiler_params=pltpu.CompilerParams(vmem_limit_bytes=SMALL),
        cost_estimate=pl.CostEstimate(
            flops=4 * ck.size, bytes_accessed=12 * q.size + 8 * ck.size, transcendentals=0
        ),
        name="prepare",
    )(*[pltpu.with_memory_space_constraint(x, pltpu.HBM) for x in operands])
    return list(outs[:groups]), list(outs[groups:])


def rows_of(refs, start, count, cols):
    parts = []
    for ref in refs:
        if len(ref.shape) == 2:
            parts.append(ref[start : start + count, cols])
        else:
            parts.append(ref[:, start : start + count, cols].reshape(-1, cols.stop - cols.start))
    return parts[0] if len(parts) == 1 else jnp.concatenate(parts, axis=0)


def attend_sets(queries, sets):
    scale = math.log2(math.e) / math.sqrt(DH)
    scores = []
    for keys, _, bias in sets:
        x = lax.dot_general(
            queries, keys, (((1,), (1,)), ((), ())), preferred_element_type=jnp.float32
        )
        scores.append(x * scale if bias is None else x * scale + bias)
    peak = functools.reduce(
        jnp.maximum, [jnp.max(x, axis=1, keepdims=True) for x in scores]
    )
    total, product = 0.0, 0.0
    for x, (_, values, _) in zip(scores, sets):
        raised = jnp.exp2(x - peak)
        total += jnp.sum(raised, axis=1, keepdims=True)
        product += jnp.dot(
            raised.astype(jnp.bfloat16), values, preferred_element_type=jnp.float32
        )
    return peak, total, product


def bias_rows(bias_ref, pieces, blocks):
    width = bias_ref.shape[1]
    return jnp.concatenate(
        [
            jnp.broadcast_to(bias_ref[row : row + 1], (QBLK, width))
            for t in pieces
            for row in range(t * blocks, (t + 1) * blocks)
        ],
        axis=0,
    )


def attend_kernel(pieces, counts, q_start, rows, merge, final, *refs):
    q_refs, refs = refs[: len(pieces)], refs[len(pieces) :]
    sets = []
    for count, masked in counts:
        bias = bias_rows(refs[count], pieces, rows // QBLK) if masked else None
        sets.append((refs[:count], refs[0].shape[0] // 2 if masked else rows, bias))
        refs = refs[count + masked :]
    state, refs = (refs[:3], refs[3:]) if merge else (None, refs)
    width = q_refs[0].shape[1]
    for at in range(0, width, DH):
        cols = slice(at, at + DH)
        queries = rows_of(q_refs, q_start, rows, cols)
        peak, total, product = attend_sets(
            queries,
            [
                (rows_of(k_refs, 0, half, cols), rows_of(k_refs, half, half, cols), bias)
                for k_refs, half, bias in sets
            ],
        )
        if merge:
            peak_1, total_1, product_1 = [ref[:, cols] for ref in state]
            top = jnp.maximum(peak, peak_1)
            share, share_1 = jnp.exp2(peak - top), jnp.exp2(peak_1 - top)
            total = total * share + total_1 * share_1
            product = product * share + product_1 * share_1
            peak = top
        if final:
            result = (product / total).astype(jnp.bfloat16)
            for i in range(len(pieces)):
                refs[i][:, cols] = result[i * rows : (i + 1) * rows]
        else:
            for ref, x in zip(refs, (peak, total, product)):
                ref[:, cols] = jnp.broadcast_to(x, product.shape)


def attend(q, pieces, sets, state=(), final=False, hidden=False):
    groups = len(pieces)
    rows, width = q[0].shape[0] // 3, q[0].shape[1]
    count = 0
    for arrays, bias in sets:
        for x in arrays:
            count += rows * (x.shape[0] if x.ndim == 3 else 1) if bias is None else x.shape[0] // 2
    if final:
        out_shape = [jax.ShapeDtypeStruct((rows, width), jnp.bfloat16)] * groups
    else:
        out_shape = [jax.ShapeDtypeStruct((groups * rows, width), jnp.float32)] * 3
    operands = [q[t] for t in pieces]
    for arrays, bias in sets:
        operands += [*arrays] if bias is None else [*arrays, bias]
    operands += state
    return pl.pallas_call(
        functools.partial(
            attend_kernel,
            tuple(pieces),
            tuple((len(arrays), bias is not None) for arrays, bias in sets),
            2 * rows,
            rows,
            bool(state),
            final,
        ),
        out_shape=out_shape,
        in_specs=vmem(len(operands)),
        out_specs=vmem(len(out_shape)),
        compiler_params=pltpu.CompilerParams(vmem_limit_bytes=LARGE),
        cost_estimate=pl.CostEstimate(
            flops=0 if hidden else 4 * groups * rows * count * width,
            bytes_accessed=4 * count * width,
            transcendentals=0 if hidden else groups * rows * count * width // DH,
        ),
        name="attend",
    )(*operands)


def unpack_kernel(steps, gather, width, *refs):
    groups = len(steps)
    parts, out_ref, sems = refs[:groups], refs[groups], refs[groups + 1]
    me = lax.axis_index("seq") // gather
    copies = [
        pltpu.make_async_copy(
            parts[i], out_ref.at[:, columns(partner(me, t, groups), width)], sems.at[i]
        )
        for i, t in enumerate(steps)
    ]
    for copy in copies:
        copy.start()
    for copy in copies:
        copy.wait()


def unpack(parts, steps, gather):
    rows, width = parts[0].shape
    groups = len(steps)
    return pl.pallas_call(
        functools.partial(unpack_kernel, tuple(steps), gather, width),
        out_shape=jax.ShapeDtypeStruct((rows, groups * width), jnp.bfloat16),
        in_specs=vmem(groups),
        out_specs=pl.BlockSpec(memory_space=pl.ANY),
        scratch_shapes=[pltpu.SemaphoreType.DMA((groups,))],
        compiler_params=pltpu.CompilerParams(vmem_limit_bytes=SMALL),
        cost_estimate=pl.CostEstimate(
            flops=0, bytes_accessed=4 * groups * rows * width, transcendentals=0
        ),
        name="unpack_heads",
    )(*parts)


def per_device(
    seq_count,
    head_count,
    query_new,
    key_new,
    value_new,
    cache_keys,
    cache_values,
    key_exponent,
    value_exponent,
    block_mask,
):
    tok_rows, width_dev = query_new.shape
    groups = math.gcd(width_dev // DH, seq_count)
    gather = seq_count // groups
    width = width_dev // groups
    cache_rows = cache_keys.shape[0]
    seq_index = lax.axis_index("seq")
    head_index = lax.axis_index("head")
    group, member = seq_index // gather, seq_index % gather

    def to_group(x, t):
        if t == 0:
            return x
        pairs = [
            (s, partner(s // gather, t, groups) * gather + s % gather) for s in range(seq_count)
        ]
        return lax.ppermute(x, "seq", pairs)

    def from_group(x, t):
        if t == 0:
            return x
        pairs = [
            (s, origin(s // gather, t, groups) * gather + s % gather) for s in range(seq_count)
        ]
        return lax.ppermute(x, "seq", pairs)

    def to_member(x, t):
        pairs = [
            (s, s // gather * gather + partner(s % gather, t, gather)) for s in range(seq_count)
        ]
        return lax.ppermute(x, "seq", pairs)

    def to_head(x, t):
        if t == 0:
            return x
        return lax.ppermute(x, "head", [(h, partner(h, t, head_count)) for h in range(head_count)])

    members = range(1, gather)
    kv_own, stored = prepare(
        query_new,
        key_new,
        value_new,
        cache_keys,
        cache_values,
        key_exponent,
        value_exponent,
        groups,
        gather,
        head_count,
    )
    kv_other = [to_member(kv_own[0][: 2 * tok_rows], s) for s in members]
    kv = [to_group(kv_own[t], t) for t in range(groups)]
    if gather > 1:
        *stored, kv_other[0] = lax.optimization_barrier((*stored, kv_other[0]))
    by_head = []
    for s in range(head_count):
        x = stored[s]
        if s > 2:
            x, by_head[s - 2] = lax.optimization_barrier((x, by_head[s - 2]))
        by_head.append(to_head(x, s))
    kv[1:] = [lax.optimization_barrier((x, by_head))[0] for x in kv[1:]]
    block_mask, group, member, head_index, _ = lax.optimization_barrier(
        (block_mask, group, member, head_index, by_head)
    )
    cache = [to_group(jnp.stack([x[t] for x in by_head]), t) for t in range(groups)]
    if groups > 1:
        swap = jnp.stack([x[: 2 * tok_rows] for x in kv[1:]])
        kv_other += [to_member(swap, s) for s in members]

    q_source = jnp.stack([origin(group, t, groups) * gather + member for t in range(groups)])
    blocks = tok_rows // QBLK
    q_block = (q_source[:, None] * blocks + jnp.arange(blocks)[None, :]).reshape(-1)
    q_pick = (q_block[:, None] == jnp.arange(block_mask.shape[0])[None, :]).astype(jnp.float32)
    row_mask = jnp.dot(q_pick, block_mask.astype(jnp.float32))

    def bias_of(steps):
        device = jnp.stack(
            [
                (origin(group, t, groups) * gather + origin(member, s, gather)) * head_count
                + origin(head_index, z, head_count)
                for s in steps
                for t in range(groups)
                for z in range(head_count)
            ]
        )
        block = (device[:, None] * cache_rows + jnp.arange(cache_rows)[None, :]).reshape(-1)
        pick = jnp.arange(block_mask.shape[1])[:, None] == (block // CBLK)[None, :]
        seen = jnp.dot(row_mask, pick.astype(jnp.float32))
        return jnp.where(seen > 0.5, 0.0, MASKED).astype(jnp.float32)

    every = range(groups)
    steps = [*every[-1:], *every[1:-1], *every[:1]] if groups > 1 else [0]
    bias = [bias_of([0])] + ([bias_of(members)] if gather > 1 else [])
    away = steps[:-1]
    if groups > 1:
        state = attend(kv, away, [(kv, None)], hidden=True)
        cache, state = lax.optimization_barrier((cache, state))
    cache = jnp.stack(cache).transpose(2, 0, 1, 3, 4).reshape(-1, width)
    own, other = [([cache], bias[0])], []
    if gather > 1:
        other = [(kv_other, None), ([to_member(cache, s) for s in members], bias[1])]
    parts = {}
    if groups > 1:
        state = attend(kv, away, own, state, not other)
        if other:
            state = attend(kv, away, other, state, True)
        parts.update(zip(away, state))
    parts[0] = attend(kv, [0], [(kv, None), *own, *other], (), True)[0]
    return unpack([from_group(parts[t], t) for t in steps], steps, gather)


def solution(mesh):
    return jax.shard_map(
        functools.partial(per_device, mesh.shape["seq"], mesh.shape["head"]),
        mesh=mesh,
        in_specs=(
            P("seq", "head"),
            P("seq", "head"),
            P("seq", "head"),
            P(("seq", "head"), None),
            P(("seq", "head"), None),
            P(("seq", "head"), None),
            P(("seq", "head"), None),
            P(),
        ),
        out_specs=P("seq", "head"),
        check_vma=False,
    )
```

```python
import functools
import math

import jax
import jax.numpy as jnp
from jax import lax
from jax.experimental import pallas as pl
from jax.experimental.pallas import tpu as pltpu
from jax.sharding import PartitionSpec as P

DH = 128
QBLK = 64
CBLK = 32
SBLK = 4
MASKED = -1e30
SMALL = 16 * 2**20
LARGE = 16 * 2**20


def partner(index, step, count):
    if count & (count - 1) == 0:
        return index ^ step
    return (index + step) % count


def origin(index, step, count):
    if count & (count - 1) == 0:
        return index ^ step
    return (index + count - step) % count


def columns(chunk, width):
    return pl.ds(pl.multiple_of(chunk * width, DH), width)


def vmem(count):
    return [pl.BlockSpec(memory_space=pltpu.VMEM)] * count


def prepare_kernel(groups, gather, shards, *refs):
    new_refs, cache_refs, outs, scratch = refs[:3], refs[3:7], refs[7:-6], refs[-6:]
    pieces, cached = outs[:groups], outs[groups:]
    ck_buf, cv_buf, ke_buf, ve_buf, cache_sems, new_sems = scratch
    group, shard = lax.axis_index("seq") // gather, lax.axis_index("head")

    loads = [
        pltpu.make_async_copy(src, dst, cache_sems.at[i])
        for i, (src, dst) in enumerate(zip(cache_refs, (ck_buf, cv_buf, ke_buf, ve_buf)))
    ]
    rows, width = pieces[0].shape[0] // 3, pieces[0].shape[1]
    copies = []
    for t in range(groups):
        cols = columns(partner(group, t, groups), width)
        for i, src in enumerate(new_refs):
            dst = pieces[t].at[pl.ds(i * rows, rows)]
            copies.append(pltpu.make_async_copy(src.at[:, cols], dst, new_sems.at[t, i]))
    for copy in loads + copies:
        copy.start()
    for copy in loads:
        copy.wait()

    blocks, heads = ke_buf.shape
    cache_rows = ck_buf.shape[0]
    exponent = jnp.concatenate(
        [
            jnp.broadcast_to(ref[i : i + 1], (SBLK, heads))
            for ref in (ke_buf, ve_buf)
            for i in range(blocks)
        ],
        axis=0,
    )
    power = jnp.left_shift(1, exponent + 16).astype(jnp.float32) * 2.0**-16
    power = power.astype(jnp.bfloat16)
    head = lax.broadcasted_iota(jnp.int32, (heads, width), 0)
    head -= lax.broadcasted_iota(jnp.int32, (heads, width), 1) // DH
    for t in range(groups):
        for s in range(shards):
            part = partner(shard, s, shards) * groups + partner(group, t, groups)
            spread = (head == part * (width // DH)).astype(jnp.float32).astype(jnp.bfloat16)
            factor = jnp.dot(power, spread, preferred_element_type=jnp.float32)
            for which, buf in enumerate((ck_buf, cv_buf)):
                mantissa = buf[:, columns(part, width)].astype(jnp.float32)
                scaled = mantissa * factor[which * cache_rows : (which + 1) * cache_rows]
                cached[s][t, which] = scaled.astype(jnp.bfloat16)
    for copy in copies:
        copy.wait()


def prepare(q, k, v, ck, cv, ke, ve, groups, gather, shards):
    rows, width = q.shape[0], q.shape[1] // groups
    operands = (k, v, q, ck, cv, ke, ve)
    outs = pl.pallas_call(
        functools.partial(prepare_kernel, groups, gather, shards),
        out_shape=[jax.ShapeDtypeStruct((3 * rows, width), jnp.bfloat16)] * groups
        + [jax.ShapeDtypeStruct((groups, 2, ck.shape[0], width), jnp.bfloat16)] * shards,
        in_specs=[pl.BlockSpec(memory_space=pltpu.HBM)] * len(operands),
        out_specs=vmem(groups + shards),
        scratch_shapes=[pltpu.VMEM(x.shape, x.dtype) for x in (ck, cv, ke, ve)]
        + [pltpu.SemaphoreType.DMA((4,)), pltpu.SemaphoreType.DMA((groups, 3))],
        compiler_params=pltpu.CompilerParams(vmem_limit_bytes=SMALL),
        cost_estimate=pl.CostEstimate(
            flops=4 * ck.size, bytes_accessed=12 * q.size + 8 * ck.size, transcendentals=0
        ),
        name="prepare",
    )(*[pltpu.with_memory_space_constraint(x, pltpu.HBM) for x in operands])
    return list(outs[:groups]), list(outs[groups:])


def rows_of(refs, start, count, cols):
    parts = []
    for ref in refs:
        if len(ref.shape) == 2:
            parts.append(ref[start : start + count, cols])
        else:
            parts.append(ref[:, start : start + count, cols].reshape(-1, cols.stop - cols.start))
    return parts[0] if len(parts) == 1 else jnp.concatenate(parts, axis=0)


def attend_sets(queries, sets):
    scale = math.log2(math.e) / math.sqrt(DH)
    scores = []
    for keys, _, bias in sets:
        x = lax.dot_general(
            queries, keys, (((1,), (1,)), ((), ())), preferred_element_type=jnp.float32
        )
        scores.append(x * scale if bias is None else x * scale + bias)
    peak = functools.reduce(
        jnp.maximum, [jnp.max(x, axis=1, keepdims=True) for x in scores]
    )
    total, product = 0.0, 0.0
    for x, (_, values, _) in zip(scores, sets):
        raised = jnp.exp2(x - peak)
        total += jnp.sum(raised, axis=1, keepdims=True)
        product += jnp.dot(
            raised.astype(jnp.bfloat16), values, preferred_element_type=jnp.float32
        )
    return peak, total, product


def bias_rows(bias_ref, pieces, blocks):
    width = bias_ref.shape[1]
    return jnp.concatenate(
        [
            jnp.broadcast_to(bias_ref[row : row + 1], (QBLK, width))
            for t in pieces
            for row in range(t * blocks, (t + 1) * blocks)
        ],
        axis=0,
    )


def attend_kernel(pieces, counts, q_start, rows, merge, final, *refs):
    q_refs, refs = refs[: len(pieces)], refs[len(pieces) :]
    sets = []
    for count, masked in counts:
        bias = bias_rows(refs[count], pieces, rows // QBLK) if masked else None
        sets.append((refs[:count], refs[0].shape[0] // 2 if masked else rows, bias))
        refs = refs[count + masked :]
    state, refs = (refs[:3], refs[3:]) if merge else (None, refs)
    width = q_refs[0].shape[1]
    for at in range(0, width, DH):
        cols = slice(at, at + DH)
        queries = rows_of(q_refs, q_start, rows, cols)
        peak, total, product = attend_sets(
            queries,
            [
                (rows_of(k_refs, 0, half, cols), rows_of(k_refs, half, half, cols), bias)
                for k_refs, half, bias in sets
            ],
        )
        if merge:
            peak_1, total_1, product_1 = [ref[:, cols] for ref in state]
            top = jnp.maximum(peak, peak_1)
            share, share_1 = jnp.exp2(peak - top), jnp.exp2(peak_1 - top)
            total = total * share + total_1 * share_1
            product = product * share + product_1 * share_1
            peak = top
        if final:
            result = (product / total).astype(jnp.bfloat16)
            for i in range(len(pieces)):
                refs[i][:, cols] = result[i * rows : (i + 1) * rows]
        else:
            for ref, x in zip(refs, (peak, total, product)):
                ref[:, cols] = jnp.broadcast_to(x, product.shape)


def attend(q, pieces, sets, state=(), final=False):
    groups = len(pieces)
    rows, width = q[0].shape[0] // 3, q[0].shape[1]
    count = 0
    for arrays, bias in sets:
        for x in arrays:
            count += rows * (x.shape[0] if x.ndim == 3 else 1) if bias is None else x.shape[0] // 2
    if final:
        out_shape = [jax.ShapeDtypeStruct((rows, width), jnp.bfloat16)] * groups
    else:
        out_shape = [jax.ShapeDtypeStruct((groups * rows, width), jnp.float32)] * 3
    operands = [q[t] for t in pieces]
    for arrays, bias in sets:
        operands += [*arrays] if bias is None else [*arrays, bias]
    operands += state
    return pl.pallas_call(
        functools.partial(
            attend_kernel,
            tuple(pieces),
            tuple((len(arrays), bias is not None) for arrays, bias in sets),
            2 * rows,
            rows,
            bool(state),
            final,
        ),
        out_shape=out_shape,
        in_specs=vmem(len(operands)),
        out_specs=vmem(len(out_shape)),
        compiler_params=pltpu.CompilerParams(vmem_limit_bytes=LARGE),
        cost_estimate=pl.CostEstimate(
            flops=4 * groups * rows * count * width,
            bytes_accessed=4 * count * width,
            transcendentals=groups * rows * count * width // DH,
        ),
        name="attend",
    )(*operands)


def unpack_kernel(steps, gather, width, *refs):
    groups = len(steps)
    parts, out_ref, sems = refs[:groups], refs[groups], refs[groups + 1]
    me = lax.axis_index("seq") // gather
    copies = [
        pltpu.make_async_copy(
            parts[i], out_ref.at[:, columns(partner(me, t, groups), width)], sems.at[i]
        )
        for i, t in enumerate(steps)
    ]
    for copy in copies:
        copy.start()
    for copy in copies:
        copy.wait()


def unpack(parts, steps, gather):
    rows, width = parts[0].shape
    groups = len(steps)
    return pl.pallas_call(
        functools.partial(unpack_kernel, tuple(steps), gather, width),
        out_shape=jax.ShapeDtypeStruct((rows, groups * width), jnp.bfloat16),
        in_specs=vmem(groups),
        out_specs=pl.BlockSpec(memory_space=pl.ANY),
        scratch_shapes=[pltpu.SemaphoreType.DMA((groups,))],
        compiler_params=pltpu.CompilerParams(vmem_limit_bytes=SMALL),
        cost_estimate=pl.CostEstimate(
            flops=0, bytes_accessed=4 * groups * rows * width, transcendentals=0
        ),
        name="unpack_heads",
    )(*parts)


def per_device(
    seq_count,
    head_count,
    query_new,
    key_new,
    value_new,
    cache_keys,
    cache_values,
    key_exponent,
    value_exponent,
    block_mask,
):
    tok_rows, width_dev = query_new.shape
    groups = math.gcd(width_dev // DH, seq_count)
    gather = seq_count // groups
    width = width_dev // groups
    cache_rows = cache_keys.shape[0]
    seq_index = lax.axis_index("seq")
    head_index = lax.axis_index("head")
    group, member = seq_index // gather, seq_index % gather

    def to_group(x, t):
        if t == 0:
            return x
        pairs = [
            (s, partner(s // gather, t, groups) * gather + s % gather) for s in range(seq_count)
        ]
        return lax.ppermute(x, "seq", pairs)

    def from_group(x, t):
        if t == 0:
            return x
        pairs = [
            (s, origin(s // gather, t, groups) * gather + s % gather) for s in range(seq_count)
        ]
        return lax.ppermute(x, "seq", pairs)

    def to_member(x, t):
        pairs = [
            (s, s // gather * gather + partner(s % gather, t, gather)) for s in range(seq_count)
        ]
        return lax.ppermute(x, "seq", pairs)

    def to_head(x, t):
        if t == 0:
            return x
        return lax.ppermute(x, "head", [(h, partner(h, t, head_count)) for h in range(head_count)])

    members = range(1, gather)
    kv_own, stored = prepare(
        query_new,
        key_new,
        value_new,
        cache_keys,
        cache_values,
        key_exponent,
        value_exponent,
        groups,
        gather,
        head_count,
    )
    kv_other = [to_member(kv_own[0][: 2 * tok_rows], s) for s in members]
    kv = [to_group(kv_own[t], t) for t in range(groups)]
    if gather > 1:
        *stored, kv_other[0] = lax.optimization_barrier((*stored, kv_other[0]))
    by_head = []
    for s in range(head_count):
        x = stored[s]
        if s > 2:
            x, by_head[s - 2] = lax.optimization_barrier((x, by_head[s - 2]))
        by_head.append(to_head(x, s))
    kv[1:] = [lax.optimization_barrier((x, by_head))[0] for x in kv[1:]]
    block_mask, group, member, head_index, _ = lax.optimization_barrier(
        (block_mask, group, member, head_index, by_head)
    )
    cache = [to_group(jnp.stack([x[t] for x in by_head]), t) for t in range(groups)]
    if groups > 1:
        swap = jnp.stack([x[: 2 * tok_rows] for x in kv[1:]])
        kv_other += [to_member(swap, s) for s in members]

    q_source = jnp.stack([origin(group, t, groups) * gather + member for t in range(groups)])
    blocks = tok_rows // QBLK
    q_block = (q_source[:, None] * blocks + jnp.arange(blocks)[None, :]).reshape(-1)
    q_pick = (q_block[:, None] == jnp.arange(block_mask.shape[0])[None, :]).astype(jnp.float32)
    row_mask = jnp.dot(q_pick, block_mask.astype(jnp.float32))

    def bias_of(steps):
        device = jnp.stack(
            [
                (origin(group, t, groups) * gather + origin(member, s, gather)) * head_count
                + origin(head_index, z, head_count)
                for s in steps
                for t in range(groups)
                for z in range(head_count)
            ]
        )
        block = (device[:, None] * cache_rows + jnp.arange(cache_rows)[None, :]).reshape(-1)
        pick = jnp.arange(block_mask.shape[1])[:, None] == (block // CBLK)[None, :]
        seen = jnp.dot(row_mask, pick.astype(jnp.float32))
        return jnp.where(seen > 0.5, 0.0, MASKED).astype(jnp.float32)

    every = range(groups)
    steps = [*every[-1:], *every[1:-1], *every[:1]] if groups > 1 else [0]
    bias = [bias_of([0])] + ([bias_of(members)] if gather > 1 else [])
    away = steps[:-1]
    if groups > 1:
        state = attend(kv, away, [(kv, None)])
        cache, state = lax.optimization_barrier((cache, state))
    cache = jnp.stack(cache).transpose(2, 0, 1, 3, 4).reshape(-1, width)
    own, other = [([cache], bias[0])], []
    if gather > 1:
        other = [(kv_other, None), ([to_member(cache, s) for s in members], bias[1])]
    parts = {}
    if groups > 1:
        state = attend(kv, away, own, state, not other)
        if other:
            state = attend(kv, away, other, state, True)
        parts.update(zip(away, state))
    parts[0] = attend(kv, [0], [(kv, None), *own, *other], (), True)[0]
    return unpack([from_group(parts[t], t) for t in steps], steps, gather)


def solution(mesh):
    return jax.shard_map(
        functools.partial(per_device, mesh.shape["seq"], mesh.shape["head"]),
        mesh=mesh,
        in_specs=(
            P("seq", "head"),
            P("seq", "head"),
            P("seq", "head"),
            P(("seq", "head"), None),
            P(("seq", "head"), None),
            P(("seq", "head"), None),
            P(("seq", "head"), None),
            P(),
        ),
        out_specs=P("seq", "head"),
        check_vma=False,
    )
```

```python
import functools
import math

import jax
import jax.numpy as jnp
from jax import lax
from jax.experimental import pallas as pl
from jax.experimental.pallas import tpu as pltpu
from jax.sharding import PartitionSpec as P

DH = 128
QBLK = 64
CBLK = 32
SBLK = 4
MASKED = -1e30
SMALL = 8 * 2**20
LARGE = 16 * 2**20


def partner(index, step, count):
    if count & (count - 1) == 0:
        return index ^ step
    return (index + step) % count


def origin(index, step, count):
    if count & (count - 1) == 0:
        return index ^ step
    return (index + count - step) % count


def columns(chunk, width):
    return pl.ds(pl.multiple_of(chunk * width, DH), width)


def vmem(count):
    return [pl.BlockSpec(memory_space=pltpu.VMEM)] * count


def prepare_kernel(groups, gather, shards, *refs):
    new_refs, cache_refs, outs, scratch = refs[:3], refs[3:7], refs[7:-6], refs[-6:]
    pieces, cached = outs[:groups], outs[groups:]
    ck_buf, cv_buf, ke_buf, ve_buf, cache_sems, new_sems = scratch
    group, shard = lax.axis_index("seq") // gather, lax.axis_index("head")

    loads = [
        pltpu.make_async_copy(src, dst, cache_sems.at[i])
        for i, (src, dst) in enumerate(zip(cache_refs, (ck_buf, cv_buf, ke_buf, ve_buf)))
    ]
    rows, width = pieces[0].shape[0] // 3, pieces[0].shape[1]
    copies = []
    for t in range(groups):
        cols = columns(partner(group, t, groups), width)
        for i, src in enumerate(new_refs):
            dst = pieces[t].at[pl.ds(i * rows, rows)]
            copies.append(pltpu.make_async_copy(src.at[:, cols], dst, new_sems.at[t, i]))
    for copy in loads + copies:
        copy.start()
    for copy in loads:
        copy.wait()

    blocks, heads = ke_buf.shape
    cache_rows = ck_buf.shape[0]
    exponent = jnp.concatenate(
        [
            jnp.broadcast_to(ref[i : i + 1], (SBLK, heads))
            for ref in (ke_buf, ve_buf)
            for i in range(blocks)
        ],
        axis=0,
    )
    power = jnp.left_shift(1, exponent + 16).astype(jnp.float32) * 2.0**-16
    power = power.astype(jnp.bfloat16)
    head = lax.broadcasted_iota(jnp.int32, (heads, width), 0)
    head -= lax.broadcasted_iota(jnp.int32, (heads, width), 1) // DH
    for t in range(groups):
        for s in range(shards):
            part = partner(shard, s, shards) * groups + partner(group, t, groups)
            spread = (head == part * (width // DH)).astype(jnp.float32).astype(jnp.bfloat16)
            factor = jnp.dot(power, spread, preferred_element_type=jnp.float32)
            for which, buf in enumerate((ck_buf, cv_buf)):
                mantissa = buf[:, columns(part, width)].astype(jnp.float32)
                scaled = mantissa * factor[which * cache_rows : (which + 1) * cache_rows]
                cached[s][t, which] = scaled.astype(jnp.bfloat16)
    for copy in copies:
        copy.wait()


def prepare(q, k, v, ck, cv, ke, ve, groups, gather, shards):
    rows, width = q.shape[0], q.shape[1] // groups
    operands = (k, v, q, ck, cv, ke, ve)
    outs = pl.pallas_call(
        functools.partial(prepare_kernel, groups, gather, shards),
        out_shape=[jax.ShapeDtypeStruct((3 * rows, width), jnp.bfloat16)] * groups
        + [jax.ShapeDtypeStruct((groups, 2, ck.shape[0], width), jnp.bfloat16)] * shards,
        in_specs=[pl.BlockSpec(memory_space=pltpu.HBM)] * len(operands),
        out_specs=vmem(groups + shards),
        scratch_shapes=[pltpu.VMEM(x.shape, x.dtype) for x in (ck, cv, ke, ve)]
        + [pltpu.SemaphoreType.DMA((4,)), pltpu.SemaphoreType.DMA((groups, 3))],
        compiler_params=pltpu.CompilerParams(vmem_limit_bytes=SMALL),
        cost_estimate=pl.CostEstimate(
            flops=4 * ck.size, bytes_accessed=12 * q.size + 8 * ck.size, transcendentals=0
        ),
        name="prepare",
    )(*[pltpu.with_memory_space_constraint(x, pltpu.HBM) for x in operands])
    return list(outs[:groups]), list(outs[groups:])


def interleave_kernel(*refs):
    rows = refs[0].shape[1]
    for which in range(2):
        for s, ref in enumerate(refs[:-1]):
            refs[-1][pl.ds((which * len(refs[:-1]) + s) * rows, rows)] = ref[which]


def interleave(pieces):
    _, rows, width = pieces[0].shape
    count = len(pieces)
    if rows % 16:
        return jnp.stack(pieces, axis=1).reshape(-1, width)
    return pl.pallas_call(
        interleave_kernel,
        out_shape=jax.ShapeDtypeStruct((2 * count * rows, width), jnp.bfloat16),
        in_specs=vmem(count),
        out_specs=vmem(1)[0],
        compiler_params=pltpu.CompilerParams(vmem_limit_bytes=SMALL),
        cost_estimate=pl.CostEstimate(
            flops=0, bytes_accessed=8 * count * rows * width, transcendentals=0
        ),
        name="interleave",
    )(*pieces)


def join_kernel(rows, *refs):
    for i, ref in enumerate(refs[:-1]):
        refs[-1][i] = ref[pl.ds(0, rows)]


def join(pieces, rows):
    shape = (len(pieces), rows, pieces[0].shape[1])
    return pl.pallas_call(
        functools.partial(join_kernel, rows),
        out_shape=jax.ShapeDtypeStruct(shape, jnp.bfloat16),
        in_specs=vmem(len(pieces)),
        out_specs=vmem(1)[0],
        compiler_params=pltpu.CompilerParams(vmem_limit_bytes=SMALL),
        cost_estimate=pl.CostEstimate(
            flops=0, bytes_accessed=4 * math.prod(shape), transcendentals=0
        ),
        name="join",
    )(*pieces)


def rows_of(refs, start, count, cols):
    parts = []
    for ref in refs:
        if len(ref.shape) == 2:
            parts.append(ref[start : start + count, cols])
        else:
            parts.append(ref[:, start : start + count, cols].reshape(-1, cols.stop - cols.start))
    return parts[0] if len(parts) == 1 else jnp.concatenate(parts, axis=0)


def attend_sets(queries, sets):
    scale = math.log2(math.e) / math.sqrt(DH)
    scores = []
    for keys, _, bias in sets:
        x = lax.dot_general(
            queries, keys, (((1,), (1,)), ((), ())), preferred_element_type=jnp.float32
        )
        scores.append(x * scale if bias is None else x * scale + bias)
    peak = functools.reduce(
        jnp.maximum, [jnp.max(x, axis=1, keepdims=True) for x in scores]
    )
    total, product = 0.0, 0.0
    for x, (_, values, _) in zip(scores, sets):
        raised = jnp.exp2(x - peak)
        total += jnp.sum(raised, axis=1, keepdims=True)
        product += jnp.dot(
            raised.astype(jnp.bfloat16), values, preferred_element_type=jnp.float32
        )
    return peak, total, product


def bias_rows(bias_ref, pieces, blocks):
    width = bias_ref.shape[1]
    return jnp.concatenate(
        [
            jnp.broadcast_to(bias_ref[row : row + 1], (QBLK, width))
            for t in pieces
            for row in range(t * blocks, (t + 1) * blocks)
        ],
        axis=0,
    )


def attend_kernel(pieces, counts, q_start, rows, merge, final, *refs):
    q_refs, refs = refs[: len(pieces)], refs[len(pieces) :]
    sets = []
    for count, masked in counts:
        bias = bias_rows(refs[count], pieces, rows // QBLK) if masked else None
        sets.append((refs[:count], refs[0].shape[-2] // 2 if masked else rows, bias))
        refs = refs[count + masked :]
    state, refs = (refs[:3], refs[3:]) if merge else (None, refs)
    width = q_refs[0].shape[1]
    for at in range(0, width, DH):
        cols = slice(at, at + DH)
        queries = rows_of(q_refs, q_start, rows, cols)
        peak, total, product = attend_sets(
            queries,
            [
                (rows_of(k_refs, 0, half, cols), rows_of(k_refs, half, half, cols), bias)
                for k_refs, half, bias in sets
            ],
        )
        if merge:
            peak_1, total_1, product_1 = [ref[:, cols] for ref in state]
            top = jnp.maximum(peak, peak_1)
            share, share_1 = jnp.exp2(peak - top), jnp.exp2(peak_1 - top)
            total = total * share + total_1 * share_1
            product = product * share + product_1 * share_1
            peak = top
        if final:
            result = (product / total).astype(jnp.bfloat16)
            for i in range(len(pieces)):
                refs[i][:, cols] = result[i * rows : (i + 1) * rows]
        else:
            for ref, x in zip(refs, (peak, total, product)):
                ref[:, cols] = jnp.broadcast_to(x, product.shape)


def attend(q, pieces, sets, state=(), final=False):
    groups = len(pieces)
    rows, width = q[0].shape[0] // 3, q[0].shape[1]
    count = 0
    for arrays, bias in sets:
        for x in arrays:
            stacked = x.shape[0] if x.ndim == 3 else 1
            count += stacked * (rows if bias is None else x.shape[-2] // 2)
    if final:
        out_shape = [jax.ShapeDtypeStruct((rows, width), jnp.bfloat16)] * groups
    else:
        out_shape = [jax.ShapeDtypeStruct((groups * rows, width), jnp.float32)] * 3
    operands = [q[t] for t in pieces]
    for arrays, bias in sets:
        operands += [*arrays] if bias is None else [*arrays, bias]
    operands += state
    return pl.pallas_call(
        functools.partial(
            attend_kernel,
            tuple(pieces),
            tuple((len(arrays), bias is not None) for arrays, bias in sets),
            2 * rows,
            rows,
            bool(state),
            final,
        ),
        out_shape=out_shape,
        in_specs=vmem(len(operands)),
        out_specs=vmem(len(out_shape)),
        compiler_params=pltpu.CompilerParams(vmem_limit_bytes=LARGE),
        cost_estimate=pl.CostEstimate(
            flops=4 * groups * rows * count * width,
            bytes_accessed=4 * count * width,
            transcendentals=groups * rows * count * width // DH,
        ),
        name="attend",
    )(*operands)


def unpack_kernel(steps, gather, width, *refs):
    groups = len(steps)
    parts, out_ref, sems = refs[:groups], refs[groups], refs[groups + 1]
    me = lax.axis_index("seq") // gather
    copies = [
        pltpu.make_async_copy(
            parts[i], out_ref.at[:, columns(partner(me, t, groups), width)], sems.at[i]
        )
        for i, t in enumerate(steps)
    ]
    for copy in copies:
        copy.start()
    for copy in copies:
        copy.wait()


def unpack(parts, steps, gather):
    rows, width = parts[0].shape
    groups = len(steps)
    return pl.pallas_call(
        functools.partial(unpack_kernel, tuple(steps), gather, width),
        out_shape=jax.ShapeDtypeStruct((rows, groups * width), jnp.bfloat16),
        in_specs=vmem(groups),
        out_specs=pl.BlockSpec(memory_space=pl.ANY),
        scratch_shapes=[pltpu.SemaphoreType.DMA((groups,))],
        compiler_params=pltpu.CompilerParams(vmem_limit_bytes=SMALL),
        cost_estimate=pl.CostEstimate(
            flops=0, bytes_accessed=4 * groups * rows * width, transcendentals=0
        ),
        name="unpack_heads",
    )(*parts)


def per_device(
    seq_count,
    head_count,
    query_new,
    key_new,
    value_new,
    cache_keys,
    cache_values,
    key_exponent,
    value_exponent,
    block_mask,
):
    tok_rows, width_dev = query_new.shape
    groups = math.gcd(width_dev // DH, seq_count)
    gather = seq_count // groups
    width = width_dev // groups
    cache_rows = cache_keys.shape[0]
    seq_index = lax.axis_index("seq")
    head_index = lax.axis_index("head")
    group, member = seq_index // gather, seq_index % gather

    def to_group(x, t):
        if t == 0:
            return x
        pairs = [
            (s, partner(s // gather, t, groups) * gather + s % gather) for s in range(seq_count)
        ]
        return lax.ppermute(x, "seq", pairs)

    def from_group(x, t):
        if t == 0:
            return x
        pairs = [
            (s, origin(s // gather, t, groups) * gather + s % gather) for s in range(seq_count)
        ]
        return lax.ppermute(x, "seq", pairs)

    def to_member(x, t):
        pairs = [
            (s, s // gather * gather + partner(s % gather, t, gather)) for s in range(seq_count)
        ]
        return lax.ppermute(x, "seq", pairs)

    def to_head(x, t):
        if t == 0:
            return x
        return lax.ppermute(x, "head", [(h, partner(h, t, head_count)) for h in range(head_count)])

    members = range(1, gather)
    kv_own, stored = prepare(
        query_new,
        key_new,
        value_new,
        cache_keys,
        cache_values,
        key_exponent,
        value_exponent,
        groups,
        gather,
        head_count,
    )
    kv_other = [to_member(kv_own[0][: 2 * tok_rows], s) for s in members]
    kv = [to_group(kv_own[t], t) for t in range(groups)]
    if gather > 1:
        *stored, kv_other[0] = lax.optimization_barrier((*stored, kv_other[0]))
    by_head = []
    for s in range(head_count):
        x = stored[s]
        if s > 2:
            x, by_head[s - 2] = lax.optimization_barrier((x, by_head[s - 2]))
        by_head.append(to_head(x, s))
    kv[1:] = [lax.optimization_barrier((x, by_head))[0] for x in kv[1:]]
    block_mask, group, member, head_index, _ = lax.optimization_barrier(
        (block_mask, group, member, head_index, by_head)
    )
    cache = [to_group(interleave([x[t] for x in by_head]), t) for t in range(groups)]
    if groups > 1:
        swap = join(kv[1:], 2 * tok_rows)
        kv_other += [to_member(swap, s) for s in members]

    q_source = jnp.stack([origin(group, t, groups) * gather + member for t in range(groups)])
    blocks = tok_rows // QBLK
    q_block = (q_source[:, None] * blocks + jnp.arange(blocks)[None, :]).reshape(-1)
    q_pick = (q_block[:, None] == jnp.arange(block_mask.shape[0])[None, :]).astype(jnp.float32)
    row_mask = jnp.dot(q_pick, block_mask.astype(jnp.float32))

    def bias_of(steps):
        device = jnp.stack(
            [
                (origin(group, t, groups) * gather + origin(member, s, gather)) * head_count
                + origin(head_index, z, head_count)
                for s in steps
                for t in range(groups)
                for z in range(head_count)
            ]
        )
        block = (device[:, None] * cache_rows + jnp.arange(cache_rows)[None, :]).reshape(-1)
        pick = jnp.arange(block_mask.shape[1])[:, None] == (block // CBLK)[None, :]
        seen = jnp.dot(row_mask, pick.astype(jnp.float32))
        return jnp.where(seen > 0.5, 0.0, MASKED).astype(jnp.float32)

    every = range(groups)
    steps = [*every[-1:], *every[1:-1], *every[:1]] if groups > 1 else [0]
    bias = [bias_of([0])] + ([bias_of(members)] if gather > 1 else [])
    away = steps[:-1]
    if groups > 1:
        state = attend(kv, away, [(kv, None)])
        cache, state = lax.optimization_barrier((cache, state))
    own, other = [(cache, bias[0])], []
    if gather > 1:
        swap = join(cache, cache[0].shape[0])
        other = [(kv_other, None), ([to_member(swap, s) for s in members], bias[1])]
    parts = {}
    if groups > 1:
        state = attend(kv, away, own, state, not other)
        if other:
            state = attend(kv, away, other, state, True)
        parts.update(zip(away, state))
    parts[0] = attend(kv, [0], [(kv, None), *own, *other], (), True)[0]
    return unpack([from_group(parts[t], t) for t in steps], steps, gather)


def solution(mesh):
    return jax.shard_map(
        functools.partial(per_device, mesh.shape["seq"], mesh.shape["head"]),
        mesh=mesh,
        in_specs=(
            P("seq", "head"),
            P("seq", "head"),
            P("seq", "head"),
            P(("seq", "head"), None),
            P(("seq", "head"), None),
            P(("seq", "head"), None),
            P(("seq", "head"), None),
            P(),
        ),
        out_specs=P("seq", "head"),
        check_vma=False,
    )
```

```python
import functools
import math

import jax
import jax.numpy as jnp
from jax import lax
from jax.experimental import pallas as pl
from jax.experimental.pallas import tpu as pltpu
from jax.sharding import PartitionSpec as P

DH = 128
QBLK = 64
CBLK = 32
SBLK = 4
MASKED = -1e30
SMALL = 8 * 2**20
LARGE = 16 * 2**20


def partner(index, step, count):
    if count & (count - 1) == 0:
        return index ^ step
    return (index + step) % count


def origin(index, step, count):
    if count & (count - 1) == 0:
        return index ^ step
    return (index + count - step) % count


def columns(chunk, width):
    return pl.ds(pl.multiple_of(chunk * width, DH), width)


def vmem(count):
    return [pl.BlockSpec(memory_space=pltpu.VMEM)] * count


def prepare_kernel(groups, gather, shards, *refs):
    new_refs, cache_refs, outs, scratch = refs[:3], refs[3:7], refs[7:-6], refs[-6:]
    pieces, cached = outs[:groups], outs[groups:]
    ck_buf, cv_buf, ke_buf, ve_buf, cache_sems, new_sems = scratch
    group, shard = lax.axis_index("seq") // gather, lax.axis_index("head")

    loads = [
        pltpu.make_async_copy(src, dst, cache_sems.at[i])
        for i, (src, dst) in enumerate(zip(cache_refs, (ck_buf, cv_buf, ke_buf, ve_buf)))
    ]
    rows, width = pieces[0].shape[0] // 3, pieces[0].shape[1]
    copies = []
    for t in range(groups):
        cols = columns(partner(group, t, groups), width)
        for i, src in enumerate(new_refs):
            dst = pieces[t].at[pl.ds(i * rows, rows)]
            copies.append(pltpu.make_async_copy(src.at[:, cols], dst, new_sems.at[t, i]))
    for copy in loads + copies:
        copy.start()
    for copy in loads:
        copy.wait()

    blocks, heads = ke_buf.shape
    cache_rows = ck_buf.shape[0]
    exponent = jnp.concatenate(
        [
            jnp.broadcast_to(ref[i : i + 1], (SBLK, heads))
            for ref in (ke_buf, ve_buf)
            for i in range(blocks)
        ],
        axis=0,
    )
    power = jnp.left_shift(1, exponent + 16).astype(jnp.float32) * 2.0**-16
    power = power.astype(jnp.bfloat16)
    head = lax.broadcasted_iota(jnp.int32, (heads, width), 0)
    head -= lax.broadcasted_iota(jnp.int32, (heads, width), 1) // DH
    for t in range(groups):
        for s in range(shards):
            part = partner(shard, s, shards) * groups + partner(group, t, groups)
            spread = (head == part * (width // DH)).astype(jnp.float32).astype(jnp.bfloat16)
            factor = jnp.dot(power, spread, preferred_element_type=jnp.float32)
            for which, buf in enumerate((ck_buf, cv_buf)):
                mantissa = buf[:, columns(part, width)].astype(jnp.float32)
                scaled = mantissa * factor[which * cache_rows : (which + 1) * cache_rows]
                cached[s][t, which] = scaled.astype(jnp.bfloat16)
    for copy in copies:
        copy.wait()


def prepare(q, k, v, ck, cv, ke, ve, groups, gather, shards):
    rows, width = q.shape[0], q.shape[1] // groups
    operands = (k, v, q, ck, cv, ke, ve)
    outs = pl.pallas_call(
        functools.partial(prepare_kernel, groups, gather, shards),
        out_shape=[jax.ShapeDtypeStruct((3 * rows, width), jnp.bfloat16)] * groups
        + [jax.ShapeDtypeStruct((groups, 2, ck.shape[0], width), jnp.bfloat16)] * shards,
        in_specs=[pl.BlockSpec(memory_space=pltpu.HBM)] * len(operands),
        out_specs=vmem(groups + shards),
        scratch_shapes=[pltpu.VMEM(x.shape, x.dtype) for x in (ck, cv, ke, ve)]
        + [pltpu.SemaphoreType.DMA((4,)), pltpu.SemaphoreType.DMA((groups, 3))],
        compiler_params=pltpu.CompilerParams(vmem_limit_bytes=SMALL),
        cost_estimate=pl.CostEstimate(
            flops=4 * ck.size, bytes_accessed=12 * q.size + 8 * ck.size, transcendentals=0
        ),
        name="prepare",
    )(*[pltpu.with_memory_space_constraint(x, pltpu.HBM) for x in operands])
    return list(outs[:groups]), list(outs[groups:])


def interleave_kernel(*refs):
    rows = refs[0].shape[1]
    for which in range(2):
        for s, ref in enumerate(refs[:-1]):
            refs[-1][pl.ds((which * len(refs[:-1]) + s) * rows, rows)] = ref[which]


def interleave(pieces):
    _, rows, width = pieces[0].shape
    count = len(pieces)
    if rows % 16:
        return jnp.stack(pieces, axis=1).reshape(-1, width)
    return pl.pallas_call(
        interleave_kernel,
        out_shape=jax.ShapeDtypeStruct((2 * count * rows, width), jnp.bfloat16),
        in_specs=vmem(count),
        out_specs=vmem(1)[0],
        compiler_params=pltpu.CompilerParams(vmem_limit_bytes=SMALL),
        cost_estimate=pl.CostEstimate(
            flops=0, bytes_accessed=8 * count * rows * width, transcendentals=0
        ),
        name="interleave",
    )(*pieces)


def join_kernel(rows, *refs):
    for i, ref in enumerate(refs[:-1]):
        refs[-1][i] = ref[pl.ds(0, rows)]


def join(pieces, rows):
    shape = (len(pieces), rows, pieces[0].shape[1])
    return pl.pallas_call(
        functools.partial(join_kernel, rows),
        out_shape=jax.ShapeDtypeStruct(shape, jnp.bfloat16),
        in_specs=vmem(len(pieces)),
        out_specs=vmem(1)[0],
        compiler_params=pltpu.CompilerParams(vmem_limit_bytes=SMALL),
        cost_estimate=pl.CostEstimate(
            flops=0, bytes_accessed=4 * math.prod(shape), transcendentals=0
        ),
        name="join",
    )(*pieces)


def rows_of(refs, start, count, cols):
    parts = []
    for ref in refs:
        if len(ref.shape) == 2:
            parts.append(ref[start : start + count, cols])
        else:
            parts.append(ref[:, start : start + count, cols].reshape(-1, cols.stop - cols.start))
    return parts[0] if len(parts) == 1 else jnp.concatenate(parts, axis=0)


def attend_sets(queries, sets):
    scale = math.log2(math.e) / math.sqrt(DH)
    scores = []
    for keys, _, bias in sets:
        x = lax.dot_general(
            queries, keys, (((1,), (1,)), ((), ())), preferred_element_type=jnp.float32
        )
        scores.append(x * scale if bias is None else x * scale + bias)
    peak = functools.reduce(
        jnp.maximum, [jnp.max(x, axis=1, keepdims=True) for x in scores]
    )
    total, product = 0.0, 0.0
    for x, (_, values, _) in zip(scores, sets):
        raised = jnp.exp2(x - peak)
        total += jnp.sum(raised, axis=1, keepdims=True)
        product += jnp.dot(
            raised.astype(jnp.bfloat16), values, preferred_element_type=jnp.float32
        )
    return peak, total, product


def bias_rows(bias_ref, pieces, blocks):
    width = bias_ref.shape[1]
    return jnp.concatenate(
        [
            jnp.broadcast_to(bias_ref[row : row + 1], (QBLK, width))
            for t in pieces
            for row in range(t * blocks, (t + 1) * blocks)
        ],
        axis=0,
    )


def attend_kernel(pieces, counts, q_start, rows, merge, final, *refs):
    q_refs, refs = refs[: len(pieces)], refs[len(pieces) :]
    sets = []
    for count, masked in counts:
        bias = bias_rows(refs[count], pieces, rows // QBLK) if masked else None
        sets.append((refs[:count], refs[0].shape[-2] // 2 if masked else rows, bias))
        refs = refs[count + masked :]
    state, refs = (refs[:3], refs[3:]) if merge else (None, refs)
    width = q_refs[0].shape[1]
    for at in range(0, width, DH):
        cols = slice(at, at + DH)
        queries = rows_of(q_refs, q_start, rows, cols)
        peak, total, product = attend_sets(
            queries,
            [
                (rows_of(k_refs, 0, half, cols), rows_of(k_refs, half, half, cols), bias)
                for k_refs, half, bias in sets
            ],
        )
        if merge:
            peak_1, total_1, product_1 = [ref[:, cols] for ref in state]
            top = jnp.maximum(peak, peak_1)
            share, share_1 = jnp.exp2(peak - top), jnp.exp2(peak_1 - top)
            total = total * share + total_1 * share_1
            product = product * share + product_1 * share_1
            peak = top
        if final:
            result = (product / total).astype(jnp.bfloat16)
            for i in range(len(pieces)):
                refs[i][:, cols] = result[i * rows : (i + 1) * rows]
        else:
            for ref, x in zip(refs, (peak, total, product)):
                ref[:, cols] = jnp.broadcast_to(x, product.shape)


def attend(q, pieces, sets, state=(), final=False):
    groups = len(pieces)
    rows, width = q[0].shape[0] // 3, q[0].shape[1]
    count = 0
    for arrays, bias in sets:
        for x in arrays:
            stacked = x.shape[0] if x.ndim == 3 else 1
            count += stacked * (rows if bias is None else x.shape[-2] // 2)
    if final:
        out_shape = [jax.ShapeDtypeStruct((rows, width), jnp.bfloat16)] * groups
    else:
        out_shape = [jax.ShapeDtypeStruct((groups * rows, width), jnp.float32)] * 3
    operands = [q[t] for t in pieces]
    for arrays, bias in sets:
        operands += [*arrays] if bias is None else [*arrays, bias]
    operands += state
    return pl.pallas_call(
        functools.partial(
            attend_kernel,
            tuple(pieces),
            tuple((len(arrays), bias is not None) for arrays, bias in sets),
            2 * rows,
            rows,
            bool(state),
            final,
        ),
        out_shape=out_shape,
        in_specs=vmem(len(operands)),
        out_specs=vmem(len(out_shape)),
        compiler_params=pltpu.CompilerParams(vmem_limit_bytes=LARGE),
        cost_estimate=pl.CostEstimate(
            flops=4 * groups * rows * count * width,
            bytes_accessed=4 * count * width,
            transcendentals=groups * rows * count * width // DH,
        ),
        name="attend",
    )(*operands)


def unpack_kernel(steps, gather, width, *refs):
    groups = len(steps)
    parts, out_ref, sems = refs[:groups], refs[groups], refs[groups + 1]
    me = lax.axis_index("seq") // gather
    copies = [
        pltpu.make_async_copy(
            parts[i], out_ref.at[:, columns(partner(me, t, groups), width)], sems.at[i]
        )
        for i, t in enumerate(steps)
    ]
    for copy in copies:
        copy.start()
    for copy in copies:
        copy.wait()


def unpack(parts, steps, gather):
    rows, width = parts[0].shape
    groups = len(steps)
    return pl.pallas_call(
        functools.partial(unpack_kernel, tuple(steps), gather, width),
        out_shape=jax.ShapeDtypeStruct((rows, groups * width), jnp.bfloat16),
        in_specs=vmem(groups),
        out_specs=pl.BlockSpec(memory_space=pl.ANY),
        scratch_shapes=[pltpu.SemaphoreType.DMA((groups,))],
        compiler_params=pltpu.CompilerParams(vmem_limit_bytes=SMALL),
        cost_estimate=pl.CostEstimate(
            flops=0, bytes_accessed=4 * groups * rows * width, transcendentals=0
        ),
        name="unpack_heads",
    )(*parts)


def per_device(
    seq_count,
    head_count,
    query_new,
    key_new,
    value_new,
    cache_keys,
    cache_values,
    key_exponent,
    value_exponent,
    block_mask,
):
    tok_rows, width_dev = query_new.shape
    groups = math.gcd(width_dev // DH, seq_count)
    gather = seq_count // groups
    width = width_dev // groups
    cache_rows = cache_keys.shape[0]
    seq_index = lax.axis_index("seq")
    head_index = lax.axis_index("head")
    group, member = seq_index // gather, seq_index % gather

    def to_group(x, t):
        if t == 0:
            return x
        pairs = [
            (s, partner(s // gather, t, groups) * gather + s % gather) for s in range(seq_count)
        ]
        return lax.ppermute(x, "seq", pairs)

    def from_group(x, t):
        if t == 0:
            return x
        pairs = [
            (s, origin(s // gather, t, groups) * gather + s % gather) for s in range(seq_count)
        ]
        return lax.ppermute(x, "seq", pairs)

    def to_member(x, t):
        pairs = [
            (s, s // gather * gather + partner(s % gather, t, gather)) for s in range(seq_count)
        ]
        return lax.ppermute(x, "seq", pairs)

    def to_head(x, t):
        if t == 0:
            return x
        return lax.ppermute(x, "head", [(h, partner(h, t, head_count)) for h in range(head_count)])

    members = range(1, gather)
    kv_own, stored = prepare(
        query_new,
        key_new,
        value_new,
        cache_keys,
        cache_values,
        key_exponent,
        value_exponent,
        groups,
        gather,
        head_count,
    )
    kv_other = [to_member(kv_own[0][: 2 * tok_rows], s) for s in members]
    if gather > 1:
        kv_own[1:-1], stored, kv_other[0] = lax.optimization_barrier(
            (kv_own[1:-1], stored, kv_other[0])
        )
    kv = [to_group(kv_own[t], t) for t in range(groups)]
    by_head = []
    for s in range(head_count):
        x = stored[s]
        if s > 2:
            x, by_head[s - 2] = lax.optimization_barrier((x, by_head[s - 2]))
        by_head.append(to_head(x, s))
    kv[1:] = [lax.optimization_barrier((x, by_head))[0] for x in kv[1:]]
    block_mask, group, member, head_index, _ = lax.optimization_barrier(
        (block_mask, group, member, head_index, by_head)
    )
    cache = [to_group(interleave([x[t] for x in by_head]), t) for t in range(groups)]
    if groups > 1:
        swap = join(kv[1:], 2 * tok_rows)
        kv_other += [to_member(swap, s) for s in members]

    q_source = jnp.stack([origin(group, t, groups) * gather + member for t in range(groups)])
    blocks = tok_rows // QBLK
    q_block = (q_source[:, None] * blocks + jnp.arange(blocks)[None, :]).reshape(-1)
    q_pick = (q_block[:, None] == jnp.arange(block_mask.shape[0])[None, :]).astype(jnp.float32)
    row_mask = jnp.dot(q_pick, block_mask.astype(jnp.float32))

    def bias_of(steps):
        device = jnp.stack(
            [
                (origin(group, t, groups) * gather + origin(member, s, gather)) * head_count
                + origin(head_index, z, head_count)
                for s in steps
                for t in range(groups)
                for z in range(head_count)
            ]
        )
        block = (device[:, None] * cache_rows + jnp.arange(cache_rows)[None, :]).reshape(-1)
        pick = jnp.arange(block_mask.shape[1])[:, None] == (block // CBLK)[None, :]
        seen = jnp.dot(row_mask, pick.astype(jnp.float32))
        return jnp.where(seen > 0.5, 0.0, MASKED).astype(jnp.float32)

    every = range(groups)
    steps = [*every[-1:], *every[1:-1], *every[:1]] if groups > 1 else [0]
    bias = [bias_of([0])] + ([bias_of(members)] if gather > 1 else [])
    away = steps[:-1]
    if groups > 1:
        state = attend(kv, away, [(kv, None)])
        cache, state = lax.optimization_barrier((cache, state))
    own, other = [(cache, bias[0])], []
    if gather > 1:
        swap = join(cache, cache[0].shape[0])
        other = [(kv_other, None), ([to_member(swap, s) for s in members], bias[1])]
    parts = {}
    if groups > 1:
        state = attend(kv, away, own, state, not other)
        if other:
            state = attend(kv, away, other, state, True)
        parts.update(zip(away, state))
    parts[0] = attend(kv, [0], [(kv, None), *own, *other], (), True)[0]
    return unpack([from_group(parts[t], t) for t in steps], steps, gather)


def solution(mesh):
    return jax.shard_map(
        functools.partial(per_device, mesh.shape["seq"], mesh.shape["head"]),
        mesh=mesh,
        in_specs=(
            P("seq", "head"),
            P("seq", "head"),
            P("seq", "head"),
            P(("seq", "head"), None),
            P(("seq", "head"), None),
            P(("seq", "head"), None),
            P(("seq", "head"), None),
            P(),
        ),
        out_specs=P("seq", "head"),
        check_vma=False,
    )
```

```python
import functools
import math

import jax
import jax.numpy as jnp
from jax import lax
from jax.experimental import pallas as pl
from jax.experimental.pallas import tpu as pltpu
from jax.sharding import PartitionSpec as P

DH = 128
QBLK = 64
CBLK = 32
SBLK = 4
MASKED = -1e30
SMALL = 8 * 2**20
LARGE = 16 * 2**20


def partner(index, step, count):
    if count & (count - 1) == 0:
        return index ^ step
    return (index + step) % count


def origin(index, step, count):
    if count & (count - 1) == 0:
        return index ^ step
    return (index + count - step) % count


def columns(chunk, width):
    return pl.ds(pl.multiple_of(chunk * width, DH), width)


def vmem(count):
    return [pl.BlockSpec(memory_space=pltpu.VMEM)] * count


def prepare_kernel(groups, gather, shards, *refs):
    new_refs, cache_refs, outs, scratch = refs[:3], refs[3:7], refs[7:-6], refs[-6:]
    pieces, cached = outs[:groups], outs[groups:]
    ck_buf, cv_buf, ke_buf, ve_buf, cache_sems, new_sems = scratch
    group, shard = lax.axis_index("seq") // gather, lax.axis_index("head")

    loads = [
        pltpu.make_async_copy(src, dst, cache_sems.at[i])
        for i, (src, dst) in enumerate(zip(cache_refs, (ck_buf, cv_buf, ke_buf, ve_buf)))
    ]
    rows, width = pieces[0].shape[0] // 3, pieces[0].shape[1]
    copies = []
    for t in range(groups):
        cols = columns(partner(group, t, groups), width)
        for i, src in enumerate(new_refs):
            dst = pieces[t].at[pl.ds(i * rows, rows)]
            copies.append(pltpu.make_async_copy(src.at[:, cols], dst, new_sems.at[t, i]))
    for copy in loads + copies:
        copy.start()
    for copy in loads:
        copy.wait()

    blocks, heads = ke_buf.shape
    cache_rows = ck_buf.shape[0]
    exponent = jnp.concatenate(
        [
            jnp.broadcast_to(ref[i : i + 1], (SBLK, heads))
            for ref in (ke_buf, ve_buf)
            for i in range(blocks)
        ],
        axis=0,
    )
    power = jnp.left_shift(1, exponent + 16).astype(jnp.float32) * 2.0**-16
    power = power.astype(jnp.bfloat16)
    head = lax.broadcasted_iota(jnp.int32, (heads, width), 0)
    head -= lax.broadcasted_iota(jnp.int32, (heads, width), 1) // DH
    for t in range(groups):
        for s in range(shards):
            part = partner(shard, s, shards) * groups + partner(group, t, groups)
            spread = (head == part * (width // DH)).astype(jnp.float32).astype(jnp.bfloat16)
            factor = jnp.dot(power, spread, preferred_element_type=jnp.float32)
            for which, buf in enumerate((ck_buf, cv_buf)):
                mantissa = buf[:, columns(part, width)].astype(jnp.float32)
                scaled = mantissa * factor[which * cache_rows : (which + 1) * cache_rows]
                cached[s][t, which] = scaled.astype(jnp.bfloat16)
    for copy in copies:
        copy.wait()


def prepare(q, k, v, ck, cv, ke, ve, groups, gather, shards):
    rows, width = q.shape[0], q.shape[1] // groups
    operands = (k, v, q, ck, cv, ke, ve)
    outs = pl.pallas_call(
        functools.partial(prepare_kernel, groups, gather, shards),
        out_shape=[jax.ShapeDtypeStruct((3 * rows, width), jnp.bfloat16)] * groups
        + [jax.ShapeDtypeStruct((groups, 2, ck.shape[0], width), jnp.bfloat16)] * shards,
        in_specs=[pl.BlockSpec(memory_space=pltpu.HBM)] * len(operands),
        out_specs=vmem(groups + shards),
        scratch_shapes=[pltpu.VMEM(x.shape, x.dtype) for x in (ck, cv, ke, ve)]
        + [pltpu.SemaphoreType.DMA((4,)), pltpu.SemaphoreType.DMA((groups, 3))],
        compiler_params=pltpu.CompilerParams(vmem_limit_bytes=SMALL),
        cost_estimate=pl.CostEstimate(
            flops=4 * ck.size, bytes_accessed=12 * q.size + 8 * ck.size, transcendentals=0
        ),
        name="prepare",
    )(*[pltpu.with_memory_space_constraint(x, pltpu.HBM) for x in operands])
    return list(outs[:groups]), list(outs[groups:])


def interleave_kernel(*refs):
    rows = refs[0].shape[1]
    for which in range(2):
        for s, ref in enumerate(refs[:-1]):
            refs[-1][pl.ds((which * len(refs[:-1]) + s) * rows, rows)] = ref[which]


def interleave(pieces):
    _, rows, width = pieces[0].shape
    count = len(pieces)
    if rows % 16:
        return jnp.stack(pieces, axis=1).reshape(-1, width)
    return pl.pallas_call(
        interleave_kernel,
        out_shape=jax.ShapeDtypeStruct((2 * count * rows, width), jnp.bfloat16),
        in_specs=vmem(count),
        out_specs=vmem(1)[0],
        compiler_params=pltpu.CompilerParams(vmem_limit_bytes=SMALL),
        cost_estimate=pl.CostEstimate(
            flops=0, bytes_accessed=8 * count * rows * width, transcendentals=0
        ),
        name="interleave",
    )(*pieces)


def join_kernel(rows, *refs):
    for i, ref in enumerate(refs[:-1]):
        refs[-1][i] = ref[pl.ds(0, rows)]


def join(pieces, rows):
    shape = (len(pieces), rows, pieces[0].shape[1])
    return pl.pallas_call(
        functools.partial(join_kernel, rows),
        out_shape=jax.ShapeDtypeStruct(shape, jnp.bfloat16),
        in_specs=vmem(len(pieces)),
        out_specs=vmem(1)[0],
        compiler_params=pltpu.CompilerParams(vmem_limit_bytes=SMALL),
        cost_estimate=pl.CostEstimate(
            flops=0, bytes_accessed=4 * math.prod(shape), transcendentals=0
        ),
        name="join",
    )(*pieces)


def rows_of(refs, start, count, cols):
    parts = []
    for ref in refs:
        if len(ref.shape) == 2:
            parts.append(ref[start : start + count, cols])
        else:
            parts.append(ref[:, start : start + count, cols].reshape(-1, cols.stop - cols.start))
    return parts[0] if len(parts) == 1 else jnp.concatenate(parts, axis=0)


def attend_sets(queries, sets):
    scale = math.log2(math.e) / math.sqrt(DH)
    scores = []
    for keys, _, bias in sets:
        x = lax.dot_general(
            queries, keys, (((1,), (1,)), ((), ())), preferred_element_type=jnp.float32
        )
        scores.append(x * scale if bias is None else x * scale + bias)
    peak = functools.reduce(
        jnp.maximum, [jnp.max(x, axis=1, keepdims=True) for x in scores]
    )
    total, product = 0.0, 0.0
    for x, (_, values, _) in zip(scores, sets):
        raised = jnp.exp2(x - peak)
        total += jnp.sum(raised, axis=1, keepdims=True)
        product += jnp.dot(
            raised.astype(jnp.bfloat16), values, preferred_element_type=jnp.float32
        )
    return peak, total, product


def bias_rows(bias_ref, pieces, blocks):
    width = bias_ref.shape[1]
    return jnp.concatenate(
        [
            jnp.broadcast_to(bias_ref[row : row + 1], (QBLK, width))
            for t in pieces
            for row in range(t * blocks, (t + 1) * blocks)
        ],
        axis=0,
    )


def attend_kernel(pieces, counts, q_start, rows, merge, final, *refs):
    q_refs, refs = refs[: len(pieces)], refs[len(pieces) :]
    sets = []
    for count, masked in counts:
        bias = bias_rows(refs[count], pieces, rows // QBLK) if masked else None
        sets.append((refs[:count], refs[0].shape[-2] // 2 if masked else rows, bias))
        refs = refs[count + masked :]
    state, refs = (refs[:3], refs[3:]) if merge else (None, refs)
    width = q_refs[0].shape[1]
    for at in range(0, width, DH):
        cols = slice(at, at + DH)
        queries = rows_of(q_refs, q_start, rows, cols)
        peak, total, product = attend_sets(
            queries,
            [
                (rows_of(k_refs, 0, half, cols), rows_of(k_refs, half, half, cols), bias)
                for k_refs, half, bias in sets
            ],
        )
        if merge:
            peak_1, total_1, product_1 = [ref[:, cols] for ref in state]
            top = jnp.maximum(peak, peak_1)
            share, share_1 = jnp.exp2(peak - top), jnp.exp2(peak_1 - top)
            total = total * share + total_1 * share_1
            product = product * share + product_1 * share_1
            peak = top
        if final:
            result = (product / total).astype(jnp.bfloat16)
            for i in range(len(pieces)):
                refs[i][:, cols] = result[i * rows : (i + 1) * rows]
        else:
            for ref, x in zip(refs, (peak, total, product)):
                ref[:, cols] = jnp.broadcast_to(x, product.shape)


def attend(q, pieces, sets, state=(), final=False):
    groups = len(pieces)
    rows, width = q[0].shape[0] // 3, q[0].shape[1]
    count = 0
    for arrays, bias in sets:
        for x in arrays:
            stacked = x.shape[0] if x.ndim == 3 else 1
            count += stacked * (rows if bias is None else x.shape[-2] // 2)
    if final:
        out_shape = [jax.ShapeDtypeStruct((rows, width), jnp.bfloat16)] * groups
    else:
        out_shape = [jax.ShapeDtypeStruct((groups * rows, width), jnp.float32)] * 3
    operands = [q[t] for t in pieces]
    for arrays, bias in sets:
        operands += [*arrays] if bias is None else [*arrays, bias]
    operands += state
    return pl.pallas_call(
        functools.partial(
            attend_kernel,
            tuple(pieces),
            tuple((len(arrays), bias is not None) for arrays, bias in sets),
            2 * rows,
            rows,
            bool(state),
            final,
        ),
        out_shape=out_shape,
        in_specs=vmem(len(operands)),
        out_specs=vmem(len(out_shape)),
        compiler_params=pltpu.CompilerParams(vmem_limit_bytes=LARGE),
        cost_estimate=pl.CostEstimate(
            flops=4 * groups * rows * count * width,
            bytes_accessed=4 * count * width,
            transcendentals=groups * rows * count * width // DH,
        ),
        name="attend",
    )(*operands)


def unpack_kernel(steps, gather, width, *refs):
    groups = len(steps)
    parts, out_ref, sems = refs[:groups], refs[groups], refs[groups + 1]
    me = lax.axis_index("seq") // gather
    copies = [
        pltpu.make_async_copy(
            parts[i], out_ref.at[:, columns(partner(me, t, groups), width)], sems.at[i]
        )
        for i, t in enumerate(steps)
    ]
    for copy in copies:
        copy.start()
    for copy in copies:
        copy.wait()


def unpack(parts, steps, gather):
    rows, width = parts[0].shape
    groups = len(steps)
    return pl.pallas_call(
        functools.partial(unpack_kernel, tuple(steps), gather, width),
        out_shape=jax.ShapeDtypeStruct((rows, groups * width), jnp.bfloat16),
        in_specs=vmem(groups),
        out_specs=pl.BlockSpec(memory_space=pl.ANY),
        scratch_shapes=[pltpu.SemaphoreType.DMA((groups,))],
        compiler_params=pltpu.CompilerParams(vmem_limit_bytes=SMALL),
        cost_estimate=pl.CostEstimate(
            flops=0, bytes_accessed=4 * groups * rows * width, transcendentals=0
        ),
        name="unpack_heads",
    )(*parts)


def per_device(
    seq_count,
    head_count,
    query_new,
    key_new,
    value_new,
    cache_keys,
    cache_values,
    key_exponent,
    value_exponent,
    block_mask,
):
    tok_rows, width_dev = query_new.shape
    groups = math.gcd(width_dev // DH, seq_count)
    gather = seq_count // groups
    width = width_dev // groups
    cache_rows = cache_keys.shape[0]
    seq_index = lax.axis_index("seq")
    head_index = lax.axis_index("head")
    group, member = seq_index // gather, seq_index % gather

    def to_group(x, t):
        if t == 0:
            return x
        pairs = [
            (s, partner(s // gather, t, groups) * gather + s % gather) for s in range(seq_count)
        ]
        return lax.ppermute(x, "seq", pairs)

    def from_group(x, t):
        if t == 0:
            return x
        pairs = [
            (s, origin(s // gather, t, groups) * gather + s % gather) for s in range(seq_count)
        ]
        return lax.ppermute(x, "seq", pairs)

    def to_member(x, t):
        pairs = [
            (s, s // gather * gather + partner(s % gather, t, gather)) for s in range(seq_count)
        ]
        return lax.ppermute(x, "seq", pairs)

    def to_head(x, t):
        if t == 0:
            return x
        return lax.ppermute(x, "head", [(h, partner(h, t, head_count)) for h in range(head_count)])

    members = range(1, gather)
    kv_own, stored = prepare(
        query_new,
        key_new,
        value_new,
        cache_keys,
        cache_values,
        key_exponent,
        value_exponent,
        groups,
        gather,
        head_count,
    )
    kv_other = [to_member(kv_own[0][: 2 * tok_rows], s) for s in members]
    if gather > 1:
        kv_own[1:-1], stored, kv_other[0] = lax.optimization_barrier(
            (kv_own[1:-1], stored, kv_other[0])
        )
    kv = [to_group(kv_own[t], t) for t in range(groups)]
    by_head = []
    for s in range(head_count):
        x = stored[s]
        if s > 2:
            x, by_head[s - 2] = lax.optimization_barrier((x, by_head[s - 2]))
        by_head.append(to_head(x, s))
    kv[1:] = [lax.optimization_barrier((x, by_head))[0] for x in kv[1:]]
    block_mask, group, member, head_index, _ = lax.optimization_barrier(
        (block_mask, group, member, head_index, kv[1:])
    )
    cache = [to_group(interleave([x[t] for x in by_head]), t) for t in range(groups)]
    if groups > 1:
        swap = join(kv[1:], 2 * tok_rows)
        kv_other += [to_member(swap, s) for s in members]

    q_source = jnp.stack([origin(group, t, groups) * gather + member for t in range(groups)])
    blocks = tok_rows // QBLK
    q_block = (q_source[:, None] * blocks + jnp.arange(blocks)[None, :]).reshape(-1)
    q_pick = (q_block[:, None] == jnp.arange(block_mask.shape[0])[None, :]).astype(jnp.float32)
    row_mask = jnp.dot(q_pick, block_mask.astype(jnp.float32))

    def bias_of(steps):
        device = jnp.stack(
            [
                (origin(group, t, groups) * gather + origin(member, s, gather)) * head_count
                + origin(head_index, z, head_count)
                for s in steps
                for t in range(groups)
                for z in range(head_count)
            ]
        )
        block = (device[:, None] * cache_rows + jnp.arange(cache_rows)[None, :]).reshape(-1)
        pick = jnp.arange(block_mask.shape[1])[:, None] == (block // CBLK)[None, :]
        seen = jnp.dot(row_mask, pick.astype(jnp.float32))
        return jnp.where(seen > 0.5, 0.0, MASKED).astype(jnp.float32)

    every = range(groups)
    steps = [*every[-1:], *every[1:-1], *every[:1]] if groups > 1 else [0]
    bias = [bias_of([0])] + ([bias_of(members)] if gather > 1 else [])
    away = steps[:-1]
    if groups > 1:
        state = attend(kv, away, [(kv, None)])
        cache, state, bias = lax.optimization_barrier((cache, state, bias))
    sets, last = [(cache, bias[0])], []
    if gather > 1:
        swap = join(cache, cache[0].shape[0])
        sets.append((kv_other, None))
        last = [([to_member(swap, s) for s in members], bias[1])]
    parts = {}
    if groups > 1:
        state = attend(kv, away, sets, state, not last)
        if last:
            state = attend(kv, away, last, state, True)
        parts.update(zip(away, state))
    parts[0] = attend(kv, [0], [(kv, None), *sets, *last], (), True)[0]
    return unpack([from_group(parts[t], t) for t in steps], steps, gather)


def solution(mesh):
    return jax.shard_map(
        functools.partial(per_device, mesh.shape["seq"], mesh.shape["head"]),
        mesh=mesh,
        in_specs=(
            P("seq", "head"),
            P("seq", "head"),
            P("seq", "head"),
            P(("seq", "head"), None),
            P(("seq", "head"), None),
            P(("seq", "head"), None),
            P(("seq", "head"), None),
            P(),
        ),
        out_specs=P("seq", "head"),
        check_vma=False,
    )
```

```python
import functools
import math

import jax
import jax.numpy as jnp
from jax import lax
from jax.experimental import pallas as pl
from jax.experimental.pallas import tpu as pltpu
from jax.sharding import PartitionSpec as P

DH = 128
QBLK = 64
CBLK = 32
SBLK = 4
MASKED = -1e30
SMALL = 8 * 2**20
LARGE = 16 * 2**20


def partner(index, step, count):
    if count & (count - 1) == 0:
        return index ^ step
    return (index + step) % count


def origin(index, step, count):
    if count & (count - 1) == 0:
        return index ^ step
    return (index + count - step) % count


def columns(chunk, width):
    return pl.ds(pl.multiple_of(chunk * width, DH), width)


def vmem(count):
    return [pl.BlockSpec(memory_space=pltpu.VMEM)] * count


def start_loads(new_refs, pieces, targets, sems):
    rows, width = pieces[0].shape[0] // 3, pieces[0].shape[1]
    copies = []
    for n, (piece, target) in enumerate(zip(pieces, targets)):
        cols = columns(target, width)
        for i, src in enumerate(new_refs):
            dst = piece.at[pl.ds(i * rows, rows)]
            copies.append(pltpu.make_async_copy(src.at[:, cols], dst, sems.at[n, i]))
    for copy in copies:
        copy.start()
    return copies


def pack_kernel(steps, groups, gather, *refs):
    group = lax.axis_index("seq") // gather
    targets = [partner(group, t, groups) for t in steps]
    for copy in start_loads(refs[:3], refs[3:-1], targets, refs[-1]):
        copy.wait()


def pack(new, steps, groups, gather):
    rows, width = new[0].shape[0], new[0].shape[1] // groups
    return pl.pallas_call(
        functools.partial(pack_kernel, tuple(steps), groups, gather),
        out_shape=[jax.ShapeDtypeStruct((3 * rows, width), jnp.bfloat16)] * len(steps),
        in_specs=[pl.BlockSpec(memory_space=pltpu.HBM)] * 3,
        out_specs=vmem(len(steps)),
        scratch_shapes=[pltpu.SemaphoreType.DMA((len(steps), 3))],
        compiler_params=pltpu.CompilerParams(vmem_limit_bytes=SMALL),
        cost_estimate=pl.CostEstimate(
            flops=0, bytes_accessed=12 * len(steps) * rows * width, transcendentals=0
        ),
        name="pack",
    )(*[pltpu.with_memory_space_constraint(x, pltpu.HBM) for x in new])


def prepare_kernel(steps, groups, gather, shards, *refs):
    new_refs, cache_refs, outs, scratch = refs[:3], refs[3:7], refs[7:-6], refs[-6:]
    pieces, cached = outs[: len(steps)], outs[len(steps) :]
    ck_buf, cv_buf, ke_buf, ve_buf, cache_sems, new_sems = scratch
    group, shard = lax.axis_index("seq") // gather, lax.axis_index("head")

    loads = [
        pltpu.make_async_copy(src, dst, cache_sems.at[i])
        for i, (src, dst) in enumerate(zip(cache_refs, (ck_buf, cv_buf, ke_buf, ve_buf)))
    ]
    for copy in loads:
        copy.start()
    targets = [partner(group, t, groups) for t in steps]
    copies = start_loads(new_refs, pieces, targets, new_sems)
    for copy in loads:
        copy.wait()

    width = cached[0].shape[-1]
    blocks, heads = ke_buf.shape
    cache_rows = ck_buf.shape[0]
    exponent = jnp.concatenate(
        [
            jnp.broadcast_to(ref[i : i + 1], (SBLK, heads))
            for ref in (ke_buf, ve_buf)
            for i in range(blocks)
        ],
        axis=0,
    )
    power = jnp.left_shift(1, exponent + 16).astype(jnp.float32) * 2.0**-16
    power = power.astype(jnp.bfloat16)
    head = lax.broadcasted_iota(jnp.int32, (heads, width), 0)
    head -= lax.broadcasted_iota(jnp.int32, (heads, width), 1) // DH
    for t in range(groups):
        for s in range(shards):
            part = partner(shard, s, shards) * groups + partner(group, t, groups)
            spread = (head == part * (width // DH)).astype(jnp.float32).astype(jnp.bfloat16)
            factor = jnp.dot(power, spread, preferred_element_type=jnp.float32)
            for which, buf in enumerate((ck_buf, cv_buf)):
                mantissa = buf[:, columns(part, width)].astype(jnp.float32)
                scaled = mantissa * factor[which * cache_rows : (which + 1) * cache_rows]
                cached[s][t, which] = scaled.astype(jnp.bfloat16)
    for copy in copies:
        copy.wait()


def prepare(new, stored, steps, groups, gather, shards):
    rows, width = new[0].shape[0], new[0].shape[1] // groups
    cache_rows = stored[0].shape[0]
    operands = (*new, *stored)
    outs = pl.pallas_call(
        functools.partial(prepare_kernel, tuple(steps), groups, gather, shards),
        out_shape=[jax.ShapeDtypeStruct((3 * rows, width), jnp.bfloat16)] * len(steps)
        + [jax.ShapeDtypeStruct((groups, 2, cache_rows, width), jnp.bfloat16)] * shards,
        in_specs=[pl.BlockSpec(memory_space=pltpu.HBM)] * len(operands),
        out_specs=vmem(len(steps) + shards),
        scratch_shapes=[pltpu.VMEM(x.shape, x.dtype) for x in stored]
        + [pltpu.SemaphoreType.DMA((4,)), pltpu.SemaphoreType.DMA((len(steps), 3))],
        compiler_params=pltpu.CompilerParams(vmem_limit_bytes=SMALL),
        cost_estimate=pl.CostEstimate(
            flops=4 * stored[0].size,
            bytes_accessed=12 * len(steps) * rows * width + 8 * stored[0].size,
            transcendentals=0,
        ),
        name="prepare",
    )(*[pltpu.with_memory_space_constraint(x, pltpu.HBM) for x in operands])
    return list(outs[: len(steps)]), list(outs[len(steps) :])


def interleave_kernel(*refs):
    rows = refs[0].shape[1]
    for which in range(2):
        for s, ref in enumerate(refs[:-1]):
            refs[-1][pl.ds((which * len(refs[:-1]) + s) * rows, rows)] = ref[which]


def interleave(pieces):
    _, rows, width = pieces[0].shape
    count = len(pieces)
    if rows % 16:
        return jnp.stack(pieces, axis=1).reshape(-1, width)
    return pl.pallas_call(
        interleave_kernel,
        out_shape=jax.ShapeDtypeStruct((2 * count * rows, width), jnp.bfloat16),
        in_specs=vmem(count),
        out_specs=vmem(1)[0],
        compiler_params=pltpu.CompilerParams(vmem_limit_bytes=SMALL),
        cost_estimate=pl.CostEstimate(
            flops=0, bytes_accessed=8 * count * rows * width, transcendentals=0
        ),
        name="interleave",
    )(*pieces)


def join_kernel(rows, *refs):
    for i, ref in enumerate(refs[:-1]):
        refs[-1][i] = ref[pl.ds(0, rows)]


def join(pieces, rows):
    shape = (len(pieces), rows, pieces[0].shape[1])
    return pl.pallas_call(
        functools.partial(join_kernel, rows),
        out_shape=jax.ShapeDtypeStruct(shape, jnp.bfloat16),
        in_specs=vmem(len(pieces)),
        out_specs=vmem(1)[0],
        compiler_params=pltpu.CompilerParams(vmem_limit_bytes=SMALL),
        cost_estimate=pl.CostEstimate(
            flops=0, bytes_accessed=4 * math.prod(shape), transcendentals=0
        ),
        name="join",
    )(*pieces)


def rows_of(refs, start, count, cols):
    parts = []
    for ref in refs:
        if len(ref.shape) == 2:
            parts.append(ref[start : start + count, cols])
        else:
            parts.append(ref[:, start : start + count, cols].reshape(-1, cols.stop - cols.start))
    return parts[0] if len(parts) == 1 else jnp.concatenate(parts, axis=0)


def attend_sets(queries, sets):
    scale = math.log2(math.e) / math.sqrt(DH)
    scores = []
    for keys, _, bias in sets:
        x = lax.dot_general(
            queries, keys, (((1,), (1,)), ((), ())), preferred_element_type=jnp.float32
        )
        scores.append(x * scale if bias is None else x * scale + bias)
    peak = functools.reduce(
        jnp.maximum, [jnp.max(x, axis=1, keepdims=True) for x in scores]
    )
    total, product = 0.0, 0.0
    for x, (_, values, _) in zip(scores, sets):
        raised = jnp.exp2(x - peak)
        total += jnp.sum(raised, axis=1, keepdims=True)
        product += jnp.dot(
            raised.astype(jnp.bfloat16), values, preferred_element_type=jnp.float32
        )
    return peak, total, product


def bias_rows(bias_ref, pieces, blocks):
    width = bias_ref.shape[1]
    return jnp.concatenate(
        [
            jnp.broadcast_to(bias_ref[row : row + 1], (QBLK, width))
            for t in pieces
            for row in range(t * blocks, (t + 1) * blocks)
        ],
        axis=0,
    )


def attend_kernel(pieces, counts, q_start, rows, merge, final, *refs):
    q_refs, refs = refs[: len(pieces)], refs[len(pieces) :]
    sets = []
    for count, masked in counts:
        bias = bias_rows(refs[count], pieces, rows // QBLK) if masked else None
        sets.append((refs[:count], refs[0].shape[-2] // 2 if masked else rows, bias))
        refs = refs[count + masked :]
    state, refs = (refs[:3], refs[3:]) if merge else (None, refs)
    width = q_refs[0].shape[1]
    for at in range(0, width, DH):
        cols = slice(at, at + DH)
        queries = rows_of(q_refs, q_start, rows, cols)
        peak, total, product = attend_sets(
            queries,
            [
                (rows_of(k_refs, 0, half, cols), rows_of(k_refs, half, half, cols), bias)
                for k_refs, half, bias in sets
            ],
        )
        if merge:
            peak_1, total_1, product_1 = [ref[:, cols] for ref in state]
            top = jnp.maximum(peak, peak_1)
            share, share_1 = jnp.exp2(peak - top), jnp.exp2(peak_1 - top)
            total = total * share + total_1 * share_1
            product = product * share + product_1 * share_1
            peak = top
        if final:
            result = (product / total).astype(jnp.bfloat16)
            for i in range(len(pieces)):
                refs[i][:, cols] = result[i * rows : (i + 1) * rows]
        else:
            for ref, x in zip(refs, (peak, total, product)):
                ref[:, cols] = jnp.broadcast_to(x, product.shape)


def attend(q, pieces, sets, state=(), final=False):
    groups = len(pieces)
    rows, width = q[0].shape[0] // 3, q[0].shape[1]
    count = 0
    for arrays, bias in sets:
        for x in arrays:
            stacked = x.shape[0] if x.ndim == 3 else 1
            count += stacked * (rows if bias is None else x.shape[-2] // 2)
    if final:
        out_shape = [jax.ShapeDtypeStruct((rows, width), jnp.bfloat16)] * groups
    else:
        out_shape = [jax.ShapeDtypeStruct((groups * rows, width), jnp.float32)] * 3
    operands = [q[t] for t in pieces]
    for arrays, bias in sets:
        operands += [*arrays] if bias is None else [*arrays, bias]
    operands += state
    return pl.pallas_call(
        functools.partial(
            attend_kernel,
            tuple(pieces),
            tuple((len(arrays), bias is not None) for arrays, bias in sets),
            2 * rows,
            rows,
            bool(state),
            final,
        ),
        out_shape=out_shape,
        in_specs=vmem(len(operands)),
        out_specs=vmem(len(out_shape)),
        compiler_params=pltpu.CompilerParams(vmem_limit_bytes=LARGE),
        cost_estimate=pl.CostEstimate(
            flops=4 * groups * rows * count * width,
            bytes_accessed=4 * count * width,
            transcendentals=groups * rows * count * width // DH,
        ),
        name="attend",
    )(*operands)


def unpack_kernel(steps, gather, width, *refs):
    groups = len(steps)
    parts, out_ref, sems = refs[:groups], refs[groups], refs[groups + 1]
    me = lax.axis_index("seq") // gather
    copies = [
        pltpu.make_async_copy(
            parts[i], out_ref.at[:, columns(partner(me, t, groups), width)], sems.at[i]
        )
        for i, t in enumerate(steps)
    ]
    for copy in copies:
        copy.start()
    for copy in copies:
        copy.wait()


def unpack(parts, steps, gather):
    rows, width = parts[0].shape
    groups = len(steps)
    return pl.pallas_call(
        functools.partial(unpack_kernel, tuple(steps), gather, width),
        out_shape=jax.ShapeDtypeStruct((rows, groups * width), jnp.bfloat16),
        in_specs=vmem(groups),
        out_specs=pl.BlockSpec(memory_space=pl.ANY),
        scratch_shapes=[pltpu.SemaphoreType.DMA((groups,))],
        compiler_params=pltpu.CompilerParams(vmem_limit_bytes=SMALL),
        cost_estimate=pl.CostEstimate(
            flops=0, bytes_accessed=4 * groups * rows * width, transcendentals=0
        ),
        name="unpack_heads",
    )(*parts)


def per_device(
    seq_count,
    head_count,
    query_new,
    key_new,
    value_new,
    cache_keys,
    cache_values,
    key_exponent,
    value_exponent,
    block_mask,
):
    tok_rows, width_dev = query_new.shape
    groups = math.gcd(width_dev // DH, seq_count)
    gather = seq_count // groups
    width = width_dev // groups
    cache_rows = cache_keys.shape[0]
    seq_index = lax.axis_index("seq")
    head_index = lax.axis_index("head")
    group, member = seq_index // gather, seq_index % gather

    def to_group(x, t):
        if t == 0:
            return x
        pairs = [
            (s, partner(s // gather, t, groups) * gather + s % gather) for s in range(seq_count)
        ]
        return lax.ppermute(x, "seq", pairs)

    def from_group(x, t):
        if t == 0:
            return x
        pairs = [
            (s, origin(s // gather, t, groups) * gather + s % gather) for s in range(seq_count)
        ]
        return lax.ppermute(x, "seq", pairs)

    def to_member(x, t):
        pairs = [
            (s, s // gather * gather + partner(s % gather, t, gather)) for s in range(seq_count)
        ]
        return lax.ppermute(x, "seq", pairs)

    def to_head(x, t):
        if t == 0:
            return x
        return lax.ppermute(x, "head", [(h, partner(h, t, head_count)) for h in range(head_count)])

    members = range(1, gather)
    every = range(groups)
    steps = [*every[-1:], *every[1:-1], *every[:1]] if groups > 1 else [0]
    new = (key_new, value_new, query_new)
    stored = (cache_keys, cache_values, key_exponent, value_exponent)
    first = sorted({steps[0], 0})
    kv_own, stored = prepare(new, stored, first, groups, gather, head_count)
    kv_own = dict(zip(first, kv_own))
    kv_other = [to_member(kv_own[0][: 2 * tok_rows], s) for s in members]
    if gather > 1:
        new, stored, kv_other[0] = lax.optimization_barrier((new, stored, kv_other[0]))
    if groups > 2:
        kv_own.update(zip(steps[1:-1], pack(new, steps[1:-1], groups, gather)))
    kv = [to_group(kv_own[t], t) for t in range(groups)]
    by_head = []
    for s in range(head_count):
        x = stored[s]
        if s > 2:
            x, by_head[s - 2] = lax.optimization_barrier((x, by_head[s - 2]))
        by_head.append(to_head(x, s))
    kv[1:] = [lax.optimization_barrier((x, by_head))[0] for x in kv[1:]]
    block_mask, group, member, head_index, _ = lax.optimization_barrier(
        (block_mask, group, member, head_index, kv[1:])
    )
    cache = [to_group(interleave([x[t] for x in by_head]), t) for t in steps]
    if groups > 1:
        swap = join(kv[1:], 2 * tok_rows)
        kv_other += [to_member(swap, s) for s in members]

    q_source = jnp.stack([origin(group, t, groups) * gather + member for t in range(groups)])
    blocks = tok_rows // QBLK
    q_block = (q_source[:, None] * blocks + jnp.arange(blocks)[None, :]).reshape(-1)
    q_pick = (q_block[:, None] == jnp.arange(block_mask.shape[0])[None, :]).astype(jnp.float32)
    row_mask = jnp.dot(q_pick, block_mask.astype(jnp.float32))

    def bias_of(swaps):
        device = jnp.stack(
            [
                (origin(group, t, groups) * gather + origin(member, s, gather)) * head_count
                + origin(head_index, z, head_count)
                for s in swaps
                for t in steps
                for z in range(head_count)
            ]
        )
        block = (device[:, None] * cache_rows + jnp.arange(cache_rows)[None, :]).reshape(-1)
        pick = jnp.arange(block_mask.shape[1])[:, None] == (block // CBLK)[None, :]
        seen = jnp.dot(row_mask, pick.astype(jnp.float32))
        return jnp.where(seen > 0.5, 0.0, MASKED).astype(jnp.float32)

    bias = [bias_of([0])] + ([bias_of(members)] if gather > 1 else [])
    away = steps[:-1]
    if groups > 1:
        state = attend(kv, away, [(kv, None)])
        cache, state, bias = lax.optimization_barrier((cache, state, bias))
    sets, last = [(cache, bias[0])], []
    if gather > 1:
        swap = join(cache, cache[0].shape[0])
        sets.append((kv_other, None))
        last = [([to_member(swap, s) for s in members], bias[1])]
    parts = {}
    if groups > 1:
        state = attend(kv, away, sets, state, not last)
        if last:
            state = attend(kv, away, last, state, True)
        parts.update(zip(away, state))
    parts[0] = attend(kv, [0], [(kv, None), *sets, *last], (), True)[0]
    return unpack([from_group(parts[t], t) for t in steps], steps, gather)


def solution(mesh):
    return jax.shard_map(
        functools.partial(per_device, mesh.shape["seq"], mesh.shape["head"]),
        mesh=mesh,
        in_specs=(
            P("seq", "head"),
            P("seq", "head"),
            P("seq", "head"),
            P(("seq", "head"), None),
            P(("seq", "head"), None),
            P(("seq", "head"), None),
            P(("seq", "head"), None),
            P(),
        ),
        out_specs=P("seq", "head"),
        check_vma=False,
    )
```

```python
import functools
import math

import jax
import jax.numpy as jnp
from jax import lax
from jax.experimental import pallas as pl
from jax.experimental.pallas import tpu as pltpu
from jax.sharding import PartitionSpec as P

DH = 128
QBLK = 64
CBLK = 32
SBLK = 4
MASKED = -1e30
SMALL = 8 * 2**20
LARGE = 16 * 2**20


def partner(index, step, count):
    if count & (count - 1) == 0:
        return index ^ step
    return (index + step) % count


def origin(index, step, count):
    if count & (count - 1) == 0:
        return index ^ step
    return (index + count - step) % count


def columns(chunk, width):
    return pl.ds(pl.multiple_of(chunk * width, DH), width)


def vmem(count):
    return [pl.BlockSpec(memory_space=pltpu.VMEM)] * count


def prepare_kernel(groups, gather, shards, *refs):
    new_refs, cache_refs, outs, scratch = refs[:3], refs[3:7], refs[7:-6], refs[-6:]
    pieces, cached = outs[:groups], outs[groups:]
    ck_buf, cv_buf, ke_buf, ve_buf, cache_sems, new_sems = scratch
    group, shard = lax.axis_index("seq") // gather, lax.axis_index("head")

    loads = [
        pltpu.make_async_copy(src, dst, cache_sems.at[i])
        for i, (src, dst) in enumerate(zip(cache_refs, (ck_buf, cv_buf, ke_buf, ve_buf)))
    ]
    rows, width = pieces[0].shape[0] // 3, pieces[0].shape[1]
    copies = []
    for t in range(groups):
        cols = columns(partner(group, t, groups), width)
        for i, src in enumerate(new_refs):
            dst = pieces[t].at[pl.ds(i * rows, rows)]
            copies.append(pltpu.make_async_copy(src.at[:, cols], dst, new_sems.at[t, i]))
    for copy in loads + copies:
        copy.start()
    for copy in loads:
        copy.wait()

    blocks, heads = ke_buf.shape
    cache_rows = ck_buf.shape[0]
    exponent = jnp.concatenate(
        [
            jnp.broadcast_to(ref[i : i + 1], (SBLK, heads))
            for ref in (ke_buf, ve_buf)
            for i in range(blocks)
        ],
        axis=0,
    )
    power = jnp.left_shift(1, exponent + 16).astype(jnp.float32) * 2.0**-16
    power = power.astype(jnp.bfloat16)
    head = lax.broadcasted_iota(jnp.int32, (heads, width), 0)
    head -= lax.broadcasted_iota(jnp.int32, (heads, width), 1) // DH
    for t in range(groups):
        for s in range(shards):
            part = partner(shard, s, shards) * groups + partner(group, t, groups)
            spread = (head == part * (width // DH)).astype(jnp.float32).astype(jnp.bfloat16)
            factor = jnp.dot(power, spread, preferred_element_type=jnp.float32)
            for which, buf in enumerate((ck_buf, cv_buf)):
                mantissa = buf[:, columns(part, width)].astype(jnp.float32)
                scaled = mantissa * factor[which * cache_rows : (which + 1) * cache_rows]
                cached[s][t, which] = scaled.astype(jnp.bfloat16)
    for copy in copies:
        copy.wait()


def prepare(q, k, v, ck, cv, ke, ve, groups, gather, shards):
    rows, width = q.shape[0], q.shape[1] // groups
    operands = (k, v, q, ck, cv, ke, ve)
    outs = pl.pallas_call(
        functools.partial(prepare_kernel, groups, gather, shards),
        out_shape=[jax.ShapeDtypeStruct((3 * rows, width), jnp.bfloat16)] * groups
        + [jax.ShapeDtypeStruct((groups, 2, ck.shape[0], width), jnp.bfloat16)] * shards,
        in_specs=[pl.BlockSpec(memory_space=pltpu.HBM)] * len(operands),
        out_specs=vmem(groups + shards),
        scratch_shapes=[pltpu.VMEM(x.shape, x.dtype) for x in (ck, cv, ke, ve)]
        + [pltpu.SemaphoreType.DMA((4,)), pltpu.SemaphoreType.DMA((groups, 3))],
        compiler_params=pltpu.CompilerParams(vmem_limit_bytes=SMALL),
        cost_estimate=pl.CostEstimate(
            flops=4 * ck.size, bytes_accessed=12 * q.size + 8 * ck.size, transcendentals=0
        ),
        name="prepare",
    )(*[pltpu.with_memory_space_constraint(x, pltpu.HBM) for x in operands])
    return list(outs[:groups]), list(outs[groups:])


def interleave_kernel(*refs):
    rows = refs[0].shape[1]
    for which in range(2):
        for s, ref in enumerate(refs[:-1]):
            refs[-1][pl.ds((which * len(refs[:-1]) + s) * rows, rows)] = ref[which]


def interleave(pieces):
    _, rows, width = pieces[0].shape
    count = len(pieces)
    if rows % 16:
        return jnp.stack(pieces, axis=1).reshape(-1, width)
    return pl.pallas_call(
        interleave_kernel,
        out_shape=jax.ShapeDtypeStruct((2 * count * rows, width), jnp.bfloat16),
        in_specs=vmem(count),
        out_specs=vmem(1)[0],
        compiler_params=pltpu.CompilerParams(vmem_limit_bytes=SMALL),
        cost_estimate=pl.CostEstimate(
            flops=0, bytes_accessed=8 * count * rows * width, transcendentals=0
        ),
        name="interleave",
    )(*pieces)


def join_kernel(rows, *refs):
    for i, ref in enumerate(refs[:-1]):
        refs[-1][i] = ref[pl.ds(0, rows)]


def join(pieces, rows):
    shape = (len(pieces), rows, pieces[0].shape[1])
    return pl.pallas_call(
        functools.partial(join_kernel, rows),
        out_shape=jax.ShapeDtypeStruct(shape, jnp.bfloat16),
        in_specs=vmem(len(pieces)),
        out_specs=vmem(1)[0],
        compiler_params=pltpu.CompilerParams(vmem_limit_bytes=SMALL),
        cost_estimate=pl.CostEstimate(
            flops=0, bytes_accessed=4 * math.prod(shape), transcendentals=0
        ),
        name="join",
    )(*pieces)


def rows_of(refs, start, count, cols):
    parts = []
    for ref in refs:
        if len(ref.shape) == 2:
            parts.append(ref[start : start + count, cols])
        else:
            parts.append(ref[:, start : start + count, cols].reshape(-1, cols.stop - cols.start))
    return parts[0] if len(parts) == 1 else jnp.concatenate(parts, axis=0)


def attend_sets(queries, sets):
    scale = math.log2(math.e) / math.sqrt(DH)
    scores = []
    for keys, _, bias in sets:
        x = lax.dot_general(
            queries, keys, (((1,), (1,)), ((), ())), preferred_element_type=jnp.float32
        )
        scores.append(x * scale if bias is None else x * scale + bias)
    peak = functools.reduce(
        jnp.maximum, [jnp.max(x, axis=1, keepdims=True) for x in scores]
    )
    total, product = 0.0, 0.0
    for x, (_, values, _) in zip(scores, sets):
        raised = jnp.exp2(x - peak)
        total += jnp.sum(raised, axis=1, keepdims=True)
        product += jnp.dot(
            raised.astype(jnp.bfloat16), values, preferred_element_type=jnp.float32
        )
    return peak, total, product


def bias_rows(bias_ref, pieces, blocks):
    width = bias_ref.shape[1]
    return jnp.concatenate(
        [
            jnp.broadcast_to(bias_ref[row : row + 1], (QBLK, width))
            for t in pieces
            for row in range(t * blocks, (t + 1) * blocks)
        ],
        axis=0,
    )


def attend_kernel(pieces, counts, q_start, rows, merge, final, *refs):
    q_refs, refs = refs[: len(pieces)], refs[len(pieces) :]
    sets = []
    for count, masked in counts:
        bias = bias_rows(refs[count], pieces, rows // QBLK) if masked else None
        sets.append((refs[:count], refs[0].shape[-2] // 2 if masked else rows, bias))
        refs = refs[count + masked :]
    state, refs = (refs[:3], refs[3:]) if merge else (None, refs)
    width = q_refs[0].shape[1]
    for at in range(0, width, DH):
        cols = slice(at, at + DH)
        queries = rows_of(q_refs, q_start, rows, cols)
        peak, total, product = attend_sets(
            queries,
            [
                (rows_of(k_refs, 0, half, cols), rows_of(k_refs, half, half, cols), bias)
                for k_refs, half, bias in sets
            ],
        )
        if merge:
            peak_1, total_1, product_1 = [ref[:, cols] for ref in state]
            top = jnp.maximum(peak, peak_1)
            share, share_1 = jnp.exp2(peak - top), jnp.exp2(peak_1 - top)
            total = total * share + total_1 * share_1
            product = product * share + product_1 * share_1
            peak = top
        if final:
            result = (product / total).astype(jnp.bfloat16)
            for i in range(len(pieces)):
                refs[i][:, cols] = result[i * rows : (i + 1) * rows]
        else:
            for ref, x in zip(refs, (peak, total, product)):
                ref[:, cols] = jnp.broadcast_to(x, product.shape)


def attend(q, pieces, sets, state=(), final=False):
    groups = len(pieces)
    rows, width = q[0].shape[0] // 3, q[0].shape[1]
    count = 0
    for arrays, bias in sets:
        for x in arrays:
            stacked = x.shape[0] if x.ndim == 3 else 1
            count += stacked * (rows if bias is None else x.shape[-2] // 2)
    if final:
        out_shape = [jax.ShapeDtypeStruct((rows, width), jnp.bfloat16)] * groups
    else:
        out_shape = [jax.ShapeDtypeStruct((groups * rows, width), jnp.float32)] * 3
    operands = [q[t] for t in pieces]
    for arrays, bias in sets:
        operands += [*arrays] if bias is None else [*arrays, bias]
    operands += state
    return pl.pallas_call(
        functools.partial(
            attend_kernel,
            tuple(pieces),
            tuple((len(arrays), bias is not None) for arrays, bias in sets),
            2 * rows,
            rows,
            bool(state),
            final,
        ),
        out_shape=out_shape,
        in_specs=vmem(len(operands)),
        out_specs=vmem(len(out_shape)),
        compiler_params=pltpu.CompilerParams(vmem_limit_bytes=LARGE),
        cost_estimate=pl.CostEstimate(
            flops=4 * groups * rows * count * width,
            bytes_accessed=4 * count * width,
            transcendentals=groups * rows * count * width // DH,
        ),
        name="attend",
    )(*operands)


def unpack_kernel(steps, gather, width, *refs):
    groups = len(steps)
    parts, out_ref, sems = refs[:groups], refs[groups], refs[groups + 1]
    me = lax.axis_index("seq") // gather
    copies = [
        pltpu.make_async_copy(
            parts[i], out_ref.at[:, columns(partner(me, t, groups), width)], sems.at[i]
        )
        for i, t in enumerate(steps)
    ]
    for copy in copies:
        copy.start()
    for copy in copies:
        copy.wait()


def unpack(parts, steps, gather):
    rows, width = parts[0].shape
    groups = len(steps)
    return pl.pallas_call(
        functools.partial(unpack_kernel, tuple(steps), gather, width),
        out_shape=jax.ShapeDtypeStruct((rows, groups * width), jnp.bfloat16),
        in_specs=vmem(groups),
        out_specs=pl.BlockSpec(memory_space=pl.ANY),
        scratch_shapes=[pltpu.SemaphoreType.DMA((groups,))],
        compiler_params=pltpu.CompilerParams(vmem_limit_bytes=SMALL),
        cost_estimate=pl.CostEstimate(
            flops=0, bytes_accessed=4 * groups * rows * width, transcendentals=0
        ),
        name="unpack_heads",
    )(*parts)


def per_device(
    seq_count,
    head_count,
    query_new,
    key_new,
    value_new,
    cache_keys,
    cache_values,
    key_exponent,
    value_exponent,
    block_mask,
):
    tok_rows, width_dev = query_new.shape
    groups = math.gcd(width_dev // DH, seq_count)
    gather = seq_count // groups
    width = width_dev // groups
    cache_rows = cache_keys.shape[0]
    seq_index = lax.axis_index("seq")
    head_index = lax.axis_index("head")
    group, member = seq_index // gather, seq_index % gather

    def to_group(x, t):
        if t == 0:
            return x
        pairs = [
            (s, partner(s // gather, t, groups) * gather + s % gather) for s in range(seq_count)
        ]
        return lax.ppermute(x, "seq", pairs)

    def from_group(x, t):
        if t == 0:
            return x
        pairs = [
            (s, origin(s // gather, t, groups) * gather + s % gather) for s in range(seq_count)
        ]
        return lax.ppermute(x, "seq", pairs)

    def to_member(x, t):
        pairs = [
            (s, s // gather * gather + partner(s % gather, t, gather)) for s in range(seq_count)
        ]
        return lax.ppermute(x, "seq", pairs)

    def to_head(x, t):
        if t == 0:
            return x
        return lax.ppermute(x, "head", [(h, partner(h, t, head_count)) for h in range(head_count)])

    members = range(1, gather)
    every = range(groups)
    steps = [*every[-1:], *every[1:-1], *every[:1]] if groups > 1 else [0]
    kv_own, stored = prepare(
        query_new,
        key_new,
        value_new,
        cache_keys,
        cache_values,
        key_exponent,
        value_exponent,
        groups,
        gather,
        head_count,
    )
    kv_other = [to_member(kv_own[0][: 2 * tok_rows], s) for s in members]
    if gather > 1:
        kv_own[1:-1], stored, kv_other[0] = lax.optimization_barrier(
            (kv_own[1:-1], stored, kv_other[0])
        )
    kv = [to_group(kv_own[t], t) for t in range(groups)]
    by_head = []
    for s in range(head_count):
        x = stored[s]
        if s > 2:
            x, by_head[s - 2] = lax.optimization_barrier((x, by_head[s - 2]))
        by_head.append(to_head(x, s))
    kv[1:] = [lax.optimization_barrier((x, by_head))[0] for x in kv[1:]]
    block_mask, group, member, head_index, _ = lax.optimization_barrier(
        (block_mask, group, member, head_index, kv[1:])
    )
    cache = [to_group(interleave([x[t] for x in by_head]), t) for t in steps]
    if groups > 1:
        swap = join(kv[1:], 2 * tok_rows)
        kv_other += [to_member(swap, s) for s in members]

    q_source = jnp.stack([origin(group, t, groups) * gather + member for t in range(groups)])
    blocks = tok_rows // QBLK
    q_block = (q_source[:, None] * blocks + jnp.arange(blocks)[None, :]).reshape(-1)
    q_pick = (q_block[:, None] == jnp.arange(block_mask.shape[0])[None, :]).astype(jnp.float32)
    row_mask = jnp.dot(q_pick, block_mask.astype(jnp.float32))

    def bias_of(swaps):
        device = jnp.stack(
            [
                (origin(group, t, groups) * gather + origin(member, s, gather)) * head_count
                + origin(head_index, z, head_count)
                for s in swaps
                for t in steps
                for z in range(head_count)
            ]
        )
        block = (device[:, None] * cache_rows + jnp.arange(cache_rows)[None, :]).reshape(-1)
        pick = jnp.arange(block_mask.shape[1])[:, None] == (block // CBLK)[None, :]
        seen = jnp.dot(row_mask, pick.astype(jnp.float32))
        return jnp.where(seen > 0.5, 0.0, MASKED).astype(jnp.float32)

    bias = [bias_of([0])] + ([bias_of(members)] if gather > 1 else [])
    away = steps[:-1]
    if groups > 1:
        state = attend(kv, away, [(kv, None)])
        cache, state, bias = lax.optimization_barrier((cache, state, bias))
    sets, last = [(cache, bias[0])], []
    if gather > 1:
        swap = join(cache, cache[0].shape[0])
        sets.append((kv_other, None))
        last = [([to_member(swap, s) for s in members], bias[1])]
    parts = {}
    if groups > 1:
        state = attend(kv, away, sets, state, not last)
        if last:
            state = attend(kv, away, last, state, True)
        parts.update(zip(away, state))
    parts[0] = attend(kv, [0], [(kv, None), *sets, *last], (), True)[0]
    return unpack([from_group(parts[t], t) for t in steps], steps, gather)


def solution(mesh):
    return jax.shard_map(
        functools.partial(per_device, mesh.shape["seq"], mesh.shape["head"]),
        mesh=mesh,
        in_specs=(
            P("seq", "head"),
            P("seq", "head"),
            P("seq", "head"),
            P(("seq", "head"), None),
            P(("seq", "head"), None),
            P(("seq", "head"), None),
            P(("seq", "head"), None),
            P(),
        ),
        out_specs=P("seq", "head"),
        check_vma=False,
    )
```

```python
import functools
import math

import jax
import jax.numpy as jnp
from jax import lax
from jax.experimental import pallas as pl
from jax.experimental.pallas import tpu as pltpu
from jax.sharding import PartitionSpec as P

DH = 128
QBLK = 64
CBLK = 32
SBLK = 4
MASKED = -1e30
SMALL = 8 * 2**20
LARGE = 16 * 2**20


def partner(index, step, count):
    if count & (count - 1) == 0:
        return index ^ step
    return (index + step) % count


def origin(index, step, count):
    if count & (count - 1) == 0:
        return index ^ step
    return (index + count - step) % count


def columns(chunk, width):
    return pl.ds(pl.multiple_of(chunk * width, DH), width)


def vmem(count):
    return [pl.BlockSpec(memory_space=pltpu.VMEM)] * count


def prepare_kernel(groups, gather, shards, *refs):
    new_refs, cache_refs, outs, scratch = refs[:3], refs[3:7], refs[7:-6], refs[-6:]
    pieces, cached = outs[:groups], outs[groups:]
    ck_buf, cv_buf, ke_buf, ve_buf, cache_sems, new_sems = scratch
    group, shard = lax.axis_index("seq") // gather, lax.axis_index("head")

    loads = [
        pltpu.make_async_copy(src, dst, cache_sems.at[i])
        for i, (src, dst) in enumerate(zip(cache_refs, (ck_buf, cv_buf, ke_buf, ve_buf)))
    ]
    rows, width = pieces[0].shape[0] // 3, pieces[0].shape[1]
    copies = []
    for t in range(groups):
        cols = columns(partner(group, t, groups), width)
        for i, src in enumerate(new_refs):
            dst = pieces[t].at[pl.ds(i * rows, rows)]
            copies.append(pltpu.make_async_copy(src.at[:, cols], dst, new_sems.at[t, i]))
    for copy in loads + copies:
        copy.start()
    for copy in loads:
        copy.wait()

    blocks, heads = ke_buf.shape
    cache_rows = ck_buf.shape[0]
    exponent = jnp.concatenate(
        [
            jnp.broadcast_to(ref[i : i + 1], (SBLK, heads))
            for ref in (ke_buf, ve_buf)
            for i in range(blocks)
        ],
        axis=0,
    )
    power = jnp.left_shift(1, exponent + 16).astype(jnp.float32) * 2.0**-16
    power = power.astype(jnp.bfloat16)
    head = lax.broadcasted_iota(jnp.int32, (heads, width), 0)
    head -= lax.broadcasted_iota(jnp.int32, (heads, width), 1) // DH
    for t in range(groups):
        for s in range(shards):
            part = partner(shard, s, shards) * groups + partner(group, t, groups)
            spread = (head == part * (width // DH)).astype(jnp.float32).astype(jnp.bfloat16)
            factor = jnp.dot(power, spread, preferred_element_type=jnp.float32)
            for which, buf in enumerate((ck_buf, cv_buf)):
                mantissa = buf[:, columns(part, width)].astype(jnp.float32)
                scaled = mantissa * factor[which * cache_rows : (which + 1) * cache_rows]
                cached[s][t, which] = scaled.astype(jnp.bfloat16)
    for copy in copies:
        copy.wait()


def prepare(q, k, v, ck, cv, ke, ve, groups, gather, shards):
    rows, width = q.shape[0], q.shape[1] // groups
    operands = (k, v, q, ck, cv, ke, ve)
    outs = pl.pallas_call(
        functools.partial(prepare_kernel, groups, gather, shards),
        out_shape=[jax.ShapeDtypeStruct((3 * rows, width), jnp.bfloat16)] * groups
        + [jax.ShapeDtypeStruct((groups, 2, ck.shape[0], width), jnp.bfloat16)] * shards,
        in_specs=[pl.BlockSpec(memory_space=pltpu.HBM)] * len(operands),
        out_specs=vmem(groups + shards),
        scratch_shapes=[pltpu.VMEM(x.shape, x.dtype) for x in (ck, cv, ke, ve)]
        + [pltpu.SemaphoreType.DMA((4,)), pltpu.SemaphoreType.DMA((groups, 3))],
        compiler_params=pltpu.CompilerParams(vmem_limit_bytes=SMALL),
        cost_estimate=pl.CostEstimate(
            flops=4 * ck.size, bytes_accessed=12 * q.size + 8 * ck.size, transcendentals=0
        ),
        name="prepare",
    )(*[pltpu.with_memory_space_constraint(x, pltpu.HBM) for x in operands])
    return list(outs[:groups]), list(outs[groups:])


def interleave_kernel(*refs):
    rows = refs[0].shape[1]
    for which in range(2):
        for s, ref in enumerate(refs[:-1]):
            refs[-1][pl.ds((which * len(refs[:-1]) + s) * rows, rows)] = ref[which]


def interleave(pieces):
    _, rows, width = pieces[0].shape
    count = len(pieces)
    if rows % 16:
        return jnp.stack(pieces, axis=1).reshape(-1, width)
    return pl.pallas_call(
        interleave_kernel,
        out_shape=jax.ShapeDtypeStruct((2 * count * rows, width), jnp.bfloat16),
        in_specs=vmem(count),
        out_specs=vmem(1)[0],
        compiler_params=pltpu.CompilerParams(vmem_limit_bytes=SMALL),
        cost_estimate=pl.CostEstimate(
            flops=0, bytes_accessed=8 * count * rows * width, transcendentals=0
        ),
        name="interleave",
    )(*pieces)


def join_kernel(rows, *refs):
    for i, ref in enumerate(refs[:-1]):
        refs[-1][i] = ref[pl.ds(0, rows)]


def join(pieces, rows):
    shape = (len(pieces), rows, pieces[0].shape[1])
    return pl.pallas_call(
        functools.partial(join_kernel, rows),
        out_shape=jax.ShapeDtypeStruct(shape, jnp.bfloat16),
        in_specs=vmem(len(pieces)),
        out_specs=vmem(1)[0],
        compiler_params=pltpu.CompilerParams(vmem_limit_bytes=SMALL),
        cost_estimate=pl.CostEstimate(
            flops=0, bytes_accessed=4 * math.prod(shape), transcendentals=0
        ),
        name="join",
    )(*pieces)


def rows_of(refs, start, count, cols):
    parts = []
    for ref in refs:
        if len(ref.shape) == 2:
            parts.append(ref[start : start + count, cols])
        else:
            parts.append(ref[:, start : start + count, cols].reshape(-1, cols.stop - cols.start))
    return parts[0] if len(parts) == 1 else jnp.concatenate(parts, axis=0)


def attend_sets(queries, sets):
    scale = math.log2(math.e) / math.sqrt(DH)
    scores = []
    for keys, _, bias in sets:
        x = lax.dot_general(
            queries, keys, (((1,), (1,)), ((), ())), preferred_element_type=jnp.float32
        )
        scores.append(x * scale if bias is None else x * scale + bias)
    peak = functools.reduce(
        jnp.maximum, [jnp.max(x, axis=1, keepdims=True) for x in scores]
    )
    total, product = 0.0, 0.0
    for x, (_, values, _) in zip(scores, sets):
        raised = jnp.exp2(x - peak)
        total += jnp.sum(raised, axis=1, keepdims=True)
        product += jnp.dot(
            raised.astype(jnp.bfloat16), values, preferred_element_type=jnp.float32
        )
    return peak, total, product


def bias_rows(bias_ref, pieces, blocks):
    width = bias_ref.shape[1]
    return jnp.concatenate(
        [
            jnp.broadcast_to(bias_ref[row : row + 1], (QBLK, width))
            for t in pieces
            for row in range(t * blocks, (t + 1) * blocks)
        ],
        axis=0,
    )


def attend_kernel(pieces, counts, q_start, rows, merge, final, *refs):
    q_refs, refs = refs[: len(pieces)], refs[len(pieces) :]
    sets = []
    for count, masked in counts:
        bias = bias_rows(refs[count], pieces, rows // QBLK) if masked else None
        sets.append((refs[:count], refs[0].shape[-2] // 2 if masked else rows, bias))
        refs = refs[count + masked :]
    state, refs = (refs[:3], refs[3:]) if merge else (None, refs)
    width = q_refs[0].shape[1]
    for at in range(0, width, DH):
        cols = slice(at, at + DH)
        queries = rows_of(q_refs, q_start, rows, cols)
        peak, total, product = attend_sets(
            queries,
            [
                (rows_of(k_refs, 0, half, cols), rows_of(k_refs, half, half, cols), bias)
                for k_refs, half, bias in sets
            ],
        )
        if merge:
            peak_1, total_1, product_1 = [ref[:, cols] for ref in state]
            top = jnp.maximum(peak, peak_1)
            share, share_1 = jnp.exp2(peak - top), jnp.exp2(peak_1 - top)
            total = total * share + total_1 * share_1
            product = product * share + product_1 * share_1
            peak = top
        if final:
            result = (product / total).astype(jnp.bfloat16)
            for i in range(len(pieces)):
                refs[i][:, cols] = result[i * rows : (i + 1) * rows]
        else:
            for ref, x in zip(refs, (peak, total, product)):
                ref[:, cols] = jnp.broadcast_to(x, product.shape)


def attend(q, pieces, sets, state=(), final=False):
    groups = len(pieces)
    rows, width = q[0].shape[0] // 3, q[0].shape[1]
    count = 0
    for arrays, bias in sets:
        for x in arrays:
            stacked = x.shape[0] if x.ndim == 3 else 1
            count += stacked * (rows if bias is None else x.shape[-2] // 2)
    if final:
        out_shape = [jax.ShapeDtypeStruct((rows, width), jnp.bfloat16)] * groups
    else:
        out_shape = [jax.ShapeDtypeStruct((groups * rows, width), jnp.float32)] * 3
    operands = [q[t] for t in pieces]
    for arrays, bias in sets:
        operands += [*arrays] if bias is None else [*arrays, bias]
    operands += state
    return pl.pallas_call(
        functools.partial(
            attend_kernel,
            tuple(pieces),
            tuple((len(arrays), bias is not None) for arrays, bias in sets),
            2 * rows,
            rows,
            bool(state),
            final,
        ),
        out_shape=out_shape,
        in_specs=vmem(len(operands)),
        out_specs=vmem(len(out_shape)),
        compiler_params=pltpu.CompilerParams(vmem_limit_bytes=LARGE),
        cost_estimate=pl.CostEstimate(
            flops=4 * groups * rows * count * width,
            bytes_accessed=4 * count * width,
            transcendentals=groups * rows * count * width // DH,
        ),
        name="attend",
    )(*operands)


def unpack_kernel(steps, gather, width, *refs):
    groups = len(steps)
    parts, out_ref, sems = refs[:groups], refs[groups], refs[groups + 1]
    me = lax.axis_index("seq") // gather
    copies = [
        pltpu.make_async_copy(
            parts[i], out_ref.at[:, columns(partner(me, t, groups), width)], sems.at[i]
        )
        for i, t in enumerate(steps)
    ]
    for copy in copies:
        copy.start()
    for copy in copies:
        copy.wait()


def unpack(parts, steps, gather):
    rows, width = parts[0].shape
    groups = len(steps)
    return pl.pallas_call(
        functools.partial(unpack_kernel, tuple(steps), gather, width),
        out_shape=jax.ShapeDtypeStruct((rows, groups * width), jnp.bfloat16),
        in_specs=vmem(groups),
        out_specs=pl.BlockSpec(memory_space=pl.ANY),
        scratch_shapes=[pltpu.SemaphoreType.DMA((groups,))],
        compiler_params=pltpu.CompilerParams(vmem_limit_bytes=SMALL),
        cost_estimate=pl.CostEstimate(
            flops=0, bytes_accessed=4 * groups * rows * width, transcendentals=0
        ),
        name="unpack_heads",
    )(*parts)


def per_device(
    seq_count,
    head_count,
    query_new,
    key_new,
    value_new,
    cache_keys,
    cache_values,
    key_exponent,
    value_exponent,
    block_mask,
):
    tok_rows, width_dev = query_new.shape
    groups = math.gcd(width_dev // DH, seq_count)
    gather = seq_count // groups
    width = width_dev // groups
    cache_rows = cache_keys.shape[0]
    seq_index = lax.axis_index("seq")
    head_index = lax.axis_index("head")
    group, member = seq_index // gather, seq_index % gather

    def to_group(x, t):
        if t == 0:
            return x
        pairs = [
            (s, partner(s // gather, t, groups) * gather + s % gather) for s in range(seq_count)
        ]
        return lax.ppermute(x, "seq", pairs)

    def from_group(x, t):
        if t == 0:
            return x
        pairs = [
            (s, origin(s // gather, t, groups) * gather + s % gather) for s in range(seq_count)
        ]
        return lax.ppermute(x, "seq", pairs)

    def to_member(x, t):
        pairs = [
            (s, s // gather * gather + partner(s % gather, t, gather)) for s in range(seq_count)
        ]
        return lax.ppermute(x, "seq", pairs)

    def to_head(x, t):
        if t == 0:
            return x
        return lax.ppermute(x, "head", [(h, partner(h, t, head_count)) for h in range(head_count)])

    members = range(1, gather)
    every = range(groups)
    steps = [*every[-1:], *every[1:-1], *every[:1]] if groups > 1 else [0]
    kv_own, stored = prepare(
        query_new,
        key_new,
        value_new,
        cache_keys,
        cache_values,
        key_exponent,
        value_exponent,
        groups,
        gather,
        head_count,
    )
    kv_other = [to_member(kv_own[0][: 2 * tok_rows], s) for s in members]
    if gather > 1:
        kv_own[1:-1], stored[2:], kv_other[0] = lax.optimization_barrier(
            (kv_own[1:-1], stored[2:], kv_other[0])
        )
    kv = [to_group(kv_own[t], t) for t in range(groups)]
    by_head = [to_head(x, s) for s, x in enumerate(stored)]
    kv[1:] = [lax.optimization_barrier((x, by_head))[0] for x in kv[1:]]
    block_mask, group, member, head_index, _ = lax.optimization_barrier(
        (block_mask, group, member, head_index, kv[1:])
    )
    cache = [to_group(interleave([x[t] for x in by_head]), t) for t in steps]
    if groups > 1:
        swap = join(kv[1:], 2 * tok_rows)
        kv_other += [to_member(swap, s) for s in members]

    q_source = jnp.stack([origin(group, t, groups) * gather + member for t in range(groups)])
    blocks = tok_rows // QBLK
    q_block = (q_source[:, None] * blocks + jnp.arange(blocks)[None, :]).reshape(-1)
    q_pick = (q_block[:, None] == jnp.arange(block_mask.shape[0])[None, :]).astype(jnp.float32)
    row_mask = jnp.dot(q_pick, block_mask.astype(jnp.float32))

    def bias_of(swaps):
        device = jnp.stack(
            [
                (origin(group, t, groups) * gather + origin(member, s, gather)) * head_count
                + origin(head_index, z, head_count)
                for s in swaps
                for t in steps
                for z in range(head_count)
            ]
        )
        block = (device[:, None] * cache_rows + jnp.arange(cache_rows)[None, :]).reshape(-1)
        pick = jnp.arange(block_mask.shape[1])[:, None] == (block // CBLK)[None, :]
        seen = jnp.dot(row_mask, pick.astype(jnp.float32))
        return jnp.where(seen > 0.5, 0.0, MASKED).astype(jnp.float32)

    bias = [bias_of([0])] + ([bias_of(members)] if gather > 1 else [])
    away = steps[:-1]
    if groups > 1:
        state = attend(kv, away, [(kv, None)])
        cache, state, bias = lax.optimization_barrier((cache, state, bias))
    sets, last = [(cache, bias[0])], []
    if gather > 1:
        swap = join(cache, cache[0].shape[0])
        sets.append((kv_other, None))
        last = [([to_member(swap, s) for s in members], bias[1])]
    parts = {}
    if groups > 1:
        state = attend(kv, away, sets, state, not last)
        if last:
            state = attend(kv, away, last, state, True)
        parts.update(zip(away, state))
    parts[0] = attend(kv, [0], [(kv, None), *sets, *last], (), True)[0]
    return unpack([from_group(parts[t], t) for t in steps], steps, gather)


def solution(mesh):
    return jax.shard_map(
        functools.partial(per_device, mesh.shape["seq"], mesh.shape["head"]),
        mesh=mesh,
        in_specs=(
            P("seq", "head"),
            P("seq", "head"),
            P("seq", "head"),
            P(("seq", "head"), None),
            P(("seq", "head"), None),
            P(("seq", "head"), None),
            P(("seq", "head"), None),
            P(),
        ),
        out_specs=P("seq", "head"),
        check_vma=False,
    )
```

```python
import functools
import math

import jax
import jax.numpy as jnp
from jax import lax
from jax.experimental import pallas as pl
from jax.experimental.pallas import tpu as pltpu
from jax.sharding import PartitionSpec as P

DH = 128
QBLK = 64
CBLK = 32
SBLK = 4
MASKED = -1e30
SMALL = 8 * 2**20
LARGE = 16 * 2**20


def partner(index, step, count):
    if count & (count - 1) == 0:
        return index ^ step
    return (index + step) % count


def origin(index, step, count):
    if count & (count - 1) == 0:
        return index ^ step
    return (index + count - step) % count


def columns(chunk, width):
    return pl.ds(pl.multiple_of(chunk * width, DH), width)


def vmem(count):
    return [pl.BlockSpec(memory_space=pltpu.VMEM)] * count


def prepare_kernel(groups, gather, shards, *refs):
    new_refs, cache_refs, outs, scratch = refs[:3], refs[3:7], refs[7:-6], refs[-6:]
    pieces, cached = outs[:groups], outs[groups:]
    ck_buf, cv_buf, ke_buf, ve_buf, cache_sems, new_sems = scratch
    group, shard = lax.axis_index("seq") // gather, lax.axis_index("head")

    loads = [
        pltpu.make_async_copy(src, dst, cache_sems.at[i])
        for i, (src, dst) in enumerate(zip(cache_refs, (ck_buf, cv_buf, ke_buf, ve_buf)))
    ]
    rows, width = pieces[0].shape[0] // 3, pieces[0].shape[1]
    copies = []
    for t in range(groups):
        cols = columns(partner(group, t, groups), width)
        for i, src in enumerate(new_refs):
            dst = pieces[t].at[pl.ds(i * rows, rows)]
            copies.append(pltpu.make_async_copy(src.at[:, cols], dst, new_sems.at[t, i]))
    for copy in loads + copies:
        copy.start()
    for copy in loads:
        copy.wait()

    blocks, heads = ke_buf.shape
    cache_rows = ck_buf.shape[0]
    exponent = jnp.concatenate(
        [
            jnp.broadcast_to(ref[i : i + 1], (SBLK, heads))
            for ref in (ke_buf, ve_buf)
            for i in range(blocks)
        ],
        axis=0,
    )
    power = jnp.left_shift(1, exponent + 16).astype(jnp.float32) * 2.0**-16
    power = power.astype(jnp.bfloat16)
    head = lax.broadcasted_iota(jnp.int32, (heads, width), 0)
    head -= lax.broadcasted_iota(jnp.int32, (heads, width), 1) // DH
    for t in range(groups):
        for s in range(shards):
            part = partner(shard, s, shards) * groups + partner(group, t, groups)
            spread = (head == part * (width // DH)).astype(jnp.float32).astype(jnp.bfloat16)
            factor = jnp.dot(power, spread, preferred_element_type=jnp.float32)
            for which, buf in enumerate((ck_buf, cv_buf)):
                mantissa = buf[:, columns(part, width)].astype(jnp.float32)
                scaled = mantissa * factor[which * cache_rows : (which + 1) * cache_rows]
                cached[s][t, which] = scaled.astype(jnp.bfloat16)
    for copy in copies:
        copy.wait()


def prepare(q, k, v, ck, cv, ke, ve, groups, gather, shards):
    rows, width = q.shape[0], q.shape[1] // groups
    operands = (k, v, q, ck, cv, ke, ve)
    outs = pl.pallas_call(
        functools.partial(prepare_kernel, groups, gather, shards),
        out_shape=[jax.ShapeDtypeStruct((3 * rows, width), jnp.bfloat16)] * groups
        + [jax.ShapeDtypeStruct((groups, 2, ck.shape[0], width), jnp.bfloat16)] * shards,
        in_specs=[pl.BlockSpec(memory_space=pltpu.HBM)] * len(operands),
        out_specs=vmem(groups + shards),
        scratch_shapes=[pltpu.VMEM(x.shape, x.dtype) for x in (ck, cv, ke, ve)]
        + [pltpu.SemaphoreType.DMA((4,)), pltpu.SemaphoreType.DMA((groups, 3))],
        compiler_params=pltpu.CompilerParams(vmem_limit_bytes=SMALL),
        cost_estimate=pl.CostEstimate(
            flops=4 * ck.size, bytes_accessed=12 * q.size + 8 * ck.size, transcendentals=0
        ),
        name="prepare",
    )(*[pltpu.with_memory_space_constraint(x, pltpu.HBM) for x in operands])
    return list(outs[:groups]), list(outs[groups:])


def interleave_kernel(*refs):
    rows = refs[0].shape[1]
    for which in range(2):
        for s, ref in enumerate(refs[:-1]):
            refs[-1][pl.ds((which * len(refs[:-1]) + s) * rows, rows)] = ref[which]


def interleave(pieces):
    _, rows, width = pieces[0].shape
    count = len(pieces)
    if rows % 16:
        return jnp.stack(pieces, axis=1).reshape(-1, width)
    return pl.pallas_call(
        interleave_kernel,
        out_shape=jax.ShapeDtypeStruct((2 * count * rows, width), jnp.bfloat16),
        in_specs=vmem(count),
        out_specs=vmem(1)[0],
        compiler_params=pltpu.CompilerParams(vmem_limit_bytes=SMALL),
        cost_estimate=pl.CostEstimate(
            flops=0, bytes_accessed=8 * count * rows * width, transcendentals=0
        ),
        name="interleave",
    )(*pieces)


def join_kernel(rows, *refs):
    for i, ref in enumerate(refs[:-1]):
        refs[-1][i] = ref[pl.ds(0, rows)]


def join(pieces, rows):
    shape = (len(pieces), rows, pieces[0].shape[1])
    return pl.pallas_call(
        functools.partial(join_kernel, rows),
        out_shape=jax.ShapeDtypeStruct(shape, jnp.bfloat16),
        in_specs=vmem(len(pieces)),
        out_specs=vmem(1)[0],
        compiler_params=pltpu.CompilerParams(vmem_limit_bytes=SMALL),
        cost_estimate=pl.CostEstimate(
            flops=0, bytes_accessed=4 * math.prod(shape), transcendentals=0
        ),
        name="join",
    )(*pieces)


def rows_of(refs, start, count, cols):
    parts = []
    for ref in refs:
        if len(ref.shape) == 2:
            parts.append(ref[start : start + count, cols])
        else:
            parts.append(ref[:, start : start + count, cols].reshape(-1, cols.stop - cols.start))
    return parts[0] if len(parts) == 1 else jnp.concatenate(parts, axis=0)


def attend_sets(queries, sets):
    scale = math.log2(math.e) / math.sqrt(DH)
    scores = []
    for keys, _, bias in sets:
        x = lax.dot_general(
            queries, keys, (((1,), (1,)), ((), ())), preferred_element_type=jnp.float32
        )
        scores.append(x * scale if bias is None else x * scale + bias)
    peak = functools.reduce(
        jnp.maximum, [jnp.max(x, axis=1, keepdims=True) for x in scores]
    )
    total, product = 0.0, 0.0
    for x, (_, values, _) in zip(scores, sets):
        raised = jnp.exp2(x - peak)
        total += jnp.sum(raised, axis=1, keepdims=True)
        product += jnp.dot(
            raised.astype(jnp.bfloat16), values, preferred_element_type=jnp.float32
        )
    return peak, total, product


def bias_rows(bias_ref, pieces, blocks):
    width = bias_ref.shape[1]
    return jnp.concatenate(
        [
            jnp.broadcast_to(bias_ref[row : row + 1], (QBLK, width))
            for t in pieces
            for row in range(t * blocks, (t + 1) * blocks)
        ],
        axis=0,
    )


def attend_kernel(pieces, counts, q_start, rows, merge, final, *refs):
    q_refs, refs = refs[: len(pieces)], refs[len(pieces) :]
    sets = []
    for count, masked in counts:
        bias = bias_rows(refs[count], pieces, rows // QBLK) if masked else None
        sets.append((refs[:count], refs[0].shape[-2] // 2 if masked else rows, bias))
        refs = refs[count + masked :]
    state, refs = (refs[:3], refs[3:]) if merge else (None, refs)
    width = q_refs[0].shape[1]
    for at in range(0, width, DH):
        cols = slice(at, at + DH)
        queries = rows_of(q_refs, q_start, rows, cols)
        peak, total, product = attend_sets(
            queries,
            [
                (rows_of(k_refs, 0, half, cols), rows_of(k_refs, half, half, cols), bias)
                for k_refs, half, bias in sets
            ],
        )
        if merge:
            peak_1, total_1, product_1 = [ref[:, cols] for ref in state]
            top = jnp.maximum(peak, peak_1)
            share, share_1 = jnp.exp2(peak - top), jnp.exp2(peak_1 - top)
            total = total * share + total_1 * share_1
            product = product * share + product_1 * share_1
            peak = top
        if final:
            result = (product / total).astype(jnp.bfloat16)
            for i in range(len(pieces)):
                refs[i][:, cols] = result[i * rows : (i + 1) * rows]
        else:
            for ref, x in zip(refs, (peak, total, product)):
                ref[:, cols] = jnp.broadcast_to(x, product.shape)


def attend(q, pieces, sets, state=(), final=False):
    groups = len(pieces)
    rows, width = q[0].shape[0] // 3, q[0].shape[1]
    count = 0
    for arrays, bias in sets:
        for x in arrays:
            stacked = x.shape[0] if x.ndim == 3 else 1
            count += stacked * (rows if bias is None else x.shape[-2] // 2)
    if final:
        out_shape = [jax.ShapeDtypeStruct((rows, width), jnp.bfloat16)] * groups
    else:
        out_shape = [jax.ShapeDtypeStruct((groups * rows, width), jnp.float32)] * 3
    operands = [q[t] for t in pieces]
    for arrays, bias in sets:
        operands += [*arrays] if bias is None else [*arrays, bias]
    operands += state
    return pl.pallas_call(
        functools.partial(
            attend_kernel,
            tuple(pieces),
            tuple((len(arrays), bias is not None) for arrays, bias in sets),
            2 * rows,
            rows,
            bool(state),
            final,
        ),
        out_shape=out_shape,
        in_specs=vmem(len(operands)),
        out_specs=vmem(len(out_shape)),
        compiler_params=pltpu.CompilerParams(vmem_limit_bytes=LARGE),
        cost_estimate=pl.CostEstimate(
            flops=4 * groups * rows * count * width,
            bytes_accessed=4 * count * width,
            transcendentals=groups * rows * count * width // DH,
        ),
        name="attend",
    )(*operands)


def unpack_kernel(steps, gather, width, *refs):
    groups = len(steps)
    parts, out_ref, sems = refs[:groups], refs[groups], refs[groups + 1]
    me = lax.axis_index("seq") // gather
    copies = [
        pltpu.make_async_copy(
            parts[i], out_ref.at[:, columns(partner(me, t, groups), width)], sems.at[i]
        )
        for i, t in enumerate(steps)
    ]
    for copy in copies:
        copy.start()
    for copy in copies:
        copy.wait()


def unpack(parts, steps, gather):
    rows, width = parts[0].shape
    groups = len(steps)
    return pl.pallas_call(
        functools.partial(unpack_kernel, tuple(steps), gather, width),
        out_shape=jax.ShapeDtypeStruct((rows, groups * width), jnp.bfloat16),
        in_specs=vmem(groups),
        out_specs=pl.BlockSpec(memory_space=pl.ANY),
        scratch_shapes=[pltpu.SemaphoreType.DMA((groups,))],
        compiler_params=pltpu.CompilerParams(vmem_limit_bytes=SMALL),
        cost_estimate=pl.CostEstimate(
            flops=0, bytes_accessed=4 * groups * rows * width, transcendentals=0
        ),
        name="unpack_heads",
    )(*parts)


def per_device(
    seq_count,
    head_count,
    query_new,
    key_new,
    value_new,
    cache_keys,
    cache_values,
    key_exponent,
    value_exponent,
    block_mask,
):
    tok_rows, width_dev = query_new.shape
    groups = math.gcd(width_dev // DH, seq_count)
    gather = seq_count // groups
    width = width_dev // groups
    cache_rows = cache_keys.shape[0]
    seq_index = lax.axis_index("seq")
    head_index = lax.axis_index("head")
    group, member = seq_index // gather, seq_index % gather

    def to_group(x, t):
        if t == 0:
            return x
        pairs = [
            (s, partner(s // gather, t, groups) * gather + s % gather) for s in range(seq_count)
        ]
        return lax.ppermute(x, "seq", pairs)

    def from_group(x, t):
        if t == 0:
            return x
        pairs = [
            (s, origin(s // gather, t, groups) * gather + s % gather) for s in range(seq_count)
        ]
        return lax.ppermute(x, "seq", pairs)

    def to_member(x, t):
        pairs = [
            (s, s // gather * gather + partner(s % gather, t, gather)) for s in range(seq_count)
        ]
        return lax.ppermute(x, "seq", pairs)

    def to_head(x, t):
        if t == 0:
            return x
        return lax.ppermute(x, "head", [(h, partner(h, t, head_count)) for h in range(head_count)])

    members = range(1, gather)
    every = range(groups)
    steps = [*every[-1:], *every[1:-1], *every[:1]] if groups > 1 else [0]
    kv_own, stored = prepare(
        query_new,
        key_new,
        value_new,
        cache_keys,
        cache_values,
        key_exponent,
        value_exponent,
        groups,
        gather,
        head_count,
    )
    kv_other = [to_member(kv_own[0][: 2 * tok_rows], s) for s in members]
    if gather > 1:
        kv_own[1:-1], stored, kv_other[0] = lax.optimization_barrier(
            (kv_own[1:-1], stored, kv_other[0])
        )
    kv = [to_group(kv_own[t], t) for t in range(groups)]
    by_head = []
    for s in range(head_count):
        x = stored[s]
        if s > 2:
            x, by_head[s - 1] = lax.optimization_barrier((x, by_head[s - 1]))
        by_head.append(to_head(x, s))
    kv[1:] = [lax.optimization_barrier((x, by_head))[0] for x in kv[1:]]
    block_mask, group, member, head_index, _ = lax.optimization_barrier(
        (block_mask, group, member, head_index, kv[1:])
    )
    cache = [to_group(interleave([x[t] for x in by_head]), t) for t in steps]
    if groups > 1:
        swap = join(kv[1:], 2 * tok_rows)
        kv_other += [to_member(swap, s) for s in members]

    q_source = jnp.stack([origin(group, t, groups) * gather + member for t in range(groups)])
    blocks = tok_rows // QBLK
    q_block = (q_source[:, None] * blocks + jnp.arange(blocks)[None, :]).reshape(-1)
    q_pick = (q_block[:, None] == jnp.arange(block_mask.shape[0])[None, :]).astype(jnp.float32)
    row_mask = jnp.dot(q_pick, block_mask.astype(jnp.float32))

    def bias_of(swaps):
        device = jnp.stack(
            [
                (origin(group, t, groups) * gather + origin(member, s, gather)) * head_count
                + origin(head_index, z, head_count)
                for s in swaps
                for t in steps
                for z in range(head_count)
            ]
        )
        block = (device[:, None] * cache_rows + jnp.arange(cache_rows)[None, :]).reshape(-1)
        pick = jnp.arange(block_mask.shape[1])[:, None] == (block // CBLK)[None, :]
        seen = jnp.dot(row_mask, pick.astype(jnp.float32))
        return jnp.where(seen > 0.5, 0.0, MASKED).astype(jnp.float32)

    bias = [bias_of([0])] + ([bias_of(members)] if gather > 1 else [])
    away = steps[:-1]
    if groups > 1:
        state = attend(kv, away, [(kv, None)])
        cache, state, bias = lax.optimization_barrier((cache, state, bias))
    sets, last = [(cache, bias[0])], []
    if gather > 1:
        swap = join(cache, cache[0].shape[0])
        sets.append((kv_other, None))
        last = [([to_member(swap, s) for s in members], bias[1])]
    parts = {}
    if groups > 1:
        state = attend(kv, away, sets, state, not last)
        if last:
            state = attend(kv, away, last, state, True)
        parts.update(zip(away, state))
    parts[0] = attend(kv, [0], [(kv, None), *sets, *last], (), True)[0]
    return unpack([from_group(parts[t], t) for t in steps], steps, gather)


def solution(mesh):
    return jax.shard_map(
        functools.partial(per_device, mesh.shape["seq"], mesh.shape["head"]),
        mesh=mesh,
        in_specs=(
            P("seq", "head"),
            P("seq", "head"),
            P("seq", "head"),
            P(("seq", "head"), None),
            P(("seq", "head"), None),
            P(("seq", "head"), None),
            P(("seq", "head"), None),
            P(),
        ),
        out_specs=P("seq", "head"),
        check_vma=False,
    )
```

```python
import functools
import math

import jax
import jax.numpy as jnp
from jax import lax
from jax.experimental import pallas as pl
from jax.experimental.pallas import tpu as pltpu
from jax.sharding import PartitionSpec as P

DH = 128
QBLK = 64
CBLK = 32
SBLK = 4
MASKED = -1e30
SMALL = 8 * 2**20
LARGE = 16 * 2**20


def partner(index, step, count):
    if count & (count - 1) == 0:
        return index ^ step
    return (index + step) % count


def origin(index, step, count):
    if count & (count - 1) == 0:
        return index ^ step
    return (index + count - step) % count


def columns(chunk, width):
    return pl.ds(pl.multiple_of(chunk * width, DH), width)


def vmem(count):
    return [pl.BlockSpec(memory_space=pltpu.VMEM)] * count


def prepare_kernel(groups, gather, shards, *refs):
    new_refs, cache_refs, outs, scratch = refs[:3], refs[3:7], refs[7:-6], refs[-6:]
    pieces, cached = outs[:groups], outs[groups:]
    ck_buf, cv_buf, ke_buf, ve_buf, cache_sems, new_sems = scratch
    group, shard = lax.axis_index("seq") // gather, lax.axis_index("head")

    loads = [
        pltpu.make_async_copy(src, dst, cache_sems.at[i])
        for i, (src, dst) in enumerate(zip(cache_refs, (ck_buf, cv_buf, ke_buf, ve_buf)))
    ]
    rows, width = pieces[0].shape[0] // 3, pieces[0].shape[1]
    copies = []
    for t in range(groups):
        cols = columns(partner(group, t, groups), width)
        for i, src in enumerate(new_refs):
            dst = pieces[t].at[pl.ds(i * rows, rows)]
            copies.append(pltpu.make_async_copy(src.at[:, cols], dst, new_sems.at[t, i]))
    for copy in loads + copies:
        copy.start()
    for copy in loads:
        copy.wait()

    blocks, heads = ke_buf.shape
    cache_rows = ck_buf.shape[0]
    exponent = jnp.concatenate(
        [
            jnp.broadcast_to(ref[i : i + 1], (SBLK, heads))
            for ref in (ke_buf, ve_buf)
            for i in range(blocks)
        ],
        axis=0,
    )
    power = jnp.left_shift(1, exponent + 16).astype(jnp.float32) * 2.0**-16
    power = power.astype(jnp.bfloat16)
    head = lax.broadcasted_iota(jnp.int32, (heads, width), 0)
    head -= lax.broadcasted_iota(jnp.int32, (heads, width), 1) // DH
    for t in range(groups):
        for s in range(shards):
            part = partner(shard, s, shards) * groups + partner(group, t, groups)
            spread = (head == part * (width // DH)).astype(jnp.float32).astype(jnp.bfloat16)
            factor = jnp.dot(power, spread, preferred_element_type=jnp.float32)
            for which, buf in enumerate((ck_buf, cv_buf)):
                mantissa = buf[:, columns(part, width)].astype(jnp.float32)
                scaled = mantissa * factor[which * cache_rows : (which + 1) * cache_rows]
                cached[s][t, which] = scaled.astype(jnp.bfloat16)
    for copy in copies:
        copy.wait()


def prepare(q, k, v, ck, cv, ke, ve, groups, gather, shards):
    rows, width = q.shape[0], q.shape[1] // groups
    operands = (k, v, q, ck, cv, ke, ve)
    outs = pl.pallas_call(
        functools.partial(prepare_kernel, groups, gather, shards),
        out_shape=[jax.ShapeDtypeStruct((3 * rows, width), jnp.bfloat16)] * groups
        + [jax.ShapeDtypeStruct((groups, 2, ck.shape[0], width), jnp.bfloat16)] * shards,
        in_specs=[pl.BlockSpec(memory_space=pltpu.HBM)] * len(operands),
        out_specs=vmem(groups + shards),
        scratch_shapes=[pltpu.VMEM(x.shape, x.dtype) for x in (ck, cv, ke, ve)]
        + [pltpu.SemaphoreType.DMA((4,)), pltpu.SemaphoreType.DMA((groups, 3))],
        compiler_params=pltpu.CompilerParams(vmem_limit_bytes=SMALL),
        cost_estimate=pl.CostEstimate(
            flops=4 * ck.size, bytes_accessed=12 * q.size + 8 * ck.size, transcendentals=0
        ),
        name="prepare",
    )(*[pltpu.with_memory_space_constraint(x, pltpu.HBM) for x in operands])
    return list(outs[:groups]), list(outs[groups:])


def interleave_kernel(*refs):
    rows = refs[0].shape[1]
    for which in range(2):
        for s, ref in enumerate(refs[:-1]):
            refs[-1][pl.ds((which * len(refs[:-1]) + s) * rows, rows)] = ref[which]


def interleave(pieces):
    _, rows, width = pieces[0].shape
    count = len(pieces)
    if rows % 16:
        return jnp.stack(pieces, axis=1).reshape(-1, width)
    return pl.pallas_call(
        interleave_kernel,
        out_shape=jax.ShapeDtypeStruct((2 * count * rows, width), jnp.bfloat16),
        in_specs=vmem(count),
        out_specs=vmem(1)[0],
        compiler_params=pltpu.CompilerParams(vmem_limit_bytes=SMALL),
        cost_estimate=pl.CostEstimate(
            flops=0, bytes_accessed=8 * count * rows * width, transcendentals=0
        ),
        name="interleave",
    )(*pieces)


def join_kernel(rows, *refs):
    for i, ref in enumerate(refs[:-1]):
        refs[-1][i] = ref[pl.ds(0, rows)]


def join(pieces, rows):
    shape = (len(pieces), rows, pieces[0].shape[1])
    return pl.pallas_call(
        functools.partial(join_kernel, rows),
        out_shape=jax.ShapeDtypeStruct(shape, jnp.bfloat16),
        in_specs=vmem(len(pieces)),
        out_specs=vmem(1)[0],
        compiler_params=pltpu.CompilerParams(vmem_limit_bytes=SMALL),
        cost_estimate=pl.CostEstimate(
            flops=0, bytes_accessed=4 * math.prod(shape), transcendentals=0
        ),
        name="join",
    )(*pieces)


def rows_of(refs, start, count, cols):
    parts = []
    for ref in refs:
        if len(ref.shape) == 2:
            parts.append(ref[start : start + count, cols])
        else:
            parts.append(ref[:, start : start + count, cols].reshape(-1, cols.stop - cols.start))
    return parts[0] if len(parts) == 1 else jnp.concatenate(parts, axis=0)


def attend_sets(queries, sets):
    scale = math.log2(math.e) / math.sqrt(DH)
    scores = []
    for keys, _, bias in sets:
        x = lax.dot_general(
            queries, keys, (((1,), (1,)), ((), ())), preferred_element_type=jnp.float32
        )
        scores.append(x * scale if bias is None else x * scale + bias)
    peak = functools.reduce(
        jnp.maximum, [jnp.max(x, axis=1, keepdims=True) for x in scores]
    )
    total, product = 0.0, 0.0
    for x, (_, values, _) in zip(scores, sets):
        raised = jnp.exp2(x - peak)
        total += jnp.sum(raised, axis=1, keepdims=True)
        product += jnp.dot(
            raised.astype(jnp.bfloat16), values, preferred_element_type=jnp.float32
        )
    return peak, total, product


def bias_rows(bias_ref, pieces, blocks):
    width = bias_ref.shape[1]
    return jnp.concatenate(
        [
            jnp.broadcast_to(bias_ref[row : row + 1], (QBLK, width))
            for t in pieces
            for row in range(t * blocks, (t + 1) * blocks)
        ],
        axis=0,
    )


def attend_kernel(pieces, counts, q_start, rows, merge, final, *refs):
    q_refs, refs = refs[: len(pieces)], refs[len(pieces) :]
    sets = []
    for count, masked in counts:
        bias = bias_rows(refs[count], pieces, rows // QBLK) if masked else None
        sets.append((refs[:count], refs[0].shape[-2] // 2 if masked else rows, bias))
        refs = refs[count + masked :]
    state, refs = (refs[:3], refs[3:]) if merge else (None, refs)
    width = q_refs[0].shape[1]
    for at in range(0, width, DH):
        cols = slice(at, at + DH)
        queries = rows_of(q_refs, q_start, rows, cols)
        peak, total, product = attend_sets(
            queries,
            [
                (rows_of(k_refs, 0, half, cols), rows_of(k_refs, half, half, cols), bias)
                for k_refs, half, bias in sets
            ],
        )
        if merge:
            peak_1, total_1, product_1 = [ref[:, cols] for ref in state]
            top = jnp.maximum(peak, peak_1)
            share, share_1 = jnp.exp2(peak - top), jnp.exp2(peak_1 - top)
            total = total * share + total_1 * share_1
            product = product * share + product_1 * share_1
            peak = top
        if final:
            result = (product / total).astype(jnp.bfloat16)
            for i in range(len(pieces)):
                refs[i][:, cols] = result[i * rows : (i + 1) * rows]
        else:
            for ref, x in zip(refs, (peak, total, product)):
                ref[:, cols] = jnp.broadcast_to(x, product.shape)


def attend(q, pieces, sets, state=(), final=False):
    groups = len(pieces)
    rows, width = q[0].shape[0] // 3, q[0].shape[1]
    count = 0
    for arrays, bias in sets:
        for x in arrays:
            stacked = x.shape[0] if x.ndim == 3 else 1
            count += stacked * (rows if bias is None else x.shape[-2] // 2)
    if final:
        out_shape = [jax.ShapeDtypeStruct((rows, width), jnp.bfloat16)] * groups
    else:
        out_shape = [jax.ShapeDtypeStruct((groups * rows, width), jnp.float32)] * 3
    operands = [q[t] for t in pieces]
    for arrays, bias in sets:
        operands += [*arrays] if bias is None else [*arrays, bias]
    operands += state
    return pl.pallas_call(
        functools.partial(
            attend_kernel,
            tuple(pieces),
            tuple((len(arrays), bias is not None) for arrays, bias in sets),
            2 * rows,
            rows,
            bool(state),
            final,
        ),
        out_shape=out_shape,
        in_specs=vmem(len(operands)),
        out_specs=vmem(len(out_shape)),
        compiler_params=pltpu.CompilerParams(vmem_limit_bytes=LARGE),
        cost_estimate=pl.CostEstimate(
            flops=4 * groups * rows * count * width,
            bytes_accessed=4 * count * width,
            transcendentals=groups * rows * count * width // DH,
        ),
        name="attend",
    )(*operands)


def unpack_kernel(steps, gather, width, *refs):
    groups = len(steps)
    parts, out_ref, sems = refs[:groups], refs[groups], refs[groups + 1]
    me = lax.axis_index("seq") // gather
    copies = [
        pltpu.make_async_copy(
            parts[i], out_ref.at[:, columns(partner(me, t, groups), width)], sems.at[i]
        )
        for i, t in enumerate(steps)
    ]
    for copy in copies:
        copy.start()
    for copy in copies:
        copy.wait()


def unpack(parts, steps, gather):
    rows, width = parts[0].shape
    groups = len(steps)
    return pl.pallas_call(
        functools.partial(unpack_kernel, tuple(steps), gather, width),
        out_shape=jax.ShapeDtypeStruct((rows, groups * width), jnp.bfloat16),
        in_specs=vmem(groups),
        out_specs=pl.BlockSpec(memory_space=pl.ANY),
        scratch_shapes=[pltpu.SemaphoreType.DMA((groups,))],
        compiler_params=pltpu.CompilerParams(vmem_limit_bytes=SMALL),
        cost_estimate=pl.CostEstimate(
            flops=0, bytes_accessed=4 * groups * rows * width, transcendentals=0
        ),
        name="unpack_heads",
    )(*parts)


def per_device(
    seq_count,
    head_count,
    query_new,
    key_new,
    value_new,
    cache_keys,
    cache_values,
    key_exponent,
    value_exponent,
    block_mask,
):
    tok_rows, width_dev = query_new.shape
    groups = math.gcd(width_dev // DH, seq_count)
    gather = seq_count // groups
    width = width_dev // groups
    cache_rows = cache_keys.shape[0]
    seq_index = lax.axis_index("seq")
    head_index = lax.axis_index("head")
    group, member = seq_index // gather, seq_index % gather

    def to_group(x, t):
        if t == 0:
            return x
        pairs = [
            (s, partner(s // gather, t, groups) * gather + s % gather) for s in range(seq_count)
        ]
        return lax.ppermute(x, "seq", pairs)

    def from_group(x, t):
        if t == 0:
            return x
        pairs = [
            (s, origin(s // gather, t, groups) * gather + s % gather) for s in range(seq_count)
        ]
        return lax.ppermute(x, "seq", pairs)

    def to_member(x, t):
        pairs = [
            (s, s // gather * gather + partner(s % gather, t, gather)) for s in range(seq_count)
        ]
        return lax.ppermute(x, "seq", pairs)

    def to_head(x, t):
        if t == 0:
            return x
        return lax.ppermute(x, "head", [(h, partner(h, t, head_count)) for h in range(head_count)])

    members = range(1, gather)
    every = range(groups)
    steps = [*every[-1:], *every[1:-1], *every[:1]] if groups > 1 else [0]
    kv_own, stored = prepare(
        query_new,
        key_new,
        value_new,
        cache_keys,
        cache_values,
        key_exponent,
        value_exponent,
        groups,
        gather,
        head_count,
    )
    kv_other = [to_member(kv_own[0][: 2 * tok_rows], s) for s in members]
    if gather > 1:
        kv_own[1:-1], stored, kv_other[0] = lax.optimization_barrier(
            (kv_own[1:-1], stored, kv_other[0])
        )
    kv = [to_group(kv_own[t], t) for t in range(groups)]
    by_head = []
    for s in range(head_count):
        x = stored[s]
        if s > 2:
            x, by_head[s - 2] = lax.optimization_barrier((x, by_head[s - 2]))
        by_head.append(to_head(x, s))
    kv[1:] = [lax.optimization_barrier((x, by_head))[0] for x in kv[1:]]
    block_mask, group, member, head_index, _ = lax.optimization_barrier(
        (block_mask, group, member, head_index, kv[1:])
    )
    cache = [to_group(interleave([x[t] for x in by_head]), t) for t in steps]
    if groups > 1:
        swap = join(kv[1:], 2 * tok_rows)
        kv_other += [to_member(swap, s) for s in members]

    q_source = jnp.stack([origin(group, t, groups) * gather + member for t in range(groups)])
    blocks = tok_rows // QBLK
    q_block = (q_source[:, None] * blocks + jnp.arange(blocks)[None, :]).reshape(-1)
    q_pick = (q_block[:, None] == jnp.arange(block_mask.shape[0])[None, :]).astype(jnp.float32)
    row_mask = jnp.dot(q_pick, block_mask.astype(jnp.float32))

    def bias_of(swaps):
        device = jnp.stack(
            [
                (origin(group, t, groups) * gather + origin(member, s, gather)) * head_count
                + origin(head_index, z, head_count)
                for s in swaps
                for t in steps
                for z in range(head_count)
            ]
        )
        block = (device[:, None] * cache_rows + jnp.arange(cache_rows)[None, :]).reshape(-1)
        pick = jnp.arange(block_mask.shape[1])[:, None] == (block // CBLK)[None, :]
        seen = jnp.dot(row_mask, pick.astype(jnp.float32))
        return jnp.where(seen > 0.5, 0.0, MASKED).astype(jnp.float32)

    bias = [bias_of([0])] + ([bias_of(members)] if gather > 1 else [])
    away, home = every[1:], [*every[1:], 0]
    if groups > 1:
        state = attend(kv, away, [(kv, None)])
        cache, state, bias = lax.optimization_barrier((cache, state, bias))
    sets, last = [(cache, bias[0])], []
    if gather > 1:
        swap = join(cache, cache[0].shape[0])
        sets.append((kv_other, None))
        last = [([to_member(swap, s) for s in members], bias[1])]
    parts = {}
    if groups > 1:
        state = attend(kv, away, sets, state, not last)
        if last:
            state = attend(kv, away, last, state, True)
        parts.update(zip(away, state))
    parts[0] = attend(kv, [0], [(kv, None), *sets, *last], (), True)[0]
    return unpack([from_group(parts[t], t) for t in home], home, gather)


def solution(mesh):
    return jax.shard_map(
        functools.partial(per_device, mesh.shape["seq"], mesh.shape["head"]),
        mesh=mesh,
        in_specs=(
            P("seq", "head"),
            P("seq", "head"),
            P("seq", "head"),
            P(("seq", "head"), None),
            P(("seq", "head"), None),
            P(("seq", "head"), None),
            P(("seq", "head"), None),
            P(),
        ),
        out_specs=P("seq", "head"),
        check_vma=False,
    )
```

```python
import functools
import math

import jax
import jax.numpy as jnp
from jax import lax
from jax.experimental import pallas as pl
from jax.experimental.pallas import tpu as pltpu
from jax.sharding import PartitionSpec as P

DH = 128
QBLK = 64
CBLK = 32
SBLK = 4
MASKED = -1e30
SMALL = 8 * 2**20
LARGE = 16 * 2**20


def partner(index, step, count):
    if count & (count - 1) == 0:
        return index ^ step
    return (index + step) % count


def origin(index, step, count):
    if count & (count - 1) == 0:
        return index ^ step
    return (index + count - step) % count


def columns(chunk, width):
    return pl.ds(pl.multiple_of(chunk * width, DH), width)


def vmem(count):
    return [pl.BlockSpec(memory_space=pltpu.VMEM)] * count


def prepare_kernel(groups, gather, shards, *refs):
    new_refs, cache_refs, outs, scratch = refs[:3], refs[3:7], refs[7:-6], refs[-6:]
    pieces, cached = outs[:groups], outs[groups:]
    ck_buf, cv_buf, ke_buf, ve_buf, cache_sems, new_sems = scratch
    group, shard = lax.axis_index("seq") // gather, lax.axis_index("head")

    loads = [
        pltpu.make_async_copy(src, dst, cache_sems.at[i])
        for i, (src, dst) in enumerate(zip(cache_refs, (ck_buf, cv_buf, ke_buf, ve_buf)))
    ]
    rows, width = pieces[0].shape[0] // 3, pieces[0].shape[1]
    copies = []
    for t in range(groups):
        cols = columns(partner(group, t, groups), width)
        for i, src in enumerate(new_refs):
            for j in range(2):
                part = pl.ds(j * (rows // 2), rows // 2)
                dst = pieces[t].at[pl.ds(i * rows + j * (rows // 2), rows // 2)]
                copies.append(
                    pltpu.make_async_copy(src.at[part, cols], dst, new_sems.at[t, i, j])
                )
    for copy in loads + copies:
        copy.start()
    for copy in loads:
        copy.wait()

    blocks, heads = ke_buf.shape
    cache_rows = ck_buf.shape[0]
    exponent = jnp.concatenate(
        [
            jnp.broadcast_to(ref[i : i + 1], (SBLK, heads))
            for ref in (ke_buf, ve_buf)
            for i in range(blocks)
        ],
        axis=0,
    )
    power = jnp.left_shift(1, exponent + 16).astype(jnp.float32) * 2.0**-16
    power = power.astype(jnp.bfloat16)
    head = lax.broadcasted_iota(jnp.int32, (heads, width), 0)
    head -= lax.broadcasted_iota(jnp.int32, (heads, width), 1) // DH
    for t in range(groups):
        for s in range(shards):
            part = partner(shard, s, shards) * groups + partner(group, t, groups)
            spread = (head == part * (width // DH)).astype(jnp.float32).astype(jnp.bfloat16)
            factor = jnp.dot(power, spread, preferred_element_type=jnp.float32)
            for which, buf in enumerate((ck_buf, cv_buf)):
                mantissa = buf[:, columns(part, width)].astype(jnp.float32)
                scaled = mantissa * factor[which * cache_rows : (which + 1) * cache_rows]
                cached[s][t, which] = scaled.astype(jnp.bfloat16)
    for copy in copies:
        copy.wait()


def prepare(q, k, v, ck, cv, ke, ve, groups, gather, shards):
    rows, width = q.shape[0], q.shape[1] // groups
    operands = (k, v, q, ck, cv, ke, ve)
    outs = pl.pallas_call(
        functools.partial(prepare_kernel, groups, gather, shards),
        out_shape=[jax.ShapeDtypeStruct((3 * rows, width), jnp.bfloat16)] * groups
        + [jax.ShapeDtypeStruct((groups, 2, ck.shape[0], width), jnp.bfloat16)] * shards,
        in_specs=[pl.BlockSpec(memory_space=pltpu.HBM)] * len(operands),
        out_specs=vmem(groups + shards),
        scratch_shapes=[pltpu.VMEM(x.shape, x.dtype) for x in (ck, cv, ke, ve)]
        + [pltpu.SemaphoreType.DMA((4,)), pltpu.SemaphoreType.DMA((groups, 3, 2))],
        compiler_params=pltpu.CompilerParams(vmem_limit_bytes=SMALL),
        cost_estimate=pl.CostEstimate(
            flops=4 * ck.size, bytes_accessed=12 * q.size + 8 * ck.size, transcendentals=0
        ),
        name="prepare",
    )(*[pltpu.with_memory_space_constraint(x, pltpu.HBM) for x in operands])
    return list(outs[:groups]), list(outs[groups:])


def interleave_kernel(*refs):
    rows = refs[0].shape[1]
    for which in range(2):
        for s, ref in enumerate(refs[:-1]):
            refs[-1][pl.ds((which * len(refs[:-1]) + s) * rows, rows)] = ref[which]


def interleave(pieces):
    _, rows, width = pieces[0].shape
    count = len(pieces)
    if rows % 16:
        return jnp.stack(pieces, axis=1).reshape(-1, width)
    return pl.pallas_call(
        interleave_kernel,
        out_shape=jax.ShapeDtypeStruct((2 * count * rows, width), jnp.bfloat16),
        in_specs=vmem(count),
        out_specs=vmem(1)[0],
        compiler_params=pltpu.CompilerParams(vmem_limit_bytes=SMALL),
        cost_estimate=pl.CostEstimate(
            flops=0, bytes_accessed=8 * count * rows * width, transcendentals=0
        ),
        name="interleave",
    )(*pieces)


def join_kernel(rows, *refs):
    for i, ref in enumerate(refs[:-1]):
        refs[-1][i] = ref[pl.ds(0, rows)]


def join(pieces, rows):
    shape = (len(pieces), rows, pieces[0].shape[1])
    return pl.pallas_call(
        functools.partial(join_kernel, rows),
        out_shape=jax.ShapeDtypeStruct(shape, jnp.bfloat16),
        in_specs=vmem(len(pieces)),
        out_specs=vmem(1)[0],
        compiler_params=pltpu.CompilerParams(vmem_limit_bytes=SMALL),
        cost_estimate=pl.CostEstimate(
            flops=0, bytes_accessed=4 * math.prod(shape), transcendentals=0
        ),
        name="join",
    )(*pieces)


def rows_of(refs, start, count, cols):
    parts = []
    for ref in refs:
        if len(ref.shape) == 2:
            parts.append(ref[start : start + count, cols])
        else:
            parts.append(ref[:, start : start + count, cols].reshape(-1, cols.stop - cols.start))
    return parts[0] if len(parts) == 1 else jnp.concatenate(parts, axis=0)


def scores_of(queries, sets, cols):
    scale = math.log2(math.e) / math.sqrt(DH)
    scores = []
    for refs, half, bias in sets:
        x = lax.dot_general(
            queries,
            rows_of(refs, 0, half, cols),
            (((1,), (1,)), ((), ())),
            preferred_element_type=jnp.float32,
        )
        scores.append(x * scale if bias is None else x * scale + bias)
    return scores


def weigh(scores):
    peak = functools.reduce(
        jnp.maximum, [jnp.max(x, axis=1, keepdims=True) for x in scores]
    )
    total, weights = 0.0, []
    for x in scores:
        raised = jnp.exp2(x - peak)
        total += jnp.sum(raised, axis=1, keepdims=True)
        weights.append(raised.astype(jnp.bfloat16))
    return peak, total, weights


def bias_rows(bias_ref, pieces, blocks):
    width = bias_ref.shape[1]
    return jnp.concatenate(
        [
            jnp.broadcast_to(bias_ref[row : row + 1], (QBLK, width))
            for t in pieces
            for row in range(t * blocks, (t + 1) * blocks)
        ],
        axis=0,
    )


def attend_kernel(pieces, counts, q_start, rows, merge, final, *refs):
    q_refs, refs = refs[: len(pieces)], refs[len(pieces) :]
    sets = []
    for count, masked in counts:
        bias = bias_rows(refs[count], pieces, rows // QBLK) if masked else None
        sets.append((refs[:count], refs[0].shape[-2] // 2 if masked else rows, bias))
        refs = refs[count + masked :]
    state, refs = (refs[:3], refs[3:]) if merge else (None, refs)
    width = q_refs[0].shape[1]
    heads = [slice(at, at + DH) for at in range(0, width, DH)]
    scores = [
        scores_of(rows_of(q_refs, q_start, rows, cols), sets, cols) for cols in heads
    ]
    weighed = [weigh(x) for x in scores]
    for cols, (peak, total, weights) in zip(heads, weighed):
        product = 0.0
        for x, (refs_of, half, _) in zip(weights, sets):
            product += jnp.dot(
                x, rows_of(refs_of, half, half, cols), preferred_element_type=jnp.float32
            )
        if merge:
            peak_1, total_1, product_1 = [ref[:, cols] for ref in state]
            top = jnp.maximum(peak, peak_1)
            share, share_1 = jnp.exp2(peak - top), jnp.exp2(peak_1 - top)
            total = total * share + total_1 * share_1
            product = product * share + product_1 * share_1
            peak = top
        if final:
            result = (product / total).astype(jnp.bfloat16)
            for i in range(len(pieces)):
                refs[i][:, cols] = result[i * rows : (i + 1) * rows]
        else:
            for ref, x in zip(refs, (peak, total, product)):
                ref[:, cols] = jnp.broadcast_to(x, product.shape)


def attend(q, pieces, sets, state=(), final=False):
    groups = len(pieces)
    rows, width = q[0].shape[0] // 3, q[0].shape[1]
    count = 0
    for arrays, bias in sets:
        for x in arrays:
            stacked = x.shape[0] if x.ndim == 3 else 1
            count += stacked * (rows if bias is None else x.shape[-2] // 2)
    if final:
        out_shape = [jax.ShapeDtypeStruct((rows, width), jnp.bfloat16)] * groups
    else:
        out_shape = [jax.ShapeDtypeStruct((groups * rows, width), jnp.float32)] * 3
    operands = [q[t] for t in pieces]
    for arrays, bias in sets:
        operands += [*arrays] if bias is None else [*arrays, bias]
    operands += state
    return pl.pallas_call(
        functools.partial(
            attend_kernel,
            tuple(pieces),
            tuple((len(arrays), bias is not None) for arrays, bias in sets),
            2 * rows,
            rows,
            bool(state),
            final,
        ),
        out_shape=out_shape,
        in_specs=vmem(len(operands)),
        out_specs=vmem(len(out_shape)),
        compiler_params=pltpu.CompilerParams(vmem_limit_bytes=LARGE),
        cost_estimate=pl.CostEstimate(
            flops=4 * groups * rows * count * width,
            bytes_accessed=4 * count * width,
            transcendentals=groups * rows * count * width // DH,
        ),
        name="attend",
    )(*operands)


def unpack_kernel(steps, gather, width, *refs):
    groups = len(steps)
    parts, out_ref, sems = refs[:groups], refs[groups], refs[groups + 1]
    me = lax.axis_index("seq") // gather
    copies = [
        pltpu.make_async_copy(
            parts[i], out_ref.at[:, columns(partner(me, t, groups), width)], sems.at[i]
        )
        for i, t in enumerate(steps)
    ]
    for copy in copies:
        copy.start()
    for copy in copies:
        copy.wait()


def unpack(parts, steps, gather):
    rows, width = parts[0].shape
    groups = len(steps)
    return pl.pallas_call(
        functools.partial(unpack_kernel, tuple(steps), gather, width),
        out_shape=jax.ShapeDtypeStruct((rows, groups * width), jnp.bfloat16),
        in_specs=vmem(groups),
        out_specs=pl.BlockSpec(memory_space=pl.ANY),
        scratch_shapes=[pltpu.SemaphoreType.DMA((groups,))],
        compiler_params=pltpu.CompilerParams(vmem_limit_bytes=SMALL),
        cost_estimate=pl.CostEstimate(
            flops=0, bytes_accessed=4 * groups * rows * width, transcendentals=0
        ),
        name="unpack_heads",
    )(*parts)


def per_device(
    seq_count,
    head_count,
    query_new,
    key_new,
    value_new,
    cache_keys,
    cache_values,
    key_exponent,
    value_exponent,
    block_mask,
):
    tok_rows, width_dev = query_new.shape
    groups = math.gcd(width_dev // DH, seq_count)
    gather = seq_count // groups
    width = width_dev // groups
    cache_rows = cache_keys.shape[0]
    seq_index = lax.axis_index("seq")
    head_index = lax.axis_index("head")
    group, member = seq_index // gather, seq_index % gather

    def to_group(x, t):
        if t == 0:
            return x
        pairs = [
            (s, partner(s // gather, t, groups) * gather + s % gather) for s in range(seq_count)
        ]
        return lax.ppermute(x, "seq", pairs)

    def from_group(x, t):
        if t == 0:
            return x
        pairs = [
            (s, origin(s // gather, t, groups) * gather + s % gather) for s in range(seq_count)
        ]
        return lax.ppermute(x, "seq", pairs)

    def to_member(x, t):
        pairs = [
            (s, s // gather * gather + partner(s % gather, t, gather)) for s in range(seq_count)
        ]
        return lax.ppermute(x, "seq", pairs)

    def to_head(x, t):
        if t == 0:
            return x
        return lax.ppermute(x, "head", [(h, partner(h, t, head_count)) for h in range(head_count)])

    members = range(1, gather)
    every = range(groups)
    steps = [*every[-1:], *every[1:-1], *every[:1]] if groups > 1 else [0]
    kv_own, stored = prepare(
        query_new,
        key_new,
        value_new,
        cache_keys,
        cache_values,
        key_exponent,
        value_exponent,
        groups,
        gather,
        head_count,
    )
    kv_other = [to_member(kv_own[0][: 2 * tok_rows], s) for s in members]
    if gather > 1:
        kv_own[1:-1], stored, kv_other[0] = lax.optimization_barrier(
            (kv_own[1:-1], stored, kv_other[0])
        )
    kv = [to_group(kv_own[t], t) for t in range(groups)]
    by_head = []
    for s in range(head_count):
        x = stored[s]
        if s > 2:
            x, by_head[s - 2] = lax.optimization_barrier((x, by_head[s - 2]))
        by_head.append(to_head(x, s))
    kv[1:] = [lax.optimization_barrier((x, by_head))[0] for x in kv[1:]]
    block_mask, group, member, head_index, _ = lax.optimization_barrier(
        (block_mask, group, member, head_index, kv[1:])
    )
    cache = [to_group(interleave([x[t] for x in by_head]), t) for t in steps]
    if groups > 1:
        swap = join(kv[1:], 2 * tok_rows)
        kv_other += [to_member(swap, s) for s in members]

    q_source = jnp.stack([origin(group, t, groups) * gather + member for t in range(groups)])
    blocks = tok_rows // QBLK
    q_block = (q_source[:, None] * blocks + jnp.arange(blocks)[None, :]).reshape(-1)
    q_pick = (q_block[:, None] == jnp.arange(block_mask.shape[0])[None, :]).astype(jnp.float32)
    row_mask = jnp.dot(q_pick, block_mask.astype(jnp.float32))

    def bias_of(swaps):
        device = jnp.stack(
            [
                (origin(group, t, groups) * gather + origin(member, s, gather)) * head_count
                + origin(head_index, z, head_count)
                for s in swaps
                for t in steps
                for z in range(head_count)
            ]
        )
        block = (device[:, None] * cache_rows + jnp.arange(cache_rows)[None, :]).reshape(-1)
        pick = jnp.arange(block_mask.shape[1])[:, None] == (block // CBLK)[None, :]
        seen = jnp.dot(row_mask, pick.astype(jnp.float32))
        return jnp.where(seen > 0.5, 0.0, MASKED).astype(jnp.float32)

    bias = [bias_of([0])] + ([bias_of(members)] if gather > 1 else [])
    away = steps[:-1]
    if groups > 1:
        state = attend(kv, away, [(kv, None)])
        cache, state, bias = lax.optimization_barrier((cache, state, bias))
    sets, last = [(cache, bias[0])], []
    if gather > 1:
        swap = join(cache, cache[0].shape[0])
        sets.append((kv_other, None))
        last = [([to_member(swap, s) for s in members], bias[1])]
    parts = {}
    if groups > 1:
        state = attend(kv, away, sets, state, not last)
        if last:
            state = attend(kv, away, last, state, True)
        parts.update(zip(away, state))
    parts[0] = attend(kv, [0], [(kv, None), *sets, *last], (), True)[0]
    return unpack([from_group(parts[t], t) for t in steps], steps, gather)


def solution(mesh):
    return jax.shard_map(
        functools.partial(per_device, mesh.shape["seq"], mesh.shape["head"]),
        mesh=mesh,
        in_specs=(
            P("seq", "head"),
            P("seq", "head"),
            P("seq", "head"),
            P(("seq", "head"), None),
            P(("seq", "head"), None),
            P(("seq", "head"), None),
            P(("seq", "head"), None),
            P(),
        ),
        out_specs=P("seq", "head"),
        check_vma=False,
    )
```

```python
import functools
import math

import jax
import jax.numpy as jnp
from jax import lax
from jax.experimental import pallas as pl
from jax.experimental.pallas import tpu as pltpu
from jax.sharding import PartitionSpec as P

DH = 128
QBLK = 64
CBLK = 32
SBLK = 4
MASKED = -1e30
SMALL = 8 * 2**20
LARGE = 16 * 2**20


def partner(index, step, count):
    if count & (count - 1) == 0:
        return index ^ step
    return (index + step) % count


def origin(index, step, count):
    if count & (count - 1) == 0:
        return index ^ step
    return (index + count - step) % count


def columns(chunk, width):
    return pl.ds(pl.multiple_of(chunk * width, DH), width)


def vmem(count):
    return [pl.BlockSpec(memory_space=pltpu.VMEM)] * count


def prepare_kernel(groups, gather, shards, *refs):
    new_refs, cache_refs, outs, scratch = refs[:3], refs[3:7], refs[7:-7], refs[-7:]
    pieces, cached = outs[:groups], outs[groups:]
    ck_buf, cv_buf, ke_buf, ve_buf, new_buf, cache_sems, new_sems = scratch
    group, shard = lax.axis_index("seq") // gather, lax.axis_index("head")

    loads = [
        pltpu.make_async_copy(src, dst, cache_sems.at[i])
        for i, (src, dst) in enumerate(zip(cache_refs, (ck_buf, cv_buf, ke_buf, ve_buf)))
    ]
    rows, width = pieces[0].shape[0] // 3, pieces[0].shape[1]
    copies = []
    for i, src in enumerate(new_refs):
        for j in range(2):
            part = pl.ds(j * (rows // 2), rows // 2)
            copies.append(
                pltpu.make_async_copy(src.at[part], new_buf.at[i, part], new_sems.at[i, j])
            )
    for copy in loads + copies:
        copy.start()
    for copy in loads:
        copy.wait()

    blocks, heads = ke_buf.shape
    cache_rows = ck_buf.shape[0]
    exponent = jnp.concatenate(
        [
            jnp.broadcast_to(ref[i : i + 1], (SBLK, heads))
            for ref in (ke_buf, ve_buf)
            for i in range(blocks)
        ],
        axis=0,
    )
    power = jnp.left_shift(1, exponent + 16).astype(jnp.float32) * 2.0**-16
    power = power.astype(jnp.bfloat16)
    head = lax.broadcasted_iota(jnp.int32, (heads, width), 0)
    head -= lax.broadcasted_iota(jnp.int32, (heads, width), 1) // DH
    for t in range(groups):
        for s in range(shards):
            part = partner(shard, s, shards) * groups + partner(group, t, groups)
            spread = (head == part * (width // DH)).astype(jnp.float32).astype(jnp.bfloat16)
            factor = jnp.dot(power, spread, preferred_element_type=jnp.float32)
            for which, buf in enumerate((ck_buf, cv_buf)):
                mantissa = buf[:, columns(part, width)].astype(jnp.float32)
                scaled = mantissa * factor[which * cache_rows : (which + 1) * cache_rows]
                cached[s][t, which] = scaled.astype(jnp.bfloat16)
    for i in range(3):
        for copy in copies[2 * i : 2 * i + 2]:
            copy.wait()
        for t in range(groups):
            cols = columns(partner(group, t, groups), width)
            pieces[t][pl.ds(i * rows, rows)] = new_buf[i, :, cols]


def prepare(q, k, v, ck, cv, ke, ve, groups, gather, shards):
    rows, width = q.shape[0], q.shape[1] // groups
    operands = (k, v, q, ck, cv, ke, ve)
    outs = pl.pallas_call(
        functools.partial(prepare_kernel, groups, gather, shards),
        out_shape=[jax.ShapeDtypeStruct((3 * rows, width), jnp.bfloat16)] * groups
        + [jax.ShapeDtypeStruct((groups, 2, ck.shape[0], width), jnp.bfloat16)] * shards,
        in_specs=[pl.BlockSpec(memory_space=pltpu.HBM)] * len(operands),
        out_specs=vmem(groups + shards),
        scratch_shapes=[pltpu.VMEM(x.shape, x.dtype) for x in (ck, cv, ke, ve)]
        + [pltpu.VMEM((3, *q.shape), q.dtype)]
        + [pltpu.SemaphoreType.DMA((4,)), pltpu.SemaphoreType.DMA((3, 2))],
        compiler_params=pltpu.CompilerParams(vmem_limit_bytes=SMALL),
        cost_estimate=pl.CostEstimate(
            flops=4 * ck.size, bytes_accessed=12 * q.size + 8 * ck.size, transcendentals=0
        ),
        name="prepare",
    )(*[pltpu.with_memory_space_constraint(x, pltpu.HBM) for x in operands])
    return list(outs[:groups]), list(outs[groups:])


def interleave_kernel(*refs):
    rows = refs[0].shape[1]
    for which in range(2):
        for s, ref in enumerate(refs[:-1]):
            refs[-1][pl.ds((which * len(refs[:-1]) + s) * rows, rows)] = ref[which]


def interleave(pieces):
    _, rows, width = pieces[0].shape
    count = len(pieces)
    if rows % 16:
        return jnp.stack(pieces, axis=1).reshape(-1, width)
    return pl.pallas_call(
        interleave_kernel,
        out_shape=jax.ShapeDtypeStruct((2 * count * rows, width), jnp.bfloat16),
        in_specs=vmem(count),
        out_specs=vmem(1)[0],
        compiler_params=pltpu.CompilerParams(vmem_limit_bytes=SMALL),
        cost_estimate=pl.CostEstimate(
            flops=0, bytes_accessed=8 * count * rows * width, transcendentals=0
        ),
        name="interleave",
    )(*pieces)


def join_kernel(rows, *refs):
    for i, ref in enumerate(refs[:-1]):
        refs[-1][i] = ref[pl.ds(0, rows)]


def join(pieces, rows):
    shape = (len(pieces), rows, pieces[0].shape[1])
    return pl.pallas_call(
        functools.partial(join_kernel, rows),
        out_shape=jax.ShapeDtypeStruct(shape, jnp.bfloat16),
        in_specs=vmem(len(pieces)),
        out_specs=vmem(1)[0],
        compiler_params=pltpu.CompilerParams(vmem_limit_bytes=SMALL),
        cost_estimate=pl.CostEstimate(
            flops=0, bytes_accessed=4 * math.prod(shape), transcendentals=0
        ),
        name="join",
    )(*pieces)


def rows_of(refs, start, count, cols):
    parts = []
    for ref in refs:
        if len(ref.shape) == 2:
            parts.append(ref[start : start + count, cols])
        else:
            parts.append(ref[:, start : start + count, cols].reshape(-1, cols.stop - cols.start))
    return parts[0] if len(parts) == 1 else jnp.concatenate(parts, axis=0)


def attend_sets(queries, sets):
    scale = math.log2(math.e) / math.sqrt(DH)
    scores = []
    for keys, _, bias in sets:
        x = lax.dot_general(
            queries, keys, (((1,), (1,)), ((), ())), preferred_element_type=jnp.float32
        )
        scores.append(x * scale if bias is None else x * scale + bias)
    peak = functools.reduce(
        jnp.maximum, [jnp.max(x, axis=1, keepdims=True) for x in scores]
    )
    total, product = 0.0, 0.0
    for x, (_, values, _) in zip(scores, sets):
        raised = jnp.exp2(x - peak)
        total += jnp.sum(raised, axis=1, keepdims=True)
        product += jnp.dot(
            raised.astype(jnp.bfloat16), values, preferred_element_type=jnp.float32
        )
    return peak, total, product


def bias_rows(bias_ref, pieces, blocks):
    width = bias_ref.shape[1]
    return jnp.concatenate(
        [
            jnp.broadcast_to(bias_ref[row : row + 1], (QBLK, width))
            for t in pieces
            for row in range(t * blocks, (t + 1) * blocks)
        ],
        axis=0,
    )


def attend_kernel(pieces, counts, q_start, rows, merge, final, *refs):
    q_refs, refs = refs[: len(pieces)], refs[len(pieces) :]
    sets = []
    for count, masked in counts:
        bias = bias_rows(refs[count], pieces, rows // QBLK) if masked else None
        sets.append((refs[:count], refs[0].shape[-2] // 2 if masked else rows, bias))
        refs = refs[count + masked :]
    state, refs = (refs[:3], refs[3:]) if merge else (None, refs)
    width = q_refs[0].shape[1]
    for at in range(0, width, DH):
        cols = slice(at, at + DH)
        queries = rows_of(q_refs, q_start, rows, cols)
        peak, total, product = attend_sets(
            queries,
            [
                (rows_of(k_refs, 0, half, cols), rows_of(k_refs, half, half, cols), bias)
                for k_refs, half, bias in sets
            ],
        )
        if merge:
            peak_1, total_1, product_1 = [ref[:, cols] for ref in state]
            top = jnp.maximum(peak, peak_1)
            share, share_1 = jnp.exp2(peak - top), jnp.exp2(peak_1 - top)
            total = total * share + total_1 * share_1
            product = product * share + product_1 * share_1
            peak = top
        if final:
            result = (product / total).astype(jnp.bfloat16)
            for i in range(len(pieces)):
                refs[i][:, cols] = result[i * rows : (i + 1) * rows]
        else:
            for ref, x in zip(refs, (peak, total, product)):
                ref[:, cols] = jnp.broadcast_to(x, product.shape)


def attend(q, pieces, sets, state=(), final=False):
    groups = len(pieces)
    rows, width = q[0].shape[0] // 3, q[0].shape[1]
    count = 0
    for arrays, bias in sets:
        for x in arrays:
            stacked = x.shape[0] if x.ndim == 3 else 1
            count += stacked * (rows if bias is None else x.shape[-2] // 2)
    if final:
        out_shape = [jax.ShapeDtypeStruct((rows, width), jnp.bfloat16)] * groups
    else:
        out_shape = [jax.ShapeDtypeStruct((groups * rows, width), jnp.float32)] * 3
    operands = [q[t] for t in pieces]
    for arrays, bias in sets:
        operands += [*arrays] if bias is None else [*arrays, bias]
    operands += state
    return pl.pallas_call(
        functools.partial(
            attend_kernel,
            tuple(pieces),
            tuple((len(arrays), bias is not None) for arrays, bias in sets),
            2 * rows,
            rows,
            bool(state),
            final,
        ),
        out_shape=out_shape,
        in_specs=vmem(len(operands)),
        out_specs=vmem(len(out_shape)),
        compiler_params=pltpu.CompilerParams(vmem_limit_bytes=LARGE),
        cost_estimate=pl.CostEstimate(
            flops=4 * groups * rows * count * width,
            bytes_accessed=4 * count * width,
            transcendentals=groups * rows * count * width // DH,
        ),
        name="attend",
    )(*operands)


def unpack_kernel(steps, gather, width, *refs):
    groups = len(steps)
    parts, out_ref, sems = refs[:groups], refs[groups], refs[groups + 1]
    me = lax.axis_index("seq") // gather
    copies = [
        pltpu.make_async_copy(
            parts[i], out_ref.at[:, columns(partner(me, t, groups), width)], sems.at[i]
        )
        for i, t in enumerate(steps)
    ]
    for copy in copies:
        copy.start()
    for copy in copies:
        copy.wait()


def unpack(parts, steps, gather):
    rows, width = parts[0].shape
    groups = len(steps)
    return pl.pallas_call(
        functools.partial(unpack_kernel, tuple(steps), gather, width),
        out_shape=jax.ShapeDtypeStruct((rows, groups * width), jnp.bfloat16),
        in_specs=vmem(groups),
        out_specs=pl.BlockSpec(memory_space=pl.ANY),
        scratch_shapes=[pltpu.SemaphoreType.DMA((groups,))],
        compiler_params=pltpu.CompilerParams(vmem_limit_bytes=SMALL),
        cost_estimate=pl.CostEstimate(
            flops=0, bytes_accessed=4 * groups * rows * width, transcendentals=0
        ),
        name="unpack_heads",
    )(*parts)


def per_device(
    seq_count,
    head_count,
    query_new,
    key_new,
    value_new,
    cache_keys,
    cache_values,
    key_exponent,
    value_exponent,
    block_mask,
):
    tok_rows, width_dev = query_new.shape
    groups = math.gcd(width_dev // DH, seq_count)
    gather = seq_count // groups
    width = width_dev // groups
    cache_rows = cache_keys.shape[0]
    seq_index = lax.axis_index("seq")
    head_index = lax.axis_index("head")
    group, member = seq_index // gather, seq_index % gather

    def to_group(x, t):
        if t == 0:
            return x
        pairs = [
            (s, partner(s // gather, t, groups) * gather + s % gather) for s in range(seq_count)
        ]
        return lax.ppermute(x, "seq", pairs)

    def from_group(x, t):
        if t == 0:
            return x
        pairs = [
            (s, origin(s // gather, t, groups) * gather + s % gather) for s in range(seq_count)
        ]
        return lax.ppermute(x, "seq", pairs)

    def to_member(x, t):
        pairs = [
            (s, s // gather * gather + partner(s % gather, t, gather)) for s in range(seq_count)
        ]
        return lax.ppermute(x, "seq", pairs)

    def to_head(x, t):
        if t == 0:
            return x
        return lax.ppermute(x, "head", [(h, partner(h, t, head_count)) for h in range(head_count)])

    members = range(1, gather)
    every = range(groups)
    steps = [*every[-1:], *every[1:-1], *every[:1]] if groups > 1 else [0]
    kv_own, stored = prepare(
        query_new,
        key_new,
        value_new,
        cache_keys,
        cache_values,
        key_exponent,
        value_exponent,
        groups,
        gather,
        head_count,
    )
    kv_other = [to_member(kv_own[0][: 2 * tok_rows], s) for s in members]
    if gather > 1:
        kv_own[1:-1], stored, kv_other[0] = lax.optimization_barrier(
            (kv_own[1:-1], stored, kv_other[0])
        )
    kv = [to_group(kv_own[t], t) for t in range(groups)]
    by_head = []
    for s in range(head_count):
        x = stored[s]
        if s > 2:
            x, by_head[s - 2] = lax.optimization_barrier((x, by_head[s - 2]))
        by_head.append(to_head(x, s))
    kv[1:] = [lax.optimization_barrier((x, by_head))[0] for x in kv[1:]]
    block_mask, group, member, head_index, _ = lax.optimization_barrier(
        (block_mask, group, member, head_index, kv[1:])
    )
    cache = [to_group(interleave([x[t] for x in by_head]), t) for t in steps]
    if groups > 1:
        swap = join(kv[1:], 2 * tok_rows)
        kv_other += [to_member(swap, s) for s in members]

    q_source = jnp.stack([origin(group, t, groups) * gather + member for t in range(groups)])
    blocks = tok_rows // QBLK
    q_block = (q_source[:, None] * blocks + jnp.arange(blocks)[None, :]).reshape(-1)
    q_pick = (q_block[:, None] == jnp.arange(block_mask.shape[0])[None, :]).astype(jnp.float32)
    row_mask = jnp.dot(q_pick, block_mask.astype(jnp.float32))

    def bias_of(swaps):
        device = jnp.stack(
            [
                (origin(group, t, groups) * gather + origin(member, s, gather)) * head_count
                + origin(head_index, z, head_count)
                for s in swaps
                for t in steps
                for z in range(head_count)
            ]
        )
        block = (device[:, None] * cache_rows + jnp.arange(cache_rows)[None, :]).reshape(-1)
        pick = jnp.arange(block_mask.shape[1])[:, None] == (block // CBLK)[None, :]
        seen = jnp.dot(row_mask, pick.astype(jnp.float32))
        return jnp.where(seen > 0.5, 0.0, MASKED).astype(jnp.float32)

    bias = [bias_of([0])] + ([bias_of(members)] if gather > 1 else [])
    away = steps[:-1]
    if groups > 1:
        state = attend(kv, away, [(kv, None)])
        cache, state, bias = lax.optimization_barrier((cache, state, bias))
    sets, last = [(cache, bias[0])], []
    if gather > 1:
        swap = join(cache, cache[0].shape[0])
        sets.append((kv_other, None))
        last = [([to_member(swap, s) for s in members], bias[1])]
    parts = {}
    if groups > 1:
        state = attend(kv, away, sets, state, not last)
        if last:
            state = attend(kv, away, last, state, True)
        parts.update(zip(away, state))
    parts[0] = attend(kv, [0], [(kv, None), *sets, *last], (), True)[0]
    return unpack([from_group(parts[t], t) for t in steps], steps, gather)


def solution(mesh):
    return jax.shard_map(
        functools.partial(per_device, mesh.shape["seq"], mesh.shape["head"]),
        mesh=mesh,
        in_specs=(
            P("seq", "head"),
            P("seq", "head"),
            P("seq", "head"),
            P(("seq", "head"), None),
            P(("seq", "head"), None),
            P(("seq", "head"), None),
            P(("seq", "head"), None),
            P(),
        ),
        out_specs=P("seq", "head"),
        check_vma=False,
    )
```

```python
import functools
import math

import jax
import jax.numpy as jnp
from jax import lax
from jax.experimental import pallas as pl
from jax.experimental.pallas import tpu as pltpu
from jax.sharding import PartitionSpec as P

DH = 128
QBLK = 64
CBLK = 32
SBLK = 4
MASKED = -1e30
SMALL = 8 * 2**20
LARGE = 16 * 2**20


def partner(index, step, count):
    if count & (count - 1) == 0:
        return index ^ step
    return (index + step) % count


def origin(index, step, count):
    if count & (count - 1) == 0:
        return index ^ step
    return (index + count - step) % count


def columns(chunk, width):
    return pl.ds(pl.multiple_of(chunk * width, DH), width)


def vmem(count):
    return [pl.BlockSpec(memory_space=pltpu.VMEM)] * count


def prepare_kernel(groups, gather, shards, *refs):
    new_refs, cache_refs, outs, scratch = refs[:3], refs[3:7], refs[7:-7], refs[-7:]
    pieces, cached = outs[:groups], outs[groups:]
    ck_buf, cv_buf, ke_buf, ve_buf, new_buf, cache_sems, new_sems = scratch
    group, shard = lax.axis_index("seq") // gather, lax.axis_index("head")

    loads = [
        pltpu.make_async_copy(src, dst, cache_sems.at[i])
        for i, (src, dst) in enumerate(zip(cache_refs, (ck_buf, cv_buf, ke_buf, ve_buf)))
    ]
    rows, width = pieces[0].shape[0] // 3, pieces[0].shape[1]
    copies = []
    for i, src in enumerate(new_refs):
        for j in range(2):
            part = pl.ds(j * (rows // 2), rows // 2)
            copies.append(
                pltpu.make_async_copy(src.at[part], new_buf.at[i, part], new_sems.at[i, j])
            )
    for copy in loads + copies:
        copy.start()
    for copy in loads:
        copy.wait()

    blocks, heads = ke_buf.shape
    cache_rows = ck_buf.shape[0]
    exponent = jnp.concatenate(
        [
            jnp.broadcast_to(ref[i : i + 1], (SBLK, heads))
            for ref in (ke_buf, ve_buf)
            for i in range(blocks)
        ],
        axis=0,
    )
    power = jnp.left_shift(1, exponent + 16).astype(jnp.float32) * 2.0**-16
    power = power.astype(jnp.bfloat16)
    head = lax.broadcasted_iota(jnp.int32, (heads, width), 0)
    head -= lax.broadcasted_iota(jnp.int32, (heads, width), 1) // DH
    for t in range(groups):
        for s in range(shards):
            part = partner(shard, s, shards) * groups + partner(group, t, groups)
            spread = (head == part * (width // DH)).astype(jnp.float32).astype(jnp.bfloat16)
            factor = jnp.dot(power, spread, preferred_element_type=jnp.float32)
            for which, buf in enumerate((ck_buf, cv_buf)):
                mantissa = buf[:, columns(part, width)].astype(jnp.float32)
                scaled = mantissa * factor[which * cache_rows : (which + 1) * cache_rows]
                cached[s][t, which] = scaled.astype(jnp.bfloat16)
    for i in range(3):
        for copy in copies[2 * i : 2 * i + 2]:
            copy.wait()
        for t in range(groups):
            cols = columns(partner(group, t, groups), width)
            pieces[t][pl.ds(i * rows, rows)] = new_buf[i, :, cols]


def prepare(q, k, v, ck, cv, ke, ve, groups, gather, shards):
    rows, width = q.shape[0], q.shape[1] // groups
    operands = (k, v, q, ck, cv, ke, ve)
    outs = pl.pallas_call(
        functools.partial(prepare_kernel, groups, gather, shards),
        out_shape=[jax.ShapeDtypeStruct((3 * rows, width), jnp.bfloat16)] * groups
        + [jax.ShapeDtypeStruct((groups, 2, ck.shape[0], width), jnp.bfloat16)] * shards,
        in_specs=[pl.BlockSpec(memory_space=pltpu.HBM)] * len(operands),
        out_specs=vmem(groups + shards),
        scratch_shapes=[pltpu.VMEM(x.shape, x.dtype) for x in (ck, cv, ke, ve)]
        + [pltpu.VMEM((3, *q.shape), q.dtype)]
        + [pltpu.SemaphoreType.DMA((4,)), pltpu.SemaphoreType.DMA((3, 2))],
        compiler_params=pltpu.CompilerParams(vmem_limit_bytes=SMALL),
        cost_estimate=pl.CostEstimate(
            flops=4 * ck.size, bytes_accessed=12 * q.size + 8 * ck.size, transcendentals=0
        ),
        name="prepare",
    )(*[pltpu.with_memory_space_constraint(x, pltpu.HBM) for x in operands])
    return list(outs[:groups]), list(outs[groups:])


def interleave_kernel(*refs):
    rows = refs[0].shape[1]
    for which in range(2):
        for s, ref in enumerate(refs[:-1]):
            refs[-1][pl.ds((which * len(refs[:-1]) + s) * rows, rows)] = ref[which]


def interleave(pieces):
    _, rows, width = pieces[0].shape
    count = len(pieces)
    if rows % 16:
        return jnp.stack(pieces, axis=1).reshape(-1, width)
    return pl.pallas_call(
        interleave_kernel,
        out_shape=jax.ShapeDtypeStruct((2 * count * rows, width), jnp.bfloat16),
        in_specs=vmem(count),
        out_specs=vmem(1)[0],
        compiler_params=pltpu.CompilerParams(vmem_limit_bytes=SMALL),
        cost_estimate=pl.CostEstimate(
            flops=0, bytes_accessed=8 * count * rows * width, transcendentals=0
        ),
        name="interleave",
    )(*pieces)


def join_kernel(rows, *refs):
    for i, ref in enumerate(refs[:-1]):
        refs[-1][i] = ref[pl.ds(0, rows)]


def join(pieces, rows):
    shape = (len(pieces), rows, pieces[0].shape[1])
    return pl.pallas_call(
        functools.partial(join_kernel, rows),
        out_shape=jax.ShapeDtypeStruct(shape, jnp.bfloat16),
        in_specs=vmem(len(pieces)),
        out_specs=vmem(1)[0],
        compiler_params=pltpu.CompilerParams(vmem_limit_bytes=SMALL),
        cost_estimate=pl.CostEstimate(
            flops=0, bytes_accessed=4 * math.prod(shape), transcendentals=0
        ),
        name="join",
    )(*pieces)


def rows_of(refs, start, count, cols):
    parts = []
    for ref in refs:
        if len(ref.shape) == 2:
            parts.append(ref[start : start + count, cols])
        else:
            parts.append(ref[:, start : start + count, cols].reshape(-1, cols.stop - cols.start))
    return parts[0] if len(parts) == 1 else jnp.concatenate(parts, axis=0)


def scores_of(queries, sets, cols):
    scale = math.log2(math.e) / math.sqrt(DH)
    scores = []
    for refs, half, bias in sets:
        x = lax.dot_general(
            queries,
            rows_of(refs, 0, half, cols),
            (((1,), (1,)), ((), ())),
            preferred_element_type=jnp.float32,
        )
        scores.append(x * scale if bias is None else x * scale + bias)
    return scores


def weigh(scores):
    peak = functools.reduce(
        jnp.maximum, [jnp.max(x, axis=1, keepdims=True) for x in scores]
    )
    total, weights = 0.0, []
    for x in scores:
        raised = jnp.exp2(x - peak)
        total += jnp.sum(raised, axis=1, keepdims=True)
        weights.append(raised.astype(jnp.bfloat16))
    return peak, total, weights


def bias_rows(bias_ref, pieces, blocks):
    width = bias_ref.shape[1]
    return jnp.concatenate(
        [
            jnp.broadcast_to(bias_ref[row : row + 1], (QBLK, width))
            for t in pieces
            for row in range(t * blocks, (t + 1) * blocks)
        ],
        axis=0,
    )


def attend_kernel(pieces, counts, q_start, rows, merge, final, *refs):
    q_refs, refs = refs[: len(pieces)], refs[len(pieces) :]
    sets = []
    for count, masked in counts:
        bias = bias_rows(refs[count], pieces, rows // QBLK) if masked else None
        sets.append((refs[:count], refs[0].shape[-2] // 2 if masked else rows, bias))
        refs = refs[count + masked :]
    state, refs = (refs[:3], refs[3:]) if merge else (None, refs)
    width = q_refs[0].shape[1]
    heads = [slice(at, at + DH) for at in range(0, width, DH)]
    scores = [
        scores_of(rows_of(q_refs, q_start, rows, cols), sets, cols) for cols in heads
    ]
    weighed = [weigh(x) for x in scores]
    for cols, (peak, total, weights) in zip(heads, weighed):
        product = 0.0
        for x, (refs_of, half, _) in zip(weights, sets):
            product += jnp.dot(
                x, rows_of(refs_of, half, half, cols), preferred_element_type=jnp.float32
            )
        if merge:
            peak_1, total_1, product_1 = [ref[:, cols] for ref in state]
            top = jnp.maximum(peak, peak_1)
            share, share_1 = jnp.exp2(peak - top), jnp.exp2(peak_1 - top)
            total = total * share + total_1 * share_1
            product = product * share + product_1 * share_1
            peak = top
        if final:
            result = (product / total).astype(jnp.bfloat16)
            for i in range(len(pieces)):
                refs[i][:, cols] = result[i * rows : (i + 1) * rows]
        else:
            for ref, x in zip(refs, (peak, total, product)):
                ref[:, cols] = jnp.broadcast_to(x, product.shape)


def attend(q, pieces, sets, state=(), final=False):
    groups = len(pieces)
    rows, width = q[0].shape[0] // 3, q[0].shape[1]
    count = 0
    for arrays, bias in sets:
        for x in arrays:
            stacked = x.shape[0] if x.ndim == 3 else 1
            count += stacked * (rows if bias is None else x.shape[-2] // 2)
    if final:
        out_shape = [jax.ShapeDtypeStruct((rows, width), jnp.bfloat16)] * groups
    else:
        out_shape = [jax.ShapeDtypeStruct((groups * rows, width), jnp.float32)] * 3
    operands = [q[t] for t in pieces]
    for arrays, bias in sets:
        operands += [*arrays] if bias is None else [*arrays, bias]
    operands += state
    return pl.pallas_call(
        functools.partial(
            attend_kernel,
            tuple(pieces),
            tuple((len(arrays), bias is not None) for arrays, bias in sets),
            2 * rows,
            rows,
            bool(state),
            final,
        ),
        out_shape=out_shape,
        in_specs=vmem(len(operands)),
        out_specs=vmem(len(out_shape)),
        compiler_params=pltpu.CompilerParams(vmem_limit_bytes=LARGE),
        cost_estimate=pl.CostEstimate(
            flops=4 * groups * rows * count * width,
            bytes_accessed=4 * count * width,
            transcendentals=groups * rows * count * width // DH,
        ),
        name="attend",
    )(*operands)


def unpack_kernel(steps, gather, width, *refs):
    groups = len(steps)
    parts, out_ref, sems = refs[:groups], refs[groups], refs[groups + 1]
    me = lax.axis_index("seq") // gather
    copies = [
        pltpu.make_async_copy(
            parts[i], out_ref.at[:, columns(partner(me, t, groups), width)], sems.at[i]
        )
        for i, t in enumerate(steps)
    ]
    for copy in copies:
        copy.start()
    for copy in copies:
        copy.wait()


def unpack(parts, steps, gather):
    rows, width = parts[0].shape
    groups = len(steps)
    return pl.pallas_call(
        functools.partial(unpack_kernel, tuple(steps), gather, width),
        out_shape=jax.ShapeDtypeStruct((rows, groups * width), jnp.bfloat16),
        in_specs=vmem(groups),
        out_specs=pl.BlockSpec(memory_space=pl.ANY),
        scratch_shapes=[pltpu.SemaphoreType.DMA((groups,))],
        compiler_params=pltpu.CompilerParams(vmem_limit_bytes=SMALL),
        cost_estimate=pl.CostEstimate(
            flops=0, bytes_accessed=4 * groups * rows * width, transcendentals=0
        ),
        name="unpack_heads",
    )(*parts)


def per_device(
    seq_count,
    head_count,
    query_new,
    key_new,
    value_new,
    cache_keys,
    cache_values,
    key_exponent,
    value_exponent,
    block_mask,
):
    tok_rows, width_dev = query_new.shape
    groups = math.gcd(width_dev // DH, seq_count)
    gather = seq_count // groups
    width = width_dev // groups
    cache_rows = cache_keys.shape[0]
    seq_index = lax.axis_index("seq")
    head_index = lax.axis_index("head")
    group, member = seq_index // gather, seq_index % gather

    def to_group(x, t):
        if t == 0:
            return x
        pairs = [
            (s, partner(s // gather, t, groups) * gather + s % gather) for s in range(seq_count)
        ]
        return lax.ppermute(x, "seq", pairs)

    def from_group(x, t):
        if t == 0:
            return x
        pairs = [
            (s, origin(s // gather, t, groups) * gather + s % gather) for s in range(seq_count)
        ]
        return lax.ppermute(x, "seq", pairs)

    def to_member(x, t):
        pairs = [
            (s, s // gather * gather + partner(s % gather, t, gather)) for s in range(seq_count)
        ]
        return lax.ppermute(x, "seq", pairs)

    def to_head(x, t):
        if t == 0:
            return x
        return lax.ppermute(x, "head", [(h, partner(h, t, head_count)) for h in range(head_count)])

    members = range(1, gather)
    every = range(groups)
    steps = [*every[-1:], *every[1:-1], *every[:1]] if groups > 1 else [0]
    kv_own, stored = prepare(
        query_new,
        key_new,
        value_new,
        cache_keys,
        cache_values,
        key_exponent,
        value_exponent,
        groups,
        gather,
        head_count,
    )
    kv_other = [to_member(kv_own[0][: 2 * tok_rows], s) for s in members]
    if gather > 1:
        kv_own[1:-1], stored, kv_other[0] = lax.optimization_barrier(
            (kv_own[1:-1], stored, kv_other[0])
        )
    kv = [to_group(kv_own[t], t) for t in range(groups)]
    by_head = []
    for s in range(head_count):
        x = stored[s]
        if s > 2:
            x, by_head[s - 2] = lax.optimization_barrier((x, by_head[s - 2]))
        by_head.append(to_head(x, s))
    kv[1:] = [lax.optimization_barrier((x, by_head))[0] for x in kv[1:]]
    block_mask, group, member, head_index, _ = lax.optimization_barrier(
        (block_mask, group, member, head_index, kv[1:])
    )
    cache = [to_group(interleave([x[t] for x in by_head]), t) for t in steps]
    if groups > 1:
        swap = join(kv[1:], 2 * tok_rows)
        kv_other += [to_member(swap, s) for s in members]

    q_source = jnp.stack([origin(group, t, groups) * gather + member for t in range(groups)])
    blocks = tok_rows // QBLK
    q_block = (q_source[:, None] * blocks + jnp.arange(blocks)[None, :]).reshape(-1)
    q_pick = (q_block[:, None] == jnp.arange(block_mask.shape[0])[None, :]).astype(jnp.float32)
    row_mask = jnp.dot(q_pick, block_mask.astype(jnp.float32))

    def bias_of(swaps):
        device = jnp.stack(
            [
                (origin(group, t, groups) * gather + origin(member, s, gather)) * head_count
                + origin(head_index, z, head_count)
                for s in swaps
                for t in steps
                for z in range(head_count)
            ]
        )
        block = (device[:, None] * cache_rows + jnp.arange(cache_rows)[None, :]).reshape(-1)
        pick = jnp.arange(block_mask.shape[1])[:, None] == (block // CBLK)[None, :]
        seen = jnp.dot(row_mask, pick.astype(jnp.float32))
        return jnp.where(seen > 0.5, 0.0, MASKED).astype(jnp.float32)

    bias = [bias_of([0])] + ([bias_of(members)] if gather > 1 else [])
    away = steps[:-1]
    if groups > 1:
        state = attend(kv, away, [(kv, None)])
        cache, state, bias = lax.optimization_barrier((cache, state, bias))
    sets, last = [(cache, bias[0])], []
    if gather > 1:
        swap = join(cache, cache[0].shape[0])
        sets.append((kv_other, None))
        last = [([to_member(swap, s) for s in members], bias[1])]
    parts = {}
    if groups > 1:
        state = attend(kv, away, sets, state, not last)
        if last:
            state = attend(kv, away, last, state, True)
        parts.update(zip(away, state))
    parts[0] = attend(kv, [0], [(kv, None), *sets, *last], (), True)[0]
    return unpack([from_group(parts[t], t) for t in steps], steps, gather)


def solution(mesh):
    return jax.shard_map(
        functools.partial(per_device, mesh.shape["seq"], mesh.shape["head"]),
        mesh=mesh,
        in_specs=(
            P("seq", "head"),
            P("seq", "head"),
            P("seq", "head"),
            P(("seq", "head"), None),
            P(("seq", "head"), None),
            P(("seq", "head"), None),
            P(("seq", "head"), None),
            P(),
        ),
        out_specs=P("seq", "head"),
        check_vma=False,
    )
```

```python
import functools
import math

import jax
import jax.numpy as jnp
from jax import lax
from jax.experimental import pallas as pl
from jax.experimental.pallas import tpu as pltpu
from jax.sharding import PartitionSpec as P

DH = 128
QBLK = 64
CBLK = 32
SBLK = 4
MASKED = -1e30
SMALL = 8 * 2**20
LARGE = 16 * 2**20


def partner(index, step, count):
    if count & (count - 1) == 0:
        return index ^ step
    return (index + step) % count


def origin(index, step, count):
    if count & (count - 1) == 0:
        return index ^ step
    return (index + count - step) % count


def columns(chunk, width):
    return pl.ds(pl.multiple_of(chunk * width, DH), width)


def vmem(count):
    return [pl.BlockSpec(memory_space=pltpu.VMEM)] * count


def prepare_kernel(groups, gather, shards, *refs):
    new_refs, cache_refs, outs, scratch = refs[:3], refs[3:7], refs[7:-7], refs[-7:]
    pieces, cached = outs[:groups], outs[groups:]
    ck_buf, cv_buf, ke_buf, ve_buf, new_buf, cache_sems, new_sems = scratch
    group, shard = lax.axis_index("seq") // gather, lax.axis_index("head")

    loads = [
        pltpu.make_async_copy(src, dst, cache_sems.at[i])
        for i, (src, dst) in enumerate(zip(cache_refs, (ck_buf, cv_buf, ke_buf, ve_buf)))
    ]
    rows, width = pieces[0].shape[0] // 3, pieces[0].shape[1]
    copies = []
    for i, src in enumerate(new_refs):
        for j in range(2):
            part = pl.ds(j * (rows // 2), rows // 2)
            copies.append(
                pltpu.make_async_copy(src.at[part], new_buf.at[i, part], new_sems.at[i, j])
            )
    for copy in loads + copies:
        copy.start()
    for copy in loads:
        copy.wait()

    blocks, heads = ke_buf.shape
    cache_rows = ck_buf.shape[0]
    exponent = jnp.concatenate(
        [
            jnp.broadcast_to(ref[i : i + 1], (SBLK, heads))
            for ref in (ke_buf, ve_buf)
            for i in range(blocks)
        ],
        axis=0,
    )
    power = jnp.left_shift(1, exponent + 16).astype(jnp.float32) * 2.0**-16
    power = power.astype(jnp.bfloat16)
    head = lax.broadcasted_iota(jnp.int32, (heads, width), 0)
    head -= lax.broadcasted_iota(jnp.int32, (heads, width), 1) // DH
    for t in range(groups):
        for s in range(shards):
            part = partner(shard, s, shards) * groups + partner(group, t, groups)
            spread = (head == part * (width // DH)).astype(jnp.float32).astype(jnp.bfloat16)
            factor = jnp.dot(power, spread, preferred_element_type=jnp.float32)
            for which, buf in enumerate((ck_buf, cv_buf)):
                mantissa = buf[:, columns(part, width)].astype(jnp.float32)
                scaled = mantissa * factor[which * cache_rows : (which + 1) * cache_rows]
                cached[s][t, which] = scaled.astype(jnp.bfloat16)
    for i in range(3):
        for copy in copies[2 * i : 2 * i + 2]:
            copy.wait()
        for t in range(groups):
            cols = columns(partner(group, t, groups), width)
            pieces[t][pl.ds(i * rows, rows)] = new_buf[i, :, cols]


def prepare(q, k, v, ck, cv, ke, ve, groups, gather, shards):
    rows, width = q.shape[0], q.shape[1] // groups
    operands = (k, v, q, ck, cv, ke, ve)
    outs = pl.pallas_call(
        functools.partial(prepare_kernel, groups, gather, shards),
        out_shape=[jax.ShapeDtypeStruct((3 * rows, width), jnp.bfloat16)] * groups
        + [jax.ShapeDtypeStruct((groups, 2, ck.shape[0], width), jnp.bfloat16)] * shards,
        in_specs=[pl.BlockSpec(memory_space=pltpu.HBM)] * len(operands),
        out_specs=vmem(groups + shards),
        scratch_shapes=[pltpu.VMEM(x.shape, x.dtype) for x in (ck, cv, ke, ve)]
        + [pltpu.VMEM((3, *q.shape), q.dtype)]
        + [pltpu.SemaphoreType.DMA((4,)), pltpu.SemaphoreType.DMA((3, 2))],
        compiler_params=pltpu.CompilerParams(vmem_limit_bytes=SMALL),
        cost_estimate=pl.CostEstimate(
            flops=4 * ck.size, bytes_accessed=12 * q.size + 8 * ck.size, transcendentals=0
        ),
        name="prepare",
    )(*[pltpu.with_memory_space_constraint(x, pltpu.HBM) for x in operands])
    return list(outs[:groups]), list(outs[groups:])


def interleave_kernel(*refs):
    rows = refs[0].shape[1]
    for which in range(2):
        for s, ref in enumerate(refs[:-1]):
            refs[-1][pl.ds((which * len(refs[:-1]) + s) * rows, rows)] = ref[which]


def interleave(pieces):
    _, rows, width = pieces[0].shape
    count = len(pieces)
    if rows % 16:
        return jnp.stack(pieces, axis=1).reshape(-1, width)
    return pl.pallas_call(
        interleave_kernel,
        out_shape=jax.ShapeDtypeStruct((2 * count * rows, width), jnp.bfloat16),
        in_specs=vmem(count),
        out_specs=vmem(1)[0],
        compiler_params=pltpu.CompilerParams(vmem_limit_bytes=SMALL),
        cost_estimate=pl.CostEstimate(
            flops=0, bytes_accessed=8 * count * rows * width, transcendentals=0
        ),
        name="interleave",
    )(*pieces)


def join_kernel(rows, *refs):
    for i, ref in enumerate(refs[:-1]):
        refs[-1][i] = ref[pl.ds(0, rows)]


def join(pieces, rows):
    shape = (len(pieces), rows, pieces[0].shape[1])
    return pl.pallas_call(
        functools.partial(join_kernel, rows),
        out_shape=jax.ShapeDtypeStruct(shape, jnp.bfloat16),
        in_specs=vmem(len(pieces)),
        out_specs=vmem(1)[0],
        compiler_params=pltpu.CompilerParams(vmem_limit_bytes=SMALL),
        cost_estimate=pl.CostEstimate(
            flops=0, bytes_accessed=4 * math.prod(shape), transcendentals=0
        ),
        name="join",
    )(*pieces)


def rows_of(refs, start, count, cols):
    parts = []
    for ref in refs:
        if len(ref.shape) == 2:
            parts.append(ref[start : start + count, cols])
        else:
            parts.append(ref[:, start : start + count, cols].reshape(-1, cols.stop - cols.start))
    return parts[0] if len(parts) == 1 else jnp.concatenate(parts, axis=0)


def scores_of(queries, sets, cols):
    scale = math.log2(math.e) / math.sqrt(DH)
    scores = []
    for refs, half, bias in sets:
        x = lax.dot_general(
            queries,
            rows_of(refs, 0, half, cols),
            (((1,), (1,)), ((), ())),
            preferred_element_type=jnp.float32,
        )
        scores.append(x * scale if bias is None else x * scale + bias)
    return scores


def weigh(scores):
    peak = functools.reduce(
        jnp.maximum, [jnp.max(x, axis=1, keepdims=True) for x in scores]
    )
    total, weights = 0.0, []
    for x in scores:
        raised = jnp.exp2(x - peak)
        total += jnp.sum(raised, axis=1, keepdims=True)
        weights.append(raised.astype(jnp.bfloat16))
    return peak, total, weights


def bias_rows(bias_ref, pieces, blocks):
    width = bias_ref.shape[1]
    return jnp.concatenate(
        [
            jnp.broadcast_to(bias_ref[row : row + 1], (QBLK, width))
            for t in pieces
            for row in range(t * blocks, (t + 1) * blocks)
        ],
        axis=0,
    )


def attend_kernel(pieces, counts, q_start, rows, merge, final, *refs):
    q_refs, refs = refs[: len(pieces)], refs[len(pieces) :]
    sets = []
    for count, masked in counts:
        bias = bias_rows(refs[count], pieces, rows // QBLK) if masked else None
        sets.append((refs[:count], refs[0].shape[-2] // 2 if masked else rows, bias))
        refs = refs[count + masked :]
    state, refs = (refs[:3], refs[3:]) if merge else (None, refs)
    width = q_refs[0].shape[1]
    heads = [slice(at, at + DH) for at in range(0, width, DH)]
    weighed = []
    together = heads if len(sets) > 1 or not merge else heads[:1]
    for n in range(0, len(heads), len(together)):
        scores = [
            scores_of(rows_of(q_refs, q_start, rows, cols), sets, cols)
            for cols in heads[n : n + len(together)]
        ]
        weighed += [weigh(x) for x in scores]
    for cols, (peak, total, weights) in zip(heads, weighed):
        product = 0.0
        for x, (refs_of, half, _) in zip(weights, sets):
            product += jnp.dot(
                x, rows_of(refs_of, half, half, cols), preferred_element_type=jnp.float32
            )
        if merge:
            peak_1, total_1, product_1 = [ref[:, cols] for ref in state]
            top = jnp.maximum(peak, peak_1)
            share, share_1 = jnp.exp2(peak - top), jnp.exp2(peak_1 - top)
            total = total * share + total_1 * share_1
            product = product * share + product_1 * share_1
            peak = top
        if final:
            result = (product / total).astype(jnp.bfloat16)
            for i in range(len(pieces)):
                refs[i][:, cols] = result[i * rows : (i + 1) * rows]
        else:
            for ref, x in zip(refs, (peak, total, product)):
                ref[:, cols] = jnp.broadcast_to(x, product.shape)


def attend(q, pieces, sets, state=(), final=False):
    groups = len(pieces)
    rows, width = q[0].shape[0] // 3, q[0].shape[1]
    count = 0
    for arrays, bias in sets:
        for x in arrays:
            stacked = x.shape[0] if x.ndim == 3 else 1
            count += stacked * (rows if bias is None else x.shape[-2] // 2)
    if final:
        out_shape = [jax.ShapeDtypeStruct((rows, width), jnp.bfloat16)] * groups
    else:
        out_shape = [jax.ShapeDtypeStruct((groups * rows, width), jnp.float32)] * 3
    operands = [q[t] for t in pieces]
    for arrays, bias in sets:
        operands += [*arrays] if bias is None else [*arrays, bias]
    operands += state
    return pl.pallas_call(
        functools.partial(
            attend_kernel,
            tuple(pieces),
            tuple((len(arrays), bias is not None) for arrays, bias in sets),
            2 * rows,
            rows,
            bool(state),
            final,
        ),
        out_shape=out_shape,
        in_specs=vmem(len(operands)),
        out_specs=vmem(len(out_shape)),
        compiler_params=pltpu.CompilerParams(vmem_limit_bytes=LARGE),
        cost_estimate=pl.CostEstimate(
            flops=4 * groups * rows * count * width,
            bytes_accessed=4 * count * width,
            transcendentals=groups * rows * count * width // DH,
        ),
        name="attend",
    )(*operands)


def unpack_kernel(steps, gather, width, *refs):
    groups = len(steps)
    parts, out_ref, sems = refs[:groups], refs[groups], refs[groups + 1]
    me = lax.axis_index("seq") // gather
    copies = [
        pltpu.make_async_copy(
            parts[i], out_ref.at[:, columns(partner(me, t, groups), width)], sems.at[i]
        )
        for i, t in enumerate(steps)
    ]
    for copy in copies:
        copy.start()
    for copy in copies:
        copy.wait()


def unpack(parts, steps, gather):
    rows, width = parts[0].shape
    groups = len(steps)
    return pl.pallas_call(
        functools.partial(unpack_kernel, tuple(steps), gather, width),
        out_shape=jax.ShapeDtypeStruct((rows, groups * width), jnp.bfloat16),
        in_specs=vmem(groups),
        out_specs=pl.BlockSpec(memory_space=pl.ANY),
        scratch_shapes=[pltpu.SemaphoreType.DMA((groups,))],
        compiler_params=pltpu.CompilerParams(vmem_limit_bytes=SMALL),
        cost_estimate=pl.CostEstimate(
            flops=0, bytes_accessed=4 * groups * rows * width, transcendentals=0
        ),
        name="unpack_heads",
    )(*parts)


def per_device(
    seq_count,
    head_count,
    query_new,
    key_new,
    value_new,
    cache_keys,
    cache_values,
    key_exponent,
    value_exponent,
    block_mask,
):
    tok_rows, width_dev = query_new.shape
    groups = math.gcd(width_dev // DH, seq_count)
    gather = seq_count // groups
    width = width_dev // groups
    cache_rows = cache_keys.shape[0]
    seq_index = lax.axis_index("seq")
    head_index = lax.axis_index("head")
    group, member = seq_index // gather, seq_index % gather

    def to_group(x, t):
        if t == 0:
            return x
        pairs = [
            (s, partner(s // gather, t, groups) * gather + s % gather) for s in range(seq_count)
        ]
        return lax.ppermute(x, "seq", pairs)

    def from_group(x, t):
        if t == 0:
            return x
        pairs = [
            (s, origin(s // gather, t, groups) * gather + s % gather) for s in range(seq_count)
        ]
        return lax.ppermute(x, "seq", pairs)

    def to_member(x, t):
        pairs = [
            (s, s // gather * gather + partner(s % gather, t, gather)) for s in range(seq_count)
        ]
        return lax.ppermute(x, "seq", pairs)

    def to_head(x, t):
        if t == 0:
            return x
        return lax.ppermute(x, "head", [(h, partner(h, t, head_count)) for h in range(head_count)])

    members = range(1, gather)
    every = range(groups)
    steps = [*every[-1:], *every[1:-1], *every[:1]] if groups > 1 else [0]
    kv_own, stored = prepare(
        query_new,
        key_new,
        value_new,
        cache_keys,
        cache_values,
        key_exponent,
        value_exponent,
        groups,
        gather,
        head_count,
    )
    kv_other = [to_member(kv_own[0][: 2 * tok_rows], s) for s in members]
    if gather > 1:
        kv_own[1:-1], stored, kv_other[0] = lax.optimization_barrier(
            (kv_own[1:-1], stored, kv_other[0])
        )
    kv = [to_group(kv_own[t], t) for t in range(groups)]
    by_head = []
    for s in range(head_count):
        x = stored[s]
        if s > 2:
            x, by_head[s - 2] = lax.optimization_barrier((x, by_head[s - 2]))
        by_head.append(to_head(x, s))
    kv[1:] = [lax.optimization_barrier((x, by_head))[0] for x in kv[1:]]
    block_mask, group, member, head_index, _ = lax.optimization_barrier(
        (block_mask, group, member, head_index, kv[1:])
    )
    cache = [to_group(interleave([x[t] for x in by_head]), t) for t in steps]
    if groups > 1:
        swap = join(kv[1:], 2 * tok_rows)
        kv_other += [to_member(swap, s) for s in members]

    q_source = jnp.stack([origin(group, t, groups) * gather + member for t in range(groups)])
    blocks = tok_rows // QBLK
    q_block = (q_source[:, None] * blocks + jnp.arange(blocks)[None, :]).reshape(-1)
    q_pick = (q_block[:, None] == jnp.arange(block_mask.shape[0])[None, :]).astype(jnp.float32)
    row_mask = jnp.dot(q_pick, block_mask.astype(jnp.float32))

    def bias_of(swaps):
        device = jnp.stack(
            [
                (origin(group, t, groups) * gather + origin(member, s, gather)) * head_count
                + origin(head_index, z, head_count)
                for s in swaps
                for t in steps
                for z in range(head_count)
            ]
        )
        block = (device[:, None] * cache_rows + jnp.arange(cache_rows)[None, :]).reshape(-1)
        pick = jnp.arange(block_mask.shape[1])[:, None] == (block // CBLK)[None, :]
        seen = jnp.dot(row_mask, pick.astype(jnp.float32))
        return jnp.where(seen > 0.5, 0.0, MASKED).astype(jnp.float32)

    bias = [bias_of([0])] + ([bias_of(members)] if gather > 1 else [])
    away = steps[:-1]
    if groups > 1:
        state = attend(kv, away, [(kv, None)])
        cache, state, bias = lax.optimization_barrier((cache, state, bias))
    sets, last = [(cache, bias[0])], []
    if gather > 1:
        swap = join(cache, cache[0].shape[0])
        sets.append((kv_other, None))
        last = [([to_member(swap, s) for s in members], bias[1])]
    parts = {}
    if groups > 1:
        state = attend(kv, away, sets, state, not last)
        if last:
            state = attend(kv, away, last, state, True)
        parts.update(zip(away, state))
    parts[0] = attend(kv, [0], [(kv, None), *sets, *last], (), True)[0]
    return unpack([from_group(parts[t], t) for t in steps], steps, gather)


def solution(mesh):
    return jax.shard_map(
        functools.partial(per_device, mesh.shape["seq"], mesh.shape["head"]),
        mesh=mesh,
        in_specs=(
            P("seq", "head"),
            P("seq", "head"),
            P("seq", "head"),
            P(("seq", "head"), None),
            P(("seq", "head"), None),
            P(("seq", "head"), None),
            P(("seq", "head"), None),
            P(),
        ),
        out_specs=P("seq", "head"),
        check_vma=False,
    )
```
